32 devices in a mesh: blk: 8 (over z, y), grp: 4 (over x, core).
Axes of the slice: x: 2, y: 2, z: 4, core: 2. Of those that a mesh axis runs over, the one named last changes fastest.
Arguments:
- inputs: bfloat16 [4, 1024, 1024], P('grp', 'blk'), may hold values from -6 to 6
- skipped: bfloat16 [4, 1024, 1024], P('grp', 'blk'), may hold values from -6 to 6
- w_skip: bfloat16 [2048, 1024], P('grp'), may hold values from -0.125 to 0.125
- w_mod: bfloat16 [1024, 2048], P('grp'), may hold values from -0.1875 to 0.1875
- w_qkv: bfloat16 [1024, 3072], P('grp'), may hold values from -0.1875 to 0.1875
- w_out: bfloat16 [1024, 1024], P('grp'), may hold values from -12 to 12
- ff_gain: bfloat16 [1024], P('grp'), may hold values from 0.099609375 to 1.8984375
- w_up: bfloat16 [1024, 4096], P('grp'), may hold values from -0.1875 to 0.1875
- w_down: bfloat16 [4096, 1024], P('grp'), may hold values from -0.09375 to 0.09375
- cotangent: bfloat16 [4, 1024, 1024], P('grp', 'blk'), may hold values from -6 to 6
- lengths: int32 [4, 8], P('grp'), may hold values from 1 to 960, 1024 in all within a row
- flow_steps: int32 [4, 8], P('grp'), may hold values from 0 to 31
Outputs:
- output: bfloat16 [4, 1024, 1024], P('grp', 'blk')
- grad_inputs: float32 [4, 1024, 1024], P('grp', 'blk')
- grad_skipped: float32 [4, 1024, 1024], P('grp', 'blk')
- grad_w_skip: float32 [2048, 1024], P('grp')
- grad_w_mod: float32 [1024, 2048], P('grp')
- grad_w_qkv: float32 [1024, 3072], P('grp')
- grad_w_out: float32 [1024, 1024], P('grp')
- grad_ff_gain: float32 [1024], P('grp')
- grad_w_up: float32 [1024, 4096], P('grp')
- grad_w_down: float32 [4096, 1024], P('grp')
The draws below stay inside these ranges and needn't reach their ends.
Inputs may be any that keep to these rules, and one draw needn't show every extreme that they name: Each row's lengths sum to 1024; the longest utterance of a row has exactly 960 frames.
All inputs are finite; a program needn't handle non-finite values.
Results may differ from the reference program's by a relative error of at most 0.018.
Values may be sent and summed in bfloat16 or wider, within the bound.
A program may use at most 192 MiB of HBM per device.

```python
import math
import jax
import jax.numpy as jnp
import numpy as np
from jax import lax

D = 1024
HEADS = 16
HEAD_DIM = 64
FF = 4096
FR_DEV = 128
NUTT = 8
STEPS = 32
ROWS = 4
FRAMES = 1024
N_BLK = 8


def place_ends(values, own_key, low, top_value):
    longest = values.shape.index(max(values.shape))
    spots = []
    for shift in (0, 1):
        where = [jax.random.randint(jax.random.fold_in(own_key, axis), (), 0, length) for axis, length in enumerate(values.shape)]
        where[longest] = (where[longest] + shift) % values.shape[longest]
        spots.append(tuple(where))
    return values.at[spots[0]].set(low).at[spots[1]].set(top_value)


def shard_levels(key, shape, pieces, smallest, top_value):
    loudness = 1.0
    for dim, shards_of in pieces:
        heights = jax.random.uniform(jax.random.fold_in(jax.random.fold_in(key, 6), dim), (shards_of,), jnp.float32, smallest / len(pieces), top_value / len(pieces))
        loudness = loudness * jnp.repeat(jnp.exp(heights), shape[dim] // shards_of).reshape((-1,) + (1,) * (len(shape) - 1 - dim))
    return loudness


def length_profile(number_of, total, reach, lean):
    weights = [(1 << 20) // math.isqrt(grade ** lean) + 1 for grade in range(2, number_of + 1)]
    spare, holding = total - reach - (number_of - 1), [1] * (number_of - 1)
    while spare > 0:
        movable = [i for i in range(number_of - 1) if holding[i] < reach]
        whole, remaining = sum([weights[i] for i in movable]), spare
        for i in movable:
            extra = min(reach - holding[i], max(1, remaining * weights[i] // whole), spare)
            holding[i] = holding[i] + extra
            spare = spare - extra
    return np.array([reach] + holding)


def uneven_parts(stream_key, amount, total, bound, lean):
    if amount == 2:
        one = jax.random.randint(stream_key, (), max(1, total - bound), min(bound, total - 1) + 1)
        return jnp.stack([one, total - one])
    tallies = jnp.asarray(length_profile(amount, total, bound, lean), jnp.int32)
    pairs = (amount - 1) // 2
    source_of, taker = tallies[1:1 + 2 * pairs:2], tallies[2:2 + 2 * pairs:2]
    room = jnp.minimum(source_of - 1, bound - taker)
    passed = jax.random.randint(jax.random.fold_in(stream_key, 1), (pairs,), 0, 1 << 20) % (room + 1)
    tallies = tallies.at[1:1 + 2 * pairs:2].set(source_of - passed).at[2:2 + 2 * pairs:2].set(taker + passed)
    return tallies[jax.random.permutation(jax.random.fold_in(stream_key, 2), amount)]


def noise(rng, shape, scale, limit, shards=(), kind=jnp.bfloat16):
    result = scale * jax.random.normal(rng, shape, jnp.float32)
    if shards:
        result = result * shard_levels(rng, shape, shards, -0.22, 0.18)
    return jnp.clip(result, -limit, limit).astype(kind)


def setup_inputs(seed: int = 0) -> dict:
    key_of = jax.random.split(jax.random.key(seed), 13)
    return {
        "inputs": noise(key_of[0], (ROWS, FRAMES, D), 1.0, 6.0, ((0, 4), (1, 8))),
        "skipped": noise(key_of[1], (ROWS, FRAMES, D), 1.0, 6.0, ((0, 4), (1, 8))),
        "w_skip": noise(key_of[2], (2 * D, D), (2 * D) ** -0.5, 0.125, ((0, 4),)),
        "w_mod": noise(key_of[3], (D, 2 * D), D ** -0.5, 0.1875, ((0, 4),)),
        "w_qkv": noise(key_of[4], (D, 3 * D), D ** -0.5, 0.1875, ((0, 4),)),
        "w_out": noise(key_of[5], (D, D), 2.0, 12.0, ((0, 4),)),
        "ff_gain": jnp.clip(1.0 + 0.18 * jax.random.normal(key_of[6], (D,), jnp.float32), 0.099609375, 1.8984375).astype(jnp.bfloat16),
        "w_up": noise(key_of[7], (D, FF), D ** -0.5, 0.1875, ((0, 4),)),
        "w_down": noise(key_of[8], (FF, D), FF ** -0.5, 0.09375, ((0, 4),)),
        "cotangent": noise(key_of[9], (ROWS, FRAMES, D), 1.0, 6.0, ((0, 4), (1, 8))),
        "lengths": jax.vmap(lambda own: uneven_parts(own, NUTT, FR_DEV * N_BLK, FR_DEV * N_BLK - FR_DEV // 2, 2))(jax.random.split(key_of[10], ROWS)).reshape((ROWS, NUTT)).astype(jnp.int32),
        "flow_steps": place_ends(jax.random.randint(key_of[11], (ROWS, NUTT), 0, STEPS), jax.random.fold_in(key_of[11], 1), 0, STEPS - 1).astype(jnp.int32),
    }


EPSILON = 1e-06
NEGATIVE = -1e+30
HIGHEST = lax.Precision.HIGHEST

@jax.custom_vjp
def low(v):
    return lax.optimization_barrier(v.astype(jnp.bfloat16)).astype(jnp.float32)

@jax.custom_vjp
def low_back(v):
    return v

def low_keep(v):
    return (low(v), None)

def low_pass(kept, grad):
    return (grad,)

def back_keep(v):
    return (v, None)

def back_low(kept, grad):
    return (low(grad),)
low.defvjp(low_keep, low_pass)
low_back.defvjp(back_keep, back_low)

def layout(lengths_row, frames):
    end_frame = jnp.cumsum(lengths_row).astype(jnp.int32)
    start_frame = (end_frame - lengths_row).astype(jnp.int32)
    segment = lax.optimization_barrier(jnp.sum((frames[:, None] >= end_frame[None, :]).astype(jnp.int32), axis=1)).astype(jnp.int32)
    chosen = segment[:, None] == jnp.arange(lengths_row.shape[0], dtype=jnp.int32)[None, :]
    position = (frames - lax.optimization_barrier(jnp.sum(jnp.where(chosen, start_frame[None, :], 0), axis=1))).astype(jnp.int32)
    return (segment, position)

def flow_condition(steps_row, model_width):
    half_width = model_width // 2
    rate_table = jnp.exp(-math.log(10000.0) * jnp.arange(half_width, dtype=jnp.float32) / half_width)
    angles = 1000.0 * (steps_row.astype(jnp.float32) / STEPS)[:, None] * rate_table[None, :]
    return jax.nn.silu(jnp.concatenate([jnp.sin(angles), jnp.cos(angles)], axis=1))

def rotate(head_block, position):
    half_width = head_block.shape[-1] // 2
    rate_table = jnp.exp(-math.log(10000.0) * jnp.arange(half_width, dtype=jnp.float32) / half_width)
    angles = position.astype(jnp.float32)[:, None] * rate_table[None, :]
    cosine_part = jnp.cos(angles)[:, None, :]
    sine_part = jnp.sin(angles)[:, None, :]
    first_half = head_block[..., :half_width]
    second_half = head_block[..., half_width:]
    return jnp.concatenate([first_half * cosine_part - second_half * sine_part, second_half * cosine_part + first_half * sine_part], axis=-1)

def normalize(hidden):
    centred = hidden - lax.optimization_barrier(jnp.mean(hidden, axis=-1, keepdims=True))
    scaled = lax.rsqrt(lax.optimization_barrier(jnp.mean(centred * centred, axis=-1, keepdims=True)) + EPSILON)
    return (centred * scaled, scaled)

def attention(queries, keys, values, segment):
    block_rows = min(512, FRAMES)
    blocks = FRAMES // block_rows
    score_scale = HEAD_DIM ** (-0.5)

    def one_block(inputs_pair):
        query_block, segment_block = inputs_pair
        scores = low_back(jnp.einsum('qhd,khd->hqk', query_block, keys, precision=HIGHEST) * score_scale)
        allowed = (segment_block[:, None] == segment[None, :])[None]
        scores = jnp.where(allowed, scores, NEGATIVE)
        weights = jnp.exp(scores - lax.optimization_barrier(jnp.max(scores, axis=2, keepdims=True)))
        weights = low(weights / lax.optimization_barrier(jnp.sum(weights, axis=2, keepdims=True)))
        return jnp.einsum('hqk,khd->qhd', weights, values, precision=HIGHEST)
    outputs = lax.map(jax.checkpoint(one_block), (queries.reshape(blocks, block_rows, HEADS, HEAD_DIM), segment.reshape(blocks, block_rows)))
    return outputs.reshape(FRAMES, HEADS * HEAD_DIM)

def row_forward(weight_set, inputs_row, skipped_row, lengths_row, steps_row):
    w_skip, w_mod, w_qkv, w_out, ff_gain, w_up, w_down = weight_set
    frames = jnp.arange(FRAMES, dtype=jnp.int32)
    segment, position = layout(lengths_row, frames)
    joined = jnp.concatenate([inputs_row, skipped_row], axis=1)
    hidden = low_back(jnp.dot(joined, w_skip, precision=HIGHEST))
    condition = low(flow_condition(steps_row, D))
    modulation = jnp.dot(condition, w_mod, precision=HIGHEST)
    picker = (segment[:, None] == jnp.arange(NUTT, dtype=jnp.int32)[None, :]).astype(jnp.float32)
    per_frame = jnp.dot(picker, modulation, precision=HIGHEST)
    normal_one, unused = normalize(hidden)
    attn_in = low(normal_one * (1.0 + per_frame[:, :D]) + per_frame[:, D:])
    project = low_back(jnp.dot(attn_in, w_qkv, precision=HIGHEST)).reshape(FRAMES, 3, HEADS, HEAD_DIM)
    queries = low(rotate(project[:, 0], position))
    keys = low(rotate(project[:, 1], position))
    values = low(project[:, 2])
    attended = low(low_back(attention(queries, keys, values, segment)))
    hidden_two = hidden + low_back(jnp.dot(attended, w_out, precision=HIGHEST))
    normal_two, unused = normalize(hidden_two)
    widened = low_back(jnp.dot(low(normal_two * ff_gain), w_up, precision=HIGHEST))
    activated = low(jax.nn.gelu(widened, approximate=False))
    return hidden_two + jnp.dot(activated, w_down, precision=HIGHEST)

def to_float(array_value):
    return array_value.astype(jnp.float32)

def reference(inputs, skipped, w_skip, w_mod, w_qkv, w_out, ff_gain, w_up, w_down, cotangent, lengths, flow_steps):
    floats = tuple(map(to_float, (inputs, skipped, w_skip, w_mod, w_qkv, w_out, ff_gain, w_up, w_down)))

    def whole(inputs_f, skipped_f, *weight_set):

        def row_step(carried, row_data):
            return (carried, row_forward(weight_set, *row_data))
        unused, outputs = lax.scan(row_step, jnp.float32(0.0), (inputs_f, skipped_f, lengths, flow_steps))
        return outputs
    outputs, pullback = jax.vjp(whole, *floats)
    gradients = pullback(cotangent.astype(jnp.float32))
    return (outputs.astype(jnp.bfloat16), gradients[0], gradients[1], gradients[2], gradients[3], gradients[4], gradients[5], gradients[6], gradients[7], gradients[8])
```

```python
import math

import jax
import jax.numpy as jnp
from jax import lax
from jax.sharding import PartitionSpec as P

HEADS = 16
HEAD_DIM = 64
STEPS = 32


EPSILON = 1e-06
NEGATIVE = -1e30
HIGHEST = lax.Precision.HIGHEST


def from_behind(block, axis, distance):
    devices = range(lax.axis_size(axis))
    route = [((i - distance) % len(devices), i) for i in devices]
    return lax.ppermute(block, axis, route)


def layout(lengths_row, frames):
    end_frame = jnp.cumsum(lengths_row)
    start_frame = end_frame - lengths_row
    segment = jnp.sum((frames[:, None] >= end_frame[None, :]).astype(jnp.int32), axis=1)
    chosen = segment[:, None] == jnp.arange(lengths_row.shape[0], dtype=jnp.int32)[None, :]
    position = frames - jnp.sum(jnp.where(chosen, start_frame[None, :], 0), axis=1)
    return (segment, position)


def flow_condition(steps_row, model_width):
    half_width = model_width // 2
    rate_table = jnp.exp(
        -math.log(10000.0) * jnp.arange(half_width, dtype=jnp.float32) / half_width
    )
    angles = 1000.0 * (steps_row.astype(jnp.float32) / STEPS)[:, None] * rate_table[None, :]
    return jax.nn.silu(jnp.concatenate([jnp.sin(angles), jnp.cos(angles)], axis=1))


def rotation_tables(position, head_width):
    half_width = head_width // 2
    rate_table = jnp.exp(
        -math.log(10000.0) * jnp.arange(half_width, dtype=jnp.float32) / half_width
    )
    angles = position.astype(jnp.float32)[:, None] * rate_table[None, :]
    return (jnp.cos(angles)[:, None, :], jnp.sin(angles)[:, None, :], half_width)


def rotate(head_block, position):
    cosine_part, sine_part, half_width = rotation_tables(position, head_block.shape[-1])
    first_half = head_block[..., :half_width]
    second_half = head_block[..., half_width:]
    return jnp.concatenate(
        [
            first_half * cosine_part - second_half * sine_part,
            second_half * cosine_part + first_half * sine_part,
        ],
        axis=-1,
    )


def rotate_back(head_block, position):
    cosine_part, sine_part, half_width = rotation_tables(position, head_block.shape[-1])
    first_half = head_block[..., :half_width]
    second_half = head_block[..., half_width:]
    return jnp.concatenate(
        [
            first_half * cosine_part + second_half * sine_part,
            second_half * cosine_part - first_half * sine_part,
        ],
        axis=-1,
    )


def normalize(hidden):
    centred = hidden - jnp.mean(hidden, axis=-1, keepdims=True)
    scaled = lax.rsqrt(jnp.mean(centred * centred, axis=-1, keepdims=True) + EPSILON)
    return (centred * scaled, scaled)


def norm_back(grad_normal, normal, scaled):
    centred_grad = grad_normal - jnp.mean(grad_normal, axis=-1, keepdims=True)
    return scaled * (centred_grad - normal * jnp.mean(grad_normal * normal, axis=-1, keepdims=True))


def exact_gelu(values_in):
    return jax.nn.gelu(values_in, approximate=False)


def contract_rows(left_side, right_side):
    return lax.dot_general(
        left_side, right_side, (((0,), (0,)), ((), ())), preferred_element_type=jnp.float32
    )


def heads_of(flat_block):
    return flat_block.reshape(flat_block.shape[0], HEADS, HEAD_DIM)


def per_device(
    inputs,
    skipped,
    w_skip,
    w_mod,
    w_qkv,
    w_out,
    ff_gain,
    w_up,
    w_down,
    cotangent,
    lengths,
    flow_steps,
):
    w_skip, w_mod, w_qkv, w_out, ff_gain, w_up, w_down = (
        lax.all_gather(w_skip, "grp", axis=0, tiled=True),
        lax.all_gather(w_mod, "grp", axis=0, tiled=True),
        lax.all_gather(w_qkv, "grp", axis=0, tiled=True),
        lax.all_gather(w_out, "grp", axis=0, tiled=True),
        lax.all_gather(ff_gain, "grp", axis=0, tiled=True),
        lax.all_gather(w_up, "grp", axis=0, tiled=True),
        lax.all_gather(w_down, "grp", axis=0, tiled=True),
    )
    frame_count = inputs.shape[1]
    model_width = inputs.shape[2]
    cycle_size = lax.axis_size("blk")
    device_rank = lax.axis_index("blk")
    score_scale = HEAD_DIM ** (-0.5)
    local_frames = jnp.arange(frame_count, dtype=jnp.int32)
    lengths_row = lengths[0]
    own_segment, own_position = layout(lengths_row, device_rank * frame_count + local_frames)

    def segment_of(source):
        return layout(lengths_row, source * frame_count + local_frames)[0]

    def scored(query_block, key_block, query_segment, key_segment):
        raw_scores = (
            jnp.einsum(
                "qhd,khd->hqk",
                heads_of(query_block),
                heads_of(key_block),
                preferred_element_type=jnp.float32,
            )
            * score_scale
        )
        allowed = (query_segment[:, None] == key_segment[None, :])[None]
        return (raw_scores, allowed)

    joined = jnp.concatenate([inputs[0], skipped[0]], axis=1)
    hidden = jnp.dot(joined, w_skip, preferred_element_type=jnp.float32)
    condition = flow_condition(flow_steps[0], model_width).astype(jnp.bfloat16)
    modulation = jnp.dot(condition, w_mod, preferred_element_type=jnp.float32)
    picker = (
        own_segment[:, None] == jnp.arange(lengths_row.shape[0], dtype=jnp.int32)[None, :]
    ).astype(jnp.float32)
    per_frame = jnp.dot(picker, modulation, precision=HIGHEST)
    scale_one = 1.0 + per_frame[:, :model_width]
    normal_one, spread_one = normalize(hidden)
    attn_in = (normal_one * scale_one + per_frame[:, model_width:]).astype(jnp.bfloat16)
    project = jnp.dot(attn_in, w_qkv, preferred_element_type=jnp.float32).reshape(
        frame_count, 3, HEADS, HEAD_DIM
    )
    queries = (
        rotate(project[:, 0], own_position).astype(jnp.bfloat16).reshape(frame_count, model_width)
    )
    keys_own = (
        rotate(project[:, 1], own_position).astype(jnp.bfloat16).reshape(frame_count, model_width)
    )
    values_own = project[:, 2].astype(jnp.bfloat16).reshape(frame_count, model_width)

    def forward_turn(turn_index, carried):
        key_now, value_now, running_top, running_total, running_sum = carried
        source = (device_rank - turn_index) % cycle_size
        raw_scores, allowed = scored(queries, key_now, own_segment, segment_of(source))
        raw_scores = jnp.where(allowed, raw_scores, NEGATIVE)
        new_top = jnp.maximum(running_top, jnp.max(raw_scores, axis=2, keepdims=True))
        weights = jnp.where(allowed, jnp.exp(raw_scores - new_top), 0.0)
        shrink = jnp.exp(running_top - new_top)
        running_total = running_total * shrink + jnp.sum(weights, axis=2, keepdims=True)
        running_sum = running_sum * shrink + jnp.einsum(
            "hqk,khd->hqd",
            weights.astype(jnp.bfloat16),
            heads_of(value_now),
            preferred_element_type=jnp.float32,
        )
        key_now, value_now = from_behind((key_now, value_now), "blk", 1)
        return (key_now, value_now, new_top, running_total, running_sum)

    initial = (
        keys_own,
        values_own,
        jnp.full((HEADS, frame_count, 1), NEGATIVE, jnp.float32),
        jnp.zeros((HEADS, frame_count, 1), jnp.float32),
        jnp.zeros((HEADS, frame_count, HEAD_DIM), jnp.float32),
    )
    finished = lax.fori_loop(0, cycle_size, forward_turn, initial)
    running_top, running_total, running_sum = (finished[2], finished[3], finished[4])
    attended = jnp.transpose(running_sum / running_total, (1, 0, 2)).reshape(
        frame_count, model_width
    )
    log_total = (running_top + jnp.log(running_total))[:, :, 0]
    attended_low = attended.astype(jnp.bfloat16)
    hidden_two = hidden + jnp.dot(attended_low, w_out, preferred_element_type=jnp.float32)
    normal_two, spread_two = normalize(hidden_two)
    gain_vector = ff_gain.astype(jnp.float32)
    ff_in = (normal_two * gain_vector).astype(jnp.bfloat16)
    widened = jnp.dot(ff_in, w_up, preferred_element_type=jnp.float32)
    activated, gelu_back = jax.vjp(exact_gelu, widened)
    activated_low = activated.astype(jnp.bfloat16)
    output = (
        hidden_two + jnp.dot(activated_low, w_down, preferred_element_type=jnp.float32)
    ).astype(jnp.bfloat16)
    upstream = cotangent[0]
    grad_down = contract_rows(activated_low, upstream)
    grad_activated = jnp.dot(upstream, w_down.T, preferred_element_type=jnp.float32)
    grad_widened = gelu_back(grad_activated)[0].astype(jnp.bfloat16)
    grad_up = contract_rows(ff_in, grad_widened)
    grad_ff_in = jnp.dot(grad_widened, w_up.T, preferred_element_type=jnp.float32)
    grad_gain = jnp.sum(grad_ff_in * normal_two, axis=0)
    grad_hidden_two = upstream.astype(jnp.float32) + norm_back(
        grad_ff_in * gain_vector, normal_two, spread_two
    )
    grad_two_low = grad_hidden_two.astype(jnp.bfloat16)
    grad_out = contract_rows(attended_low, grad_two_low)
    grad_attended = jnp.dot(grad_two_low, w_out.T, preferred_element_type=jnp.float32).astype(
        jnp.bfloat16
    )
    delta = jnp.transpose(jnp.sum(heads_of(grad_attended.astype(jnp.float32) * attended), axis=2))
    zero_grad = jnp.zeros((frame_count, model_width), jnp.float32)

    def pair_terms(
        query_block,
        upstream_block,
        key_block,
        value_block,
        total_block,
        delta_block,
        query_segment,
        key_segment,
    ):
        raw_scores, allowed = scored(query_block, key_block, query_segment, key_segment)
        prob_block = jnp.where(allowed, jnp.exp(raw_scores - total_block[:, :, None]), 0.0)
        value_term = jnp.einsum(
            "hqk,qhd->khd",
            prob_block.astype(jnp.bfloat16),
            heads_of(upstream_block),
            preferred_element_type=jnp.float32,
        ).reshape(frame_count, model_width)
        prob_grad = jnp.einsum(
            "qhd,khd->hqk",
            heads_of(upstream_block),
            heads_of(value_block),
            preferred_element_type=jnp.float32,
        )
        score_grad = (prob_block * (prob_grad - delta_block[:, :, None])).astype(jnp.bfloat16)
        query_term = (
            jnp.einsum(
                "hqk,khd->qhd", score_grad, heads_of(key_block), preferred_element_type=jnp.float32
            ).reshape(frame_count, model_width)
            * score_scale
        )
        key_term = (
            jnp.einsum(
                "hqk,qhd->khd",
                score_grad,
                heads_of(query_block),
                preferred_element_type=jnp.float32,
            ).reshape(frame_count, model_width)
            * score_scale
        )
        return (query_term, key_term, value_term)

    def keys_turn(turn_index, carried):
        key_now, value_now, key_grad, value_grad, query_grad = carried
        source = (device_rank - turn_index) % cycle_size
        query_term, key_term, value_term = pair_terms(
            queries,
            grad_attended,
            key_now,
            value_now,
            log_total,
            delta,
            own_segment,
            segment_of(source),
        )
        key_now, value_now = from_behind((key_now, value_now), "blk", 1)
        key_grad, value_grad = (
            from_behind((key_grad + key_term).astype(jnp.bfloat16), "blk", 1).astype(jnp.float32),
            from_behind((value_grad + value_term).astype(jnp.bfloat16), "blk", 1).astype(
                jnp.float32
            ),
        )
        return (key_now, value_now, key_grad, value_grad, query_grad + query_term)

    done = lax.fori_loop(
        0, cycle_size, keys_turn, (keys_own, values_own, zero_grad, zero_grad, zero_grad)
    )
    key_grad, value_grad, query_grad = (done[2], done[3], done[4])
    grad_project = jnp.concatenate(
        [
            rotate_back(heads_of(query_grad), own_position).reshape(frame_count, model_width),
            rotate_back(heads_of(key_grad), own_position).reshape(frame_count, model_width),
            value_grad,
        ],
        axis=1,
    ).astype(jnp.bfloat16)
    grad_qkv = contract_rows(attn_in, grad_project)
    grad_attn_in = jnp.dot(grad_project, w_qkv.T, preferred_element_type=jnp.float32)
    mod_terms = jnp.concatenate([grad_attn_in * normal_one, grad_attn_in], axis=1)
    grad_modulation = jnp.dot(picker.T, mod_terms, precision=HIGHEST)
    grad_mod = jnp.dot(condition.astype(jnp.float32).T, grad_modulation, precision=HIGHEST)
    grad_hidden = grad_hidden_two + norm_back(grad_attn_in * scale_one, normal_one, spread_one)
    grad_hidden_low = grad_hidden.astype(jnp.bfloat16)
    grad_skip_weight = contract_rows(joined, grad_hidden_low)
    grad_joined = jnp.dot(grad_hidden_low, w_skip.T, preferred_element_type=jnp.float32)
    shards = (
        lax.psum_scatter(
            grad_skip_weight.astype(jnp.bfloat16), "grp", scatter_dimension=0, tiled=True
        ).astype(jnp.float32),
        lax.psum_scatter(
            grad_mod.astype(jnp.bfloat16), "grp", scatter_dimension=0, tiled=True
        ).astype(jnp.float32),
        lax.psum_scatter(
            grad_qkv.astype(jnp.bfloat16), "grp", scatter_dimension=0, tiled=True
        ).astype(jnp.float32),
        lax.psum_scatter(
            grad_out.astype(jnp.bfloat16), "grp", scatter_dimension=0, tiled=True
        ).astype(jnp.float32),
        lax.psum_scatter(
            grad_gain.astype(jnp.bfloat16), "grp", scatter_dimension=0, tiled=True
        ).astype(jnp.float32),
        lax.psum_scatter(
            grad_up.astype(jnp.bfloat16), "grp", scatter_dimension=0, tiled=True
        ).astype(jnp.float32),
        lax.psum_scatter(
            grad_down.astype(jnp.bfloat16), "grp", scatter_dimension=0, tiled=True
        ).astype(jnp.float32),
    )
    totals = lax.psum(
        (shards[0], shards[1], shards[2], shards[3], shards[4], shards[5], shards[6]), "blk"
    )
    return (
        output[None],
        grad_joined[:, :model_width][None],
        grad_joined[:, model_width:][None],
        totals[0],
        totals[1],
        totals[2],
        totals[3],
        totals[4],
        totals[5],
        totals[6],
    )


def rows_dot(left_side, right_side):
    return jnp.dot(left_side, right_side, preferred_element_type=jnp.float32)


def dot_columns(left_side, right_side):
    return lax.dot_general(
        left_side, right_side, (((1,), (1,)), ((), ())), preferred_element_type=jnp.float32
    )


def summed_rows(partial, axis="grp"):
    return lax.psum_scatter(
        partial.astype(jnp.bfloat16), axis, scatter_dimension=0, tiled=True
    ).astype(jnp.float32)


def gathered(block, axis="grp"):
    return lax.all_gather(block, axis, axis=0, tiled=True)


def per_device_shards(
    inputs,
    skipped,
    w_skip,
    w_mod,
    w_qkv,
    w_out,
    ff_gain,
    w_up,
    w_down,
    cotangent,
    lengths,
    flow_steps,
):
    frame_count = inputs.shape[1]
    model_width = inputs.shape[2]
    rows = lax.axis_size("grp")
    blocks = lax.axis_size("blk")
    group_rank = lax.axis_index("grp")
    block_rank = lax.axis_index("blk")
    tokens = rows * frame_count
    heads_here = HEADS // rows
    columns_here = model_width // rows
    pairs_per_row = blocks // rows
    pair_heads = heads_here // pairs_per_row
    pair_columns = pair_heads * HEAD_DIM
    score_scale = HEAD_DIM ** (-0.5)
    utterances = lengths.shape[1]

    lengths_all = gathered(lengths)
    steps_all = gathered(flow_steps)
    gain_vector = gathered(ff_gain).astype(jnp.float32)
    w_qkv_here = lax.all_to_all(
        w_qkv.reshape(columns_here, 3, rows, columns_here), "grp", 2, 0, tiled=True
    ).reshape(model_width, 3 * columns_here)
    w_up_here = lax.all_to_all(
        w_up.reshape(columns_here, rows, -1), "grp", 1, 0, tiled=True
    ).reshape(model_width, -1)
    upstream = cotangent[0]
    upstream_all = gathered(upstream)

    frames = block_rank * frame_count + jnp.arange(frame_count, dtype=jnp.int32)
    lengths_row = lengths[0]
    own_segment, own_position = layout(lengths_row, frames)
    all_position = jax.vmap(lambda row: layout(row, frames)[1])(lengths_all).reshape(tokens)

    joined = jnp.concatenate([inputs[0], skipped[0]], axis=1)
    joined_here = lax.all_to_all(
        joined.reshape(frame_count, rows, -1), "grp", 1, 0, tiled=True
    ).reshape(tokens, -1)
    hidden = summed_rows(rows_dot(joined_here, w_skip))

    condition = flow_condition(steps_all.reshape(-1), model_width).astype(jnp.bfloat16)
    condition_here = lax.dynamic_slice_in_dim(
        condition, group_rank * columns_here, columns_here, axis=1
    )
    modulation = lax.psum_scatter(
        rows_dot(condition_here, w_mod), "grp", scatter_dimension=0, tiled=True
    )
    picker = (
        own_segment[:, None] == jnp.arange(utterances, dtype=jnp.int32)[None, :]
    ).astype(jnp.float32)
    per_frame = jnp.dot(picker, modulation, precision=HIGHEST)
    scale_one = 1.0 + per_frame[:, :model_width]
    normal_one, spread_one = normalize(hidden)
    attn_in = gathered(
        (normal_one * scale_one + per_frame[:, model_width:]).astype(jnp.bfloat16)
    )

    def rotated(block, position, turn):
        return turn(heads_of_block(block), position).reshape(block.shape)

    def heads_of_block(block):
        return block.reshape(block.shape[0], -1, HEAD_DIM)

    project = rows_dot(attn_in, w_qkv_here)
    sent = jnp.concatenate(
        [
            rotated(project[:, :columns_here], all_position, rotate),
            rotated(project[:, columns_here : 2 * columns_here], all_position, rotate),
            project[:, 2 * columns_here :],
        ],
        axis=1,
    ).astype(jnp.bfloat16)

    def to_pairs(block, kinds):
        block = block.reshape(rows, frame_count, kinds, pairs_per_row, pair_columns)
        block = jnp.transpose(block, (0, 3, 1, 2, 4)).reshape(
            blocks, frame_count, kinds * pair_columns
        )
        return lax.all_to_all(block, "blk", 0, 0, tiled=True).reshape(
            blocks * frame_count, kinds * pair_columns
        )

    def from_pairs(block, kinds):
        block = lax.all_to_all(
            block.reshape(blocks, frame_count, kinds * pair_columns), "blk", 0, 0, tiled=True
        ).reshape(rows, pairs_per_row, frame_count, kinds, pair_columns)
        return jnp.transpose(block, (0, 2, 3, 1, 4)).reshape(
            tokens, kinds * pairs_per_row * pair_columns
        )

    paired = to_pairs(sent, 3)
    queries, keys, values = (
        heads_of_block(paired[:, :pair_columns]),
        heads_of_block(paired[:, pair_columns : 2 * pair_columns]),
        heads_of_block(paired[:, 2 * pair_columns :]),
    )
    pair_lengths = lax.dynamic_index_in_dim(
        lengths_all, block_rank // pairs_per_row, axis=0, keepdims=False
    )
    row_segment, row_position = layout(
        pair_lengths, jnp.arange(blocks * frame_count, dtype=jnp.int32)
    )
    allowed = (row_segment[:, None] == row_segment[None, :])[None]
    raw_scores = (
        jnp.einsum("qhd,khd->hqk", queries, keys, preferred_element_type=jnp.float32)
        * score_scale
    )
    raw_scores = jnp.where(allowed, raw_scores, NEGATIVE)
    top = jnp.max(raw_scores, axis=2, keepdims=True)
    weights = jnp.exp(raw_scores - top)
    total = jnp.sum(weights, axis=2, keepdims=True)
    probabilities = weights / total
    prob_low = probabilities.astype(jnp.bfloat16)
    attended_pair = jnp.einsum(
        "hqk,khd->qhd", prob_low, values, preferred_element_type=jnp.float32
    )
    attended_here = from_pairs(
        attended_pair.astype(jnp.bfloat16).reshape(-1, pair_columns), 1
    )

    hidden_two = hidden + summed_rows(rows_dot(attended_here, w_out))
    normal_two, spread_two = normalize(hidden_two)
    ff_in = gathered((normal_two * gain_vector).astype(jnp.bfloat16))
    widened = rows_dot(ff_in, w_up_here)
    activated, gelu_back = jax.vjp(exact_gelu, widened)
    activated_low = activated.astype(jnp.bfloat16)
    output = (hidden_two + summed_rows(rows_dot(activated_low, w_down))).astype(jnp.bfloat16)
    grad_down = contract_rows(activated_low, upstream_all)
    grad_widened = gelu_back(dot_columns(upstream_all, w_down))[0].astype(jnp.bfloat16)
    grad_up = contract_rows(ff_in, grad_widened)
    grad_ff_in = summed_rows(dot_columns(grad_widened, w_up_here))
    grad_gain = jnp.sum(grad_ff_in * normal_two, axis=0)
    grad_hidden_two = upstream.astype(jnp.float32) + norm_back(
        grad_ff_in * gain_vector, normal_two, spread_two
    )

    def over_blocks(grad):
        shard = lax.psum_scatter(
            grad.astype(jnp.bfloat16), "blk", scatter_dimension=0, tiled=True
        )
        return gathered(shard, "blk").astype(jnp.float32)

    def over_blocks_columns(grad, kinds):
        wide = grad.shape[1] // kinds
        grad = grad.reshape(rows, blocks, columns_here // blocks, grad.shape[1])
        grad = jnp.transpose(grad, (1, 0, 2, 3)).astype(jnp.bfloat16)
        shard = lax.psum_scatter(grad, "blk", scatter_dimension=0, tiled=True)[0]
        shard = lax.all_to_all(
            shard.reshape(rows, columns_here // blocks, kinds, 1, wide), "grp", 0, 3, tiled=True
        )
        return gathered(shard.reshape(columns_here // blocks, -1), "blk").astype(jnp.float32)

    total_down = over_blocks(grad_down)
    total_up = over_blocks_columns(grad_up, 1)

    grad_two_low = gathered(grad_hidden_two.astype(jnp.bfloat16))
    total_out = over_blocks(contract_rows(attended_here, grad_two_low))
    grad_attended = heads_of_block(
        to_pairs(dot_columns(grad_two_low, w_out).astype(jnp.bfloat16), 1)
    )
    delta = jnp.transpose(jnp.sum(grad_attended.astype(jnp.float32) * attended_pair, axis=2))
    value_grad = jnp.einsum(
        "hqk,qhd->khd", prob_low, grad_attended, preferred_element_type=jnp.float32
    )
    prob_grad = jnp.einsum(
        "qhd,khd->hqk", grad_attended, values, preferred_element_type=jnp.float32
    )
    score_grad = (probabilities * (prob_grad - delta[:, :, None])).astype(jnp.bfloat16)
    query_grad = (
        jnp.einsum("hqk,khd->qhd", score_grad, keys, preferred_element_type=jnp.float32)
        * score_scale
    )
    key_grad = (
        jnp.einsum("hqk,qhd->khd", score_grad, queries, preferred_element_type=jnp.float32)
        * score_scale
    )
    grad_paired = jnp.concatenate(
        [
            rotate_back(query_grad, row_position).reshape(-1, pair_columns),
            rotate_back(key_grad, row_position).reshape(-1, pair_columns),
            value_grad.reshape(-1, pair_columns),
        ],
        axis=1,
    ).astype(jnp.bfloat16)
    grad_project = from_pairs(grad_paired, 3)
    total_qkv = over_blocks_columns(contract_rows(attn_in, grad_project), 3)
    grad_attn_in = summed_rows(dot_columns(grad_project, w_qkv_here))

    mod_terms = jnp.concatenate([grad_attn_in * normal_one, grad_attn_in], axis=1)
    grad_modulation = gathered(lax.psum(jnp.dot(picker.T, mod_terms, precision=HIGHEST), "blk"))
    grad_mod = jnp.dot(
        condition_here.astype(jnp.float32).T, grad_modulation, precision=HIGHEST
    )

    grad_hidden = grad_hidden_two + norm_back(grad_attn_in * scale_one, normal_one, spread_one)
    grad_hidden_low = gathered(grad_hidden.astype(jnp.bfloat16))
    total_skip = over_blocks(contract_rows(joined_here, grad_hidden_low))
    grad_joined = lax.all_to_all(
        dot_columns(grad_hidden_low, w_skip)
        .astype(jnp.bfloat16)
        .reshape(rows, frame_count, 1, -1),
        "grp",
        0,
        2,
        tiled=True,
    ).reshape(frame_count, -1).astype(jnp.float32)
    total_gain = lax.psum_scatter(
        lax.psum(grad_gain, "blk"), "grp", scatter_dimension=0, tiled=True
    )
    return (
        output[None],
        grad_joined[:, :model_width][None],
        grad_joined[:, model_width:][None],
        total_skip,
        grad_mod,
        total_qkv,
        total_out,
        total_gain,
        total_up,
        total_down,
    )


def solution(mesh):
    placed = (
        P("grp", "blk", None),
        P("grp", "blk", None),
        P("grp", None),
        P("grp", None),
        P("grp", None),
        P("grp", None),
        P("grp"),
        P("grp", None),
        P("grp", None),
        P("grp", "blk", None),
        P("grp", None),
        P("grp", None),
    )
    rows, blocks = mesh.shape["grp"], mesh.shape["blk"]
    body = per_device
    if blocks % rows == 0 and HEADS % blocks == 0:
        body = per_device_shards
    return jax.shard_map(
        body,
        mesh=mesh,
        in_specs=placed,
        out_specs=(
            P("grp", "blk", None),
            P("grp", "blk", None),
            P("grp", "blk", None),
            P("grp", None),
            P("grp", None),
            P("grp", None),
            P("grp", None),
            P("grp"),
            P("grp", None),
            P("grp", None),
        ),
        check_vma=False,
    )
```

```python
import math

import jax
import jax.numpy as jnp
from jax import lax
from jax.experimental import pallas as pl
from jax.experimental.pallas import tpu as pltpu
from jax.sharding import PartitionSpec as P

HEADS = 16
HEAD_DIM = 64
STEPS = 32


EPSILON = 1e-06
NEGATIVE = -1e30
HIGHEST = lax.Precision.HIGHEST
MESH = pl.DeviceIdType.MESH
RING = 8


def from_behind(block, axis, distance):
    devices = range(lax.axis_size(axis))
    route = [((i - distance) % len(devices), i) for i in devices]
    return lax.ppermute(block, axis, route)


def layout(lengths_row, frames):
    end_frame = jnp.cumsum(lengths_row)
    start_frame = end_frame - lengths_row
    segment = jnp.sum((frames[:, None] >= end_frame[None, :]).astype(jnp.int32), axis=1)
    chosen = segment[:, None] == jnp.arange(lengths_row.shape[0], dtype=jnp.int32)[None, :]
    position = frames - jnp.sum(jnp.where(chosen, start_frame[None, :], 0), axis=1)
    return (segment, position)


def flow_condition(steps_row, model_width):
    half_width = model_width // 2
    rate_table = jnp.exp(
        -math.log(10000.0) * jnp.arange(half_width, dtype=jnp.float32) / half_width
    )
    angles = 1000.0 * (steps_row.astype(jnp.float32) / STEPS)[:, None] * rate_table[None, :]
    return jax.nn.silu(jnp.concatenate([jnp.sin(angles), jnp.cos(angles)], axis=1))


def rotation_tables(position, head_width):
    half_width = head_width // 2
    rate_table = jnp.exp(
        -math.log(10000.0) * jnp.arange(half_width, dtype=jnp.float32) / half_width
    )
    angles = position.astype(jnp.float32)[:, None] * rate_table[None, :]
    return (jnp.cos(angles)[:, None, :], jnp.sin(angles)[:, None, :], half_width)


def rotate(head_block, position):
    cosine_part, sine_part, half_width = rotation_tables(position, head_block.shape[-1])
    first_half = head_block[..., :half_width]
    second_half = head_block[..., half_width:]
    return jnp.concatenate(
        [
            first_half * cosine_part - second_half * sine_part,
            second_half * cosine_part + first_half * sine_part,
        ],
        axis=-1,
    )


def rotate_back(head_block, position):
    cosine_part, sine_part, half_width = rotation_tables(position, head_block.shape[-1])
    first_half = head_block[..., :half_width]
    second_half = head_block[..., half_width:]
    return jnp.concatenate(
        [
            first_half * cosine_part + second_half * sine_part,
            second_half * cosine_part - first_half * sine_part,
        ],
        axis=-1,
    )


def normalize(hidden):
    centred = hidden - jnp.mean(hidden, axis=-1, keepdims=True)
    scaled = lax.rsqrt(jnp.mean(centred * centred, axis=-1, keepdims=True) + EPSILON)
    return (centred * scaled, scaled)


def norm_back(grad_normal, normal, scaled):
    centred_grad = grad_normal - jnp.mean(grad_normal, axis=-1, keepdims=True)
    return scaled * (centred_grad - normal * jnp.mean(grad_normal * normal, axis=-1, keepdims=True))


def exact_gelu(values_in):
    return jax.nn.gelu(values_in, approximate=False)


def contract_rows(left_side, right_side):
    return lax.dot_general(
        left_side, right_side, (((0,), (0,)), ((), ())), preferred_element_type=jnp.float32
    )


def heads_of(flat_block):
    return flat_block.reshape(flat_block.shape[0], HEADS, HEAD_DIM)


def per_device(
    inputs,
    skipped,
    w_skip,
    w_mod,
    w_qkv,
    w_out,
    ff_gain,
    w_up,
    w_down,
    cotangent,
    lengths,
    flow_steps,
):
    w_skip, w_mod, w_qkv, w_out, ff_gain, w_up, w_down = (
        lax.all_gather(w_skip, "grp", axis=0, tiled=True),
        lax.all_gather(w_mod, "grp", axis=0, tiled=True),
        lax.all_gather(w_qkv, "grp", axis=0, tiled=True),
        lax.all_gather(w_out, "grp", axis=0, tiled=True),
        lax.all_gather(ff_gain, "grp", axis=0, tiled=True),
        lax.all_gather(w_up, "grp", axis=0, tiled=True),
        lax.all_gather(w_down, "grp", axis=0, tiled=True),
    )
    frame_count = inputs.shape[1]
    model_width = inputs.shape[2]
    cycle_size = lax.axis_size("blk")
    device_rank = lax.axis_index("blk")
    score_scale = HEAD_DIM ** (-0.5)
    local_frames = jnp.arange(frame_count, dtype=jnp.int32)
    lengths_row = lengths[0]
    own_segment, own_position = layout(lengths_row, device_rank * frame_count + local_frames)

    def segment_of(source):
        return layout(lengths_row, source * frame_count + local_frames)[0]

    def scored(query_block, key_block, query_segment, key_segment):
        raw_scores = (
            jnp.einsum(
                "qhd,khd->hqk",
                heads_of(query_block),
                heads_of(key_block),
                preferred_element_type=jnp.float32,
            )
            * score_scale
        )
        allowed = (query_segment[:, None] == key_segment[None, :])[None]
        return (raw_scores, allowed)

    joined = jnp.concatenate([inputs[0], skipped[0]], axis=1)
    hidden = jnp.dot(joined, w_skip, preferred_element_type=jnp.float32)
    condition = flow_condition(flow_steps[0], model_width).astype(jnp.bfloat16)
    modulation = jnp.dot(condition, w_mod, preferred_element_type=jnp.float32)
    picker = (
        own_segment[:, None] == jnp.arange(lengths_row.shape[0], dtype=jnp.int32)[None, :]
    ).astype(jnp.float32)
    per_frame = jnp.dot(picker, modulation, precision=HIGHEST)
    scale_one = 1.0 + per_frame[:, :model_width]
    normal_one, spread_one = normalize(hidden)
    attn_in = (normal_one * scale_one + per_frame[:, model_width:]).astype(jnp.bfloat16)
    project = jnp.dot(attn_in, w_qkv, preferred_element_type=jnp.float32).reshape(
        frame_count, 3, HEADS, HEAD_DIM
    )
    queries = (
        rotate(project[:, 0], own_position).astype(jnp.bfloat16).reshape(frame_count, model_width)
    )
    keys_own = (
        rotate(project[:, 1], own_position).astype(jnp.bfloat16).reshape(frame_count, model_width)
    )
    values_own = project[:, 2].astype(jnp.bfloat16).reshape(frame_count, model_width)

    def forward_turn(turn_index, carried):
        key_now, value_now, running_top, running_total, running_sum = carried
        source = (device_rank - turn_index) % cycle_size
        raw_scores, allowed = scored(queries, key_now, own_segment, segment_of(source))
        raw_scores = jnp.where(allowed, raw_scores, NEGATIVE)
        new_top = jnp.maximum(running_top, jnp.max(raw_scores, axis=2, keepdims=True))
        weights = jnp.where(allowed, jnp.exp(raw_scores - new_top), 0.0)
        shrink = jnp.exp(running_top - new_top)
        running_total = running_total * shrink + jnp.sum(weights, axis=2, keepdims=True)
        running_sum = running_sum * shrink + jnp.einsum(
            "hqk,khd->hqd",
            weights.astype(jnp.bfloat16),
            heads_of(value_now),
            preferred_element_type=jnp.float32,
        )
        key_now, value_now = from_behind((key_now, value_now), "blk", 1)
        return (key_now, value_now, new_top, running_total, running_sum)

    initial = (
        keys_own,
        values_own,
        jnp.full((HEADS, frame_count, 1), NEGATIVE, jnp.float32),
        jnp.zeros((HEADS, frame_count, 1), jnp.float32),
        jnp.zeros((HEADS, frame_count, HEAD_DIM), jnp.float32),
    )
    finished = lax.fori_loop(0, cycle_size, forward_turn, initial)
    running_top, running_total, running_sum = (finished[2], finished[3], finished[4])
    attended = jnp.transpose(running_sum / running_total, (1, 0, 2)).reshape(
        frame_count, model_width
    )
    log_total = (running_top + jnp.log(running_total))[:, :, 0]
    attended_low = attended.astype(jnp.bfloat16)
    hidden_two = hidden + jnp.dot(attended_low, w_out, preferred_element_type=jnp.float32)
    normal_two, spread_two = normalize(hidden_two)
    gain_vector = ff_gain.astype(jnp.float32)
    ff_in = (normal_two * gain_vector).astype(jnp.bfloat16)
    widened = jnp.dot(ff_in, w_up, preferred_element_type=jnp.float32)
    activated, gelu_back = jax.vjp(exact_gelu, widened)
    activated_low = activated.astype(jnp.bfloat16)
    output = (
        hidden_two + jnp.dot(activated_low, w_down, preferred_element_type=jnp.float32)
    ).astype(jnp.bfloat16)
    upstream = cotangent[0]
    grad_down = contract_rows(activated_low, upstream)
    grad_activated = jnp.dot(upstream, w_down.T, preferred_element_type=jnp.float32)
    grad_widened = gelu_back(grad_activated)[0].astype(jnp.bfloat16)
    grad_up = contract_rows(ff_in, grad_widened)
    grad_ff_in = jnp.dot(grad_widened, w_up.T, preferred_element_type=jnp.float32)
    grad_gain = jnp.sum(grad_ff_in * normal_two, axis=0)
    grad_hidden_two = upstream.astype(jnp.float32) + norm_back(
        grad_ff_in * gain_vector, normal_two, spread_two
    )
    grad_two_low = grad_hidden_two.astype(jnp.bfloat16)
    grad_out = contract_rows(attended_low, grad_two_low)
    grad_attended = jnp.dot(grad_two_low, w_out.T, preferred_element_type=jnp.float32).astype(
        jnp.bfloat16
    )
    delta = jnp.transpose(jnp.sum(heads_of(grad_attended.astype(jnp.float32) * attended), axis=2))
    zero_grad = jnp.zeros((frame_count, model_width), jnp.float32)

    def pair_terms(
        query_block,
        upstream_block,
        key_block,
        value_block,
        total_block,
        delta_block,
        query_segment,
        key_segment,
    ):
        raw_scores, allowed = scored(query_block, key_block, query_segment, key_segment)
        prob_block = jnp.where(allowed, jnp.exp(raw_scores - total_block[:, :, None]), 0.0)
        value_term = jnp.einsum(
            "hqk,qhd->khd",
            prob_block.astype(jnp.bfloat16),
            heads_of(upstream_block),
            preferred_element_type=jnp.float32,
        ).reshape(frame_count, model_width)
        prob_grad = jnp.einsum(
            "qhd,khd->hqk",
            heads_of(upstream_block),
            heads_of(value_block),
            preferred_element_type=jnp.float32,
        )
        score_grad = (prob_block * (prob_grad - delta_block[:, :, None])).astype(jnp.bfloat16)
        query_term = (
            jnp.einsum(
                "hqk,khd->qhd", score_grad, heads_of(key_block), preferred_element_type=jnp.float32
            ).reshape(frame_count, model_width)
            * score_scale
        )
        key_term = (
            jnp.einsum(
                "hqk,qhd->khd",
                score_grad,
                heads_of(query_block),
                preferred_element_type=jnp.float32,
            ).reshape(frame_count, model_width)
            * score_scale
        )
        return (query_term, key_term, value_term)

    def keys_turn(turn_index, carried):
        key_now, value_now, key_grad, value_grad, query_grad = carried
        source = (device_rank - turn_index) % cycle_size
        query_term, key_term, value_term = pair_terms(
            queries,
            grad_attended,
            key_now,
            value_now,
            log_total,
            delta,
            own_segment,
            segment_of(source),
        )
        key_now, value_now = from_behind((key_now, value_now), "blk", 1)
        key_grad, value_grad = (
            from_behind((key_grad + key_term).astype(jnp.bfloat16), "blk", 1).astype(jnp.float32),
            from_behind((value_grad + value_term).astype(jnp.bfloat16), "blk", 1).astype(
                jnp.float32
            ),
        )
        return (key_now, value_now, key_grad, value_grad, query_grad + query_term)

    done = lax.fori_loop(
        0, cycle_size, keys_turn, (keys_own, values_own, zero_grad, zero_grad, zero_grad)
    )
    key_grad, value_grad, query_grad = (done[2], done[3], done[4])
    grad_project = jnp.concatenate(
        [
            rotate_back(heads_of(query_grad), own_position).reshape(frame_count, model_width),
            rotate_back(heads_of(key_grad), own_position).reshape(frame_count, model_width),
            value_grad,
        ],
        axis=1,
    ).astype(jnp.bfloat16)
    grad_qkv = contract_rows(attn_in, grad_project)
    grad_attn_in = jnp.dot(grad_project, w_qkv.T, preferred_element_type=jnp.float32)
    mod_terms = jnp.concatenate([grad_attn_in * normal_one, grad_attn_in], axis=1)
    grad_modulation = jnp.dot(picker.T, mod_terms, precision=HIGHEST)
    grad_mod = jnp.dot(condition.astype(jnp.float32).T, grad_modulation, precision=HIGHEST)
    grad_hidden = grad_hidden_two + norm_back(grad_attn_in * scale_one, normal_one, spread_one)
    grad_hidden_low = grad_hidden.astype(jnp.bfloat16)
    grad_skip_weight = contract_rows(joined, grad_hidden_low)
    grad_joined = jnp.dot(grad_hidden_low, w_skip.T, preferred_element_type=jnp.float32)
    shards = (
        lax.psum_scatter(
            grad_skip_weight.astype(jnp.bfloat16), "grp", scatter_dimension=0, tiled=True
        ).astype(jnp.float32),
        lax.psum_scatter(
            grad_mod.astype(jnp.bfloat16), "grp", scatter_dimension=0, tiled=True
        ).astype(jnp.float32),
        lax.psum_scatter(
            grad_qkv.astype(jnp.bfloat16), "grp", scatter_dimension=0, tiled=True
        ).astype(jnp.float32),
        lax.psum_scatter(
            grad_out.astype(jnp.bfloat16), "grp", scatter_dimension=0, tiled=True
        ).astype(jnp.float32),
        lax.psum_scatter(
            grad_gain.astype(jnp.bfloat16), "grp", scatter_dimension=0, tiled=True
        ).astype(jnp.float32),
        lax.psum_scatter(
            grad_up.astype(jnp.bfloat16), "grp", scatter_dimension=0, tiled=True
        ).astype(jnp.float32),
        lax.psum_scatter(
            grad_down.astype(jnp.bfloat16), "grp", scatter_dimension=0, tiled=True
        ).astype(jnp.float32),
    )
    totals = lax.psum(
        (shards[0], shards[1], shards[2], shards[3], shards[4], shards[5], shards[6]), "blk"
    )
    return (
        output[None],
        grad_joined[:, :model_width][None],
        grad_joined[:, model_width:][None],
        totals[0],
        totals[1],
        totals[2],
        totals[3],
        totals[4],
        totals[5],
        totals[6],
    )


def rows_dot(left_side, right_side):
    return jnp.dot(left_side, right_side, preferred_element_type=jnp.float32)


def dot_columns(left_side, right_side):
    return lax.dot_general(
        left_side, right_side, (((1,), (1,)), ((), ())), preferred_element_type=jnp.float32
    )


def summed_rows(partial, axis="grp"):
    return lax.psum_scatter(
        partial.astype(jnp.bfloat16), axis, scatter_dimension=0, tiled=True
    ).astype(jnp.float32)


def gathered(block, axis="grp"):
    return lax.all_gather(block, axis, axis=0, tiled=True)


def ring_place(rank):
    odd = lax.rem(rank, 2)
    return (1 - odd) * (rank // 2) + odd * ((15 - rank) // 2)


def ring_rank(place):
    upper = place // 4
    return (1 - upper) * (2 * place) + upper * (15 - 2 * place)


class Ring:
    def __init__(self, part, land, done, sems, rank, group_rank):
        self.part, self.land, self.done = part, land, done
        self.sems = sems
        self.place = ring_place(rank)
        self.group_rank = group_rank
        self.half = part.shape[1] // 2
        self.copies = {}

    def block_at(self, offset):
        return ring_rank(lax.rem(self.place + offset + 2 * RING, RING))

    def rows(self, way):
        return pl.ds(way * self.half, self.half)

    def send(self, kind, step, way, source, target):
        to = ring_rank(lax.rem(self.place + (1 if way == 0 else RING - 1), RING))
        copy = pltpu.make_async_remote_copy(
            src_ref=source,
            dst_ref=target,
            send_sem=self.sems.at[kind, 0, way, step],
            recv_sem=self.sems.at[kind, 1, way, step],
            device_id=(to, self.group_rank),
            device_id_type=MESH,
        )
        copy.start()
        self.copies[kind, step, way] = copy

    def sum_step(self, step, way):
        sign = -1 if way == 0 else 1
        block = self.block_at(sign * (step + 1))
        rows = self.rows(way)
        if step > 0:
            self.copies[0, step - 1, way].wait_recv()
            tile = min(self.half, 32)

            def add(i, carry):
                at = pl.ds(pl.multiple_of(way * self.half + i * tile, tile), tile)
                total = self.part[block, at].astype(jnp.float32) + self.land[
                    step - 1, at
                ].astype(jnp.float32)
                self.land[step - 1, at] = total.astype(jnp.bfloat16)
                return carry

            lax.fori_loop(0, self.half // tile, add, 0)
        if step < RING - 1:
            source = self.part.at[block, rows] if step == 0 else self.land.at[step - 1, rows]
            self.send(0, step, way, source, self.land.at[step, rows])

    def spread_step(self, step, way):
        sign = -1 if way == 0 else 1
        block = self.block_at(sign * step)
        rows = self.rows(way)
        if step > 0:
            self.copies[1, step - 1, way].wait_recv()
        if step < RING - 1:
            self.send(1, step, way, self.done.at[block, rows], self.done.at[block, rows])

    def finish(self):
        for copy in self.copies.values():
            copy.wait_send()


def gradient_kernel(
    down_ref, up_ref, qkv_ref, skip_ref, out_ref,
    down_done, up_done, qkv_done, skip_done, out_done,
    down_land, up_land, qkv_land, skip_land, out_land,
    down_sem, up_sem, qkv_sem, skip_sem, out_sem,
    turn_sem,
):
    rank, group_rank = lax.axis_index("blk"), lax.axis_index("grp")
    rows = 4
    place = ring_place(rank)
    barrier = pltpu.get_barrier_semaphore()
    for step in (1, RING - 1):
        pl.semaphore_signal(
            barrier,
            inc=1,
            device_id=(ring_rank(lax.rem(place + step, RING)), group_rank),
            device_id_type=MESH,
        )
    for other in range(1, rows):
        pl.semaphore_signal(
            barrier,
            inc=1,
            device_id=(rank, lax.rem(group_rank + other, rows)),
            device_id_type=MESH,
        )
    pl.semaphore_wait(barrier, 2 + rows - 1)

    rings = [
        Ring(down_ref, down_land, down_done, down_sem, rank, group_rank),
        Ring(up_ref, up_land, up_done, up_sem, rank, group_rank),
        Ring(qkv_ref, qkv_land, qkv_done, qkv_sem, rank, group_rank),
        Ring(skip_ref, skip_land, skip_done, skip_sem, rank, group_rank),
        Ring(out_ref, out_land, out_done, out_sem, rank, group_rank),
    ]
    for step in range(RING):
        for ring in rings:
            for way in range(2):
                ring.sum_step(step, way)
    turned = []
    for index, ring in enumerate(rings[1:3]):
        deep = ring.part.shape[1] // rows
        for other in range(1, rows):
            target = lax.rem(group_rank + other, rows)
            copy = pltpu.make_async_remote_copy(
                src_ref=ring.land.at[RING - 2, pl.ds(pl.multiple_of(target * deep, deep), deep)],
                dst_ref=ring.done.at[rank, pl.ds(pl.multiple_of(group_rank * deep, deep), deep)],
                send_sem=turn_sem.at[index, 0, other - 1],
                recv_sem=turn_sem.at[index, 1, other - 1],
                device_id=(rank, target),
                device_id_type=MESH,
            )
            copy.start()
            turned.append(copy)
        mine = pl.ds(pl.multiple_of(group_rank * deep, deep), deep)
        ring.done[rank, mine] = ring.land[RING - 2, mine]
    for ring in (rings[0], rings[3], rings[4]):
        ring.done[rank] = ring.land[RING - 2]
    for copy in turned:
        copy.wait_recv()
    for step in range(RING):
        for ring in rings:
            for way in range(2):
                ring.spread_step(step, way)
    for ring in rings:
        ring.finish()
    for copy in turned:
        copy.wait_send()


def sum_gradients(down, up, qkv, skip, out):
    parts = (down, up, qkv, skip, out)
    vmem = pl.BlockSpec(memory_space=pltpu.VMEM)
    return pl.pallas_call(
        gradient_kernel,
        out_shape=[jax.ShapeDtypeStruct(part.shape, jnp.bfloat16) for part in parts],
        in_specs=[vmem] * 5,
        out_specs=[vmem] * 5,
        scratch_shapes=[
            pltpu.VMEM((RING - 1,) + part.shape[1:], jnp.bfloat16) for part in parts
        ]
        + [pltpu.SemaphoreType.DMA((2, 2, 2, RING - 1))] * 5
        + [pltpu.SemaphoreType.DMA((2, 2, 3))],
        compiler_params=pltpu.CompilerParams(
            collective_id=0, has_side_effects=True, vmem_limit_bytes=56 * 1024 * 1024
        ),
    )(*parts)


def per_device_shards(
    inputs,
    skipped,
    w_skip,
    w_mod,
    w_qkv,
    w_out,
    ff_gain,
    w_up,
    w_down,
    cotangent,
    lengths,
    flow_steps,
):
    frame_count = inputs.shape[1]
    model_width = inputs.shape[2]
    rows = lax.axis_size("grp")
    blocks = lax.axis_size("blk")
    group_rank = lax.axis_index("grp")
    block_rank = lax.axis_index("blk")
    tokens = rows * frame_count
    heads_here = HEADS // rows
    columns_here = model_width // rows
    pairs_per_row = blocks // rows
    pair_heads = heads_here // pairs_per_row
    pair_columns = pair_heads * HEAD_DIM
    score_scale = HEAD_DIM ** (-0.5)
    utterances = lengths.shape[1]

    lengths_all = gathered(lengths)
    steps_all = gathered(flow_steps)
    gain_vector = gathered(ff_gain).astype(jnp.float32)
    w_qkv_here = lax.all_to_all(
        w_qkv.reshape(columns_here, 3, rows, columns_here), "grp", 2, 0, tiled=True
    ).reshape(model_width, 3 * columns_here)
    w_up_here = lax.all_to_all(
        w_up.reshape(columns_here, rows, -1), "grp", 1, 0, tiled=True
    ).reshape(model_width, -1)
    upstream = cotangent[0]
    upstream_all = gathered(upstream)

    frames = block_rank * frame_count + jnp.arange(frame_count, dtype=jnp.int32)
    lengths_row = lengths[0]
    own_segment, own_position = layout(lengths_row, frames)
    all_position = jax.vmap(lambda row: layout(row, frames)[1])(lengths_all).reshape(tokens)

    joined = jnp.concatenate([inputs[0], skipped[0]], axis=1)
    joined_here = lax.all_to_all(
        joined.reshape(frame_count, rows, -1), "grp", 1, 0, tiled=True
    ).reshape(tokens, -1)
    hidden = summed_rows(rows_dot(joined_here, w_skip))

    condition = flow_condition(steps_all.reshape(-1), model_width).astype(jnp.bfloat16)
    condition_here = lax.dynamic_slice_in_dim(
        condition, group_rank * columns_here, columns_here, axis=1
    )
    modulation = lax.psum_scatter(
        rows_dot(condition_here, w_mod), "grp", scatter_dimension=0, tiled=True
    )
    picker = (
        own_segment[:, None] == jnp.arange(utterances, dtype=jnp.int32)[None, :]
    ).astype(jnp.float32)
    per_frame = jnp.dot(picker, modulation, precision=HIGHEST)
    scale_one = 1.0 + per_frame[:, :model_width]
    normal_one, spread_one = normalize(hidden)
    attn_in = gathered(
        (normal_one * scale_one + per_frame[:, model_width:]).astype(jnp.bfloat16)
    )

    def rotated(block, position, turn):
        return turn(heads_of_block(block), position).reshape(block.shape)

    def heads_of_block(block):
        return block.reshape(block.shape[0], -1, HEAD_DIM)

    project = rows_dot(attn_in, w_qkv_here)
    sent = jnp.concatenate(
        [
            rotated(project[:, :columns_here], all_position, rotate),
            rotated(project[:, columns_here : 2 * columns_here], all_position, rotate),
            project[:, 2 * columns_here :],
        ],
        axis=1,
    ).astype(jnp.bfloat16)

    def to_pairs(block, kinds):
        block = block.reshape(rows, frame_count, kinds, pairs_per_row, pair_columns)
        block = jnp.transpose(block, (0, 3, 1, 2, 4)).reshape(
            blocks, frame_count, kinds * pair_columns
        )
        return lax.all_to_all(block, "blk", 0, 0, tiled=True).reshape(
            blocks * frame_count, kinds * pair_columns
        )

    def from_pairs(block, kinds):
        block = lax.all_to_all(
            block.reshape(blocks, frame_count, kinds * pair_columns), "blk", 0, 0, tiled=True
        ).reshape(rows, pairs_per_row, frame_count, kinds, pair_columns)
        return jnp.transpose(block, (0, 2, 3, 1, 4)).reshape(
            tokens, kinds * pairs_per_row * pair_columns
        )

    paired = to_pairs(sent, 3)
    queries, keys, values = (
        heads_of_block(paired[:, :pair_columns]),
        heads_of_block(paired[:, pair_columns : 2 * pair_columns]),
        heads_of_block(paired[:, 2 * pair_columns :]),
    )
    pair_lengths = lax.dynamic_index_in_dim(
        lengths_all, block_rank // pairs_per_row, axis=0, keepdims=False
    )
    row_segment, row_position = layout(
        pair_lengths, jnp.arange(blocks * frame_count, dtype=jnp.int32)
    )
    allowed = (row_segment[:, None] == row_segment[None, :])[None]
    raw_scores = (
        jnp.einsum("qhd,khd->hqk", queries, keys, preferred_element_type=jnp.float32)
        * score_scale
    )
    raw_scores = jnp.where(allowed, raw_scores, NEGATIVE)
    top = jnp.max(raw_scores, axis=2, keepdims=True)
    weights = jnp.exp(raw_scores - top)
    total = jnp.sum(weights, axis=2, keepdims=True)
    probabilities = weights / total
    prob_low = probabilities.astype(jnp.bfloat16)
    attended_pair = jnp.einsum(
        "hqk,khd->qhd", prob_low, values, preferred_element_type=jnp.float32
    )
    attended_here = from_pairs(
        attended_pair.astype(jnp.bfloat16).reshape(-1, pair_columns), 1
    )

    hidden_two = hidden + summed_rows(rows_dot(attended_here, w_out))
    normal_two, spread_two = normalize(hidden_two)
    ff_in = gathered((normal_two * gain_vector).astype(jnp.bfloat16))
    widened = rows_dot(ff_in, w_up_here)
    activated, gelu_back = jax.vjp(exact_gelu, widened)
    activated_low = activated.astype(jnp.bfloat16)
    output = (hidden_two + summed_rows(rows_dot(activated_low, w_down))).astype(jnp.bfloat16)
    grad_down = contract_rows(activated_low, upstream_all)
    grad_widened = gelu_back(dot_columns(upstream_all, w_down))[0].astype(jnp.bfloat16)
    grad_up = contract_rows(ff_in, grad_widened)
    grad_ff_in = summed_rows(dot_columns(grad_widened, w_up_here))
    grad_gain = jnp.sum(grad_ff_in * normal_two, axis=0)
    grad_hidden_two = upstream.astype(jnp.float32) + norm_back(
        grad_ff_in * gain_vector, normal_two, spread_two
    )

    def blocked(grad):
        return grad.astype(jnp.bfloat16).reshape(blocks, -1, grad.shape[1])

    def blocked_columns(grad):
        grad = grad.astype(jnp.bfloat16).reshape(rows, blocks, columns_here // blocks, -1)
        return jnp.transpose(grad, (1, 0, 2, 3)).reshape(
            blocks, model_width // blocks, grad.shape[3]
        )

    part_down = blocked(grad_down)
    part_up = blocked_columns(grad_up)

    grad_two_low = gathered(grad_hidden_two.astype(jnp.bfloat16))
    part_out = blocked(contract_rows(attended_here, grad_two_low))
    grad_attended = heads_of_block(
        to_pairs(dot_columns(grad_two_low, w_out).astype(jnp.bfloat16), 1)
    )
    delta = jnp.transpose(jnp.sum(grad_attended.astype(jnp.float32) * attended_pair, axis=2))
    value_grad = jnp.einsum(
        "hqk,qhd->khd", prob_low, grad_attended, preferred_element_type=jnp.float32
    )
    prob_grad = jnp.einsum(
        "qhd,khd->hqk", grad_attended, values, preferred_element_type=jnp.float32
    )
    score_grad = (probabilities * (prob_grad - delta[:, :, None])).astype(jnp.bfloat16)
    query_grad = (
        jnp.einsum("hqk,khd->qhd", score_grad, keys, preferred_element_type=jnp.float32)
        * score_scale
    )
    key_grad = (
        jnp.einsum("hqk,qhd->khd", score_grad, queries, preferred_element_type=jnp.float32)
        * score_scale
    )
    grad_paired = jnp.concatenate(
        [
            rotate_back(query_grad, row_position).reshape(-1, pair_columns),
            rotate_back(key_grad, row_position).reshape(-1, pair_columns),
            value_grad.reshape(-1, pair_columns),
        ],
        axis=1,
    ).astype(jnp.bfloat16)
    grad_project = from_pairs(grad_paired, 3)
    part_qkv = blocked_columns(contract_rows(attn_in, grad_project))
    grad_attn_in = summed_rows(dot_columns(grad_project, w_qkv_here))

    mod_terms = jnp.concatenate([grad_attn_in * normal_one, grad_attn_in], axis=1)
    grad_modulation = gathered(lax.psum(jnp.dot(picker.T, mod_terms, precision=HIGHEST), "blk"))
    grad_mod = jnp.dot(
        condition_here.astype(jnp.float32).T, grad_modulation, precision=HIGHEST
    )

    grad_hidden = grad_hidden_two + norm_back(grad_attn_in * scale_one, normal_one, spread_one)
    grad_hidden_low = gathered(grad_hidden.astype(jnp.bfloat16))
    part_skip = blocked(contract_rows(joined_here, grad_hidden_low))
    grad_joined = lax.all_to_all(
        dot_columns(grad_hidden_low, w_skip)
        .astype(jnp.bfloat16)
        .reshape(rows, frame_count, 1, -1),
        "grp",
        0,
        2,
        tiled=True,
    ).reshape(frame_count, -1).astype(jnp.float32)
    total_gain = lax.psum_scatter(
        lax.psum(grad_gain, "blk"), "grp", scatter_dimension=0, tiled=True
    )
    total_down, total_up, total_qkv, total_skip, total_out = sum_gradients(
        part_down, part_up, part_qkv, part_skip, part_out
    )

    def columns_back(total, kinds):
        total = total.astype(jnp.float32).reshape(
            blocks, rows, columns_here // blocks, kinds, total.shape[2] // kinds
        )
        return jnp.transpose(total, (0, 2, 3, 1, 4)).reshape(columns_here, -1)

    def rows_back(total):
        return total.astype(jnp.float32).reshape(-1, total.shape[2])

    total_down, total_skip, total_out = map(rows_back, (total_down, total_skip, total_out))
    total_up, total_qkv = columns_back(total_up, 1), columns_back(total_qkv, 3)
    return (
        output[None],
        grad_joined[:, :model_width][None],
        grad_joined[:, model_width:][None],
        total_skip,
        grad_mod,
        total_qkv,
        total_out,
        total_gain,
        total_up,
        total_down,
    )


def solution(mesh):
    placed = (
        P("grp", "blk", None),
        P("grp", "blk", None),
        P("grp", None),
        P("grp", None),
        P("grp", None),
        P("grp", None),
        P("grp"),
        P("grp", None),
        P("grp", None),
        P("grp", "blk", None),
        P("grp", None),
        P("grp", None),
    )
    rows, blocks = mesh.shape["grp"], mesh.shape["blk"]
    body = per_device
    if blocks == RING and rows == 4:
        body = per_device_shards
    return jax.shard_map(
        body,
        mesh=mesh,
        in_specs=placed,
        out_specs=(
            P("grp", "blk", None),
            P("grp", "blk", None),
            P("grp", "blk", None),
            P("grp", None),
            P("grp", None),
            P("grp", None),
            P("grp", None),
            P("grp"),
            P("grp", None),
            P("grp", None),
        ),
        check_vma=False,
    )
```

```python
import functools
import math
import types

import jax
import jax.numpy as jnp
from jax import lax
from jax.experimental import pallas as pl
from jax.experimental.pallas import tpu as pltpu
from jax.sharding import PartitionSpec as P

HEADS = 16
HEAD_DIM = 64
STEPS = 32


EPSILON = 1e-06
NEGATIVE = -1e30
HIGHEST = lax.Precision.HIGHEST
MESH = pl.DeviceIdType.MESH
RING = 8
ROWS = 4


def from_behind(block, axis, distance):
    devices = range(lax.axis_size(axis))
    route = [((i - distance) % len(devices), i) for i in devices]
    return lax.ppermute(block, axis, route)


def layout(lengths_row, frames):
    end_frame = jnp.cumsum(lengths_row)
    start_frame = end_frame - lengths_row
    segment = jnp.sum((frames[:, None] >= end_frame[None, :]).astype(jnp.int32), axis=1)
    chosen = segment[:, None] == jnp.arange(lengths_row.shape[0], dtype=jnp.int32)[None, :]
    position = frames - jnp.sum(jnp.where(chosen, start_frame[None, :], 0), axis=1)
    return (segment, position)


def flow_condition(steps_row, model_width):
    half_width = model_width // 2
    rate_table = jnp.exp(
        -math.log(10000.0) * jnp.arange(half_width, dtype=jnp.float32) / half_width
    )
    angles = 1000.0 * (steps_row.astype(jnp.float32) / STEPS)[:, None] * rate_table[None, :]
    return jax.nn.silu(jnp.concatenate([jnp.sin(angles), jnp.cos(angles)], axis=1))


def rotation_tables(position, head_width):
    half_width = head_width // 2
    rate_table = jnp.exp(
        -math.log(10000.0) * jnp.arange(half_width, dtype=jnp.float32) / half_width
    )
    angles = position.astype(jnp.float32)[:, None] * rate_table[None, :]
    return (jnp.cos(angles)[:, None, :], jnp.sin(angles)[:, None, :], half_width)


def rotate(head_block, position):
    cosine_part, sine_part, half_width = rotation_tables(position, head_block.shape[-1])
    first_half = head_block[..., :half_width]
    second_half = head_block[..., half_width:]
    return jnp.concatenate(
        [
            first_half * cosine_part - second_half * sine_part,
            second_half * cosine_part + first_half * sine_part,
        ],
        axis=-1,
    )


def rotate_back(head_block, position):
    cosine_part, sine_part, half_width = rotation_tables(position, head_block.shape[-1])
    first_half = head_block[..., :half_width]
    second_half = head_block[..., half_width:]
    return jnp.concatenate(
        [
            first_half * cosine_part + second_half * sine_part,
            second_half * cosine_part - first_half * sine_part,
        ],
        axis=-1,
    )


def normalize(hidden):
    centred = hidden - jnp.mean(hidden, axis=-1, keepdims=True)
    scaled = lax.rsqrt(jnp.mean(centred * centred, axis=-1, keepdims=True) + EPSILON)
    return (centred * scaled, scaled)


def norm_back(grad_normal, normal, scaled):
    centred_grad = grad_normal - jnp.mean(grad_normal, axis=-1, keepdims=True)
    return scaled * (centred_grad - normal * jnp.mean(grad_normal * normal, axis=-1, keepdims=True))


def exact_gelu(values_in):
    return jax.nn.gelu(values_in, approximate=False)


def contract_rows(left_side, right_side):
    return lax.dot_general(
        left_side, right_side, (((0,), (0,)), ((), ())), preferred_element_type=jnp.float32
    )


def heads_of(flat_block):
    return flat_block.reshape(flat_block.shape[0], HEADS, HEAD_DIM)


def per_device(
    inputs,
    skipped,
    w_skip,
    w_mod,
    w_qkv,
    w_out,
    ff_gain,
    w_up,
    w_down,
    cotangent,
    lengths,
    flow_steps,
):
    w_skip, w_mod, w_qkv, w_out, ff_gain, w_up, w_down = (
        lax.all_gather(w_skip, "grp", axis=0, tiled=True),
        lax.all_gather(w_mod, "grp", axis=0, tiled=True),
        lax.all_gather(w_qkv, "grp", axis=0, tiled=True),
        lax.all_gather(w_out, "grp", axis=0, tiled=True),
        lax.all_gather(ff_gain, "grp", axis=0, tiled=True),
        lax.all_gather(w_up, "grp", axis=0, tiled=True),
        lax.all_gather(w_down, "grp", axis=0, tiled=True),
    )
    frame_count = inputs.shape[1]
    model_width = inputs.shape[2]
    cycle_size = lax.axis_size("blk")
    device_rank = lax.axis_index("blk")
    score_scale = HEAD_DIM ** (-0.5)
    local_frames = jnp.arange(frame_count, dtype=jnp.int32)
    lengths_row = lengths[0]
    own_segment, own_position = layout(lengths_row, device_rank * frame_count + local_frames)

    def segment_of(source):
        return layout(lengths_row, source * frame_count + local_frames)[0]

    def scored(query_block, key_block, query_segment, key_segment):
        raw_scores = (
            jnp.einsum(
                "qhd,khd->hqk",
                heads_of(query_block),
                heads_of(key_block),
                preferred_element_type=jnp.float32,
            )
            * score_scale
        )
        allowed = (query_segment[:, None] == key_segment[None, :])[None]
        return (raw_scores, allowed)

    joined = jnp.concatenate([inputs[0], skipped[0]], axis=1)
    hidden = jnp.dot(joined, w_skip, preferred_element_type=jnp.float32)
    condition = flow_condition(flow_steps[0], model_width).astype(jnp.bfloat16)
    modulation = jnp.dot(condition, w_mod, preferred_element_type=jnp.float32)
    picker = (
        own_segment[:, None] == jnp.arange(lengths_row.shape[0], dtype=jnp.int32)[None, :]
    ).astype(jnp.float32)
    per_frame = jnp.dot(picker, modulation, precision=HIGHEST)
    scale_one = 1.0 + per_frame[:, :model_width]
    normal_one, spread_one = normalize(hidden)
    attn_in = (normal_one * scale_one + per_frame[:, model_width:]).astype(jnp.bfloat16)
    project = jnp.dot(attn_in, w_qkv, preferred_element_type=jnp.float32).reshape(
        frame_count, 3, HEADS, HEAD_DIM
    )
    queries = (
        rotate(project[:, 0], own_position).astype(jnp.bfloat16).reshape(frame_count, model_width)
    )
    keys_own = (
        rotate(project[:, 1], own_position).astype(jnp.bfloat16).reshape(frame_count, model_width)
    )
    values_own = project[:, 2].astype(jnp.bfloat16).reshape(frame_count, model_width)

    def forward_turn(turn_index, carried):
        key_now, value_now, running_top, running_total, running_sum = carried
        source = (device_rank - turn_index) % cycle_size
        raw_scores, allowed = scored(queries, key_now, own_segment, segment_of(source))
        raw_scores = jnp.where(allowed, raw_scores, NEGATIVE)
        new_top = jnp.maximum(running_top, jnp.max(raw_scores, axis=2, keepdims=True))
        weights = jnp.where(allowed, jnp.exp(raw_scores - new_top), 0.0)
        shrink = jnp.exp(running_top - new_top)
        running_total = running_total * shrink + jnp.sum(weights, axis=2, keepdims=True)
        running_sum = running_sum * shrink + jnp.einsum(
            "hqk,khd->hqd",
            weights.astype(jnp.bfloat16),
            heads_of(value_now),
            preferred_element_type=jnp.float32,
        )
        key_now, value_now = from_behind((key_now, value_now), "blk", 1)
        return (key_now, value_now, new_top, running_total, running_sum)

    initial = (
        keys_own,
        values_own,
        jnp.full((HEADS, frame_count, 1), NEGATIVE, jnp.float32),
        jnp.zeros((HEADS, frame_count, 1), jnp.float32),
        jnp.zeros((HEADS, frame_count, HEAD_DIM), jnp.float32),
    )
    finished = lax.fori_loop(0, cycle_size, forward_turn, initial)
    running_top, running_total, running_sum = (finished[2], finished[3], finished[4])
    attended = jnp.transpose(running_sum / running_total, (1, 0, 2)).reshape(
        frame_count, model_width
    )
    log_total = (running_top + jnp.log(running_total))[:, :, 0]
    attended_low = attended.astype(jnp.bfloat16)
    hidden_two = hidden + jnp.dot(attended_low, w_out, preferred_element_type=jnp.float32)
    normal_two, spread_two = normalize(hidden_two)
    gain_vector = ff_gain.astype(jnp.float32)
    ff_in = (normal_two * gain_vector).astype(jnp.bfloat16)
    widened = jnp.dot(ff_in, w_up, preferred_element_type=jnp.float32)
    activated, gelu_back = jax.vjp(exact_gelu, widened)
    activated_low = activated.astype(jnp.bfloat16)
    output = (
        hidden_two + jnp.dot(activated_low, w_down, preferred_element_type=jnp.float32)
    ).astype(jnp.bfloat16)
    upstream = cotangent[0]
    grad_down = contract_rows(activated_low, upstream)
    grad_activated = jnp.dot(upstream, w_down.T, preferred_element_type=jnp.float32)
    grad_widened = gelu_back(grad_activated)[0].astype(jnp.bfloat16)
    grad_up = contract_rows(ff_in, grad_widened)
    grad_ff_in = jnp.dot(grad_widened, w_up.T, preferred_element_type=jnp.float32)
    grad_gain = jnp.sum(grad_ff_in * normal_two, axis=0)
    grad_hidden_two = upstream.astype(jnp.float32) + norm_back(
        grad_ff_in * gain_vector, normal_two, spread_two
    )
    grad_two_low = grad_hidden_two.astype(jnp.bfloat16)
    grad_out = contract_rows(attended_low, grad_two_low)
    grad_attended = jnp.dot(grad_two_low, w_out.T, preferred_element_type=jnp.float32).astype(
        jnp.bfloat16
    )
    delta = jnp.transpose(jnp.sum(heads_of(grad_attended.astype(jnp.float32) * attended), axis=2))
    zero_grad = jnp.zeros((frame_count, model_width), jnp.float32)

    def pair_terms(
        query_block,
        upstream_block,
        key_block,
        value_block,
        total_block,
        delta_block,
        query_segment,
        key_segment,
    ):
        raw_scores, allowed = scored(query_block, key_block, query_segment, key_segment)
        prob_block = jnp.where(allowed, jnp.exp(raw_scores - total_block[:, :, None]), 0.0)
        value_term = jnp.einsum(
            "hqk,qhd->khd",
            prob_block.astype(jnp.bfloat16),
            heads_of(upstream_block),
            preferred_element_type=jnp.float32,
        ).reshape(frame_count, model_width)
        prob_grad = jnp.einsum(
            "qhd,khd->hqk",
            heads_of(upstream_block),
            heads_of(value_block),
            preferred_element_type=jnp.float32,
        )
        score_grad = (prob_block * (prob_grad - delta_block[:, :, None])).astype(jnp.bfloat16)
        query_term = (
            jnp.einsum(
                "hqk,khd->qhd", score_grad, heads_of(key_block), preferred_element_type=jnp.float32
            ).reshape(frame_count, model_width)
            * score_scale
        )
        key_term = (
            jnp.einsum(
                "hqk,qhd->khd",
                score_grad,
                heads_of(query_block),
                preferred_element_type=jnp.float32,
            ).reshape(frame_count, model_width)
            * score_scale
        )
        return (query_term, key_term, value_term)

    def keys_turn(turn_index, carried):
        key_now, value_now, key_grad, value_grad, query_grad = carried
        source = (device_rank - turn_index) % cycle_size
        query_term, key_term, value_term = pair_terms(
            queries,
            grad_attended,
            key_now,
            value_now,
            log_total,
            delta,
            own_segment,
            segment_of(source),
        )
        key_now, value_now = from_behind((key_now, value_now), "blk", 1)
        key_grad, value_grad = (
            from_behind((key_grad + key_term).astype(jnp.bfloat16), "blk", 1).astype(jnp.float32),
            from_behind((value_grad + value_term).astype(jnp.bfloat16), "blk", 1).astype(
                jnp.float32
            ),
        )
        return (key_now, value_now, key_grad, value_grad, query_grad + query_term)

    done = lax.fori_loop(
        0, cycle_size, keys_turn, (keys_own, values_own, zero_grad, zero_grad, zero_grad)
    )
    key_grad, value_grad, query_grad = (done[2], done[3], done[4])
    grad_project = jnp.concatenate(
        [
            rotate_back(heads_of(query_grad), own_position).reshape(frame_count, model_width),
            rotate_back(heads_of(key_grad), own_position).reshape(frame_count, model_width),
            value_grad,
        ],
        axis=1,
    ).astype(jnp.bfloat16)
    grad_qkv = contract_rows(attn_in, grad_project)
    grad_attn_in = jnp.dot(grad_project, w_qkv.T, preferred_element_type=jnp.float32)
    mod_terms = jnp.concatenate([grad_attn_in * normal_one, grad_attn_in], axis=1)
    grad_modulation = jnp.dot(picker.T, mod_terms, precision=HIGHEST)
    grad_mod = jnp.dot(condition.astype(jnp.float32).T, grad_modulation, precision=HIGHEST)
    grad_hidden = grad_hidden_two + norm_back(grad_attn_in * scale_one, normal_one, spread_one)
    grad_hidden_low = grad_hidden.astype(jnp.bfloat16)
    grad_skip_weight = contract_rows(joined, grad_hidden_low)
    grad_joined = jnp.dot(grad_hidden_low, w_skip.T, preferred_element_type=jnp.float32)
    shards = (
        lax.psum_scatter(
            grad_skip_weight.astype(jnp.bfloat16), "grp", scatter_dimension=0, tiled=True
        ).astype(jnp.float32),
        lax.psum_scatter(
            grad_mod.astype(jnp.bfloat16), "grp", scatter_dimension=0, tiled=True
        ).astype(jnp.float32),
        lax.psum_scatter(
            grad_qkv.astype(jnp.bfloat16), "grp", scatter_dimension=0, tiled=True
        ).astype(jnp.float32),
        lax.psum_scatter(
            grad_out.astype(jnp.bfloat16), "grp", scatter_dimension=0, tiled=True
        ).astype(jnp.float32),
        lax.psum_scatter(
            grad_gain.astype(jnp.bfloat16), "grp", scatter_dimension=0, tiled=True
        ).astype(jnp.float32),
        lax.psum_scatter(
            grad_up.astype(jnp.bfloat16), "grp", scatter_dimension=0, tiled=True
        ).astype(jnp.float32),
        lax.psum_scatter(
            grad_down.astype(jnp.bfloat16), "grp", scatter_dimension=0, tiled=True
        ).astype(jnp.float32),
    )
    totals = lax.psum(
        (shards[0], shards[1], shards[2], shards[3], shards[4], shards[5], shards[6]), "blk"
    )
    return (
        output[None],
        grad_joined[:, :model_width][None],
        grad_joined[:, model_width:][None],
        totals[0],
        totals[1],
        totals[2],
        totals[3],
        totals[4],
        totals[5],
        totals[6],
    )


def dot_plain(left_side, right_side):
    return jnp.dot(left_side, right_side, preferred_element_type=jnp.float32)


def dot_across(left_side, right_side):
    return lax.dot_general(
        left_side, right_side, (((1,), (1,)), ((), ())), preferred_element_type=jnp.float32
    )


def ring_place(rank):
    odd = lax.rem(rank, 2)
    return (1 - odd) * (rank // 2) + odd * ((15 - rank) // 2)


def ring_rank(place):
    upper = place // 4
    return (1 - upper) * (2 * place) + upper * (15 - 2 * place)


class Ring:
    def __init__(self, part, land, sems, rank, group_rank):
        self.part, self.land = part, land
        self.sems = sems
        self.rank, self.group_rank = rank, group_rank
        self.place = ring_place(rank)
        self.half = part.shape[1] // 2
        self.copies = {}

    def block_at(self, offset):
        return ring_rank(lax.rem(self.place + offset + 2 * RING, RING))

    def rows(self, way):
        return pl.ds(way * self.half, self.half)

    def send(self, kind, step, way, source, target):
        to = ring_rank(lax.rem(self.place + (1 if way == 0 else RING - 1), RING))
        copy = pltpu.make_async_remote_copy(
            src_ref=source,
            dst_ref=target,
            send_sem=self.sems.at[kind, 0, way, step],
            recv_sem=self.sems.at[kind, 1, way, step],
            device_id=(to, self.group_rank),
            device_id_type=MESH,
        )
        copy.start()
        self.copies[kind, step, way] = copy

    def sum_step(self, step):
        if step == 1:
            for way in range(2):
                self.copies[0, 0, way].wait_send()
        for way in range(2):
            block = self.block_at((-1 if way == 0 else 1) * (step + 1))
            rows = self.rows(way)
            if step > 0:
                self.copies[0, step - 1, way].wait_recv()
                tile = min(self.half, 32)

                def add(i, carry, way=way, block=block, tile=tile):
                    at = pl.ds(pl.multiple_of(way * self.half + i * tile, tile), tile)
                    total = self.part[block, at].astype(jnp.float32) + self.land[
                        step - 1, at
                    ].astype(jnp.float32)
                    self.land[step - 1, at] = total.astype(jnp.bfloat16)
                    return carry

                lax.fori_loop(0, self.half // tile, add, 0)
            if step < RING - 1:
                source = self.part.at[block, rows] if step == 0 else self.land.at[step - 1, rows]
                self.send(0, step, way, source, self.land.at[step, rows])

    def total(self):
        return self.land.at[RING - 2]

    def spread_step(self, step):
        for way in range(2):
            block = self.block_at((-1 if way == 0 else 1) * step)
            rows = self.rows(way)
            if step > 0:
                self.copies[1, step - 1, way].wait_recv()
            if step < RING - 1:
                target = self.part.at[block, rows]
                self.send(1, step, way, target, target)

    def finish(self):
        for (kind, step, _), copy in self.copies.items():
            if kind or step:
                copy.wait_send()


def block_kernel(names, *refs):
    n = types.SimpleNamespace(**dict(zip(names, refs)))
    low, full = jnp.bfloat16, jnp.float32
    rank, group_rank = lax.axis_index("blk"), lax.axis_index("grp")
    core, chip = lax.rem(group_rank, 2), group_rank // 2
    sibling = (rank, group_rank + 1 - 2 * core)
    across = (rank, group_rank + 2 - 4 * chip)
    frames, width = n.cotangent.shape
    half = 2 * frames
    columns = width // ROWS
    mine, theirs = core * half, (1 - core) * half
    own_slot = 2 * core + chip
    pair_row, pair_side = rank // 2, lax.rem(rank, 2)
    sent = []

    def lines(offset, size):
        return pl.ds(pl.multiple_of(offset, min(size, 128)), size)

    def slot_of(row):
        return 2 * lax.rem(row, 2) + row // 2

    def row_of(slot):
        return 2 * lax.rem(slot, 2) + slot // 2

    def group(other):
        return lax.rem(group_rank + other, ROWS)

    def block(other):
        return lax.rem(rank + other, RING)

    def link(source, target, send_sem, recv_sem, device):
        return pltpu.make_async_remote_copy(
            src_ref=source,
            dst_ref=target,
            send_sem=send_sem,
            recv_sem=recv_sem,
            device_id=device,
            device_id_type=MESH,
        )

    def push(source, target, sems, index, device):
        copy = link(source, target, sems.at[(0,) + index], sems.at[(1,) + index], device)
        copy.start()
        sent.append(copy)
        return copy

    def load(source, target, index):
        copy = pltpu.make_async_copy(source, target, n.load_sem.at[index])
        copy.start()
        return copy

    def tiles(count, tile, body):
        def step(i, carry):
            body(pl.multiple_of(i * tile, tile))
            return carry

        lax.fori_loop(0, count // tile, step, 0)

    joined_loads = [
        load((n.inputs, n.skipped)[t // 2].at[:, pl.ds((t % 2) * 512, 512)], n.joined_own.at[t], t)
        for t in range(ROWS)
    ]
    upstream_load = load(n.cotangent, n.upstream.at[lines(own_slot * frames, frames)], 4)
    skip_load = load(n.w_skip, n.skip_held, 5)
    mod_load = load(n.w_mod, n.mod_held, 6)
    out_load = load(n.w_out, n.out_held, 7)
    down_load = load(n.w_down, n.down_held, 8)
    pieces = [(side, kind) for side in range(2) for kind in range(3)]

    def qkv_piece(target, side, kind):
        return n.w_qkv.at[:, pl.ds(pl.multiple_of(kind * width + target * columns + side * 128, 128), 128)]

    def qkv_place(side, kind):
        return n.qkv_held.at[lines(group_rank * columns, columns), pl.ds((side * 3 + kind) * 128, 128)]

    qkv_loads = [
        load(qkv_piece(group_rank, *piece), qkv_place(*piece), 9 + i)
        for i, piece in enumerate(pieces)
    ]
    hidden_units = n.up_held.shape[1]

    def up_piece(target):
        return n.w_up.at[:, pl.ds(pl.multiple_of(target * hidden_units, 128), hidden_units)]

    up_place = n.up_held.at[lines(group_rank * columns, columns)]
    up_load = load(up_piece(group_rank), up_place, 15)

    barrier = pltpu.get_barrier_semaphore()
    for other in range(1, ROWS):
        pl.semaphore_signal(barrier, inc=1, device_id=(rank, group(other)), device_id_type=MESH)
    for other in range(1, RING):
        pl.semaphore_signal(barrier, inc=1, device_id=(block(other), group_rank), device_id_type=MESH)
    for copy in joined_loads:
        copy.wait()
    pl.semaphore_wait(barrier, ROWS + RING - 2)

    joined_place = n.joined.at[lines(own_slot * frames, frames)]
    joined_sends = [
        push(n.joined_own.at[group(o)], joined_place, n.joined_sem, (o - 1,), (rank, group(o)))
        for o in (2, 1, 3)
    ]
    small_sends = [
        push(n.small, n.smalls.at[group_rank], n.small_sem, (o - 1,), (rank, group(o)))
        for o in (2, 1, 3)
    ]
    qkv_sends = [
        push(
            qkv_piece(group(o), *piece),
            qkv_place(*piece),
            n.qkv_sem,
            (o - 1, i),
            (rank, group(o)),
        )
        for o in (2, 1, 3)
        for i, piece in enumerate(pieces)
    ]
    n.joined[lines(own_slot * frames, frames)] = n.joined_own[group_rank]
    n.smalls[group_rank] = n.small[...]
    for copy in small_sends:
        copy.wait_recv()

    steps = jnp.concatenate([n.smalls[(0, 2, 1, 3)[s], 0] for s in range(ROWS)], axis=0)
    steps = jnp.concatenate([steps, steps], axis=1)
    lane = lax.broadcasted_iota(jnp.int32, steps.shape, 1) + lax.rem(group_rank, 2) * columns
    rate = jnp.exp(-math.log(10000.0) * lane.astype(full) / (width // 2))
    angles = 1000.0 * (steps / STEPS) * rate
    turned = jnp.where(group_rank >= 2, jnp.cos(angles), jnp.sin(angles))
    n.condition[...] = (turned / (1.0 + jnp.exp(-turned))).astype(low)
    mod_load.wait()

    def mod_tile(at):
        where = pl.ds(at, 512)
        n.mod_part[:, where] = dot_plain(n.condition[...], n.mod_held[:, where])

    tiles(2 * width, 512, mod_tile)
    mod_first = push(
        n.mod_part.at[pl.ds(pl.multiple_of(16 * (1 - core), 16), 16)], n.mod_land.at[0], n.mod_sem, (0,), sibling
    )

    gains = [n.smalls[r, 5 + i][0:1] for r in range(ROWS) for i in range(2)]
    n.gain[...] = jnp.broadcast_to(jnp.concatenate(gains, axis=1), n.gain.shape)

    def picked(row, first, count):
        spot = (lax.broadcasted_iota(jnp.int32, (count, 128), 0) + first).astype(full)
        return (spot >= n.smalls[row, 3][0:1]) & (spot < n.smalls[row, 4][0:1]), spot

    lanes = lax.broadcasted_iota(jnp.int32, (frames, 128), 1)
    turn_rate = jnp.exp(-math.log(10000.0) * lax.rem(lanes, 32).astype(full) / 32)
    turn_sign = jnp.where(lax.rem(lanes, 64) < 32, -1.0, 1.0)

    def turn_tables(row, first, cosine, sine, at):
        chosen, spot = picked(row, first, frames)
        start = jnp.where(chosen & (lanes < 8), n.smalls[row, 3][0:1], 0.0)
        position = spot - jnp.sum(start, axis=1, keepdims=True)
        angle = position * turn_rate
        cosine[at] = jnp.cos(angle)
        sine[at] = jnp.sin(angle) * turn_sign

    def swapped(value):
        ahead = pltpu.roll(value, 96, 1)
        behind = pltpu.roll(value, 32, 1)
        return jnp.where(lax.rem(lanes, 64) < 32, ahead, behind)

    def partial_sum(index, left_ref, right_tile):
        def to_send(at):
            n.send_one[:, pl.ds(at, 256)] = right_tile(left_ref[lines(theirs, half)], at).astype(low)

        def to_keep(at):
            n.keep[:, pl.ds(at, 256)] = right_tile(left_ref[lines(mine, half)], at)

        if index > 0:
            for copy in group_copies[index - 1][0]:
                copy.wait_send()
        tiles(width, 256, to_send)
        first = [
            push(
                n.send_one.at[pl.ds(k * frames, frames)],
                n.land_one.at[index, pl.ds(k * frames, frames)],
                n.first_sem,
                (index, k),
                sibling,
            )
            for k in range(2)
        ]
        tiles(width, 256, to_keep)
        return first

    def cross_sum(index, first):
        if index > 0:
            for copy in group_copies[index - 1][1]:
                copy.wait_send()
        second = []
        for k in range(2):
            first[k].wait_recv()

            def add(at, k=k):
                where = pl.ds(k * frames + at, 32)
                total = n.keep[where] + n.land_one[index, where].astype(full)
                n.keep[where] = total
                n.send_two[where] = total.astype(low)

            tiles(frames, 32, add)
            second.append(
                push(
                    n.send_two.at[pl.ds(k * frames, frames)],
                    n.land_two.at[index, pl.ds(k * frames, frames)],
                    n.second_sem,
                    (index, k),
                    across,
                )
            )
        group_copies[index] = (first, second)
        return second

    group_copies = {}

    def mean(value):
        return jnp.mean(value, axis=-1, keepdims=True)

    def share(buffer, k, sems):
        where = lines(mine + k * frames, frames)
        return push(buffer.at[where], buffer.at[where], sems, (k,), sibling)

    skip_load.wait()
    for copy in joined_sends:
        copy.wait_recv()

    def skip_tile(left, at):
        return dot_plain(left, n.skip_held[:, pl.ds(at, 256)])

    first = partial_sum(0, n.joined, skip_tile)
    mod_first.wait_recv()
    mod_mine = n.mod_part[pl.ds(pl.multiple_of(16 * core, 16), 16)] + n.mod_land[0]
    n.mod_send[...] = mod_mine
    mod_second = push(n.mod_send, n.mod_land.at[1], n.mod_sem, (1,), across)
    second = cross_sum(0, first)
    up_sends = [
        push(up_piece(group(o)), up_place, n.up_sem, (o - 1,), (rank, group(o))) for o in (2, 1, 3)
    ]
    upstream_load.wait()
    own_lines = lines(own_slot * frames, frames)
    upstream_sends = [
        push(n.upstream.at[own_lines], n.upstream.at[own_lines], n.upstream_sem, (i,), device)
        for i, device in enumerate((across, sibling))
    ]
    for slot in range(ROWS):
        turn_tables(
            (0, 2, 1, 3)[slot],
            rank * frames,
            n.cosine,
            n.sine,
            pl.ds(slot * frames, frames),
        )
    mod_second.wait_recv()
    mod_total = n.mod_send[...] + n.mod_land[1]
    for k in range(2):
        row = 2 * k + core
        values = mod_total[8 * k : 8 * k + 8]
        high = values.astype(low).astype(full)
        stack = jnp.concatenate([high, values - high], axis=0).astype(low)
        chosen = picked(row, rank * frames, frames)[0]
        picker = jnp.where(chosen, 1.0, 0.0).astype(low)[:, :16]

        def per_frame(at, stack=stack, picker=picker, k=k):
            del at

        where = pl.ds(k * frames, frames)
        n.scale_one[where] = 1.0 + dot_plain(picker, stack[:, :width])
        n.shift_one[where] = dot_plain(picker, stack[:, width:])

    attn_sends = []
    for k in range(2):
        second[k].wait_recv()

        def norm_one(at, k=k):
            where = pl.ds(k * frames + at, 32)
            hidden = n.keep[where] + n.land_two[0, where].astype(full)
            n.hidden[where] = hidden
            centred = hidden - mean(hidden)
            spread = lax.rsqrt(mean(centred * centred) + EPSILON)
            normal = centred * spread
            n.normal_one[where] = normal
            n.spread_one[where] = jnp.broadcast_to(spread, (32, 128))
            n.attn_in[lines(mine + k * frames + at, 32)] = (
                normal * n.scale_one[where] + n.shift_one[where]
            ).astype(low)

        tiles(frames, 32, norm_one)
        attn_sends.append(share(n.attn_in, k, n.attn_sem))

    for copy in qkv_loads:
        copy.wait()
    for copy in qkv_sends:
        copy.wait_recv()

    def to_heads(offset, value_of, target, sems, wide, send_buffer):
        for k in range(2):
            slot = offset // frames + k
            for side in range(2):
                to = 2 * row_of(slot) + side
                value = value_of(k, side, slot)

                @pl.when(to != rank)
                def _():
                    send_buffer[to] = value
                    link(
                        send_buffer.at[to],
                        target.at[lines(rank * frames, frames)],
                        sems.at[0, to],
                        sems.at[1, rank],
                        (to, group_rank),
                    ).start()

                @pl.when(to == rank)
                def _():
                    target[lines(rank * frames, frames)] = value

    def heads_arrive(target, sems):
        for other in range(1, RING):
            source = block(other)
            where = target.at[lines(source * frames, frames)]
            link(where, where, sems.at[0, source], sems.at[1, source], (source, group_rank)).wait_recv()

    def project_half(offset):
        def project_tile(at):
            n.project[:, pl.ds(at, 256)] = dot_plain(
                n.attn_in[lines(offset, half)], n.qkv_held[:, pl.ds(at, 256)]
            )

        tiles(3 * columns, 256, project_tile)

        def value_of(k, side, slot):
            where = lines(slot * frames, frames)
            cosine, sine = n.cosine[where], n.sine[where]
            blocks = []
            for kind in range(3):
                value = n.project[pl.ds(k * frames, frames), pl.ds((side * 3 + kind) * 128, 128)]
                if kind < 2:
                    value = value * cosine + swapped(value) * sine
                blocks.append(value.astype(low))
            return jnp.concatenate(blocks, axis=1)

        to_heads(offset, value_of, n.paired, n.pair_sem, 384, n.pair_send)

    project_half(mine)
    for copy in attn_sends:
        copy.wait_recv()
    project_half(theirs)

    def row_tables(at):
        turn_tables(pair_row, at, n.row_cosine, n.row_sine, pl.ds(at, frames))
        chosen = jnp.where(picked(pair_row, at, frames)[0], 1.0, 0.0)
        n.chosen[pl.ds(at, frames)] = chosen.astype(low)

    tiles(RING * frames, frames, row_tables)
    heads_arrive(n.paired, n.pair_sem)

    def masked_parts(at):
        where = pl.ds(at, frames)
        query, key = n.paired[where, 0:128], n.paired[where, 128:256]
        chosen = n.chosen[where]
        first_head = lanes < 64
        blocked = jnp.where(
            lax.rem(lanes, 64) < 8, NEGATIVE * (1.0 - chosen.astype(full)), 0.0
        ).astype(low)
        scaled = (query.astype(full) * HEAD_DIM ** (-0.5)).astype(low)
        n.query_head[0, where] = jnp.where(first_head, scaled, chosen)
        n.query_head[1, where] = jnp.where(first_head, chosen, scaled)
        n.key_head[0, where] = jnp.where(first_head, key, blocked)
        n.key_head[1, where] = jnp.where(first_head, blocked, key)
        n.query_turned[:, where] = jnp.transpose(query.astype(full)).astype(low)

    tiles(RING * frames, frames, masked_parts)
    all_frames = RING * frames
    pair_place = (lines(slot_of(pair_row) * frames, frames), lines(pair_side * 128, 128))

    def attend(at):
        where = pl.ds(at, half)
        sums = []
        for head in range(2):
            scores = dot_across(n.query_head[head, where], n.key_head[head])
            top = jnp.max(scores, axis=1, keepdims=True)
            weights = jnp.exp(scores - top)
            total = jnp.sum(weights, axis=1, keepdims=True)
            shares = (weights * (1.0 / total)).astype(low)
            n.shares[head, where] = shares
            sums.append(dot_plain(shares, n.paired[:, 256:384]))
        first_head = lax.broadcasted_iota(jnp.int32, (half, 128), 1) < 64
        value = jnp.where(first_head, sums[0], sums[1])
        n.attended_pair[where] = value
        n.attended_send[where] = value.astype(low)
        for k in range(2):
            to = at // frames + k
            place = lines(at + k * frames, frames)

            @pl.when(to != rank)
            def _():
                link(
                    n.attended_send.at[place],
                    n.attended.at[pair_place],
                    n.attended_sem.at[0, to],
                    n.attended_sem.at[1, rank],
                    (to, group_rank),
                ).start()

            @pl.when(to == rank)
            def _():
                n.attended[pair_place] = n.attended_send[place]

    tiles(all_frames, half, attend)

    def pairs_arrive(buffer, sems, wide):
        for other in range(1, RING):
            source = block(other)
            where = buffer.at[
                lines(slot_of(source // 2) * frames, frames),
                pl.ds(pl.multiple_of(lax.rem(source, 2) * wide, 128), wide),
            ]
            link(where, where, sems.at[0, source], sems.at[1, source], (source, group_rank)).wait_recv()

    upstream_sends[0].wait_recv()
    other_lines = lines((2 * core + 1 - chip) * frames, frames)
    upstream_sends.append(
        push(n.upstream.at[other_lines], n.upstream.at[other_lines], n.upstream_sem, (2,), sibling)
    )
    pairs_arrive(n.attended, n.attended_sem, 128)

    out_load.wait()
    first = partial_sum(1, n.attended, lambda left, at: dot_plain(left, n.out_held[:, pl.ds(at, 256)]))
    second = cross_sum(1, first)
    ff_sends = []
    for k in range(2):
        second[k].wait_recv()

        def norm_two(at, k=k):
            where = pl.ds(k * frames + at, 32)
            hidden = n.hidden[where] + n.keep[where] + n.land_two[1, where].astype(full)
            n.hidden[where] = hidden
            centred = hidden - mean(hidden)
            spread = lax.rsqrt(mean(centred * centred) + EPSILON)
            normal = centred * spread
            n.normal_two[where] = normal
            n.spread_two[where] = jnp.broadcast_to(spread, (32, 128))
            n.ff_in[lines(mine + k * frames + at, 32)] = (normal * n.gain[0:1]).astype(low)

        tiles(frames, 32, norm_two)
        ff_sends.append(share(n.ff_in, k, n.ff_sem))

    up_load.wait()
    down_load.wait()
    for copy in up_sends:
        copy.wait_recv()
    for copy in upstream_sends[1:]:
        copy.wait_recv()

    def feed_half(offset):
        where = lines(offset, half)

        def feed_tile(at):
            widened = dot_plain(n.ff_in[where], n.up_held[:, pl.ds(at, 256)])
            grad = dot_across(n.upstream[where], n.down_held[pl.ds(at, 256)])
            share_of = 0.5 * (1.0 + lax.erf(widened * math.sqrt(0.5)))
            slope = share_of + widened * jnp.exp(-0.5 * widened * widened) * (
                1.0 / math.sqrt(2.0 * math.pi)
            )
            n.activated[where, pl.ds(at, 256)] = (widened * share_of).astype(low)
            n.grad_widened[where, pl.ds(at, 256)] = (grad * slope).astype(low)

        tiles(hidden_units, 256, feed_tile)

    feed_half(mine)
    for copy in ff_sends:
        copy.wait_recv()
    feed_half(theirs)
    first = partial_sum(
        2, n.grad_widened, lambda left, at: dot_across(left, n.up_held[pl.ds(at, 256)])
    )
    second = cross_sum(2, first)

    def down_tile(at):
        value = contract_rows(n.activated[:, pl.ds(at, 256)], n.upstream[...]).astype(low)
        n.down_total[at // 128] = value[:128]
        n.down_total[at // 128 + 1] = value[128:]

    tiles(hidden_units, 256, down_tile)

    def up_tile(at):
        value = contract_rows(n.ff_in[:, pl.ds(at, columns)], n.grad_widened[...]).astype(low)
        deep = columns // RING
        for j in range(RING):
            n.up_total[j, pl.ds(pl.multiple_of(at // RING, deep), deep)] = value[
                j * deep : (j + 1) * deep
            ]

    tiles(width, columns, up_tile)

    gain_sums = jnp.zeros((1, width), full)
    grad_sends = []
    for k in range(2):
        second[k].wait_recv()
        weight = (1 - jnp.abs(chip - k)).astype(full)

        def back_two(i, sums, k=k, weight=weight):
            at = pl.multiple_of(i * 32, 32)
            where = pl.ds(k * frames + at, 32)
            grad = n.keep[where] + n.land_two[2, where].astype(full)
            normal = n.normal_two[where]
            scaled = grad * n.gain[0:1]
            back = n.spread_two[where][:, 0:1] * (
                scaled - mean(scaled) - normal * mean(scaled * normal)
            )
            total = n.upstream[lines(mine + k * frames + at, 32)].astype(full) + back
            n.grad_two[where] = total
            n.grad_two_low[lines(mine + k * frames + at, 32)] = total.astype(low)
            return sums + weight * jnp.sum(grad * normal, axis=0, keepdims=True)

        gain_sums = lax.fori_loop(0, frames // 32, back_two, gain_sums)
        grad_sends.append(share(n.grad_two_low, k, n.grad_two_sem))
    n.mod_sums[8:16] = jnp.zeros((8, 2 * width), full)
    n.mod_sums[8:9, :width] = gain_sums

    def attended_half(offset):
        value = dot_across(n.grad_two_low[lines(offset, half)], n.out_held[...]).astype(low)

        def value_of(k, side, slot):
            return value[k * frames : (k + 1) * frames, side * 128 : side * 128 + 128]

        to_heads(offset, value_of, n.grad_pair, n.grad_pair_sem, 128, n.grad_pair_send)

    attended_half(mine)
    for copy in grad_sends:
        copy.wait_recv()
    attended_half(theirs)
    value = contract_rows(n.attended[...], n.grad_two_low[...]).astype(low)
    for j in range(RING):
        n.out_total[j] = value[j * 32 : (j + 1) * 32]

    first = partial_sum(3, n.activated, lambda left, at: dot_plain(left, n.down_held[:, pl.ds(at, 256)]))
    output_second = cross_sum(3, first)

    heads_arrive(n.grad_pair, n.grad_pair_sem)

    def turn_upstream(at):
        where = pl.ds(at, frames)
        n.grad_turned[:, where] = jnp.transpose(n.grad_pair[where].astype(full)).astype(low)

    tiles(all_frames, frames, turn_upstream)
    n.key_turned[...] = jnp.zeros(n.key_turned.shape, full)
    n.value_turned[...] = jnp.zeros(n.value_turned.shape, full)

    def back_turned(value, where):
        return value * n.row_cosine[where] - swapped(value) * n.row_sine[where]

    def attend_back(at):
        where = pl.ds(at, half)
        first_head = lax.broadcasted_iota(jnp.int32, (half, 128), 1) < 64
        grad = n.grad_pair[where]
        product = grad.astype(full) * n.attended_pair[where]
        terms = []
        for head in range(2):
            here = first_head if head == 0 else jnp.logical_not(first_head)
            delta = jnp.sum(jnp.where(here, product, 0.0), axis=1, keepdims=True)
            grad_head = jnp.where(here, grad, jnp.zeros_like(grad))
            prob_grad = dot_across(grad_head, n.paired[:, 256:384])
            shares = n.shares[head, where]
            score_grad = (shares.astype(full) * (prob_grad - delta)).astype(low)
            terms.append(dot_plain(score_grad, n.paired[:, 128:256]))
            rows = pl.ds(head * 64, 64)
            n.value_turned[rows] += dot_plain(n.grad_turned[rows, where], shares)
            n.key_turned[rows] += dot_plain(n.query_turned[rows, where], score_grad)
        query_grad = jnp.where(first_head, terms[0], terms[1]) * HEAD_DIM ** (-0.5)
        for k in range(2):
            place = lines(at + k * frames, frames)
            n.project_send[place, 0:128] = back_turned(
                query_grad[k * frames : (k + 1) * frames], place
            ).astype(low)

    tiles(all_frames, half, attend_back)
    project_place = (lines(slot_of(pair_row) * frames, frames), lines(pair_side * 384, 384))

    def keys_back(at):
        place = pl.ds(at, frames)
        key_grad = jnp.transpose(n.key_turned[:, place]) * HEAD_DIM ** (-0.5)
        n.project_send[place, 128:256] = back_turned(key_grad, place).astype(low)
        n.project_send[place, 256:384] = jnp.transpose(n.value_turned[:, place]).astype(low)
        to = at // frames

        @pl.when(to != rank)
        def _():
            link(
                n.project_send.at[place],
                n.grad_project.at[project_place],
                n.project_sem.at[0, to],
                n.project_sem.at[1, rank],
                (to, group_rank),
            ).start()

        @pl.when(to == rank)
        def _():
            n.grad_project[project_place] = n.project_send[place]

    tiles(all_frames, frames, keys_back)

    for copy in output_second:
        copy.wait_recv()

    def finish_output(at):
        where = lines(chip * frames + at, 32)
        n.output[pl.ds(at, 32)] = (
            n.hidden[where] + n.keep[where] + n.land_two[3, where].astype(full)
        ).astype(low)

    tiles(frames, 32, finish_output)
    pairs_arrive(n.grad_project, n.project_sem, 384)

    first = partial_sum(
        4, n.grad_project, lambda left, at: dot_across(left, n.qkv_held[pl.ds(at, 256)])
    )
    second = cross_sum(4, first)

    def qkv_tile(at):
        value = contract_rows(n.attn_in[:, pl.ds(at, columns)], n.grad_project[...]).astype(low)
        deep = columns // RING
        for j in range(RING):
            n.qkv_total[j, pl.ds(pl.multiple_of(at // RING, deep), deep)] = value[
                j * deep : (j + 1) * deep
            ]

    tiles(width, columns, qkv_tile)
    hidden_sends = []
    for k in range(2):
        second[k].wait_recv()

        def back_one(at, k=k):
            where = pl.ds(k * frames + at, 32)
            grad = n.keep[where] + n.land_two[4, where].astype(full)
            normal = n.normal_one[where]
            scaled = grad * n.scale_one[where]
            back = n.spread_one[where][:, 0:1] * (
                scaled - mean(scaled) - normal * mean(scaled * normal)
            )
            n.grad_hidden[lines(mine + k * frames + at, 32)] = (n.grad_two[where] + back).astype(low)

            @pl.when(chip == k)
            def _():
                n.mod_terms[pl.ds(at, 32), :width] = grad * normal
                n.mod_terms[pl.ds(at, 32), width:] = grad

        tiles(frames, 32, back_one)
        hidden_sends.append(share(n.grad_hidden, k, n.grad_hidden_sem))

    spot = (lax.broadcasted_iota(jnp.int32, (8, frames), 1) + rank * frames).astype(full)
    chosen = (spot >= n.small[1]) & (spot < n.small[2])
    picker = jnp.where(chosen, 1.0, 0.0)

    def mod_sum(at):
        where = pl.ds(at, 512)
        n.mod_sums[0:8, where] = jnp.dot(picker, n.mod_terms[:, where], precision=HIGHEST)

    tiles(2 * width, 512, mod_sum)
    for other in range(1, RING):
        to = block(other)
        push(
            n.mod_sums.at[:, pl.ds(pl.multiple_of(to * 256, 256), 256)],
            n.sums_land.at[rank],
            n.sums_sem,
            (other - 1,),
            (to, group_rank),
        )
    sums_copies = sent[-(RING - 1) :]
    n.sums_land[rank] = n.mod_sums[:, pl.ds(pl.multiple_of(rank * 256, 256), 256)]

    for copy in hidden_sends:
        copy.wait_recv()
    back = dot_across(n.grad_hidden[...], n.skip_held[...]).astype(low)
    n.joined_send[...] = back
    grad_joined_copies = []
    for other in (2, 1, 3):
        to = group(other)
        grad_joined_copies.append(
            push(
                n.joined_send.at[lines(slot_of(to) * frames, frames)],
                n.grad_joined.at[group_rank],
                n.grad_joined_sem,
                (other - 1,),
                (rank, to),
            )
        )
    n.grad_joined[group_rank] = n.joined_send[own_lines]

    def skip_weight_tile(at):
        value = contract_rows(n.joined[:, pl.ds(at, 256)], n.grad_hidden[...]).astype(low)
        for j in range(4):
            n.skip_total[at // 64 + j] = value[j * 64 : (j + 1) * 64]

    tiles(n.joined.shape[1], 256, skip_weight_tile)

    for copy in sums_copies:
        copy.wait_recv()
    n.sums_send[...] = jnp.sum(n.sums_land[...], axis=0)
    n.mod_grad[rank, group_rank] = n.sums_send[...]
    group_sums = [
        push(
            n.sums_send,
            n.mod_grad.at[rank, group_rank],
            n.sums_group_sem,
            (other - 1,),
            (rank, group(other)),
        )
        for other in (2, 1, 3)
    ]
    for copy in group_sums:
        copy.wait_recv()
    mod_spread = [
        push(
            n.mod_grad.at[rank],
            n.mod_grad.at[rank],
            n.sums_block_sem,
            (other - 1,),
            (block(other), group_rank),
        )
        for other in range(1, RING)
    ]

    rings = [
        Ring(n.down_total, n.down_land, n.down_sem, rank, group_rank),
        Ring(n.up_total, n.up_land, n.up_ring_sem, rank, group_rank),
        Ring(n.qkv_total, n.qkv_land, n.qkv_ring_sem, rank, group_rank),
        Ring(n.skip_total, n.skip_land, n.skip_ring_sem, rank, group_rank),
        Ring(n.out_total, n.out_land, n.out_ring_sem, rank, group_rank),
    ]
    for step in range(RING):
        for ring in rings:
            ring.sum_step(step)
    turns = []
    for index, (ring, place) in enumerate(((rings[1], n.up_turn), (rings[2], n.qkv_turn))):
        deep = columns // RING
        for other in (2, 1, 3):
            turns.append(
                push(
                    ring.total().at[lines(group(other) * deep, deep)],
                    place.at[lines(group_rank * deep, deep)],
                    n.turn_sem,
                    (index, other - 1),
                    (rank, group(other)),
                )
            )
        place[lines(group_rank * deep, deep)] = ring.land[RING - 2, lines(group_rank * deep, deep)]
    for ring in (rings[0], rings[3], rings[4]):
        ring.part[rank] = ring.land[RING - 2]
    for copy in turns:
        copy.wait_recv()
    n.up_total[rank] = n.up_turn[...]
    n.qkv_total[rank] = n.qkv_turn[...]
    for step in range(RING):
        for ring in rings:
            ring.spread_step(step)
    for ring in rings:
        ring.finish()
    for copy in mod_spread + grad_joined_copies:
        copy.wait_recv()
    for index, copy in enumerate(sent):
        if not any(copy is other for pair in list(group_copies.values())[:-1] for kind in pair for other in kind):
            copy.wait_send()
    for sems, wide in ((n.pair_sem, 384), (n.attended_sem, 128), (n.grad_pair_sem, 128), (n.project_sem, 384)):
        buffer = {384: n.project_send, 128: n.attended_send}[wide]
        for other in range(1, RING):
            to = block(other)
            where = buffer.at[lines(to * frames, frames)]
            link(where, where, sems.at[0, to], sems.at[1, to], (to, group_rank)).wait_send()


def block_call(
    inputs, skipped, w_skip, w_mod, w_qkv, w_out, w_up, w_down, cotangent, small
):
    low, full = jnp.bfloat16, jnp.float32
    frames, width = inputs.shape
    tokens, half = ROWS * frames, 2 * frames
    columns = width // ROWS
    hidden_units = w_down.shape[0]
    joint = w_skip.shape[0]
    all_frames = RING * frames
    deep = width // RING

    held = dict(
        inputs=inputs,
        skipped=skipped,
        w_skip=w_skip,
        w_mod=w_mod,
        w_qkv=w_qkv,
        w_out=w_out,
        w_up=w_up,
        w_down=w_down,
        cotangent=cotangent,
        small=small,
    )
    given = dict(
        output=((frames, width), low),
        grad_joined=((ROWS, frames, joint), low),
        condition=((ROWS * 8, columns), low),
        mod_grad=((RING, ROWS, 16, 256), full),
        down_total=((RING, hidden_units // RING, width), low),
        up_total=((RING, deep, hidden_units), low),
        qkv_total=((RING, deep, 3 * columns), low),
        skip_total=((RING, joint // RING, width), low),
        out_total=((RING, columns // RING, width), low),
    )
    buffers = dict(
        joined_own=((ROWS, frames, joint), low),
        joined=((tokens, joint), low),
        upstream=((tokens, width), low),
        skip_held=(w_skip.shape, low),
        mod_held=(w_mod.shape, low),
        out_held=(w_out.shape, low),
        down_held=(w_down.shape, low),
        qkv_held=((width, 3 * columns), low),
        up_held=((width, hidden_units), low),
        smalls=((ROWS,) + small.shape, full),
        mod_part=((ROWS * 8, 2 * width), full),
        mod_land=((2, 16, 2 * width), full),
        mod_send=((16, 2 * width), full),
        gain=((8, width), full),
        cosine=((tokens, 128), full),
        sine=((tokens, 128), full),
        row_cosine=((all_frames, 128), full),
        row_sine=((all_frames, 128), full),
        chosen=((all_frames, 128), low),
        send_one=((half, width), low),
        send_two=((half, width), low),
        keep=((half, width), full),
        land_one=((5, half, width), low),
        land_two=((5, half, width), low),
        scale_one=((half, width), full),
        shift_one=((half, width), full),
        hidden=((half, width), full),
        normal_one=((half, width), full),
        spread_one=((half, 128), full),
        normal_two=((half, width), full),
        spread_two=((half, 128), full),
        grad_two=((half, width), full),
        attn_in=((tokens, width), low),
        project=((half, 3 * columns), full),
        pair_send=((RING, frames, 384), low),
        paired=((all_frames, 384), low),
        query_head=((2, all_frames, 128), low),
        key_head=((2, all_frames, 128), low),
        query_turned=((128, all_frames), low),
        shares=((2, all_frames, all_frames), low),
        attended_pair=((all_frames, 128), full),
        attended_send=((all_frames, 128), low),
        attended=((tokens, columns), low),
        ff_in=((tokens, width), low),
        activated=((tokens, hidden_units), low),
        grad_widened=((tokens, hidden_units), low),
        grad_two_low=((tokens, width), low),
        grad_pair_send=((RING, frames, 128), low),
        grad_pair=((all_frames, 128), low),
        grad_turned=((128, all_frames), low),
        key_turned=((128, all_frames), full),
        value_turned=((128, all_frames), full),
        project_send=((all_frames, 384), low),
        grad_project=((tokens, 3 * columns), low),
        grad_hidden=((tokens, width), low),
        mod_terms=((frames, 2 * width), full),
        mod_sums=((16, 2 * width), full),
        sums_land=((RING, 16, 256), full),
        sums_send=((16, 256), full),
        joined_send=((tokens, joint), low),
        down_land=((RING - 1, hidden_units // RING, width), low),
        up_land=((RING - 1, deep, hidden_units), low),
        qkv_land=((RING - 1, deep, 3 * columns), low),
        skip_land=((RING - 1, joint // RING, width), low),
        out_land=((RING - 1, columns // RING, width), low),
        up_turn=((deep, hidden_units), low),
        qkv_turn=((deep, 3 * columns), low),
    )
    sems = dict(
        load_sem=(16,),
        joined_sem=(2, 3),
        small_sem=(2, 3),
        qkv_sem=(2, 3, 6),
        up_sem=(2, 3),
        mod_sem=(2, 2),
        first_sem=(2, 5, 2),
        second_sem=(2, 5, 2),
        upstream_sem=(2, 3),
        attn_sem=(2, 2),
        ff_sem=(2, 2),
        grad_two_sem=(2, 2),
        grad_hidden_sem=(2, 2),
        pair_sem=(2, RING),
        attended_sem=(2, RING),
        grad_pair_sem=(2, RING),
        project_sem=(2, RING),
        grad_joined_sem=(2, 3),
        sums_sem=(2, RING - 1),
        sums_group_sem=(2, 3),
        sums_block_sem=(2, RING - 1),
        down_sem=(2, 2, 2, RING - 1),
        up_ring_sem=(2, 2, 2, RING - 1),
        qkv_ring_sem=(2, 2, 2, RING - 1),
        skip_ring_sem=(2, 2, 2, RING - 1),
        out_ring_sem=(2, 2, 2, RING - 1),
        turn_sem=(2, 2, 3),
    )
    names = [*held, *given, *buffers, *sems]
    vmem = pl.BlockSpec(memory_space=pltpu.VMEM)
    anywhere = pl.BlockSpec(memory_space=pl.ANY)
    return pl.pallas_call(
        functools.partial(block_kernel, names),
        out_shape=[jax.ShapeDtypeStruct(*spec) for spec in given.values()],
        in_specs=[vmem if name == "small" else anywhere for name in held],
        out_specs=[vmem] * len(given),
        scratch_shapes=[pltpu.VMEM(*spec) for spec in buffers.values()]
        + [pltpu.SemaphoreType.DMA(shape) for shape in sems.values()],
        compiler_params=pltpu.CompilerParams(
            collective_id=0, has_side_effects=True, vmem_limit_bytes=62 * 1024 * 1024
        ),
    )(*held.values())


def small_table(lengths_row, steps_row, gain):
    end = jnp.cumsum(lengths_row).astype(jnp.float32)
    start = end - lengths_row.astype(jnp.float32)
    count = end.shape[0]

    def down(values):
        return jnp.broadcast_to(values[:, None], (count, 128))

    def along(values, empty):
        rest = jnp.full((64 - 2 * count,), empty, jnp.float32)
        lane = jnp.concatenate([values, values, rest, values, values, rest])
        return jnp.broadcast_to(lane[None], (8, 128))

    gain = gain.astype(jnp.float32)
    return jnp.stack(
        [
            down(steps_row.astype(jnp.float32)),
            down(start),
            down(end),
            along(start, 1e9),
            along(end, 0.0),
            jnp.broadcast_to(gain[None, :128], (8, 128)),
            jnp.broadcast_to(gain[None, 128:], (8, 128)),
        ]
    )


def per_device_block(
    inputs,
    skipped,
    w_skip,
    w_mod,
    w_qkv,
    w_out,
    ff_gain,
    w_up,
    w_down,
    cotangent,
    lengths,
    flow_steps,
):
    width = inputs.shape[2]
    columns = width // ROWS
    group_rank = lax.axis_index("grp")
    small = small_table(lengths[0], flow_steps[0], ff_gain)
    output, grad_joined, condition, mod_grad, down, up, qkv, skip, out = block_call(
        inputs[0], skipped[0], w_skip, w_mod, w_qkv, w_out, w_up, w_down, cotangent[0], small
    )

    def rows_back(total):
        return total.astype(jnp.float32).reshape(-1, total.shape[2])

    up = jnp.transpose(
        up.astype(jnp.float32).reshape(RING, ROWS, columns // RING, -1), (0, 2, 1, 3)
    ).reshape(columns, -1)
    qkv = jnp.transpose(
        qkv.astype(jnp.float32).reshape(RING, ROWS, columns // RING, 2, 3, columns // 2),
        (0, 2, 4, 1, 3, 5),
    ).reshape(columns, -1)
    joined = grad_joined.astype(jnp.float32)
    mod = jnp.transpose(mod_grad, (1, 2, 0, 3)).reshape(ROWS, 16, 2 * width)
    gain = jnp.sum(mod[:, 8, :width], axis=0)
    gain = lax.dynamic_slice_in_dim(gain, group_rank * columns, columns)
    slots = jnp.concatenate([mod[r, :8] for r in (0, 2, 1, 3)], axis=0)
    grad_mod = jnp.dot(condition.astype(jnp.float32).T, slots, precision=HIGHEST)
    return (
        output[None],
        jnp.concatenate([joined[0], joined[1]], axis=1)[None],
        jnp.concatenate([joined[2], joined[3]], axis=1)[None],
        rows_back(skip),
        grad_mod,
        qkv,
        rows_back(out),
        gain,
        up,
        rows_back(down),
    )


def solution(mesh):
    placed = (
        P("grp", "blk", None),
        P("grp", "blk", None),
        P("grp", None),
        P("grp", None),
        P("grp", None),
        P("grp", None),
        P("grp"),
        P("grp", None),
        P("grp", None),
        P("grp", "blk", None),
        P("grp", None),
        P("grp", None),
    )
    body = per_device
    if mesh.shape["blk"] == RING and mesh.shape["grp"] == ROWS:
        body = per_device_block
    return jax.shard_map(
        body,
        mesh=mesh,
        in_specs=placed,
        out_specs=(
            P("grp", "blk", None),
            P("grp", "blk", None),
            P("grp", "blk", None),
            P("grp", None),
            P("grp", None),
            P("grp", None),
            P("grp", None),
            P("grp"),
            P("grp", None),
            P("grp", None),
        ),
        check_vma=False,
    )
```

```python
import functools
import math
import types

import jax
import jax.numpy as jnp
from jax import lax
from jax.experimental import pallas as pl
from jax.experimental.pallas import tpu as pltpu
from jax.sharding import PartitionSpec as P

HEADS = 16
HEAD_DIM = 64
STEPS = 32


EPSILON = 1e-06
NEGATIVE = -1e30
HIGHEST = lax.Precision.HIGHEST
MESH = pl.DeviceIdType.MESH
RING = 8
ROWS = 4


def from_behind(block, axis, distance):
    devices = range(lax.axis_size(axis))
    route = [((i - distance) % len(devices), i) for i in devices]
    return lax.ppermute(block, axis, route)


def layout(lengths_row, frames):
    end_frame = jnp.cumsum(lengths_row)
    start_frame = end_frame - lengths_row
    segment = jnp.sum((frames[:, None] >= end_frame[None, :]).astype(jnp.int32), axis=1)
    chosen = segment[:, None] == jnp.arange(lengths_row.shape[0], dtype=jnp.int32)[None, :]
    position = frames - jnp.sum(jnp.where(chosen, start_frame[None, :], 0), axis=1)
    return (segment, position)


def flow_condition(steps_row, model_width):
    half_width = model_width // 2
    rate_table = jnp.exp(
        -math.log(10000.0) * jnp.arange(half_width, dtype=jnp.float32) / half_width
    )
    angles = 1000.0 * (steps_row.astype(jnp.float32) / STEPS)[:, None] * rate_table[None, :]
    return jax.nn.silu(jnp.concatenate([jnp.sin(angles), jnp.cos(angles)], axis=1))


def rotation_tables(position, head_width):
    half_width = head_width // 2
    rate_table = jnp.exp(
        -math.log(10000.0) * jnp.arange(half_width, dtype=jnp.float32) / half_width
    )
    angles = position.astype(jnp.float32)[:, None] * rate_table[None, :]
    return (jnp.cos(angles)[:, None, :], jnp.sin(angles)[:, None, :], half_width)


def rotate(head_block, position):
    cosine_part, sine_part, half_width = rotation_tables(position, head_block.shape[-1])
    first_half = head_block[..., :half_width]
    second_half = head_block[..., half_width:]
    return jnp.concatenate(
        [
            first_half * cosine_part - second_half * sine_part,
            second_half * cosine_part + first_half * sine_part,
        ],
        axis=-1,
    )


def rotate_back(head_block, position):
    cosine_part, sine_part, half_width = rotation_tables(position, head_block.shape[-1])
    first_half = head_block[..., :half_width]
    second_half = head_block[..., half_width:]
    return jnp.concatenate(
        [
            first_half * cosine_part + second_half * sine_part,
            second_half * cosine_part - first_half * sine_part,
        ],
        axis=-1,
    )


def normalize(hidden):
    centred = hidden - jnp.mean(hidden, axis=-1, keepdims=True)
    scaled = lax.rsqrt(jnp.mean(centred * centred, axis=-1, keepdims=True) + EPSILON)
    return (centred * scaled, scaled)


def norm_back(grad_normal, normal, scaled):
    centred_grad = grad_normal - jnp.mean(grad_normal, axis=-1, keepdims=True)
    return scaled * (centred_grad - normal * jnp.mean(grad_normal * normal, axis=-1, keepdims=True))


def exact_gelu(values_in):
    return jax.nn.gelu(values_in, approximate=False)


def contract_rows(left_side, right_side):
    return lax.dot_general(
        left_side, right_side, (((0,), (0,)), ((), ())), preferred_element_type=jnp.float32
    )


def heads_of(flat_block):
    return flat_block.reshape(flat_block.shape[0], HEADS, HEAD_DIM)


def per_device(
    inputs,
    skipped,
    w_skip,
    w_mod,
    w_qkv,
    w_out,
    ff_gain,
    w_up,
    w_down,
    cotangent,
    lengths,
    flow_steps,
):
    w_skip, w_mod, w_qkv, w_out, ff_gain, w_up, w_down = (
        lax.all_gather(w_skip, "grp", axis=0, tiled=True),
        lax.all_gather(w_mod, "grp", axis=0, tiled=True),
        lax.all_gather(w_qkv, "grp", axis=0, tiled=True),
        lax.all_gather(w_out, "grp", axis=0, tiled=True),
        lax.all_gather(ff_gain, "grp", axis=0, tiled=True),
        lax.all_gather(w_up, "grp", axis=0, tiled=True),
        lax.all_gather(w_down, "grp", axis=0, tiled=True),
    )
    frame_count = inputs.shape[1]
    model_width = inputs.shape[2]
    cycle_size = lax.axis_size("blk")
    device_rank = lax.axis_index("blk")
    score_scale = HEAD_DIM ** (-0.5)
    local_frames = jnp.arange(frame_count, dtype=jnp.int32)
    lengths_row = lengths[0]
    own_segment, own_position = layout(lengths_row, device_rank * frame_count + local_frames)

    def segment_of(source):
        return layout(lengths_row, source * frame_count + local_frames)[0]

    def scored(query_block, key_block, query_segment, key_segment):
        raw_scores = (
            jnp.einsum(
                "qhd,khd->hqk",
                heads_of(query_block),
                heads_of(key_block),
                preferred_element_type=jnp.float32,
            )
            * score_scale
        )
        allowed = (query_segment[:, None] == key_segment[None, :])[None]
        return (raw_scores, allowed)

    joined = jnp.concatenate([inputs[0], skipped[0]], axis=1)
    hidden = jnp.dot(joined, w_skip, preferred_element_type=jnp.float32)
    condition = flow_condition(flow_steps[0], model_width).astype(jnp.bfloat16)
    modulation = jnp.dot(condition, w_mod, preferred_element_type=jnp.float32)
    picker = (
        own_segment[:, None] == jnp.arange(lengths_row.shape[0], dtype=jnp.int32)[None, :]
    ).astype(jnp.float32)
    per_frame = jnp.dot(picker, modulation, precision=HIGHEST)
    scale_one = 1.0 + per_frame[:, :model_width]
    normal_one, spread_one = normalize(hidden)
    attn_in = (normal_one * scale_one + per_frame[:, model_width:]).astype(jnp.bfloat16)
    project = jnp.dot(attn_in, w_qkv, preferred_element_type=jnp.float32).reshape(
        frame_count, 3, HEADS, HEAD_DIM
    )
    queries = (
        rotate(project[:, 0], own_position).astype(jnp.bfloat16).reshape(frame_count, model_width)
    )
    keys_own = (
        rotate(project[:, 1], own_position).astype(jnp.bfloat16).reshape(frame_count, model_width)
    )
    values_own = project[:, 2].astype(jnp.bfloat16).reshape(frame_count, model_width)

    def forward_turn(turn_index, carried):
        key_now, value_now, running_top, running_total, running_sum = carried
        source = (device_rank - turn_index) % cycle_size
        raw_scores, allowed = scored(queries, key_now, own_segment, segment_of(source))
        raw_scores = jnp.where(allowed, raw_scores, NEGATIVE)
        new_top = jnp.maximum(running_top, jnp.max(raw_scores, axis=2, keepdims=True))
        weights = jnp.where(allowed, jnp.exp(raw_scores - new_top), 0.0)
        shrink = jnp.exp(running_top - new_top)
        running_total = running_total * shrink + jnp.sum(weights, axis=2, keepdims=True)
        running_sum = running_sum * shrink + jnp.einsum(
            "hqk,khd->hqd",
            weights.astype(jnp.bfloat16),
            heads_of(value_now),
            preferred_element_type=jnp.float32,
        )
        key_now, value_now = from_behind((key_now, value_now), "blk", 1)
        return (key_now, value_now, new_top, running_total, running_sum)

    initial = (
        keys_own,
        values_own,
        jnp.full((HEADS, frame_count, 1), NEGATIVE, jnp.float32),
        jnp.zeros((HEADS, frame_count, 1), jnp.float32),
        jnp.zeros((HEADS, frame_count, HEAD_DIM), jnp.float32),
    )
    finished = lax.fori_loop(0, cycle_size, forward_turn, initial)
    running_top, running_total, running_sum = (finished[2], finished[3], finished[4])
    attended = jnp.transpose(running_sum / running_total, (1, 0, 2)).reshape(
        frame_count, model_width
    )
    log_total = (running_top + jnp.log(running_total))[:, :, 0]
    attended_low = attended.astype(jnp.bfloat16)
    hidden_two = hidden + jnp.dot(attended_low, w_out, preferred_element_type=jnp.float32)
    normal_two, spread_two = normalize(hidden_two)
    gain_vector = ff_gain.astype(jnp.float32)
    ff_in = (normal_two * gain_vector).astype(jnp.bfloat16)
    widened = jnp.dot(ff_in, w_up, preferred_element_type=jnp.float32)
    activated, gelu_back = jax.vjp(exact_gelu, widened)
    activated_low = activated.astype(jnp.bfloat16)
    output = (
        hidden_two + jnp.dot(activated_low, w_down, preferred_element_type=jnp.float32)
    ).astype(jnp.bfloat16)
    upstream = cotangent[0]
    grad_down = contract_rows(activated_low, upstream)
    grad_activated = jnp.dot(upstream, w_down.T, preferred_element_type=jnp.float32)
    grad_widened = gelu_back(grad_activated)[0].astype(jnp.bfloat16)
    grad_up = contract_rows(ff_in, grad_widened)
    grad_ff_in = jnp.dot(grad_widened, w_up.T, preferred_element_type=jnp.float32)
    grad_gain = jnp.sum(grad_ff_in * normal_two, axis=0)
    grad_hidden_two = upstream.astype(jnp.float32) + norm_back(
        grad_ff_in * gain_vector, normal_two, spread_two
    )
    grad_two_low = grad_hidden_two.astype(jnp.bfloat16)
    grad_out = contract_rows(attended_low, grad_two_low)
    grad_attended = jnp.dot(grad_two_low, w_out.T, preferred_element_type=jnp.float32).astype(
        jnp.bfloat16
    )
    delta = jnp.transpose(jnp.sum(heads_of(grad_attended.astype(jnp.float32) * attended), axis=2))
    zero_grad = jnp.zeros((frame_count, model_width), jnp.float32)

    def pair_terms(
        query_block,
        upstream_block,
        key_block,
        value_block,
        total_block,
        delta_block,
        query_segment,
        key_segment,
    ):
        raw_scores, allowed = scored(query_block, key_block, query_segment, key_segment)
        prob_block = jnp.where(allowed, jnp.exp(raw_scores - total_block[:, :, None]), 0.0)
        value_term = jnp.einsum(
            "hqk,qhd->khd",
            prob_block.astype(jnp.bfloat16),
            heads_of(upstream_block),
            preferred_element_type=jnp.float32,
        ).reshape(frame_count, model_width)
        prob_grad = jnp.einsum(
            "qhd,khd->hqk",
            heads_of(upstream_block),
            heads_of(value_block),
            preferred_element_type=jnp.float32,
        )
        score_grad = (prob_block * (prob_grad - delta_block[:, :, None])).astype(jnp.bfloat16)
        query_term = (
            jnp.einsum(
                "hqk,khd->qhd", score_grad, heads_of(key_block), preferred_element_type=jnp.float32
            ).reshape(frame_count, model_width)
            * score_scale
        )
        key_term = (
            jnp.einsum(
                "hqk,qhd->khd",
                score_grad,
                heads_of(query_block),
                preferred_element_type=jnp.float32,
            ).reshape(frame_count, model_width)
            * score_scale
        )
        return (query_term, key_term, value_term)

    def keys_turn(turn_index, carried):
        key_now, value_now, key_grad, value_grad, query_grad = carried
        source = (device_rank - turn_index) % cycle_size
        query_term, key_term, value_term = pair_terms(
            queries,
            grad_attended,
            key_now,
            value_now,
            log_total,
            delta,
            own_segment,
            segment_of(source),
        )
        key_now, value_now = from_behind((key_now, value_now), "blk", 1)
        key_grad, value_grad = (
            from_behind((key_grad + key_term).astype(jnp.bfloat16), "blk", 1).astype(jnp.float32),
            from_behind((value_grad + value_term).astype(jnp.bfloat16), "blk", 1).astype(
                jnp.float32
            ),
        )
        return (key_now, value_now, key_grad, value_grad, query_grad + query_term)

    done = lax.fori_loop(
        0, cycle_size, keys_turn, (keys_own, values_own, zero_grad, zero_grad, zero_grad)
    )
    key_grad, value_grad, query_grad = (done[2], done[3], done[4])
    grad_project = jnp.concatenate(
        [
            rotate_back(heads_of(query_grad), own_position).reshape(frame_count, model_width),
            rotate_back(heads_of(key_grad), own_position).reshape(frame_count, model_width),
            value_grad,
        ],
        axis=1,
    ).astype(jnp.bfloat16)
    grad_qkv = contract_rows(attn_in, grad_project)
    grad_attn_in = jnp.dot(grad_project, w_qkv.T, preferred_element_type=jnp.float32)
    mod_terms = jnp.concatenate([grad_attn_in * normal_one, grad_attn_in], axis=1)
    grad_modulation = jnp.dot(picker.T, mod_terms, precision=HIGHEST)
    grad_mod = jnp.dot(condition.astype(jnp.float32).T, grad_modulation, precision=HIGHEST)
    grad_hidden = grad_hidden_two + norm_back(grad_attn_in * scale_one, normal_one, spread_one)
    grad_hidden_low = grad_hidden.astype(jnp.bfloat16)
    grad_skip_weight = contract_rows(joined, grad_hidden_low)
    grad_joined = jnp.dot(grad_hidden_low, w_skip.T, preferred_element_type=jnp.float32)
    shards = (
        lax.psum_scatter(
            grad_skip_weight.astype(jnp.bfloat16), "grp", scatter_dimension=0, tiled=True
        ).astype(jnp.float32),
        lax.psum_scatter(
            grad_mod.astype(jnp.bfloat16), "grp", scatter_dimension=0, tiled=True
        ).astype(jnp.float32),
        lax.psum_scatter(
            grad_qkv.astype(jnp.bfloat16), "grp", scatter_dimension=0, tiled=True
        ).astype(jnp.float32),
        lax.psum_scatter(
            grad_out.astype(jnp.bfloat16), "grp", scatter_dimension=0, tiled=True
        ).astype(jnp.float32),
        lax.psum_scatter(
            grad_gain.astype(jnp.bfloat16), "grp", scatter_dimension=0, tiled=True
        ).astype(jnp.float32),
        lax.psum_scatter(
            grad_up.astype(jnp.bfloat16), "grp", scatter_dimension=0, tiled=True
        ).astype(jnp.float32),
        lax.psum_scatter(
            grad_down.astype(jnp.bfloat16), "grp", scatter_dimension=0, tiled=True
        ).astype(jnp.float32),
    )
    totals = lax.psum(
        (shards[0], shards[1], shards[2], shards[3], shards[4], shards[5], shards[6]), "blk"
    )
    return (
        output[None],
        grad_joined[:, :model_width][None],
        grad_joined[:, model_width:][None],
        totals[0],
        totals[1],
        totals[2],
        totals[3],
        totals[4],
        totals[5],
        totals[6],
    )


def dot_plain(left_side, right_side):
    return jnp.dot(left_side, right_side, preferred_element_type=jnp.float32)


def dot_across(left_side, right_side):
    return lax.dot_general(
        left_side, right_side, (((1,), (1,)), ((), ())), preferred_element_type=jnp.float32
    )


def ring_place(rank):
    odd = lax.rem(rank, 2)
    return (1 - odd) * (rank // 2) + odd * ((15 - rank) // 2)


def ring_rank(place):
    upper = place // 4
    return (1 - upper) * (2 * place) + upper * (15 - 2 * place)


TICKS = (2, 1, 1, 2, 2, 1, 5, 3, 1, 3, 4)


class Ring:
    def __init__(self, part, land, whole, sems, whole_sems, rank, group_rank, turn=None):
        self.part, self.land, self.whole = part, land, whole
        self.sems, self.whole_sems = sems, whole_sems
        self.rank, self.group_rank = rank, group_rank
        self.place = ring_place(rank)
        self.half = part.shape[1] // 2
        self.copies = {}
        self.puts, self.turns, self.turn = [], [], turn

    def block_at(self, offset):
        return ring_rank(lax.rem(self.place + offset + 2 * RING, RING))

    def rows(self, way):
        return pl.ds(way * self.half, self.half)

    def send(self, kind, step, way, source, target):
        to = ring_rank(lax.rem(self.place + (1 if way == 0 else RING - 1), RING))
        copy = pltpu.make_async_remote_copy(
            src_ref=source,
            dst_ref=target,
            send_sem=self.sems.at[kind, 0, way, step],
            recv_sem=self.sems.at[kind, 1, way, step],
            device_id=(to, self.group_rank),
            device_id_type=MESH,
        )
        copy.start()
        self.copies[kind, step, way] = copy

    def sum_step(self, step):
        if step == 1:
            for way in range(2):
                self.copies[0, 0, way].wait_send()
        for way in range(2):
            block = self.block_at((-1 if way == 0 else 1) * (step + 1))
            rows = self.rows(way)
            if step > 0:
                self.copies[0, step - 1, way].wait_recv()
                tile = min(self.half, 32)

                def add(i, carry, way=way, block=block, tile=tile):
                    at = pl.ds(pl.multiple_of(way * self.half + i * tile, tile), tile)
                    total = self.part[block, at].astype(jnp.float32) + self.land[
                        step - 1, at
                    ].astype(jnp.float32)
                    self.land[step - 1, at] = total.astype(jnp.bfloat16)
                    return carry

                lax.fori_loop(0, self.half // tile, add, 0)
            if step < RING - 1:
                source = self.part.at[block, rows] if step == 0 else self.land.at[step - 1, rows]
                self.send(0, step, way, source, self.land.at[step, rows])

    def put(self, block, step, way):
        rows = self.rows(way)
        copy = pltpu.make_async_copy(
            self.part.at[block, rows], self.whole.at[block, rows], self.whole_sems.at[way, step]
        )
        copy.start()
        self.puts.append(copy)

    def spread_step(self, step):
        if step == 0:
            self.close_sum()
        for way in range(2):
            block = self.block_at((-1 if way == 0 else 1) * step)
            rows = self.rows(way)
            if step > 0:
                self.copies[1, step - 1, way].wait_recv()
            if step < RING - 1:
                target = self.part.at[block, rows]
                self.send(1, step, way, target, target)
            self.put(block, step, way)

    def begin(self):
        self.sum_step(0)
        self.left = [functools.partial(self.sum_step, step) for step in range(1, RING)]
        self.left += [functools.partial(self.spread_step, step) for step in range(RING)]
        if self.turn is not None:
            self.left.insert(RING - 1, self.turn_out)

    def turn_out(self):
        place, sems = self.turn
        deep = self.part.shape[1] // ROWS

        def rows(group):
            return pl.ds(pl.multiple_of(group * deep, deep), deep)

        for other in (2, 1, 3):
            to = lax.rem(self.group_rank + other, ROWS)
            copy = pltpu.make_async_remote_copy(
                src_ref=self.land.at[RING - 2, rows(to)],
                dst_ref=place.at[rows(self.group_rank)],
                send_sem=sems.at[0, other - 1],
                recv_sem=sems.at[1, other - 1],
                device_id=(self.rank, to),
                device_id_type=MESH,
            )
            copy.start()
            self.turns.append(copy)
        place[rows(self.group_rank)] = self.land[RING - 2, rows(self.group_rank)]

    def close_sum(self):
        for copy in self.turns:
            copy.wait_recv()
        self.part[self.rank] = self.land[RING - 2] if self.turn is None else self.turn[0][...]

    def finish(self):
        for copy in self.turns:
            copy.wait_send()
        for (kind, step, _), copy in self.copies.items():
            if kind or step:
                copy.wait_send()
        for copy in self.puts:
            copy.wait()


def block_kernel(names, *refs):
    n = types.SimpleNamespace(**dict(zip(names, refs)))
    low, full = jnp.bfloat16, jnp.float32
    rank, group_rank = lax.axis_index("blk"), lax.axis_index("grp")
    core, chip = lax.rem(group_rank, 2), group_rank // 2
    sibling = (rank, group_rank + 1 - 2 * core)
    across = (rank, group_rank + 2 - 4 * chip)
    frames, width = n.cotangent.shape
    half = 2 * frames
    columns = width // ROWS
    mine, theirs = core * half, (1 - core) * half
    own_slot = 2 * core + chip
    pair_row, pair_side = rank // 2, lax.rem(rank, 2)
    sent = []

    def lines(offset, size):
        return pl.ds(pl.multiple_of(offset, min(size, 128)), size)

    def slot_of(row):
        return 2 * lax.rem(row, 2) + row // 2

    def row_of(slot):
        return 2 * lax.rem(slot, 2) + slot // 2

    def group(other):
        return lax.rem(group_rank + other, ROWS)

    def block(other):
        return lax.rem(rank + other, RING)

    def link(source, target, send_sem, recv_sem, device):
        return pltpu.make_async_remote_copy(
            src_ref=source,
            dst_ref=target,
            send_sem=send_sem,
            recv_sem=recv_sem,
            device_id=device,
            device_id_type=MESH,
        )

    def push(source, target, sems, index, device):
        copy = link(source, target, sems.at[(0,) + index], sems.at[(1,) + index], device)
        copy.start()
        sent.append(copy)
        return copy

    def load(source, target, index):
        copy = pltpu.make_async_copy(source, target, n.load_sem.at[index])
        copy.start()
        return copy

    def tiles(count, tile, body):
        def step(i, carry):
            body(pl.multiple_of(i * tile, tile))
            return carry

        lax.fori_loop(0, count // tile, step, 0)

    joined_loads = [
        load((n.inputs, n.skipped)[t // 2].at[:, pl.ds((t % 2) * 512, 512)], n.joined_own.at[t], t)
        for t in range(ROWS)
    ]
    upstream_load = load(n.cotangent, n.upstream.at[lines(own_slot * frames, frames)], 4)
    skip_load = load(n.w_skip, n.skip_held, 5)
    mod_load = load(n.w_mod, n.mod_held, 6)
    out_load = load(n.w_out, n.out_held, 7)
    down_load = load(n.w_down, n.down_held, 8)
    pieces = [(side, kind) for side in range(2) for kind in range(3)]

    def qkv_piece(target, side, kind):
        return n.w_qkv.at[:, pl.ds(pl.multiple_of(kind * width + target * columns + side * 128, 128), 128)]

    def qkv_place(side, kind):
        return n.qkv_held.at[lines(group_rank * columns, columns), pl.ds((side * 3 + kind) * 128, 128)]

    qkv_loads = [
        load(qkv_piece(group_rank, *piece), qkv_place(*piece), 9 + i)
        for i, piece in enumerate(pieces)
    ]
    hidden_units = n.up_held.shape[1]

    def up_piece(target):
        return n.w_up.at[:, pl.ds(pl.multiple_of(target * hidden_units, 128), hidden_units)]

    up_place = n.up_held.at[lines(group_rank * columns, columns)]
    up_load = load(up_piece(group_rank), up_place, 15)

    barrier = pltpu.get_barrier_semaphore()
    for other in range(1, ROWS):
        pl.semaphore_signal(barrier, inc=1, device_id=(rank, group(other)), device_id_type=MESH)
    for other in range(1, RING):
        pl.semaphore_signal(barrier, inc=1, device_id=(block(other), group_rank), device_id_type=MESH)
    for copy in joined_loads:
        copy.wait()
    pl.semaphore_wait(barrier, ROWS + RING - 2)

    joined_place = n.joined.at[lines(own_slot * frames, frames)]
    joined_sends = [
        push(n.joined_own.at[group(o)], joined_place, n.joined_sem, (o - 1,), (rank, group(o)))
        for o in (2, 1, 3)
    ]
    small_sends = [
        push(n.small, n.smalls.at[group_rank], n.small_sem, (o - 1,), (rank, group(o)))
        for o in (2, 1, 3)
    ]
    qkv_sends = [
        push(
            qkv_piece(group(o), *piece),
            qkv_place(*piece),
            n.qkv_sem,
            (o - 1, i),
            (rank, group(o)),
        )
        for o in (2, 1, 3)
        for i, piece in enumerate(pieces)
    ]
    n.joined[lines(own_slot * frames, frames)] = n.joined_own[group_rank]
    n.smalls[group_rank] = n.small[...]
    for copy in small_sends:
        copy.wait_recv()

    steps = jnp.concatenate([n.smalls[(0, 2, 1, 3)[s], 0] for s in range(ROWS)], axis=0)
    steps = jnp.concatenate([steps, steps], axis=1)
    lane = lax.broadcasted_iota(jnp.int32, steps.shape, 1) + lax.rem(group_rank, 2) * columns
    rate = jnp.exp(-math.log(10000.0) * lane.astype(full) / (width // 2))
    angles = 1000.0 * (steps / STEPS) * rate
    turned = jnp.where(group_rank >= 2, jnp.cos(angles), jnp.sin(angles))
    n.condition[...] = (turned / (1.0 + jnp.exp(-turned))).astype(low)
    mod_load.wait()

    def mod_tile(at):
        where = pl.ds(at, 512)
        n.mod_part[:, where] = dot_plain(n.condition[...], n.mod_held[:, where])

    tiles(2 * width, 512, mod_tile)
    mod_first = push(
        n.mod_part.at[pl.ds(pl.multiple_of(16 * (1 - core), 16), 16)], n.mod_land.at[0], n.mod_sem, (0,), sibling
    )

    gains = [n.smalls[r, 5 + i][0:1] for r in range(ROWS) for i in range(2)]
    n.gain[...] = jnp.broadcast_to(jnp.concatenate(gains, axis=1), n.gain.shape)

    def picked(row, first, count):
        spot = (lax.broadcasted_iota(jnp.int32, (count, 128), 0) + first).astype(full)
        return (spot >= n.smalls[row, 3][0:1]) & (spot < n.smalls[row, 4][0:1]), spot

    lanes = lax.broadcasted_iota(jnp.int32, (frames, 128), 1)
    turn_rate = jnp.exp(-math.log(10000.0) * lax.rem(lanes, 32).astype(full) / 32)
    turn_sign = jnp.where(lax.rem(lanes, 64) < 32, -1.0, 1.0)

    def turn_tables(row, first, cosine, sine, at):
        chosen, spot = picked(row, first, frames)
        start = jnp.where(chosen & (lanes < 8), n.smalls[row, 3][0:1], 0.0)
        position = spot - jnp.sum(start, axis=1, keepdims=True)
        angle = position * turn_rate
        cosine[at] = jnp.cos(angle)
        sine[at] = jnp.sin(angle) * turn_sign

    def swapped(value):
        ahead = pltpu.roll(value, 96, 1)
        behind = pltpu.roll(value, 32, 1)
        return jnp.where(lax.rem(lanes, 64) < 32, ahead, behind)

    def partial_sum(index, left_ref, right_tile):
        def to_send(at):
            n.send_one[:, pl.ds(at, 256)] = right_tile(left_ref[lines(theirs, half)], at).astype(low)

        def to_keep(at):
            n.keep[:, pl.ds(at, 256)] = right_tile(left_ref[lines(mine, half)], at)

        if index > 0:
            for copy in group_copies[index - 1][0]:
                copy.wait_send()
        tiles(width, 256, to_send)
        first = [
            push(
                n.send_one.at[pl.ds(k * frames, frames)],
                n.land_one.at[index, pl.ds(k * frames, frames)],
                n.first_sem,
                (index, k),
                sibling,
            )
            for k in range(2)
        ]
        tiles(width, 256, to_keep)
        return first

    def cross_sum(index, first):
        if index > 0:
            for copy in group_copies[index - 1][1]:
                copy.wait_send()
        second = []
        for k in range(2):
            first[k].wait_recv()

            def add(at, k=k):
                where = pl.ds(k * frames + at, 32)
                total = n.keep[where] + n.land_one[index, where].astype(full)
                n.keep[where] = total
                n.send_two[where] = total.astype(low)

            tiles(frames, 32, add)
            second.append(
                push(
                    n.send_two.at[pl.ds(k * frames, frames)],
                    n.land_two.at[index, pl.ds(k * frames, frames)],
                    n.second_sem,
                    (index, k),
                    across,
                )
            )
        group_copies[index] = (first, second)
        return second

    group_copies = {}

    down_ring, up_ring, out_ring, qkv_ring, skip_ring = rings = [
        Ring(part, land, whole, sems, n.whole_sem.at[index], rank, group_rank, turn)
        for index, (part, land, whole, sems, turn) in enumerate(
            (
                (n.down_total, n.down_land, n.down_whole, n.down_sem, None),
                (n.up_total, n.up_land, n.up_whole, n.up_ring_sem, (n.up_turn, n.turn_sem.at[0])),
                (n.out_total, n.out_land, n.out_whole, n.out_ring_sem, None),
                (n.qkv_total, n.qkv_land, n.qkv_whole, n.qkv_ring_sem, (n.qkv_turn, n.turn_sem.at[1])),
                (n.skip_total, n.skip_land, n.skip_whole, n.skip_ring_sem, None),
            )
        )
    ]
    running = []

    def begin(ring):
        ring.begin()
        running.append(ring)

    def ticks(count):
        for _ in range(count):
            if running:
                ring = running.pop(0)
                ring.left.pop(0)()
                if ring.left:
                    running.append(ring)

    def mean(value):
        return jnp.mean(value, axis=-1, keepdims=True)

    def share(buffer, k, sems):
        where = lines(mine + k * frames, frames)
        return push(buffer.at[where], buffer.at[where], sems, (k,), sibling)

    skip_load.wait()
    for copy in joined_sends:
        copy.wait_recv()

    def skip_tile(left, at):
        return dot_plain(left, n.skip_held[:, pl.ds(at, 256)])

    first = partial_sum(0, n.joined, skip_tile)
    mod_first.wait_recv()
    mod_mine = n.mod_part[pl.ds(pl.multiple_of(16 * core, 16), 16)] + n.mod_land[0]
    n.mod_send[...] = mod_mine
    mod_second = push(n.mod_send, n.mod_land.at[1], n.mod_sem, (1,), across)
    second = cross_sum(0, first)
    own_lines = lines(own_slot * frames, frames)
    for slot in range(ROWS):
        turn_tables(
            (0, 2, 1, 3)[slot],
            rank * frames,
            n.cosine,
            n.sine,
            pl.ds(slot * frames, frames),
        )
    mod_second.wait_recv()
    mod_total = n.mod_send[...] + n.mod_land[1]
    for k in range(2):
        row = 2 * k + core
        values = mod_total[8 * k : 8 * k + 8]
        high = values.astype(low).astype(full)
        stack = jnp.concatenate([high, values - high], axis=0).astype(low)
        chosen = picked(row, rank * frames, frames)[0]
        picker = jnp.where(chosen, 1.0, 0.0).astype(low)[:, :16]
        where = pl.ds(k * frames, frames)
        n.scale_one[where] = 1.0 + dot_plain(picker, stack[:, :width])
        n.shift_one[where] = dot_plain(picker, stack[:, width:])

    attn_sends = []
    for k in range(2):
        second[k].wait_recv()

        def norm_one(at, k=k):
            where = pl.ds(k * frames + at, 32)
            hidden = n.keep[where] + n.land_two[0, where].astype(full)
            n.hidden[where] = hidden
            centred = hidden - mean(hidden)
            spread = lax.rsqrt(mean(centred * centred) + EPSILON)
            normal = centred * spread
            n.normal_one[where] = normal
            n.spread_one[where] = jnp.broadcast_to(spread, (32, 128))
            n.attn_in[lines(mine + k * frames + at, 32)] = (
                normal * n.scale_one[where] + n.shift_one[where]
            ).astype(low)

        tiles(frames, 32, norm_one)
        attn_sends.append(share(n.attn_in, k, n.attn_sem))

    up_sends = [
        push(up_piece(group(o)), up_place, n.up_sem, (o - 1,), (rank, group(o))) for o in (2, 1, 3)
    ]
    upstream_load.wait()
    upstream_sends = [
        push(n.upstream.at[own_lines], n.upstream.at[own_lines], n.upstream_sem, (i,), device)
        for i, device in enumerate((across, sibling))
    ]

    for copy in qkv_loads:
        copy.wait()
    for copy in qkv_sends:
        copy.wait_recv()

    def to_heads(offset, value_of, target, sems, wide, send_buffer):
        for k in range(2):
            slot = offset // frames + k
            for side in range(2):
                to = 2 * row_of(slot) + side
                value = value_of(k, side, slot)

                @pl.when(to != rank)
                def _():
                    send_buffer[to] = value
                    link(
                        send_buffer.at[to],
                        target.at[lines(rank * frames, frames)],
                        sems.at[0, to],
                        sems.at[1, rank],
                        (to, group_rank),
                    ).start()

                @pl.when(to == rank)
                def _():
                    target[lines(rank * frames, frames)] = value

    def heads_arrive(target, sems):
        for other in range(1, RING):
            source = block(other)
            where = target.at[lines(source * frames, frames)]
            link(where, where, sems.at[0, source], sems.at[1, source], (source, group_rank)).wait_recv()

    def project_half(offset):
        def project_tile(at):
            n.project[:, pl.ds(at, 256)] = dot_plain(
                n.attn_in[lines(offset, half)], n.qkv_held[:, pl.ds(at, 256)]
            )

        tiles(3 * columns, 256, project_tile)

        def value_of(k, side, slot):
            where = lines(slot * frames, frames)
            cosine, sine = n.cosine[where], n.sine[where]
            blocks = []
            for kind in range(3):
                value = n.project[pl.ds(k * frames, frames), pl.ds((side * 3 + kind) * 128, 128)]
                if kind < 2:
                    value = value * cosine + swapped(value) * sine
                blocks.append(value.astype(low))
            return jnp.concatenate(blocks, axis=1)

        to_heads(offset, value_of, n.paired, n.pair_sem, 384, n.pair_send)

    project_half(mine)
    for copy in attn_sends:
        copy.wait_recv()
    project_half(theirs)

    def row_tables(at):
        turn_tables(pair_row, at, n.row_cosine, n.row_sine, pl.ds(at, frames))
        chosen = jnp.where(picked(pair_row, at, frames)[0], 1.0, 0.0)
        n.chosen[pl.ds(at, frames)] = chosen.astype(low)

    tiles(RING * frames, frames, row_tables)
    heads_arrive(n.paired, n.pair_sem)

    def masked_parts(at):
        where = pl.ds(at, frames)
        query, key = n.paired[where, 0:128], n.paired[where, 128:256]
        chosen = n.chosen[where]
        first_head = lanes < 64
        blocked = jnp.where(
            lax.rem(lanes, 64) < 8, NEGATIVE * (1.0 - chosen.astype(full)), 0.0
        ).astype(low)
        scaled = (query.astype(full) * HEAD_DIM ** (-0.5)).astype(low)
        n.query_head[0, where] = jnp.where(first_head, scaled, chosen)
        n.query_head[1, where] = jnp.where(first_head, chosen, scaled)
        n.key_head[0, where] = jnp.where(first_head, key, blocked)
        n.key_head[1, where] = jnp.where(first_head, blocked, key)
        n.query_turned[:, where] = jnp.transpose(query.astype(full)).astype(low)

    tiles(RING * frames, frames, masked_parts)
    all_frames = RING * frames
    pair_place = (lines(slot_of(pair_row) * frames, frames), lines(pair_side * 128, 128))

    def attend(at):
        where = pl.ds(at, half)
        sums = []
        for head in range(2):
            scores = dot_across(n.query_head[head, where], n.key_head[head])
            top = jnp.max(scores, axis=1, keepdims=True)
            weights = jnp.exp(scores - top)
            total = jnp.sum(weights, axis=1, keepdims=True)
            shares = (weights * (1.0 / total)).astype(low)
            n.shares[head, where] = shares
            sums.append(dot_plain(shares, n.paired[:, 256:384]))
        first_head = lax.broadcasted_iota(jnp.int32, (half, 128), 1) < 64
        value = jnp.where(first_head, sums[0], sums[1])
        n.attended_pair[where] = value
        n.attended_send[where] = value.astype(low)
        for k in range(2):
            to = at // frames + k
            place = lines(at + k * frames, frames)

            @pl.when(to != rank)
            def _():
                link(
                    n.attended_send.at[place],
                    n.attended.at[pair_place],
                    n.attended_sem.at[0, to],
                    n.attended_sem.at[1, rank],
                    (to, group_rank),
                ).start()

            @pl.when(to == rank)
            def _():
                n.attended[pair_place] = n.attended_send[place]

    tiles(all_frames, half, attend)

    def pairs_arrive(buffer, sems, wide):
        for other in range(1, RING):
            source = block(other)
            where = buffer.at[
                lines(slot_of(source // 2) * frames, frames),
                pl.ds(pl.multiple_of(lax.rem(source, 2) * wide, 128), wide),
            ]
            link(where, where, sems.at[0, source], sems.at[1, source], (source, group_rank)).wait_recv()

    upstream_sends[0].wait_recv()
    other_lines = lines((2 * core + 1 - chip) * frames, frames)
    upstream_sends.append(
        push(n.upstream.at[other_lines], n.upstream.at[other_lines], n.upstream_sem, (2,), sibling)
    )
    pairs_arrive(n.attended, n.attended_sem, 128)

    out_load.wait()
    first = partial_sum(1, n.attended, lambda left, at: dot_plain(left, n.out_held[:, pl.ds(at, 256)]))
    second = cross_sum(1, first)
    ff_sends = []
    for k in range(2):
        second[k].wait_recv()

        def norm_two(at, k=k):
            where = pl.ds(k * frames + at, 32)
            hidden = n.hidden[where] + n.keep[where] + n.land_two[1, where].astype(full)
            n.hidden[where] = hidden
            centred = hidden - mean(hidden)
            spread = lax.rsqrt(mean(centred * centred) + EPSILON)
            normal = centred * spread
            n.normal_two[where] = normal
            n.spread_two[where] = jnp.broadcast_to(spread, (32, 128))
            n.ff_in[lines(mine + k * frames + at, 32)] = (normal * n.gain[0:1]).astype(low)

        tiles(frames, 32, norm_two)
        ff_sends.append(share(n.ff_in, k, n.ff_sem))

    up_load.wait()
    down_load.wait()
    for copy in up_sends:
        copy.wait_recv()
    for copy in upstream_sends[1:]:
        copy.wait_recv()

    def feed_half(offset):
        where = lines(offset, half)

        def feed_tile(at):
            widened = dot_plain(n.ff_in[where], n.up_held[:, pl.ds(at, 256)])
            grad = dot_across(n.upstream[where], n.down_held[pl.ds(at, 256)])
            share_of = 0.5 * (1.0 + lax.erf(widened * math.sqrt(0.5)))
            slope = share_of + widened * jnp.exp(-0.5 * widened * widened) * (
                1.0 / math.sqrt(2.0 * math.pi)
            )
            n.activated[where, pl.ds(at, 256)] = (widened * share_of).astype(low)
            n.grad_widened[where, pl.ds(at, 256)] = (grad * slope).astype(low)

        tiles(hidden_units, 256, feed_tile)

    feed_half(mine)
    for copy in ff_sends:
        copy.wait_recv()
    feed_half(theirs)
    first = partial_sum(
        2, n.grad_widened, lambda left, at: dot_across(left, n.up_held[pl.ds(at, 256)])
    )
    second = cross_sum(2, first)

    def down_tile(at):
        value = contract_rows(n.activated[:, pl.ds(at, 256)], n.upstream[...]).astype(low)
        n.down_total[at // 128] = value[:128]
        n.down_total[at // 128 + 1] = value[128:]

    tiles(hidden_units, 256, down_tile)
    begin(down_ring)

    def up_tile(at):
        value = contract_rows(n.ff_in[:, pl.ds(at, columns)], n.grad_widened[...]).astype(low)
        deep = columns // RING
        for j in range(RING):
            n.up_total[j, pl.ds(pl.multiple_of(at // RING, deep), deep)] = value[
                j * deep : (j + 1) * deep
            ]

    tiles(width, columns, up_tile)
    begin(up_ring)
    ticks(TICKS[0])

    gain_sums = jnp.zeros((1, width), full)
    grad_sends = []
    for k in range(2):
        second[k].wait_recv()
        weight = (1 - jnp.abs(chip - k)).astype(full)

        def back_two(i, sums, k=k, weight=weight):
            at = pl.multiple_of(i * 32, 32)
            where = pl.ds(k * frames + at, 32)
            grad = n.keep[where] + n.land_two[2, where].astype(full)
            normal = n.normal_two[where]
            scaled = grad * n.gain[0:1]
            back = n.spread_two[where][:, 0:1] * (
                scaled - mean(scaled) - normal * mean(scaled * normal)
            )
            total = n.upstream[lines(mine + k * frames + at, 32)].astype(full) + back
            n.grad_two[where] = total
            n.grad_two_low[lines(mine + k * frames + at, 32)] = total.astype(low)
            return sums + weight * jnp.sum(grad * normal, axis=0, keepdims=True)

        gain_sums = lax.fori_loop(0, frames // 32, back_two, gain_sums)
        grad_sends.append(share(n.grad_two_low, k, n.grad_two_sem))
    ticks(TICKS[1])
    n.mod_sums[8:16] = jnp.zeros((8, 2 * width), full)
    n.mod_sums[8:9, :width] = gain_sums

    def attended_half(offset):
        value = dot_across(n.grad_two_low[lines(offset, half)], n.out_held[...]).astype(low)

        def value_of(k, side, slot):
            return value[k * frames : (k + 1) * frames, side * 128 : side * 128 + 128]

        to_heads(offset, value_of, n.grad_pair, n.grad_pair_sem, 128, n.grad_pair_send)

    attended_half(mine)
    for copy in grad_sends:
        copy.wait_recv()
    attended_half(theirs)
    value = contract_rows(n.attended[...], n.grad_two_low[...]).astype(low)
    for j in range(RING):
        n.out_total[j] = value[j * 32 : (j + 1) * 32]
    begin(out_ring)
    ticks(TICKS[2])

    first = partial_sum(3, n.activated, lambda left, at: dot_plain(left, n.down_held[:, pl.ds(at, 256)]))
    output_second = cross_sum(3, first)
    ticks(TICKS[3])

    heads_arrive(n.grad_pair, n.grad_pair_sem)

    def turn_upstream(at):
        where = pl.ds(at, frames)
        n.grad_turned[:, where] = jnp.transpose(n.grad_pair[where].astype(full)).astype(low)

    tiles(all_frames, frames, turn_upstream)
    n.key_turned[...] = jnp.zeros(n.key_turned.shape, full)
    n.value_turned[...] = jnp.zeros(n.value_turned.shape, full)

    def back_turned(value, where):
        return value * n.row_cosine[where] - swapped(value) * n.row_sine[where]

    def attend_back(at):
        at = pl.multiple_of(at, half)
        where = pl.ds(at, half)
        first_head = lax.broadcasted_iota(jnp.int32, (half, 128), 1) < 64
        grad = n.grad_pair[where]
        product = grad.astype(full) * n.attended_pair[where]
        terms = []
        for head in range(2):
            here = first_head if head == 0 else jnp.logical_not(first_head)
            delta = jnp.sum(jnp.where(here, product, 0.0), axis=1, keepdims=True)
            grad_head = jnp.where(here, grad, jnp.zeros_like(grad))
            prob_grad = dot_across(grad_head, n.paired[:, 256:384])
            shares = n.shares[head, where]
            score_grad = (shares.astype(full) * (prob_grad - delta)).astype(low)
            terms.append(dot_plain(score_grad, n.paired[:, 128:256]))
            rows = pl.ds(head * 64, 64)
            n.value_turned[rows] += dot_plain(n.grad_turned[rows, where], shares)
            n.key_turned[rows] += dot_plain(n.query_turned[rows, where], score_grad)
        query_grad = jnp.where(first_head, terms[0], terms[1]) * HEAD_DIM ** (-0.5)
        for k in range(2):
            place = lines(at + k * frames, frames)
            n.project_send[place, 0:128] = back_turned(
                query_grad[k * frames : (k + 1) * frames], place
            ).astype(low)

    for part in range(2):
        tiles(all_frames // 2, half, lambda at, part=part: attend_back(at + part * all_frames // 2))
        ticks(TICKS[4 + part])
    project_place = (lines(slot_of(pair_row) * frames, frames), lines(pair_side * 384, 384))

    def keys_back(at):
        place = pl.ds(at, frames)
        key_grad = jnp.transpose(n.key_turned[:, place]) * HEAD_DIM ** (-0.5)
        n.project_send[place, 128:256] = back_turned(key_grad, place).astype(low)
        n.project_send[place, 256:384] = jnp.transpose(n.value_turned[:, place]).astype(low)
        to = at // frames

        @pl.when(to != rank)
        def _():
            link(
                n.project_send.at[place],
                n.grad_project.at[project_place],
                n.project_sem.at[0, to],
                n.project_sem.at[1, rank],
                (to, group_rank),
            ).start()

        @pl.when(to == rank)
        def _():
            n.grad_project[project_place] = n.project_send[place]

    tiles(all_frames, frames, keys_back)

    for copy in output_second:
        copy.wait_recv()

    def finish_output(at):
        where = lines(chip * frames + at, 32)
        n.output[pl.ds(at, 32)] = (
            n.hidden[where] + n.keep[where] + n.land_two[3, where].astype(full)
        ).astype(low)

    tiles(frames, 32, finish_output)
    ticks(TICKS[6])
    pairs_arrive(n.grad_project, n.project_sem, 384)

    first = partial_sum(
        4, n.grad_project, lambda left, at: dot_across(left, n.qkv_held[pl.ds(at, 256)])
    )
    second = cross_sum(4, first)

    def qkv_tile(at):
        value = contract_rows(n.attn_in[:, pl.ds(at, columns)], n.grad_project[...]).astype(low)
        deep = columns // RING
        for j in range(RING):
            n.qkv_total[j, pl.ds(pl.multiple_of(at // RING, deep), deep)] = value[
                j * deep : (j + 1) * deep
            ]

    tiles(width, columns, qkv_tile)
    begin(qkv_ring)
    ticks(TICKS[7])
    hidden_sends = []
    for k in range(2):
        second[k].wait_recv()

        def back_one(at, k=k):
            where = pl.ds(k * frames + at, 32)
            grad = n.keep[where] + n.land_two[4, where].astype(full)
            normal = n.normal_one[where]
            scaled = grad * n.scale_one[where]
            back = n.spread_one[where][:, 0:1] * (
                scaled - mean(scaled) - normal * mean(scaled * normal)
            )
            n.grad_hidden[lines(mine + k * frames + at, 32)] = (n.grad_two[where] + back).astype(low)

            @pl.when(chip == k)
            def _():
                n.mod_terms[pl.ds(at, 32), :width] = grad * normal
                n.mod_terms[pl.ds(at, 32), width:] = grad

        tiles(frames, 32, back_one)
        hidden_sends.append(share(n.grad_hidden, k, n.grad_hidden_sem))
    ticks(TICKS[8])

    spot = (lax.broadcasted_iota(jnp.int32, (8, frames), 1) + rank * frames).astype(full)
    chosen = (spot >= n.small[1]) & (spot < n.small[2])
    picker = jnp.where(chosen, 1.0, 0.0)

    def mod_sum(at):
        where = pl.ds(at, 512)
        n.mod_sums[0:8, where] = jnp.dot(picker, n.mod_terms[:, where], precision=HIGHEST)

    tiles(2 * width, 512, mod_sum)
    for other in range(1, RING):
        to = block(other)
        push(
            n.mod_sums.at[:, pl.ds(pl.multiple_of(to * 256, 256), 256)],
            n.sums_land.at[rank],
            n.sums_sem,
            (other - 1,),
            (to, group_rank),
        )
    sums_copies = sent[-(RING - 1) :]
    n.sums_land[rank] = n.mod_sums[:, pl.ds(pl.multiple_of(rank * 256, 256), 256)]

    for copy in hidden_sends:
        copy.wait_recv()
    back = dot_across(n.grad_hidden[...], n.skip_held[...]).astype(low)
    n.joined_send[...] = back
    grad_joined_copies = []
    for other in (2, 1, 3):
        to = group(other)
        grad_joined_copies.append(
            push(
                n.joined_send.at[lines(slot_of(to) * frames, frames)],
                n.grad_joined.at[group_rank],
                n.grad_joined_sem,
                (other - 1,),
                (rank, to),
            )
        )
    n.grad_joined[group_rank] = n.joined_send[own_lines]

    def skip_weight_tile(at):
        value = contract_rows(n.joined[:, pl.ds(at, 256)], n.grad_hidden[...]).astype(low)
        for j in range(4):
            n.skip_total[at // 64 + j] = value[j * 64 : (j + 1) * 64]

    tiles(n.joined.shape[1], 256, skip_weight_tile)
    begin(skip_ring)
    ticks(TICKS[9])

    for copy in sums_copies:
        copy.wait_recv()
    n.sums_send[...] = jnp.sum(n.sums_land[...], axis=0)
    n.mod_grad[rank, group_rank] = n.sums_send[...]
    group_sums = [
        push(
            n.sums_send,
            n.mod_grad.at[rank, group_rank],
            n.sums_group_sem,
            (other - 1,),
            (rank, group(other)),
        )
        for other in (2, 1, 3)
    ]
    ticks(TICKS[10])
    for copy in group_sums:
        copy.wait_recv()
    mod_spread = [
        push(
            n.mod_grad.at[rank],
            n.mod_grad.at[rank],
            n.sums_block_sem,
            (other - 1,),
            (block(other), group_rank),
        )
        for other in range(1, RING)
    ]

    ticks(5 * (2 * RING + 1))
    for ring in rings:
        ring.finish()
    for copy in mod_spread + grad_joined_copies:
        copy.wait_recv()
    gain_grad = n.mod_grad[group_rank, 0, 8:9]
    for row in range(1, ROWS):
        gain_grad = gain_grad + n.mod_grad[group_rank, row, 8:9]
    n.gain_grad[...] = jnp.broadcast_to(gain_grad, n.gain_grad.shape)
    for index, copy in enumerate(sent):
        if not any(copy is other for pair in list(group_copies.values())[:-1] for kind in pair for other in kind):
            copy.wait_send()
    for sems, wide in ((n.pair_sem, 384), (n.attended_sem, 128), (n.grad_pair_sem, 128), (n.project_sem, 384)):
        buffer = {384: n.project_send, 128: n.attended_send}[wide]
        for other in range(1, RING):
            to = block(other)
            where = buffer.at[lines(to * frames, frames)]
            link(where, where, sems.at[0, to], sems.at[1, to], (to, group_rank)).wait_send()


def block_call(
    inputs, skipped, w_skip, w_mod, w_qkv, w_out, w_up, w_down, cotangent, small
):
    low, full = jnp.bfloat16, jnp.float32
    frames, width = inputs.shape
    tokens, half = ROWS * frames, 2 * frames
    columns = width // ROWS
    hidden_units = w_down.shape[0]
    joint = w_skip.shape[0]
    all_frames = RING * frames
    deep = width // RING

    held = dict(
        inputs=inputs,
        skipped=skipped,
        w_skip=w_skip,
        w_mod=w_mod,
        w_qkv=w_qkv,
        w_out=w_out,
        w_up=w_up,
        w_down=w_down,
        cotangent=cotangent,
        small=small,
    )
    given = dict(
        output=((frames, width), low),
        grad_joined=((ROWS, frames, joint), low),
        condition=((ROWS * 8, columns), low),
        mod_grad=((RING, ROWS, 16, 256), full),
        gain_grad=((8, columns), full),
        down_whole=((RING, hidden_units // RING, width), low),
        up_whole=((RING, deep, hidden_units), low),
        qkv_whole=((RING, deep, 3 * columns), low),
        skip_whole=((RING, joint // RING, width), low),
        out_whole=((RING, columns // RING, width), low),
    )
    buffers = dict(
        joined_own=((ROWS, frames, joint), low),
        joined=((tokens, joint), low),
        upstream=((tokens, width), low),
        skip_held=(w_skip.shape, low),
        mod_held=(w_mod.shape, low),
        out_held=(w_out.shape, low),
        down_held=(w_down.shape, low),
        qkv_held=((width, 3 * columns), low),
        up_held=((width, hidden_units), low),
        smalls=((ROWS,) + small.shape, full),
        mod_part=((ROWS * 8, 2 * width), full),
        mod_land=((2, 16, 2 * width), full),
        mod_send=((16, 2 * width), full),
        gain=((8, width), full),
        cosine=((tokens, 128), full),
        sine=((tokens, 128), full),
        row_cosine=((all_frames, 128), full),
        row_sine=((all_frames, 128), full),
        chosen=((all_frames, 128), low),
        send_one=((half, width), low),
        send_two=((half, width), low),
        keep=((half, width), full),
        land_one=((5, half, width), low),
        land_two=((5, half, width), low),
        scale_one=((half, width), full),
        shift_one=((half, width), full),
        hidden=((half, width), full),
        normal_one=((half, width), full),
        spread_one=((half, 128), full),
        normal_two=((half, width), full),
        spread_two=((half, 128), full),
        grad_two=((half, width), full),
        attn_in=((tokens, width), low),
        project=((half, 3 * columns), full),
        pair_send=((RING, frames, 384), low),
        paired=((all_frames, 384), low),
        query_head=((2, all_frames, 128), low),
        key_head=((2, all_frames, 128), low),
        query_turned=((128, all_frames), low),
        shares=((2, all_frames, all_frames), low),
        attended_pair=((all_frames, 128), full),
        attended_send=((all_frames, 128), low),
        attended=((tokens, columns), low),
        ff_in=((tokens, width), low),
        activated=((tokens, hidden_units), low),
        grad_widened=((tokens, hidden_units), low),
        grad_two_low=((tokens, width), low),
        grad_pair_send=((RING, frames, 128), low),
        grad_pair=((all_frames, 128), low),
        grad_turned=((128, all_frames), low),
        key_turned=((128, all_frames), full),
        value_turned=((128, all_frames), full),
        project_send=((all_frames, 384), low),
        grad_project=((tokens, 3 * columns), low),
        grad_hidden=((tokens, width), low),
        mod_terms=((frames, 2 * width), full),
        mod_sums=((16, 2 * width), full),
        sums_land=((RING, 16, 256), full),
        sums_send=((16, 256), full),
        joined_send=((tokens, joint), low),
        down_total=((RING, hidden_units // RING, width), low),
        up_total=((RING, deep, hidden_units), low),
        qkv_total=((RING, deep, 3 * columns), low),
        skip_total=((RING, joint // RING, width), low),
        out_total=((RING, columns // RING, width), low),
        down_land=((RING - 1, hidden_units // RING, width), low),
        up_land=((RING - 1, deep, hidden_units), low),
        qkv_land=((RING - 1, deep, 3 * columns), low),
        skip_land=((RING - 1, joint // RING, width), low),
        out_land=((RING - 1, columns // RING, width), low),
        up_turn=((deep, hidden_units), low),
        qkv_turn=((deep, 3 * columns), low),
    )
    sems = dict(
        load_sem=(16,),
        joined_sem=(2, 3),
        small_sem=(2, 3),
        qkv_sem=(2, 3, 6),
        up_sem=(2, 3),
        mod_sem=(2, 2),
        first_sem=(2, 5, 2),
        second_sem=(2, 5, 2),
        upstream_sem=(2, 3),
        attn_sem=(2, 2),
        ff_sem=(2, 2),
        grad_two_sem=(2, 2),
        grad_hidden_sem=(2, 2),
        pair_sem=(2, RING),
        attended_sem=(2, RING),
        grad_pair_sem=(2, RING),
        project_sem=(2, RING),
        grad_joined_sem=(2, 3),
        sums_sem=(2, RING - 1),
        sums_group_sem=(2, 3),
        sums_block_sem=(2, RING - 1),
        down_sem=(2, 2, 2, RING - 1),
        up_ring_sem=(2, 2, 2, RING - 1),
        qkv_ring_sem=(2, 2, 2, RING - 1),
        skip_ring_sem=(2, 2, 2, RING - 1),
        out_ring_sem=(2, 2, 2, RING - 1),
        turn_sem=(2, 2, 3),
        whole_sem=(5, 2, RING),
    )
    names = [*held, *given, *buffers, *sems]
    vmem = pl.BlockSpec(memory_space=pltpu.VMEM)
    anywhere = pl.BlockSpec(memory_space=pl.ANY)
    return pl.pallas_call(
        functools.partial(block_kernel, names),
        out_shape=[jax.ShapeDtypeStruct(*spec) for spec in given.values()],
        in_specs=[vmem if name == "small" else anywhere for name in held],
        out_specs=[anywhere if name.endswith("_whole") else vmem for name in given],
        scratch_shapes=[pltpu.VMEM(*spec) for spec in buffers.values()]
        + [pltpu.SemaphoreType.DMA(shape) for shape in sems.values()],
        compiler_params=pltpu.CompilerParams(
            collective_id=0, has_side_effects=True, vmem_limit_bytes=62 * 1024 * 1024
        ),
    )(*held.values())


def finish_kernel(
    joined_ref,
    condition_ref,
    mod_ref,
    gain_ref,
    down_ref,
    up_ref,
    qkv_ref,
    skip_ref,
    out_ref,
    grad_inputs,
    grad_skipped,
    grad_skip,
    grad_mod,
    grad_qkv,
    grad_out,
    grad_gain,
    grad_up,
    grad_down,
):
    full = jnp.float32
    wide = joined_ref.shape[2]
    for r in range(ROWS):
        target = (grad_inputs, grad_skipped)[r // 2]
        target[:, pl.ds((r % 2) * wide, wide)] = joined_ref[r].astype(full)
    grad_down[...] = down_ref[0].astype(full)
    grad_skip[...] = skip_ref[0].astype(full)
    grad_out[...] = out_ref[0].astype(full)
    grad_gain[...] = gain_ref[0:1]
    deep, wide = up_ref.shape[1] // ROWS, up_ref.shape[2]
    for r in range(ROWS):
        rows = pl.ds(r * deep, deep)
        grad_up[:, pl.ds(r * wide, wide)] = up_ref[0, rows].astype(full)
        for side in range(2):
            for kind in range(3):
                source = qkv_ref[0, rows, pl.ds((side * 3 + kind) * 128, 128)]
                at = kind * (ROWS * 256) + r * 256 + side * 128
                grad_qkv[:, pl.ds(at, 128)] = source.astype(full)
    sums = jnp.concatenate([mod_ref[0, r, 0:8] for r in (0, 2, 1, 3)], axis=0)
    high = sums.astype(jnp.bfloat16)
    rest = (sums - high.astype(full)).astype(jnp.bfloat16)
    grad_mod[...] = contract_rows(condition_ref[...], high) + contract_rows(
        condition_ref[...], rest
    )


def finish_call(joined, condition, mod, gain, down, up, qkv, skip, out):
    full = jnp.float32
    frames, wide = joined.shape[1:]
    columns = condition.shape[1]

    def first(shape):
        return pl.BlockSpec((1,) + shape[1:], lambda i: (i,) + (0,) * (len(shape) - 1))

    def rows(count, width):
        return jax.ShapeDtypeStruct((count, width), full), pl.BlockSpec(
            (count // RING, width), lambda i: (i, 0)
        )

    deep = up.shape[1] // ROWS
    results = [
        rows(frames, 2 * wide),
        rows(frames, 2 * wide),
        rows(RING * skip.shape[1], skip.shape[2]),
        (
            jax.ShapeDtypeStruct((columns, RING * mod.shape[3]), full),
            pl.BlockSpec((columns, mod.shape[3]), lambda i: (0, i)),
        ),
        rows(RING * deep, ROWS * qkv.shape[2]),
        rows(RING * out.shape[1], out.shape[2]),
        (jax.ShapeDtypeStruct((1, columns), full), pl.BlockSpec((1, columns), lambda i: (0, 0))),
        rows(RING * deep, ROWS * up.shape[2]),
        rows(RING * down.shape[1], down.shape[2]),
    ]
    return pl.pallas_call(
        finish_kernel,
        grid=(RING,),
        out_shape=[shape for shape, _ in results],
        in_specs=[
            pl.BlockSpec((ROWS, frames // RING, wide), lambda i: (0, i, 0)),
            pl.BlockSpec(condition.shape, lambda i: (0, 0)),
            first(mod.shape),
            pl.BlockSpec(gain.shape, lambda i: (0, 0)),
            first(down.shape),
            first(up.shape),
            first(qkv.shape),
            first(skip.shape),
            first(out.shape),
        ],
        out_specs=[spec for _, spec in results],
        compiler_params=pltpu.CompilerParams(vmem_limit_bytes=62 * 1024 * 1024),
    )(joined, condition, mod, gain, down, up, qkv, skip, out)


def small_table(lengths_row, steps_row, gain):
    end = jnp.cumsum(lengths_row).astype(jnp.float32)
    start = end - lengths_row.astype(jnp.float32)
    count = end.shape[0]

    def down(values):
        return jnp.broadcast_to(values[:, None], (count, 128))

    def along(values, empty):
        rest = jnp.full((64 - 2 * count,), empty, jnp.float32)
        lane = jnp.concatenate([values, values, rest, values, values, rest])
        return jnp.broadcast_to(lane[None], (8, 128))

    gain = gain.astype(jnp.float32)
    return jnp.stack(
        [
            down(steps_row.astype(jnp.float32)),
            down(start),
            down(end),
            along(start, 1e9),
            along(end, 0.0),
            jnp.broadcast_to(gain[None, :128], (8, 128)),
            jnp.broadcast_to(gain[None, 128:], (8, 128)),
        ]
    )


def per_device_block(
    inputs,
    skipped,
    w_skip,
    w_mod,
    w_qkv,
    w_out,
    ff_gain,
    w_up,
    w_down,
    cotangent,
    lengths,
    flow_steps,
):
    width = inputs.shape[2]
    columns = width // ROWS
    group_rank = lax.axis_index("grp")
    small = small_table(lengths[0], flow_steps[0], ff_gain)
    output, *rest = block_call(
        inputs[0], skipped[0], w_skip, w_mod, w_qkv, w_out, w_up, w_down, cotangent[0], small
    )
    grad_inputs, grad_skipped, skip, mod, qkv, out, gain, up, down = finish_call(*rest)
    return (
        output[None],
        grad_inputs[None],
        grad_skipped[None],
        skip,
        mod,
        qkv,
        out,
        gain[0],
        up,
        down,
    )


def solution(mesh):
    placed = (
        P("grp", "blk", None),
        P("grp", "blk", None),
        P("grp", None),
        P("grp", None),
        P("grp", None),
        P("grp", None),
        P("grp"),
        P("grp", None),
        P("grp", None),
        P("grp", "blk", None),
        P("grp", None),
        P("grp", None),
    )
    body = per_device
    if mesh.shape["blk"] == RING and mesh.shape["grp"] == ROWS:
        body = per_device_block
    return jax.shard_map(
        body,
        mesh=mesh,
        in_specs=placed,
        out_specs=(
            P("grp", "blk", None),
            P("grp", "blk", None),
            P("grp", "blk", None),
            P("grp", None),
            P("grp", None),
            P("grp", None),
            P("grp", None),
            P("grp"),
            P("grp", None),
            P("grp", None),
        ),
        check_vma=False,
    )
```

```python
import functools
import math
import types

import jax
import jax.numpy as jnp
from jax import lax
from jax.experimental import pallas as pl
from jax.experimental.pallas import tpu as pltpu
from jax.sharding import PartitionSpec as P

HEADS = 16
HEAD_DIM = 64
STEPS = 32


EPSILON = 1e-06
NEGATIVE = -1e30
HIGHEST = lax.Precision.HIGHEST
MESH = pl.DeviceIdType.MESH
RING = 8
ROWS = 4


def from_behind(block, axis, distance):
    devices = range(lax.axis_size(axis))
    route = [((i - distance) % len(devices), i) for i in devices]
    return lax.ppermute(block, axis, route)


def layout(lengths_row, frames):
    end_frame = jnp.cumsum(lengths_row)
    start_frame = end_frame - lengths_row
    segment = jnp.sum((frames[:, None] >= end_frame[None, :]).astype(jnp.int32), axis=1)
    chosen = segment[:, None] == jnp.arange(lengths_row.shape[0], dtype=jnp.int32)[None, :]
    position = frames - jnp.sum(jnp.where(chosen, start_frame[None, :], 0), axis=1)
    return (segment, position)


def flow_condition(steps_row, model_width):
    half_width = model_width // 2
    rate_table = jnp.exp(
        -math.log(10000.0) * jnp.arange(half_width, dtype=jnp.float32) / half_width
    )
    angles = 1000.0 * (steps_row.astype(jnp.float32) / STEPS)[:, None] * rate_table[None, :]
    return jax.nn.silu(jnp.concatenate([jnp.sin(angles), jnp.cos(angles)], axis=1))


def rotation_tables(position, head_width):
    half_width = head_width // 2
    rate_table = jnp.exp(
        -math.log(10000.0) * jnp.arange(half_width, dtype=jnp.float32) / half_width
    )
    angles = position.astype(jnp.float32)[:, None] * rate_table[None, :]
    return (jnp.cos(angles)[:, None, :], jnp.sin(angles)[:, None, :], half_width)


def rotate(head_block, position):
    cosine_part, sine_part, half_width = rotation_tables(position, head_block.shape[-1])
    first_half = head_block[..., :half_width]
    second_half = head_block[..., half_width:]
    return jnp.concatenate(
        [
            first_half * cosine_part - second_half * sine_part,
            second_half * cosine_part + first_half * sine_part,
        ],
        axis=-1,
    )


def rotate_back(head_block, position):
    cosine_part, sine_part, half_width = rotation_tables(position, head_block.shape[-1])
    first_half = head_block[..., :half_width]
    second_half = head_block[..., half_width:]
    return jnp.concatenate(
        [
            first_half * cosine_part + second_half * sine_part,
            second_half * cosine_part - first_half * sine_part,
        ],
        axis=-1,
    )


def normalize(hidden):
    centred = hidden - jnp.mean(hidden, axis=-1, keepdims=True)
    scaled = lax.rsqrt(jnp.mean(centred * centred, axis=-1, keepdims=True) + EPSILON)
    return (centred * scaled, scaled)


def norm_back(grad_normal, normal, scaled):
    centred_grad = grad_normal - jnp.mean(grad_normal, axis=-1, keepdims=True)
    return scaled * (centred_grad - normal * jnp.mean(grad_normal * normal, axis=-1, keepdims=True))


def exact_gelu(values_in):
    return jax.nn.gelu(values_in, approximate=False)


def contract_rows(left_side, right_side):
    return lax.dot_general(
        left_side, right_side, (((0,), (0,)), ((), ())), preferred_element_type=jnp.float32
    )


def heads_of(flat_block):
    return flat_block.reshape(flat_block.shape[0], HEADS, HEAD_DIM)


def per_device(
    inputs,
    skipped,
    w_skip,
    w_mod,
    w_qkv,
    w_out,
    ff_gain,
    w_up,
    w_down,
    cotangent,
    lengths,
    flow_steps,
):
    w_skip, w_mod, w_qkv, w_out, ff_gain, w_up, w_down = (
        lax.all_gather(w_skip, "grp", axis=0, tiled=True),
        lax.all_gather(w_mod, "grp", axis=0, tiled=True),
        lax.all_gather(w_qkv, "grp", axis=0, tiled=True),
        lax.all_gather(w_out, "grp", axis=0, tiled=True),
        lax.all_gather(ff_gain, "grp", axis=0, tiled=True),
        lax.all_gather(w_up, "grp", axis=0, tiled=True),
        lax.all_gather(w_down, "grp", axis=0, tiled=True),
    )
    frame_count = inputs.shape[1]
    model_width = inputs.shape[2]
    cycle_size = lax.axis_size("blk")
    device_rank = lax.axis_index("blk")
    score_scale = HEAD_DIM ** (-0.5)
    local_frames = jnp.arange(frame_count, dtype=jnp.int32)
    lengths_row = lengths[0]
    own_segment, own_position = layout(lengths_row, device_rank * frame_count + local_frames)

    def segment_of(source):
        return layout(lengths_row, source * frame_count + local_frames)[0]

    def scored(query_block, key_block, query_segment, key_segment):
        raw_scores = (
            jnp.einsum(
                "qhd,khd->hqk",
                heads_of(query_block),
                heads_of(key_block),
                preferred_element_type=jnp.float32,
            )
            * score_scale
        )
        allowed = (query_segment[:, None] == key_segment[None, :])[None]
        return (raw_scores, allowed)

    joined = jnp.concatenate([inputs[0], skipped[0]], axis=1)
    hidden = jnp.dot(joined, w_skip, preferred_element_type=jnp.float32)
    condition = flow_condition(flow_steps[0], model_width).astype(jnp.bfloat16)
    modulation = jnp.dot(condition, w_mod, preferred_element_type=jnp.float32)
    picker = (
        own_segment[:, None] == jnp.arange(lengths_row.shape[0], dtype=jnp.int32)[None, :]
    ).astype(jnp.float32)
    per_frame = jnp.dot(picker, modulation, precision=HIGHEST)
    scale_one = 1.0 + per_frame[:, :model_width]
    normal_one, spread_one = normalize(hidden)
    attn_in = (normal_one * scale_one + per_frame[:, model_width:]).astype(jnp.bfloat16)
    project = jnp.dot(attn_in, w_qkv, preferred_element_type=jnp.float32).reshape(
        frame_count, 3, HEADS, HEAD_DIM
    )
    queries = (
        rotate(project[:, 0], own_position).astype(jnp.bfloat16).reshape(frame_count, model_width)
    )
    keys_own = (
        rotate(project[:, 1], own_position).astype(jnp.bfloat16).reshape(frame_count, model_width)
    )
    values_own = project[:, 2].astype(jnp.bfloat16).reshape(frame_count, model_width)

    def forward_turn(turn_index, carried):
        key_now, value_now, running_top, running_total, running_sum = carried
        source = (device_rank - turn_index) % cycle_size
        raw_scores, allowed = scored(queries, key_now, own_segment, segment_of(source))
        raw_scores = jnp.where(allowed, raw_scores, NEGATIVE)
        new_top = jnp.maximum(running_top, jnp.max(raw_scores, axis=2, keepdims=True))
        weights = jnp.where(allowed, jnp.exp(raw_scores - new_top), 0.0)
        shrink = jnp.exp(running_top - new_top)
        running_total = running_total * shrink + jnp.sum(weights, axis=2, keepdims=True)
        running_sum = running_sum * shrink + jnp.einsum(
            "hqk,khd->hqd",
            weights.astype(jnp.bfloat16),
            heads_of(value_now),
            preferred_element_type=jnp.float32,
        )
        key_now, value_now = from_behind((key_now, value_now), "blk", 1)
        return (key_now, value_now, new_top, running_total, running_sum)

    initial = (
        keys_own,
        values_own,
        jnp.full((HEADS, frame_count, 1), NEGATIVE, jnp.float32),
        jnp.zeros((HEADS, frame_count, 1), jnp.float32),
        jnp.zeros((HEADS, frame_count, HEAD_DIM), jnp.float32),
    )
    finished = lax.fori_loop(0, cycle_size, forward_turn, initial)
    running_top, running_total, running_sum = (finished[2], finished[3], finished[4])
    attended = jnp.transpose(running_sum / running_total, (1, 0, 2)).reshape(
        frame_count, model_width
    )
    log_total = (running_top + jnp.log(running_total))[:, :, 0]
    attended_low = attended.astype(jnp.bfloat16)
    hidden_two = hidden + jnp.dot(attended_low, w_out, preferred_element_type=jnp.float32)
    normal_two, spread_two = normalize(hidden_two)
    gain_vector = ff_gain.astype(jnp.float32)
    ff_in = (normal_two * gain_vector).astype(jnp.bfloat16)
    widened = jnp.dot(ff_in, w_up, preferred_element_type=jnp.float32)
    activated, gelu_back = jax.vjp(exact_gelu, widened)
    activated_low = activated.astype(jnp.bfloat16)
    output = (
        hidden_two + jnp.dot(activated_low, w_down, preferred_element_type=jnp.float32)
    ).astype(jnp.bfloat16)
    upstream = cotangent[0]
    grad_down = contract_rows(activated_low, upstream)
    grad_activated = jnp.dot(upstream, w_down.T, preferred_element_type=jnp.float32)
    grad_widened = gelu_back(grad_activated)[0].astype(jnp.bfloat16)
    grad_up = contract_rows(ff_in, grad_widened)
    grad_ff_in = jnp.dot(grad_widened, w_up.T, preferred_element_type=jnp.float32)
    grad_gain = jnp.sum(grad_ff_in * normal_two, axis=0)
    grad_hidden_two = upstream.astype(jnp.float32) + norm_back(
        grad_ff_in * gain_vector, normal_two, spread_two
    )
    grad_two_low = grad_hidden_two.astype(jnp.bfloat16)
    grad_out = contract_rows(attended_low, grad_two_low)
    grad_attended = jnp.dot(grad_two_low, w_out.T, preferred_element_type=jnp.float32).astype(
        jnp.bfloat16
    )
    delta = jnp.transpose(jnp.sum(heads_of(grad_attended.astype(jnp.float32) * attended), axis=2))
    zero_grad = jnp.zeros((frame_count, model_width), jnp.float32)

    def pair_terms(
        query_block,
        upstream_block,
        key_block,
        value_block,
        total_block,
        delta_block,
        query_segment,
        key_segment,
    ):
        raw_scores, allowed = scored(query_block, key_block, query_segment, key_segment)
        prob_block = jnp.where(allowed, jnp.exp(raw_scores - total_block[:, :, None]), 0.0)
        value_term = jnp.einsum(
            "hqk,qhd->khd",
            prob_block.astype(jnp.bfloat16),
            heads_of(upstream_block),
            preferred_element_type=jnp.float32,
        ).reshape(frame_count, model_width)
        prob_grad = jnp.einsum(
            "qhd,khd->hqk",
            heads_of(upstream_block),
            heads_of(value_block),
            preferred_element_type=jnp.float32,
        )
        score_grad = (prob_block * (prob_grad - delta_block[:, :, None])).astype(jnp.bfloat16)
        query_term = (
            jnp.einsum(
                "hqk,khd->qhd", score_grad, heads_of(key_block), preferred_element_type=jnp.float32
            ).reshape(frame_count, model_width)
            * score_scale
        )
        key_term = (
            jnp.einsum(
                "hqk,qhd->khd",
                score_grad,
                heads_of(query_block),
                preferred_element_type=jnp.float32,
            ).reshape(frame_count, model_width)
            * score_scale
        )
        return (query_term, key_term, value_term)

    def keys_turn(turn_index, carried):
        key_now, value_now, key_grad, value_grad, query_grad = carried
        source = (device_rank - turn_index) % cycle_size
        query_term, key_term, value_term = pair_terms(
            queries,
            grad_attended,
            key_now,
            value_now,
            log_total,
            delta,
            own_segment,
            segment_of(source),
        )
        key_now, value_now = from_behind((key_now, value_now), "blk", 1)
        key_grad, value_grad = (
            from_behind((key_grad + key_term).astype(jnp.bfloat16), "blk", 1).astype(jnp.float32),
            from_behind((value_grad + value_term).astype(jnp.bfloat16), "blk", 1).astype(
                jnp.float32
            ),
        )
        return (key_now, value_now, key_grad, value_grad, query_grad + query_term)

    done = lax.fori_loop(
        0, cycle_size, keys_turn, (keys_own, values_own, zero_grad, zero_grad, zero_grad)
    )
    key_grad, value_grad, query_grad = (done[2], done[3], done[4])
    grad_project = jnp.concatenate(
        [
            rotate_back(heads_of(query_grad), own_position).reshape(frame_count, model_width),
            rotate_back(heads_of(key_grad), own_position).reshape(frame_count, model_width),
            value_grad,
        ],
        axis=1,
    ).astype(jnp.bfloat16)
    grad_qkv = contract_rows(attn_in, grad_project)
    grad_attn_in = jnp.dot(grad_project, w_qkv.T, preferred_element_type=jnp.float32)
    mod_terms = jnp.concatenate([grad_attn_in * normal_one, grad_attn_in], axis=1)
    grad_modulation = jnp.dot(picker.T, mod_terms, precision=HIGHEST)
    grad_mod = jnp.dot(condition.astype(jnp.float32).T, grad_modulation, precision=HIGHEST)
    grad_hidden = grad_hidden_two + norm_back(grad_attn_in * scale_one, normal_one, spread_one)
    grad_hidden_low = grad_hidden.astype(jnp.bfloat16)
    grad_skip_weight = contract_rows(joined, grad_hidden_low)
    grad_joined = jnp.dot(grad_hidden_low, w_skip.T, preferred_element_type=jnp.float32)
    shards = (
        lax.psum_scatter(
            grad_skip_weight.astype(jnp.bfloat16), "grp", scatter_dimension=0, tiled=True
        ).astype(jnp.float32),
        lax.psum_scatter(
            grad_mod.astype(jnp.bfloat16), "grp", scatter_dimension=0, tiled=True
        ).astype(jnp.float32),
        lax.psum_scatter(
            grad_qkv.astype(jnp.bfloat16), "grp", scatter_dimension=0, tiled=True
        ).astype(jnp.float32),
        lax.psum_scatter(
            grad_out.astype(jnp.bfloat16), "grp", scatter_dimension=0, tiled=True
        ).astype(jnp.float32),
        lax.psum_scatter(
            grad_gain.astype(jnp.bfloat16), "grp", scatter_dimension=0, tiled=True
        ).astype(jnp.float32),
        lax.psum_scatter(
            grad_up.astype(jnp.bfloat16), "grp", scatter_dimension=0, tiled=True
        ).astype(jnp.float32),
        lax.psum_scatter(
            grad_down.astype(jnp.bfloat16), "grp", scatter_dimension=0, tiled=True
        ).astype(jnp.float32),
    )
    totals = lax.psum(
        (shards[0], shards[1], shards[2], shards[3], shards[4], shards[5], shards[6]), "blk"
    )
    return (
        output[None],
        grad_joined[:, :model_width][None],
        grad_joined[:, model_width:][None],
        totals[0],
        totals[1],
        totals[2],
        totals[3],
        totals[4],
        totals[5],
        totals[6],
    )


def dot_plain(left_side, right_side):
    return jnp.dot(left_side, right_side, preferred_element_type=jnp.float32)


def dot_across(left_side, right_side):
    return lax.dot_general(
        left_side, right_side, (((1,), (1,)), ((), ())), preferred_element_type=jnp.float32
    )


def ring_place(rank):
    odd = lax.rem(rank, 2)
    return (1 - odd) * (rank // 2) + odd * ((15 - rank) // 2)


def ring_rank(place):
    upper = place // 4
    return (1 - upper) * (2 * place) + upper * (15 - 2 * place)


TICKS = (1, 1, 0, 1, 0, 1, 0, 1, 1, 0, 1, 0, 1, 2, 1, 1, 1, 1, 0, 2, 1, 1, 2)


class Ring:
    def __init__(self, part, land, whole, sems, whole_sems, rank, group_rank, turn=None):
        self.part, self.land, self.whole = part, land, whole
        self.sems, self.whole_sems = sems, whole_sems
        self.rank, self.group_rank = rank, group_rank
        self.place = ring_place(rank)
        self.half = part.shape[1] // 2
        self.copies = {}
        self.puts, self.turns, self.turn = [], [], turn

    def block_at(self, offset):
        return ring_rank(lax.rem(self.place + offset + 2 * RING, RING))

    def rows(self, way):
        return pl.ds(way * self.half, self.half)

    def send(self, kind, step, way, source, target):
        to = ring_rank(lax.rem(self.place + (1 if way == 0 else RING - 1), RING))
        copy = pltpu.make_async_remote_copy(
            src_ref=source,
            dst_ref=target,
            send_sem=self.sems.at[kind, 0, way, step],
            recv_sem=self.sems.at[kind, 1, way, step],
            device_id=(to, self.group_rank),
            device_id_type=MESH,
        )
        copy.start()
        self.copies[kind, step, way] = copy

    def sum_step(self, step):
        if step == 1:
            for way in range(2):
                self.copies[0, 0, way].wait_send()
        for way in range(2):
            block = self.block_at((-1 if way == 0 else 1) * (step + 1))
            rows = self.rows(way)
            if step > 0:
                self.copies[0, step - 1, way].wait_recv()
                tile = min(self.half, 32)

                def add(i, carry, way=way, block=block, tile=tile):
                    at = pl.ds(pl.multiple_of(way * self.half + i * tile, tile), tile)
                    total = self.part[block, at].astype(jnp.float32) + self.land[
                        step - 1, at
                    ].astype(jnp.float32)
                    self.land[step - 1, at] = total.astype(jnp.bfloat16)
                    return carry

                lax.fori_loop(0, self.half // tile, add, 0)
            if step < RING - 1:
                source = self.part.at[block, rows] if step == 0 else self.land.at[step - 1, rows]
                self.send(0, step, way, source, self.land.at[step, rows])

    def put(self, block, step, way):
        rows = self.rows(way)
        copy = pltpu.make_async_copy(
            self.part.at[block, rows], self.whole.at[block, rows], self.whole_sems.at[way, step]
        )
        copy.start()
        self.puts.append(copy)

    def spread_step(self, step):
        if step == 0:
            self.close_sum()
        for way in range(2):
            block = self.block_at((-1 if way == 0 else 1) * step)
            rows = self.rows(way)
            if step > 0:
                self.copies[1, step - 1, way].wait_recv()
            if step < RING - 1:
                target = self.part.at[block, rows]
                self.send(1, step, way, target, target)
            self.put(block, step, way)

    def begin(self):
        self.sum_step(0)
        self.left = [functools.partial(self.sum_step, step) for step in range(1, RING)]
        self.left += [functools.partial(self.spread_step, step) for step in range(RING)]
        if self.turn is not None:
            self.left.insert(RING - 1, self.turn_out)

    def turn_out(self):
        place, sems = self.turn
        deep = self.part.shape[1] // ROWS

        def rows(group):
            return pl.ds(pl.multiple_of(group * deep, deep), deep)

        for other in (2, 1, 3):
            to = lax.rem(self.group_rank + other, ROWS)
            copy = pltpu.make_async_remote_copy(
                src_ref=self.land.at[RING - 2, rows(to)],
                dst_ref=place.at[rows(self.group_rank)],
                send_sem=sems.at[0, other - 1],
                recv_sem=sems.at[1, other - 1],
                device_id=(self.rank, to),
                device_id_type=MESH,
            )
            copy.start()
            self.turns.append(copy)
        place[rows(self.group_rank)] = self.land[RING - 2, rows(self.group_rank)]

    def close_sum(self):
        for copy in self.turns:
            copy.wait_recv()
        self.part[self.rank] = self.land[RING - 2] if self.turn is None else self.turn[0][...]

    def finish(self):
        for copy in self.turns:
            copy.wait_send()
        for (kind, step, _), copy in self.copies.items():
            if kind or step:
                copy.wait_send()
        for copy in self.puts:
            copy.wait()


def block_kernel(names, *refs):
    n = types.SimpleNamespace(**dict(zip(names, refs)))
    low, full = jnp.bfloat16, jnp.float32
    rank, group_rank = lax.axis_index("blk"), lax.axis_index("grp")
    core, chip = lax.rem(group_rank, 2), group_rank // 2
    sibling = (rank, group_rank + 1 - 2 * core)
    across = (rank, group_rank + 2 - 4 * chip)
    frames, width = n.cotangent.shape
    half = 2 * frames
    columns = width // ROWS
    mine, theirs = core * half, (1 - core) * half
    own_slot = 2 * core + chip
    pair_row, pair_side = rank // 2, lax.rem(rank, 2)
    sent = []

    def lines(offset, size):
        return pl.ds(pl.multiple_of(offset, min(size, 128)), size)

    def slot_of(row):
        return 2 * lax.rem(row, 2) + row // 2

    def row_of(slot):
        return 2 * lax.rem(slot, 2) + slot // 2

    def group(other):
        return lax.rem(group_rank + other, ROWS)

    def block(other):
        return lax.rem(rank + other, RING)

    def link(source, target, send_sem, recv_sem, device):
        return pltpu.make_async_remote_copy(
            src_ref=source,
            dst_ref=target,
            send_sem=send_sem,
            recv_sem=recv_sem,
            device_id=device,
            device_id_type=MESH,
        )

    def push(source, target, sems, index, device):
        copy = link(source, target, sems.at[(0,) + index], sems.at[(1,) + index], device)
        copy.start()
        sent.append(copy)
        return copy

    def load(source, target, index):
        copy = pltpu.make_async_copy(source, target, n.load_sem.at[index])
        copy.start()
        return copy

    def tiles(count, tile, body):
        def step(i, carry):
            body(pl.multiple_of(i * tile, tile))
            return carry

        lax.fori_loop(0, count // tile, step, 0)

    joined_loads = [
        load((n.inputs, n.skipped)[t // 2].at[:, pl.ds((t % 2) * 512, 512)], n.joined_own.at[t], t)
        for t in range(ROWS)
    ]
    upstream_load = load(n.cotangent, n.upstream.at[lines(own_slot * frames, frames)], 4)
    skip_load = load(n.w_skip, n.skip_held, 5)
    mod_load = load(n.w_mod, n.mod_held, 6)
    out_place = n.out_held.at[lines(group_rank * columns, columns)]
    out_load = load(n.w_out, out_place, 7)
    down_load = load(n.w_down, n.down_held, 8)
    pieces = [(side, kind) for side in range(2) for kind in range(3)]

    def qkv_piece(target, side, kind, first, count):
        at = pl.multiple_of(kind * width + target * columns + side * 128, 128)
        return n.w_qkv.at[lines(first, count), pl.ds(at, 128)]

    def qkv_place(side, kind, first, count):
        rows = lines(group_rank * columns + first, count)
        return n.qkv_held.at[rows, pl.ds((side * 3 + kind) * 128, 128)]

    qkv_loads = [
        load(qkv_piece(group_rank, *piece, 0, columns), qkv_place(*piece, 0, columns), 9 + i)
        for i, piece in enumerate(pieces)
    ]
    hidden_units = n.up_held.shape[1]

    def up_piece(target):
        return n.w_up.at[:, pl.ds(pl.multiple_of(target * hidden_units, 128), hidden_units)]

    up_place = n.up_held.at[lines(group_rank * columns, columns)]
    up_load = load(up_piece(group_rank), up_place, 15)

    def small_tables():
        down = lax.broadcasted_iota(jnp.int32, (8, 128), 0)
        across_lanes = lax.rem(lax.broadcasted_iota(jnp.int32, (8, 128), 1), 64)
        zero = jnp.zeros((8, 128), full)
        step_tile, start_tile, end_tile = zero, zero, zero
        start_lane, end_lane = zero + 1e9, zero
        start = jnp.int32(0)
        for u in range(8):
            end = start + n.lengths[0, u]
            here = down == u
            lane_here = (across_lanes == u) | (across_lanes == u + 8)
            step_tile = jnp.where(here, n.flow_steps[0, u].astype(full), step_tile)
            start_tile = jnp.where(here, start.astype(full), start_tile)
            end_tile = jnp.where(here, end.astype(full), end_tile)
            start_lane = jnp.where(lane_here, start.astype(full), start_lane)
            end_lane = jnp.where(lane_here, end.astype(full), end_lane)
            start = end
        tables = (step_tile, start_tile, end_tile, start_lane, end_lane)
        for i, tile in enumerate(tables):
            n.small[i] = tile
        n.small[5] = n.own_gain[:, 0:128]
        n.small[6] = n.own_gain[:, 128:256]

    barrier = pltpu.get_barrier_semaphore()
    for other in range(1, ROWS):
        pl.semaphore_signal(barrier, inc=1, device_id=(rank, group(other)), device_id_type=MESH)
    for other in range(1, RING):
        pl.semaphore_signal(barrier, inc=1, device_id=(block(other), group_rank), device_id_type=MESH)
    small_tables()
    for copy in joined_loads:
        copy.wait()
    pl.semaphore_wait(barrier, ROWS + RING - 2)

    joined_place = n.joined.at[lines(own_slot * frames, frames)]
    joined_sends = [
        push(n.joined_own.at[group(o)], joined_place, n.joined_sem, (o - 1,), (rank, group(o)))
        for o in (2, 1, 3)
    ]
    small_sends = [
        push(n.small, n.smalls.at[group_rank], n.small_sem, (o - 1,), (rank, group(o)))
        for o in (2, 1, 3)
    ]
    n.joined[lines(own_slot * frames, frames)] = n.joined_own[group_rank]
    n.smalls[group_rank] = n.small[...]
    for copy in small_sends:
        copy.wait_recv()

    steps = jnp.concatenate([n.smalls[(0, 2, 1, 3)[s], 0] for s in range(ROWS)], axis=0)
    steps = jnp.concatenate([steps, steps], axis=1)
    lane = lax.broadcasted_iota(jnp.int32, steps.shape, 1) + lax.rem(group_rank, 2) * columns
    rate = jnp.exp(-math.log(10000.0) * lane.astype(full) / (width // 2))
    angles = 1000.0 * (steps / STEPS) * rate
    turned = jnp.where(group_rank >= 2, jnp.cos(angles), jnp.sin(angles))
    n.condition[...] = (turned / (1.0 + jnp.exp(-turned))).astype(low)
    mod_load.wait()

    def mod_tile(at):
        where = pl.ds(at, 512)
        n.mod_part[:, where] = dot_plain(n.condition[...], n.mod_held[:, where])

    tiles(2 * width, 512, mod_tile)
    mod_first = push(
        n.mod_part.at[pl.ds(pl.multiple_of(16 * (1 - core), 16), 16)], n.mod_land.at[0], n.mod_sem, (0,), sibling
    )

    gains = [n.smalls[r, 5 + i][0:1] for r in range(ROWS) for i in range(2)]
    n.gain[...] = jnp.broadcast_to(jnp.concatenate(gains, axis=1), n.gain.shape)

    def picked(row, first, count):
        spot = (lax.broadcasted_iota(jnp.int32, (count, 128), 0) + first).astype(full)
        return (spot >= n.smalls[row, 3][0:1]) & (spot < n.smalls[row, 4][0:1]), spot

    lanes = lax.broadcasted_iota(jnp.int32, (frames, 128), 1)
    turn_rate = jnp.exp(-math.log(10000.0) * lax.rem(lanes, 32).astype(full) / 32)
    turn_sign = jnp.where(lax.rem(lanes, 64) < 32, -1.0, 1.0)

    def turn_tables(row, first, cosine, sine, at):
        chosen, spot = picked(row, first, frames)
        start = jnp.where(chosen & (lanes < 8), n.smalls[row, 3][0:1], 0.0)
        position = spot - jnp.sum(start, axis=1, keepdims=True)
        angle = position * turn_rate
        cosine[at] = jnp.cos(angle)
        sine[at] = jnp.sin(angle) * turn_sign

    def swapped(value):
        ahead = pltpu.roll(value, 96, 1)
        behind = pltpu.roll(value, 32, 1)
        return jnp.where(lax.rem(lanes, 64) < 32, ahead, behind)

    def partial_sum(index, left_ref, right_tile):
        def to_send(at):
            n.send_one[:, pl.ds(at, 256)] = right_tile(left_ref[lines(theirs, half)], at).astype(low)

        def to_keep(at):
            n.keep[:, pl.ds(at, 256)] = right_tile(left_ref[lines(mine, half)], at)

        if index > 0:
            for copy in group_copies[index - 1][0]:
                copy.wait_send()
        tiles(width, 256, to_send)
        first = [
            push(
                n.send_one.at[pl.ds(k * frames, frames)],
                n.land_one.at[index, pl.ds(k * frames, frames)],
                n.first_sem,
                (index, k),
                sibling,
            )
            for k in range(2)
        ]
        tiles(width, 256, to_keep)
        return first

    def cross_sum(index, first):
        if index > 0:
            for copy in group_copies[index - 1][1]:
                copy.wait_send()
        second = []
        for k in range(2):
            first[k].wait_recv()

            def add(at, k=k):
                where = pl.ds(k * frames + at, 32)
                total = n.keep[where] + n.land_one[index, where].astype(full)
                n.keep[where] = total
                n.send_two[where] = total.astype(low)

            tiles(frames, 32, add)
            second.append(
                push(
                    n.send_two.at[pl.ds(k * frames, frames)],
                    n.land_two.at[index, pl.ds(k * frames, frames)],
                    n.second_sem,
                    (index, k),
                    across,
                )
            )
        group_copies[index] = (first, second)
        return second

    group_copies = {}

    down_ring, up_ring, out_ring, qkv_ring, skip_ring = rings = [
        Ring(part, land, whole, sems, n.whole_sem.at[index], rank, group_rank, turn)
        for index, (part, land, whole, sems, turn) in enumerate(
            (
                (n.down_total, n.down_land, n.down_whole, n.down_sem, None),
                (n.up_total, n.up_land, n.up_whole, n.up_ring_sem, (n.up_turn, n.turn_sem.at[0])),
                (n.out_total, n.out_land, n.out_whole, n.out_ring_sem, None),
                (n.qkv_total, n.qkv_land, n.qkv_whole, n.qkv_ring_sem, (n.qkv_turn, n.turn_sem.at[1])),
                (n.skip_total, n.skip_land, n.skip_whole, n.skip_ring_sem, None),
            )
        )
    ]
    running = []

    def begin(ring):
        ring.begin()
        running.append(ring)

    def ticks(count):
        for _ in range(count):
            if running:
                ring = running.pop(0)
                ring.left.pop(0)()
                if ring.left:
                    running.append(ring)

    def mean(value):
        return jnp.mean(value, axis=-1, keepdims=True)

    def share(buffer, k, sems):
        where = lines(mine + k * frames, frames)
        return push(buffer.at[where], buffer.at[where], sems, (k,), sibling)

    skip_load.wait()
    for copy in joined_sends:
        copy.wait_recv()

    side_y, side_z = lax.rem(rank, 2), lax.rem(rank // 2, 2)
    to_y, to_z = 1 - 2 * side_y, 2 - 4 * side_z
    beside = (rank + to_y, group_rank)
    around = (beside, (rank + to_z, group_rank), (rank + to_y + to_z, group_rank))
    part_rows = columns // 2
    few_rows = columns // 4
    first_row = (2 * side_z + side_y) * few_rows
    over_x = (group_rank + 2 - 4 * chip, 2 * (1 - chip) + 1 - core)
    qkv_sends = [
        [
            push(
                qkv_piece(to, *piece, first_row, few_rows),
                qkv_place(*piece, first_row, few_rows),
                n.qkv_sem,
                (i, j),
                (rank, to),
            )
            for j, piece in enumerate(pieces)
        ]
        for i, to in enumerate(over_x)
    ]
    qkv_sends.append(
        [
            push(
                qkv_piece(sibling[1], *piece, 0, columns),
                qkv_place(*piece, 0, columns),
                n.qkv_sem,
                (2, j),
                sibling,
            )
            for j, piece in enumerate(pieces)
        ]
    )

    def skip_tile(left, at):
        return dot_plain(left, n.skip_held[:, pl.ds(at, 256)])

    first = partial_sum(0, n.joined, skip_tile)
    mod_first.wait_recv()
    mod_mine = n.mod_part[pl.ds(pl.multiple_of(16 * core, 16), 16)] + n.mod_land[0]
    n.mod_send[...] = mod_mine.astype(low)
    mod_second = push(n.mod_send, n.mod_cross, n.mod_sem, (1,), across)
    second = cross_sum(0, first)
    own_lines = lines(own_slot * frames, frames)
    for slot in range(ROWS):
        turn_tables(
            (0, 2, 1, 3)[slot],
            rank * frames,
            n.cosine,
            n.sine,
            pl.ds(slot * frames, frames),
        )
    mod_second.wait_recv()
    mod_total = n.mod_send[...].astype(full) + n.mod_cross[...].astype(full)
    for k in range(2):
        row = 2 * k + core
        values = mod_total[8 * k : 8 * k + 8]
        high = values.astype(low).astype(full)
        stack = jnp.concatenate([high, values - high], axis=0).astype(low)
        chosen = picked(row, rank * frames, frames)[0]
        picker = jnp.where(chosen, 1.0, 0.0).astype(low)[:, :16]
        where = pl.ds(k * frames, frames)
        n.scale_one[where] = 1.0 + dot_plain(picker, stack[:, :width])
        n.shift_one[where] = dot_plain(picker, stack[:, width:])

    qkv_passed = []
    for i, source in enumerate(over_x):
        for copy in qkv_sends[i]:
            copy.wait_recv()
        where = n.qkv_held.at[lines(source * columns + first_row, few_rows)]
        for j, to in enumerate(around):
            qkv_passed.append(push(where, where, n.qkv_pass_sem, (i, j), to))
    attn_sends = []
    for k in range(2):
        second[k].wait_recv()

        def norm_one(at, k=k):
            where = pl.ds(k * frames + at, 32)
            hidden = n.keep[where] + n.land_two[0, where].astype(full)
            n.hidden[where] = hidden
            centred = hidden - mean(hidden)
            spread = lax.rsqrt(mean(centred * centred) + EPSILON)
            normal = centred * spread
            n.normal_one[where] = normal
            n.spread_one[where] = jnp.broadcast_to(spread, (32, 128))
            n.attn_in[lines(mine + k * frames + at, 32)] = (
                normal * n.scale_one[where] + n.shift_one[where]
            ).astype(low)

        tiles(frames, 32, norm_one)
        attn_sends.append(share(n.attn_in, k, n.attn_sem))

    def part_of(reference, first):
        return reference.at[lines(first + side_y * part_rows, part_rows)]

    up_sends = [
        push(
            part_of(up_piece(to), 0),
            part_of(n.up_held, group_rank * columns),
            n.up_sem,
            (i,),
            (rank, to),
        )
        for i, to in enumerate(over_x)
    ]
    up_sends.append(push(up_piece(sibling[1]), up_place, n.up_sem, (2,), sibling))
    out_sends = [
        push(n.w_out, out_place, n.out_sem, (i,), device) for i, device in enumerate((across, sibling))
    ]

    def pass_on(buffer, copies, sems):
        passed = []
        for i, source in enumerate(over_x):
            copies[i].wait_recv()
            where = part_of(buffer, source * columns)
            passed.append(push(where, where, sems, (i,), beside))
        return passed

    upstream_load.wait()
    upstream_sends = [
        push(n.upstream.at[own_lines], n.upstream.at[own_lines], n.upstream_sem, (i,), device)
        for i, device in enumerate((across, sibling))
    ]

    for copy in qkv_loads:
        copy.wait()
    for copy in qkv_sends[2] + qkv_passed:
        copy.wait_recv()

    def to_heads(offset, value_of, target, sems, send_buffer, columns_of):
        for k in range(2):
            slot = offset // frames + k
            for side in range(2):
                to = 2 * row_of(slot) + side
                if value_of is not None:
                    send_buffer[to] = value_of(k, side, slot)

                @pl.when(to != rank)
                def _():
                    link(
                        send_buffer.at[to, :, columns_of],
                        target.at[lines(rank * frames, frames), columns_of],
                        sems.at[0, to],
                        sems.at[1, rank],
                        (to, group_rank),
                    ).start()

                @pl.when(to == rank)
                def _():
                    target[lines(rank * frames, frames), columns_of] = send_buffer[to, :, columns_of]

    def heads_arrive(target, sems, columns_of):
        for other in range(1, RING):
            source = block(other)
            where = target.at[lines(source * frames, frames), columns_of]
            link(where, where, sems.at[0, source], sems.at[1, source], (source, group_rank)).wait_recv()

    def project_half(offset):
        def project_tile(at):
            n.project[:, pl.ds(at, 256)] = dot_plain(
                n.attn_in[lines(offset, half)], n.qkv_held[:, pl.ds(at, 256)]
            )

        tiles(3 * columns, 256, project_tile)

        def value_of(k, side, slot):
            where = lines(slot * frames, frames)
            cosine, sine = n.cosine[where], n.sine[where]
            blocks = []
            for kind in range(3):
                value = n.project[pl.ds(k * frames, frames), pl.ds((side * 3 + kind) * 128, 128)]
                if kind < 2:
                    value = value * cosine + swapped(value) * sine
                blocks.append(value.astype(low))
            return jnp.concatenate(blocks, axis=1)

        to_heads(offset, value_of, n.paired, n.pair_sem, n.pair_send, pl.ds(0, 256))

    project_half(mine)
    for copy in attn_sends:
        copy.wait_recv()
    project_half(theirs)
    for offset in (mine, theirs):
        to_heads(offset, None, n.paired, n.value_sem, n.pair_send, pl.ds(256, 128))

    def row_tables(at):
        turn_tables(pair_row, at, n.row_cosine, n.row_sine, pl.ds(at, frames))
        chosen = jnp.where(picked(pair_row, at, frames)[0], 1.0, 0.0)
        n.chosen[pl.ds(at, frames)] = chosen.astype(low)

    tiles(RING * frames, frames, row_tables)
    heads_arrive(n.paired, n.pair_sem, pl.ds(0, 256))
    up_passed = pass_on(n.up_held, up_sends, n.up_pass_sem)
    out_sends[0].wait_recv()
    where = n.out_held.at[lines(across[1] * columns, columns)]
    out_sends.append(push(where, where, n.out_sem, (2,), sibling))

    def masked_parts(at):
        where = pl.ds(at, frames)
        query, key = n.paired[where, 0:128], n.paired[where, 128:256]
        chosen = n.chosen[where]
        first_head = lanes < 64
        blocked = jnp.where(
            lax.rem(lanes, 64) < 8, NEGATIVE * (1.0 - chosen.astype(full)), 0.0
        ).astype(low)
        scaled = (query.astype(full) * HEAD_DIM ** (-0.5)).astype(low)
        n.query_head[0, where] = jnp.where(first_head, scaled, chosen)
        n.query_head[1, where] = jnp.where(first_head, chosen, scaled)
        n.key_head[0, where] = jnp.where(first_head, key, blocked)
        n.key_head[1, where] = jnp.where(first_head, blocked, key)
        n.query_turned[:, where] = jnp.transpose(query.astype(full)).astype(low)

    tiles(RING * frames, frames, masked_parts)
    all_frames = RING * frames
    pair_place = (lines(slot_of(pair_row) * frames, frames), lines(pair_side * 128, 128))

    def score(at):
        where = pl.ds(at, half)
        for head in range(2):
            scores = dot_across(n.query_head[head, where], n.key_head[head])
            top = jnp.max(scores, axis=1, keepdims=True)
            weights = jnp.exp(scores - top)
            total = jnp.sum(weights, axis=1, keepdims=True)
            n.shares[head, where] = (weights * (1.0 / total)).astype(low)

    tiles(all_frames, half, score)
    heads_arrive(n.paired, n.value_sem, pl.ds(256, 128))

    def attend(at):
        where = pl.ds(at, half)
        sums = [dot_plain(n.shares[head, where], n.paired[:, 256:384]) for head in range(2)]
        first_head = lax.broadcasted_iota(jnp.int32, (half, 128), 1) < 64
        value = jnp.where(first_head, sums[0], sums[1])
        n.attended_pair[where] = value
        n.attended_send[where] = value.astype(low)
        for k in range(2):
            to = at // frames + k
            place = lines(at + k * frames, frames)

            @pl.when(to != rank)
            def _():
                link(
                    n.attended_send.at[place],
                    n.attended.at[pair_place],
                    n.attended_sem.at[0, to],
                    n.attended_sem.at[1, rank],
                    (to, group_rank),
                ).start()

            @pl.when(to == rank)
            def _():
                n.attended[pair_place] = n.attended_send[place]

    tiles(all_frames, half, attend)

    def pairs_arrive(buffer, sems, pitch, first, wide):
        for other in range(1, RING):
            source = block(other)
            where = buffer.at[
                lines(slot_of(source // 2) * frames, frames),
                pl.ds(pl.multiple_of(lax.rem(source, 2) * pitch + first, 128), wide),
            ]
            link(where, where, sems.at[0, source], sems.at[1, source], (source, group_rank)).wait_recv()

    upstream_sends[0].wait_recv()
    other_lines = lines((2 * core + 1 - chip) * frames, frames)
    upstream_sends.append(
        push(n.upstream.at[other_lines], n.upstream.at[other_lines], n.upstream_sem, (2,), sibling)
    )
    pairs_arrive(n.attended, n.attended_sem, 128, 0, 128)

    own_columns = pl.ds(pl.multiple_of(group_rank * columns, columns), columns)
    attended_sends = [
        push(
            n.attended.at[lines(first, half)],
            n.attended_all.at[:, own_columns],
            n.attended_all_sem,
            (i,),
            (rank, to),
        )
        for i, (first, to) in enumerate(
            ((mine, over_x[0]), (theirs, over_x[1]), (theirs, sibling[1]))
        )
    ]
    n.attended_all[:, own_columns] = n.attended[lines(mine, half)]
    out_load.wait()
    for copy in out_sends[1:] + attended_sends:
        copy.wait_recv()

    def out_tile(at):
        n.keep[:, pl.ds(at, 256)] = dot_plain(n.attended_all[...], n.out_held[:, pl.ds(at, 256)])

    tiles(width, 256, out_tile)
    ff_sends = []
    for k in range(2):

        def norm_two(at, k=k):
            where = pl.ds(k * frames + at, 32)
            hidden = n.hidden[where] + n.keep[where]
            n.hidden[where] = hidden
            centred = hidden - mean(hidden)
            spread = lax.rsqrt(mean(centred * centred) + EPSILON)
            normal = centred * spread
            n.normal_two[where] = normal
            n.spread_two[where] = jnp.broadcast_to(spread, (32, 128))
            n.ff_in[lines(mine + k * frames + at, 32)] = (normal * n.gain[0:1]).astype(low)

        tiles(frames, 32, norm_two)
        ff_sends.append(share(n.ff_in, k, n.ff_sem))

    up_load.wait()
    down_load.wait()
    for copy in up_sends[2:] + up_passed:
        copy.wait_recv()
    for copy in upstream_sends[1:]:
        copy.wait_recv()

    def feed_half(offset):
        where = lines(offset, half)

        def feed_tile(at):
            widened = dot_plain(n.ff_in[where], n.up_held[:, pl.ds(at, 256)])
            grad = dot_across(n.upstream[where], n.down_held[pl.ds(at, 256)])
            share_of = 0.5 * (1.0 + lax.erf(widened * math.sqrt(0.5)))
            slope = share_of + widened * jnp.exp(-0.5 * widened * widened) * (
                1.0 / math.sqrt(2.0 * math.pi)
            )
            n.activated[where, pl.ds(at, 256)] = (widened * share_of).astype(low)
            n.grad_widened[where, pl.ds(at, 256)] = (grad * slope).astype(low)

        tiles(hidden_units, 256, feed_tile)

    feed_half(mine)
    for copy in ff_sends:
        copy.wait_recv()
    feed_half(theirs)
    first = partial_sum(
        1, n.grad_widened, lambda left, at: dot_across(left, n.up_held[pl.ds(at, 256)])
    )
    second = cross_sum(1, first)

    def down_tile(at):
        value = contract_rows(n.activated[:, pl.ds(at, 256)], n.upstream[...]).astype(low)
        n.down_total[at // 128] = value[:128]
        n.down_total[at // 128 + 1] = value[128:]

    tiles(hidden_units, 256, down_tile)
    begin(down_ring)

    def up_tile(at):
        value = contract_rows(n.ff_in[:, pl.ds(at, columns)], n.grad_widened[...]).astype(low)
        deep = columns // RING
        for j in range(RING):
            n.up_total[j, pl.ds(pl.multiple_of(at // RING, deep), deep)] = value[
                j * deep : (j + 1) * deep
            ]

    tiles(width, columns, up_tile)
    begin(up_ring)
    ticks(TICKS[0])

    gain_sums = jnp.zeros((1, width), full)
    grad_sends = []
    for k in range(2):
        second[k].wait_recv()
        weight = (1 - jnp.abs(chip - k)).astype(full)

        def back_two(i, sums, k=k, weight=weight):
            at = pl.multiple_of(i * 32, 32)
            where = pl.ds(k * frames + at, 32)
            grad = n.keep[where] + n.land_two[1, where].astype(full)
            normal = n.normal_two[where]
            scaled = grad * n.gain[0:1]
            back = n.spread_two[where][:, 0:1] * (
                scaled - mean(scaled) - normal * mean(scaled * normal)
            )
            total = n.upstream[lines(mine + k * frames + at, 32)].astype(full) + back
            n.grad_two[where] = total
            n.grad_two_low[lines(mine + k * frames + at, 32)] = total.astype(low)
            return sums + weight * jnp.sum(grad * normal, axis=0, keepdims=True)

        gain_sums = lax.fori_loop(0, frames // 32, back_two, gain_sums)
        grad_sends.append(share(n.grad_two_low, k, n.grad_two_sem))
        ticks(TICKS[1 + k])
    n.mod_sums[8:16] = jnp.zeros((8, 2 * width), full)
    n.mod_sums[8:9, :width] = gain_sums

    def attended_half(offset):
        value = dot_across(
            n.grad_two_low[lines(offset, half)], n.out_held[lines(group_rank * columns, columns)]
        ).astype(low)

        def value_of(k, side, slot):
            return value[k * frames : (k + 1) * frames, side * 128 : side * 128 + 128]

        to_heads(
            offset, value_of, n.grad_pair, n.grad_pair_sem, n.grad_pair_send, pl.ds(0, 128)
        )

    attended_half(mine)
    ticks(TICKS[3])
    for copy in grad_sends:
        copy.wait_recv()
    attended_half(theirs)
    ticks(TICKS[4])
    value = contract_rows(n.attended[...], n.grad_two_low[...]).astype(low)
    for j in range(RING):
        n.out_total[j] = value[j * 32 : (j + 1) * 32]
    begin(out_ring)
    ticks(TICKS[5])

    first = partial_sum(2, n.activated, lambda left, at: dot_plain(left, n.down_held[:, pl.ds(at, 256)]))
    ticks(TICKS[6])
    output_second = cross_sum(2, first)
    ticks(TICKS[7])

    heads_arrive(n.grad_pair, n.grad_pair_sem, pl.ds(0, 128))

    def turn_upstream(at):
        where = pl.ds(at, frames)
        n.grad_turned[:, where] = jnp.transpose(n.grad_pair[where].astype(full)).astype(low)

    tiles(all_frames, frames, turn_upstream)
    n.key_turned[...] = jnp.zeros(n.key_turned.shape, full)
    n.value_turned[...] = jnp.zeros(n.value_turned.shape, full)

    def back_turned(value, where):
        return value * n.row_cosine[where] - swapped(value) * n.row_sine[where]

    project_slot = lines(slot_of(pair_row) * frames, frames)

    def project_back(to, place, first, wide, sems):
        source = n.project_send.at[place, pl.ds(first, wide)]
        at = pl.ds(pl.multiple_of(pair_side * 384 + first, 128), wide)

        @pl.when(to != rank)
        def _():
            target = n.grad_project.at[project_slot, at]
            link(source, target, sems.at[0, to], sems.at[1, rank], (to, group_rank)).start()

        @pl.when(to == rank)
        def _():
            n.grad_project[project_slot, at] = source[...]

    def attend_back(at):
        where = pl.ds(at, half)
        first_head = lax.broadcasted_iota(jnp.int32, (half, 128), 1) < 64
        grad = n.grad_pair[where]
        product = grad.astype(full) * n.attended_pair[where]
        terms = []
        for head in range(2):
            here = first_head if head == 0 else jnp.logical_not(first_head)
            delta = jnp.sum(jnp.where(here, product, 0.0), axis=1, keepdims=True)
            grad_head = jnp.where(here, grad, jnp.zeros_like(grad))
            prob_grad = dot_across(grad_head, n.paired[:, 256:384])
            shares = n.shares[head, where]
            score_grad = (shares.astype(full) * (prob_grad - delta)).astype(low)
            terms.append(dot_plain(score_grad, n.paired[:, 128:256]))
            rows = pl.ds(head * 64, 64)
            n.value_turned[rows] += dot_plain(n.grad_turned[rows, where], shares)
            n.key_turned[rows] += dot_plain(n.query_turned[rows, where], score_grad)
        query_grad = jnp.where(first_head, terms[0], terms[1]) * HEAD_DIM ** (-0.5)
        for k in range(2):
            place = lines(at + k * frames, frames)
            n.project_send[place, 0:128] = back_turned(
                query_grad[k * frames : (k + 1) * frames], place
            ).astype(low)
            project_back(at // frames + k, place, 0, 128, n.query_sem)

    for part in range(4):
        attend_back(part * half)
        ticks(TICKS[8 + part])
    def keys_back(at):
        place = pl.ds(at, frames)
        key_grad = jnp.transpose(n.key_turned[:, place]) * HEAD_DIM ** (-0.5)
        n.project_send[place, 128:256] = back_turned(key_grad, place).astype(low)
        n.project_send[place, 256:384] = jnp.transpose(n.value_turned[:, place]).astype(low)
        project_back(at // frames, place, 128, 256, n.project_sem)

    tiles(all_frames, frames, keys_back)

    ticks(TICKS[12])

    for copy in output_second:
        copy.wait_recv()

    def finish_output(at):
        where = lines(chip * frames + at, 32)
        n.output[pl.ds(at, 32)] = (
            n.hidden[where] + n.keep[where] + n.land_two[2, where].astype(full)
        ).astype(low)

    tiles(frames, 32, finish_output)
    ticks(TICKS[13])
    pairs_arrive(n.grad_project, n.query_sem, 384, 0, 128)
    pairs_arrive(n.grad_project, n.project_sem, 384, 128, 256)

    first = partial_sum(
        3, n.grad_project, lambda left, at: dot_across(left, n.qkv_held[pl.ds(at, 256)])
    )
    ticks(TICKS[14])
    second = cross_sum(3, first)
    ticks(TICKS[15])

    def qkv_tile(at):
        value = contract_rows(n.attn_in[:, pl.ds(at, columns)], n.grad_project[...]).astype(low)
        deep = columns // RING
        for j in range(RING):
            n.qkv_total[j, pl.ds(pl.multiple_of(at // RING, deep), deep)] = value[
                j * deep : (j + 1) * deep
            ]

    tiles(width, columns, qkv_tile)
    begin(qkv_ring)
    ticks(TICKS[16])
    hidden_sends = []
    for k in range(2):
        second[k].wait_recv()

        def back_one(at, k=k):
            where = pl.ds(k * frames + at, 32)
            grad = n.keep[where] + n.land_two[3, where].astype(full)
            normal = n.normal_one[where]
            scaled = grad * n.scale_one[where]
            back = n.spread_one[where][:, 0:1] * (
                scaled - mean(scaled) - normal * mean(scaled * normal)
            )
            n.grad_hidden[lines(mine + k * frames + at, 32)] = (n.grad_two[where] + back).astype(low)

            @pl.when(chip == k)
            def _():
                n.shift_one[pl.ds(at, 32)] = grad * normal
                n.shift_one[pl.ds(frames + at, 32)] = grad

        tiles(frames, 32, back_one)
        hidden_sends.append(share(n.grad_hidden, k, n.grad_hidden_sem))
        ticks(TICKS[17 + k])

    for copy in hidden_sends:
        copy.wait_recv()

    def skip_weight_tile(at):
        value = contract_rows(n.joined[:, pl.ds(at, 256)], n.grad_hidden[...]).astype(low)
        for j in range(4):
            n.skip_total[at // 64 + j] = value[j * 64 : (j + 1) * 64]

    tiles(n.joined.shape[1], 256, skip_weight_tile)
    begin(skip_ring)
    ticks(TICKS[19])
    spot = (lax.broadcasted_iota(jnp.int32, (8, frames), 1) + rank * frames).astype(full)
    chosen = (spot >= n.small[1]) & (spot < n.small[2])
    picker = jnp.where(chosen, 1.0, 0.0)

    def mod_sum(at):
        for part in range(2):
            n.mod_sums[0:8, pl.ds(part * width + at, 512)] = jnp.dot(
                picker, n.shift_one[pl.ds(part * frames, frames), pl.ds(at, 512)], precision=HIGHEST
            )

    tiles(width, 512, mod_sum)
    for other in range(1, RING):
        to = block(other)
        push(
            n.mod_sums.at[:, pl.ds(pl.multiple_of(to * 256, 256), 256)],
            n.sums_land.at[rank],
            n.sums_sem,
            (other - 1,),
            (to, group_rank),
        )
    sums_copies = sent[-(RING - 1) :]
    n.sums_land[rank] = n.mod_sums[:, pl.ds(pl.multiple_of(rank * 256, 256), 256)]
    ticks(TICKS[20])
    back = dot_across(n.grad_hidden[...], n.skip_held[...]).astype(low)
    n.joined_send[...] = back
    grad_joined_copies = []
    for other in (2, 1, 3):
        to = group(other)
        grad_joined_copies.append(
            push(
                n.joined_send.at[lines(slot_of(to) * frames, frames)],
                n.grad_joined.at[group_rank],
                n.grad_joined_sem,
                (other - 1,),
                (rank, to),
            )
        )
    n.grad_joined[group_rank] = n.joined_send[own_lines]
    ticks(TICKS[21])
    for copy in sums_copies:
        copy.wait_recv()
    n.sums_send[...] = jnp.sum(n.sums_land[...], axis=0).astype(low)
    n.mod_grad[rank, group_rank] = n.sums_send[...]
    group_sums = [
        push(
            n.sums_send,
            n.mod_grad.at[rank, group_rank],
            n.sums_group_sem,
            (other - 1,),
            (rank, group(other)),
        )
        for other in (2, 1, 3)
    ]
    ticks(TICKS[22])
    for copy in group_sums:
        copy.wait_recv()
    mod_spread = [
        push(
            n.mod_grad.at[rank],
            n.mod_grad.at[rank],
            n.sums_block_sem,
            (other - 1,),
            (block(other), group_rank),
        )
        for other in range(1, RING)
    ]

    ticks(5 * (2 * RING + 1))
    for ring in rings:
        ring.finish()
    for copy in mod_spread + grad_joined_copies:
        copy.wait_recv()
    gain_grad = n.mod_grad[group_rank, 0].astype(full)
    for row in range(1, ROWS):
        gain_grad = gain_grad + n.mod_grad[group_rank, row].astype(full)
    n.gain_grad[...] = gain_grad[8:16]
    for index, copy in enumerate(sent):
        if not any(copy is other for pair in list(group_copies.values())[:-1] for kind in pair for other in kind):
            copy.wait_send()
    for sems, wide in (
        (n.pair_sem, 256),
        (n.value_sem, 128),
        (n.attended_sem, 128),
        (n.grad_pair_sem, 128),
        (n.query_sem, 128),
        (n.project_sem, 256),
    ):
        for other in range(1, RING):
            to = block(other)
            where = n.project_send.at[lines(to * frames, frames), pl.ds(0, wide)]
            link(where, where, sems.at[0, to], sems.at[1, to], (to, group_rank)).wait_send()


def block_call(
    inputs,
    skipped,
    w_skip,
    w_mod,
    w_qkv,
    w_out,
    w_up,
    w_down,
    cotangent,
    own_gain,
    lengths,
    flow_steps,
):
    low, full = jnp.bfloat16, jnp.float32
    frames, width = inputs.shape
    tokens, half = ROWS * frames, 2 * frames
    columns = width // ROWS
    hidden_units = w_down.shape[0]
    joint = w_skip.shape[0]
    all_frames = RING * frames
    deep = width // RING

    held = dict(
        inputs=inputs,
        skipped=skipped,
        w_skip=w_skip,
        w_mod=w_mod,
        w_qkv=w_qkv,
        w_out=w_out,
        w_up=w_up,
        w_down=w_down,
        cotangent=cotangent,
        own_gain=own_gain,
        lengths=lengths,
        flow_steps=flow_steps,
    )
    given = dict(
        output=((frames, width), low),
        grad_joined=((ROWS, frames, joint), low),
        condition=((ROWS * 8, columns), low),
        mod_grad=((RING, ROWS, 16, 256), low),
        gain_grad=((8, columns), full),
        down_whole=((RING, hidden_units // RING, width), low),
        up_whole=((RING, deep, hidden_units), low),
        qkv_whole=((RING, deep, 3 * columns), low),
        skip_whole=((RING, joint // RING, width), low),
        out_whole=((RING, columns // RING, width), low),
    )
    buffers = dict(
        joined_own=((ROWS, frames, joint), low),
        joined=((tokens, joint), low),
        upstream=((tokens, width), low),
        skip_held=(w_skip.shape, low),
        mod_held=(w_mod.shape, low),
        out_held=((width, width), low),
        attended_all=((half, width), low),
        down_held=(w_down.shape, low),
        qkv_held=((width, 3 * columns), low),
        up_held=((width, hidden_units), low),
        small=((7, 8, 128), full),
        smalls=((ROWS, 7, 8, 128), full),
        mod_part=((ROWS * 8, 2 * width), full),
        mod_land=((1, 16, 2 * width), full),
        mod_send=((16, 2 * width), low),
        mod_cross=((16, 2 * width), low),
        gain=((8, width), full),
        cosine=((tokens, 128), full),
        sine=((tokens, 128), full),
        row_cosine=((all_frames, 128), full),
        row_sine=((all_frames, 128), full),
        chosen=((all_frames, 128), low),
        send_one=((half, width), low),
        send_two=((half, width), low),
        keep=((half, width), full),
        land_one=((4, half, width), low),
        land_two=((4, half, width), low),
        scale_one=((half, width), full),
        shift_one=((half, width), full),
        hidden=((half, width), full),
        normal_one=((half, width), full),
        spread_one=((half, 128), full),
        normal_two=((half, width), full),
        spread_two=((half, 128), full),
        grad_two=((half, width), full),
        attn_in=((tokens, width), low),
        project=((half, 3 * columns), full),
        pair_send=((RING, frames, 384), low),
        paired=((all_frames, 384), low),
        query_head=((2, all_frames, 128), low),
        key_head=((2, all_frames, 128), low),
        query_turned=((128, all_frames), low),
        shares=((2, all_frames, all_frames), low),
        attended_pair=((all_frames, 128), full),
        attended_send=((all_frames, 128), low),
        attended=((tokens, columns), low),
        ff_in=((tokens, width), low),
        activated=((tokens, hidden_units), low),
        grad_widened=((tokens, hidden_units), low),
        grad_two_low=((tokens, width), low),
        grad_pair_send=((RING, frames, 128), low),
        grad_pair=((all_frames, 128), low),
        grad_turned=((128, all_frames), low),
        key_turned=((128, all_frames), full),
        value_turned=((128, all_frames), full),
        project_send=((all_frames, 384), low),
        grad_project=((tokens, 3 * columns), low),
        grad_hidden=((tokens, width), low),
        mod_sums=((16, 2 * width), full),
        sums_land=((RING, 16, 256), full),
        sums_send=((16, 256), low),
        joined_send=((tokens, joint), low),
        down_total=((RING, hidden_units // RING, width), low),
        up_total=((RING, deep, hidden_units), low),
        qkv_total=((RING, deep, 3 * columns), low),
        skip_total=((RING, joint // RING, width), low),
        out_total=((RING, columns // RING, width), low),
        down_land=((RING - 1, hidden_units // RING, width), low),
        up_land=((RING - 1, deep, hidden_units), low),
        qkv_land=((RING - 1, deep, 3 * columns), low),
        skip_land=((RING - 1, joint // RING, width), low),
        out_land=((RING - 1, columns // RING, width), low),
        up_turn=((deep, hidden_units), low),
        qkv_turn=((deep, 3 * columns), low),
    )
    sems = dict(
        load_sem=(16,),
        joined_sem=(2, 3),
        small_sem=(2, 3),
        qkv_sem=(2, 3, 6),
        qkv_pass_sem=(2, 2, 3),
        up_sem=(2, 3),
        up_pass_sem=(2, 2),
        out_sem=(2, 3),
        attended_all_sem=(2, 3),
        mod_sem=(2, 2),
        first_sem=(2, 4, 2),
        second_sem=(2, 4, 2),
        upstream_sem=(2, 3),
        attn_sem=(2, 2),
        ff_sem=(2, 2),
        grad_two_sem=(2, 2),
        grad_hidden_sem=(2, 2),
        pair_sem=(2, RING),
        attended_sem=(2, RING),
        grad_pair_sem=(2, RING),
        query_sem=(2, RING),
        project_sem=(2, RING),
        value_sem=(2, RING),
        grad_joined_sem=(2, 3),
        sums_sem=(2, RING - 1),
        sums_group_sem=(2, 3),
        sums_block_sem=(2, RING - 1),
        down_sem=(2, 2, 2, RING - 1),
        up_ring_sem=(2, 2, 2, RING - 1),
        qkv_ring_sem=(2, 2, 2, RING - 1),
        skip_ring_sem=(2, 2, 2, RING - 1),
        out_ring_sem=(2, 2, 2, RING - 1),
        turn_sem=(2, 2, 3),
        whole_sem=(5, 2, RING),
    )
    names = [*held, *given, *buffers, *sems]
    vmem = pl.BlockSpec(memory_space=pltpu.VMEM)
    anywhere = pl.BlockSpec(memory_space=pl.ANY)
    return pl.pallas_call(
        functools.partial(block_kernel, names),
        out_shape=[jax.ShapeDtypeStruct(*spec) for spec in given.values()],
        in_specs=[anywhere] * 9 + [vmem] + [pl.BlockSpec(memory_space=pltpu.SMEM)] * 2,
        out_specs=[anywhere if name.endswith("_whole") else vmem for name in given],
        scratch_shapes=[pltpu.VMEM(*spec) for spec in buffers.values()]
        + [pltpu.SemaphoreType.DMA(shape) for shape in sems.values()],
        compiler_params=pltpu.CompilerParams(
            collective_id=0, has_side_effects=True, vmem_limit_bytes=63 * 1024 * 1024
        ),
    )(*held.values())


def finish_kernel(
    joined_ref,
    condition_ref,
    mod_ref,
    gain_ref,
    down_ref,
    up_ref,
    qkv_ref,
    skip_ref,
    out_ref,
    grad_inputs,
    grad_skipped,
    grad_skip,
    grad_mod,
    grad_qkv,
    grad_out,
    grad_gain,
    grad_up,
    grad_down,
):
    full = jnp.float32
    wide = joined_ref.shape[2]
    for r in range(ROWS):
        target = (grad_inputs, grad_skipped)[r // 2]
        target[:, pl.ds((r % 2) * wide, wide)] = joined_ref[r].astype(full)
    grad_down[...] = down_ref[0].astype(full)
    grad_skip[...] = skip_ref[0].astype(full)
    grad_out[...] = out_ref[0].astype(full)
    grad_gain[...] = gain_ref[0:1]
    deep, wide = up_ref.shape[1] // ROWS, up_ref.shape[2]
    for r in range(ROWS):
        rows = pl.ds(r * deep, deep)
        grad_up[:, pl.ds(r * wide, wide)] = up_ref[0, rows].astype(full)
        for side in range(2):
            for kind in range(3):
                source = qkv_ref[0, rows, pl.ds((side * 3 + kind) * 128, 128)]
                at = kind * (ROWS * 256) + r * 256 + side * 128
                grad_qkv[:, pl.ds(at, 128)] = source.astype(full)
    sums = [mod_ref[0, r].astype(full)[0:8] for r in (0, 2, 1, 3)]
    grad_mod[...] = contract_rows(
        condition_ref[...], jnp.concatenate(sums, axis=0).astype(jnp.bfloat16)
    )


def finish_call(joined, condition, mod, gain, down, up, qkv, skip, out):
    full = jnp.float32
    frames, wide = joined.shape[1:]
    columns = condition.shape[1]

    def first(shape):
        return pl.BlockSpec((1,) + shape[1:], lambda i: (i,) + (0,) * (len(shape) - 1))

    def rows(count, width):
        return jax.ShapeDtypeStruct((count, width), full), pl.BlockSpec(
            (count // RING, width), lambda i: (i, 0)
        )

    deep = up.shape[1] // ROWS
    results = [
        rows(frames, 2 * wide),
        rows(frames, 2 * wide),
        rows(RING * skip.shape[1], skip.shape[2]),
        (
            jax.ShapeDtypeStruct((columns, RING * mod.shape[3]), full),
            pl.BlockSpec((columns, mod.shape[3]), lambda i: (0, i)),
        ),
        rows(RING * deep, ROWS * qkv.shape[2]),
        rows(RING * out.shape[1], out.shape[2]),
        (jax.ShapeDtypeStruct((1, columns), full), pl.BlockSpec((1, columns), lambda i: (0, 0))),
        rows(RING * deep, ROWS * up.shape[2]),
        rows(RING * down.shape[1], down.shape[2]),
    ]
    return pl.pallas_call(
        finish_kernel,
        grid=(RING,),
        out_shape=[shape for shape, _ in results],
        in_specs=[
            pl.BlockSpec((ROWS, frames // RING, wide), lambda i: (0, i, 0)),
            pl.BlockSpec(condition.shape, lambda i: (0, 0)),
            first(mod.shape),
            pl.BlockSpec(gain.shape, lambda i: (0, 0)),
            first(down.shape),
            first(up.shape),
            first(qkv.shape),
            first(skip.shape),
            first(out.shape),
        ],
        out_specs=[spec for _, spec in results],
        compiler_params=pltpu.CompilerParams(vmem_limit_bytes=62 * 1024 * 1024),
    )(joined, condition, mod, gain, down, up, qkv, skip, out)


def per_device_block(
    inputs,
    skipped,
    w_skip,
    w_mod,
    w_qkv,
    w_out,
    ff_gain,
    w_up,
    w_down,
    cotangent,
    lengths,
    flow_steps,
):
    gain = jnp.broadcast_to(ff_gain.astype(jnp.float32)[None], (8, ff_gain.shape[0]))
    output, *rest = block_call(
        inputs[0],
        skipped[0],
        w_skip,
        w_mod,
        w_qkv,
        w_out,
        w_up,
        w_down,
        cotangent[0],
        gain,
        lengths,
        flow_steps,
    )
    grad_inputs, grad_skipped, skip, mod, qkv, out, gain, up, down = finish_call(*rest)
    return (
        output[None],
        grad_inputs[None],
        grad_skipped[None],
        skip,
        mod,
        qkv,
        out,
        gain[0],
        up,
        down,
    )


def solution(mesh):
    placed = (
        P("grp", "blk", None),
        P("grp", "blk", None),
        P("grp", None),
        P("grp", None),
        P("grp", None),
        P("grp", None),
        P("grp"),
        P("grp", None),
        P("grp", None),
        P("grp", "blk", None),
        P("grp", None),
        P("grp", None),
    )
    body = per_device
    if mesh.shape["blk"] == RING and mesh.shape["grp"] == ROWS:
        body = per_device_block
    return jax.shard_map(
        body,
        mesh=mesh,
        in_specs=placed,
        out_specs=(
            P("grp", "blk", None),
            P("grp", "blk", None),
            P("grp", "blk", None),
            P("grp", None),
            P("grp", None),
            P("grp", None),
            P("grp", None),
            P("grp"),
            P("grp", None),
            P("grp", None),
        ),
        check_vma=False,
    )
```

```python
import functools
import math
import types

import jax
import jax.numpy as jnp
from jax import lax
from jax.experimental import pallas as pl
from jax.experimental.pallas import tpu as pltpu
from jax.sharding import PartitionSpec as P

HEADS = 16
HEAD_DIM = 64
STEPS = 32


EPSILON = 1e-06
NEGATIVE = -1e30
HIGHEST = lax.Precision.HIGHEST
MESH = pl.DeviceIdType.MESH
RING = 8
ROWS = 4


def from_behind(block, axis, distance):
    devices = range(lax.axis_size(axis))
    route = [((i - distance) % len(devices), i) for i in devices]
    return lax.ppermute(block, axis, route)


def layout(lengths_row, frames):
    end_frame = jnp.cumsum(lengths_row)
    start_frame = end_frame - lengths_row
    segment = jnp.sum((frames[:, None] >= end_frame[None, :]).astype(jnp.int32), axis=1)
    chosen = segment[:, None] == jnp.arange(lengths_row.shape[0], dtype=jnp.int32)[None, :]
    position = frames - jnp.sum(jnp.where(chosen, start_frame[None, :], 0), axis=1)
    return (segment, position)


def flow_condition(steps_row, model_width):
    half_width = model_width // 2
    rate_table = jnp.exp(
        -math.log(10000.0) * jnp.arange(half_width, dtype=jnp.float32) / half_width
    )
    angles = 1000.0 * (steps_row.astype(jnp.float32) / STEPS)[:, None] * rate_table[None, :]
    return jax.nn.silu(jnp.concatenate([jnp.sin(angles), jnp.cos(angles)], axis=1))


def rotation_tables(position, head_width):
    half_width = head_width // 2
    rate_table = jnp.exp(
        -math.log(10000.0) * jnp.arange(half_width, dtype=jnp.float32) / half_width
    )
    angles = position.astype(jnp.float32)[:, None] * rate_table[None, :]
    return (jnp.cos(angles)[:, None, :], jnp.sin(angles)[:, None, :], half_width)


def rotate(head_block, position):
    cosine_part, sine_part, half_width = rotation_tables(position, head_block.shape[-1])
    first_half = head_block[..., :half_width]
    second_half = head_block[..., half_width:]
    return jnp.concatenate(
        [
            first_half * cosine_part - second_half * sine_part,
            second_half * cosine_part + first_half * sine_part,
        ],
        axis=-1,
    )


def rotate_back(head_block, position):
    cosine_part, sine_part, half_width = rotation_tables(position, head_block.shape[-1])
    first_half = head_block[..., :half_width]
    second_half = head_block[..., half_width:]
    return jnp.concatenate(
        [
            first_half * cosine_part + second_half * sine_part,
            second_half * cosine_part - first_half * sine_part,
        ],
        axis=-1,
    )


def normalize(hidden):
    centred = hidden - jnp.mean(hidden, axis=-1, keepdims=True)
    scaled = lax.rsqrt(jnp.mean(centred * centred, axis=-1, keepdims=True) + EPSILON)
    return (centred * scaled, scaled)


def norm_back(grad_normal, normal, scaled):
    centred_grad = grad_normal - jnp.mean(grad_normal, axis=-1, keepdims=True)
    return scaled * (centred_grad - normal * jnp.mean(grad_normal * normal, axis=-1, keepdims=True))


def exact_gelu(values_in):
    return jax.nn.gelu(values_in, approximate=False)


def contract_rows(left_side, right_side):
    return lax.dot_general(
        left_side, right_side, (((0,), (0,)), ((), ())), preferred_element_type=jnp.float32
    )


def heads_of(flat_block):
    return flat_block.reshape(flat_block.shape[0], HEADS, HEAD_DIM)


def per_device(
    inputs,
    skipped,
    w_skip,
    w_mod,
    w_qkv,
    w_out,
    ff_gain,
    w_up,
    w_down,
    cotangent,
    lengths,
    flow_steps,
):
    w_skip, w_mod, w_qkv, w_out, ff_gain, w_up, w_down = (
        lax.all_gather(w_skip, "grp", axis=0, tiled=True),
        lax.all_gather(w_mod, "grp", axis=0, tiled=True),
        lax.all_gather(w_qkv, "grp", axis=0, tiled=True),
        lax.all_gather(w_out, "grp", axis=0, tiled=True),
        lax.all_gather(ff_gain, "grp", axis=0, tiled=True),
        lax.all_gather(w_up, "grp", axis=0, tiled=True),
        lax.all_gather(w_down, "grp", axis=0, tiled=True),
    )
    frame_count = inputs.shape[1]
    model_width = inputs.shape[2]
    cycle_size = lax.axis_size("blk")
    device_rank = lax.axis_index("blk")
    score_scale = HEAD_DIM ** (-0.5)
    local_frames = jnp.arange(frame_count, dtype=jnp.int32)
    lengths_row = lengths[0]
    own_segment, own_position = layout(lengths_row, device_rank * frame_count + local_frames)

    def segment_of(source):
        return layout(lengths_row, source * frame_count + local_frames)[0]

    def scored(query_block, key_block, query_segment, key_segment):
        raw_scores = (
            jnp.einsum(
                "qhd,khd->hqk",
                heads_of(query_block),
                heads_of(key_block),
                preferred_element_type=jnp.float32,
            )
            * score_scale
        )
        allowed = (query_segment[:, None] == key_segment[None, :])[None]
        return (raw_scores, allowed)

    joined = jnp.concatenate([inputs[0], skipped[0]], axis=1)
    hidden = jnp.dot(joined, w_skip, preferred_element_type=jnp.float32)
    condition = flow_condition(flow_steps[0], model_width).astype(jnp.bfloat16)
    modulation = jnp.dot(condition, w_mod, preferred_element_type=jnp.float32)
    picker = (
        own_segment[:, None] == jnp.arange(lengths_row.shape[0], dtype=jnp.int32)[None, :]
    ).astype(jnp.float32)
    per_frame = jnp.dot(picker, modulation, precision=HIGHEST)
    scale_one = 1.0 + per_frame[:, :model_width]
    normal_one, spread_one = normalize(hidden)
    attn_in = (normal_one * scale_one + per_frame[:, model_width:]).astype(jnp.bfloat16)
    project = jnp.dot(attn_in, w_qkv, preferred_element_type=jnp.float32).reshape(
        frame_count, 3, HEADS, HEAD_DIM
    )
    queries = (
        rotate(project[:, 0], own_position).astype(jnp.bfloat16).reshape(frame_count, model_width)
    )
    keys_own = (
        rotate(project[:, 1], own_position).astype(jnp.bfloat16).reshape(frame_count, model_width)
    )
    values_own = project[:, 2].astype(jnp.bfloat16).reshape(frame_count, model_width)

    def forward_turn(turn_index, carried):
        key_now, value_now, running_top, running_total, running_sum = carried
        source = (device_rank - turn_index) % cycle_size
        raw_scores, allowed = scored(queries, key_now, own_segment, segment_of(source))
        raw_scores = jnp.where(allowed, raw_scores, NEGATIVE)
        new_top = jnp.maximum(running_top, jnp.max(raw_scores, axis=2, keepdims=True))
        weights = jnp.where(allowed, jnp.exp(raw_scores - new_top), 0.0)
        shrink = jnp.exp(running_top - new_top)
        running_total = running_total * shrink + jnp.sum(weights, axis=2, keepdims=True)
        running_sum = running_sum * shrink + jnp.einsum(
            "hqk,khd->hqd",
            weights.astype(jnp.bfloat16),
            heads_of(value_now),
            preferred_element_type=jnp.float32,
        )
        key_now, value_now = from_behind((key_now, value_now), "blk", 1)
        return (key_now, value_now, new_top, running_total, running_sum)

    initial = (
        keys_own,
        values_own,
        jnp.full((HEADS, frame_count, 1), NEGATIVE, jnp.float32),
        jnp.zeros((HEADS, frame_count, 1), jnp.float32),
        jnp.zeros((HEADS, frame_count, HEAD_DIM), jnp.float32),
    )
    finished = lax.fori_loop(0, cycle_size, forward_turn, initial)
    running_top, running_total, running_sum = (finished[2], finished[3], finished[4])
    attended = jnp.transpose(running_sum / running_total, (1, 0, 2)).reshape(
        frame_count, model_width
    )
    log_total = (running_top + jnp.log(running_total))[:, :, 0]
    attended_low = attended.astype(jnp.bfloat16)
    hidden_two = hidden + jnp.dot(attended_low, w_out, preferred_element_type=jnp.float32)
    normal_two, spread_two = normalize(hidden_two)
    gain_vector = ff_gain.astype(jnp.float32)
    ff_in = (normal_two * gain_vector).astype(jnp.bfloat16)
    widened = jnp.dot(ff_in, w_up, preferred_element_type=jnp.float32)
    activated, gelu_back = jax.vjp(exact_gelu, widened)
    activated_low = activated.astype(jnp.bfloat16)
    output = (
        hidden_two + jnp.dot(activated_low, w_down, preferred_element_type=jnp.float32)
    ).astype(jnp.bfloat16)
    upstream = cotangent[0]
    grad_down = contract_rows(activated_low, upstream)
    grad_activated = jnp.dot(upstream, w_down.T, preferred_element_type=jnp.float32)
    grad_widened = gelu_back(grad_activated)[0].astype(jnp.bfloat16)
    grad_up = contract_rows(ff_in, grad_widened)
    grad_ff_in = jnp.dot(grad_widened, w_up.T, preferred_element_type=jnp.float32)
    grad_gain = jnp.sum(grad_ff_in * normal_two, axis=0)
    grad_hidden_two = upstream.astype(jnp.float32) + norm_back(
        grad_ff_in * gain_vector, normal_two, spread_two
    )
    grad_two_low = grad_hidden_two.astype(jnp.bfloat16)
    grad_out = contract_rows(attended_low, grad_two_low)
    grad_attended = jnp.dot(grad_two_low, w_out.T, preferred_element_type=jnp.float32).astype(
        jnp.bfloat16
    )
    delta = jnp.transpose(jnp.sum(heads_of(grad_attended.astype(jnp.float32) * attended), axis=2))
    zero_grad = jnp.zeros((frame_count, model_width), jnp.float32)

    def pair_terms(
        query_block,
        upstream_block,
        key_block,
        value_block,
        total_block,
        delta_block,
        query_segment,
        key_segment,
    ):
        raw_scores, allowed = scored(query_block, key_block, query_segment, key_segment)
        prob_block = jnp.where(allowed, jnp.exp(raw_scores - total_block[:, :, None]), 0.0)
        value_term = jnp.einsum(
            "hqk,qhd->khd",
            prob_block.astype(jnp.bfloat16),
            heads_of(upstream_block),
            preferred_element_type=jnp.float32,
        ).reshape(frame_count, model_width)
        prob_grad = jnp.einsum(
            "qhd,khd->hqk",
            heads_of(upstream_block),
            heads_of(value_block),
            preferred_element_type=jnp.float32,
        )
        score_grad = (prob_block * (prob_grad - delta_block[:, :, None])).astype(jnp.bfloat16)
        query_term = (
            jnp.einsum(
                "hqk,khd->qhd", score_grad, heads_of(key_block), preferred_element_type=jnp.float32
            ).reshape(frame_count, model_width)
            * score_scale
        )
        key_term = (
            jnp.einsum(
                "hqk,qhd->khd",
                score_grad,
                heads_of(query_block),
                preferred_element_type=jnp.float32,
            ).reshape(frame_count, model_width)
            * score_scale
        )
        return (query_term, key_term, value_term)

    def keys_turn(turn_index, carried):
        key_now, value_now, key_grad, value_grad, query_grad = carried
        source = (device_rank - turn_index) % cycle_size
        query_term, key_term, value_term = pair_terms(
            queries,
            grad_attended,
            key_now,
            value_now,
            log_total,
            delta,
            own_segment,
            segment_of(source),
        )
        key_now, value_now = from_behind((key_now, value_now), "blk", 1)
        key_grad, value_grad = (
            from_behind((key_grad + key_term).astype(jnp.bfloat16), "blk", 1).astype(jnp.float32),
            from_behind((value_grad + value_term).astype(jnp.bfloat16), "blk", 1).astype(
                jnp.float32
            ),
        )
        return (key_now, value_now, key_grad, value_grad, query_grad + query_term)

    done = lax.fori_loop(
        0, cycle_size, keys_turn, (keys_own, values_own, zero_grad, zero_grad, zero_grad)
    )
    key_grad, value_grad, query_grad = (done[2], done[3], done[4])
    grad_project = jnp.concatenate(
        [
            rotate_back(heads_of(query_grad), own_position).reshape(frame_count, model_width),
            rotate_back(heads_of(key_grad), own_position).reshape(frame_count, model_width),
            value_grad,
        ],
        axis=1,
    ).astype(jnp.bfloat16)
    grad_qkv = contract_rows(attn_in, grad_project)
    grad_attn_in = jnp.dot(grad_project, w_qkv.T, preferred_element_type=jnp.float32)
    mod_terms = jnp.concatenate([grad_attn_in * normal_one, grad_attn_in], axis=1)
    grad_modulation = jnp.dot(picker.T, mod_terms, precision=HIGHEST)
    grad_mod = jnp.dot(condition.astype(jnp.float32).T, grad_modulation, precision=HIGHEST)
    grad_hidden = grad_hidden_two + norm_back(grad_attn_in * scale_one, normal_one, spread_one)
    grad_hidden_low = grad_hidden.astype(jnp.bfloat16)
    grad_skip_weight = contract_rows(joined, grad_hidden_low)
    grad_joined = jnp.dot(grad_hidden_low, w_skip.T, preferred_element_type=jnp.float32)
    shards = (
        lax.psum_scatter(
            grad_skip_weight.astype(jnp.bfloat16), "grp", scatter_dimension=0, tiled=True
        ).astype(jnp.float32),
        lax.psum_scatter(
            grad_mod.astype(jnp.bfloat16), "grp", scatter_dimension=0, tiled=True
        ).astype(jnp.float32),
        lax.psum_scatter(
            grad_qkv.astype(jnp.bfloat16), "grp", scatter_dimension=0, tiled=True
        ).astype(jnp.float32),
        lax.psum_scatter(
            grad_out.astype(jnp.bfloat16), "grp", scatter_dimension=0, tiled=True
        ).astype(jnp.float32),
        lax.psum_scatter(
            grad_gain.astype(jnp.bfloat16), "grp", scatter_dimension=0, tiled=True
        ).astype(jnp.float32),
        lax.psum_scatter(
            grad_up.astype(jnp.bfloat16), "grp", scatter_dimension=0, tiled=True
        ).astype(jnp.float32),
        lax.psum_scatter(
            grad_down.astype(jnp.bfloat16), "grp", scatter_dimension=0, tiled=True
        ).astype(jnp.float32),
    )
    totals = lax.psum(
        (shards[0], shards[1], shards[2], shards[3], shards[4], shards[5], shards[6]), "blk"
    )
    return (
        output[None],
        grad_joined[:, :model_width][None],
        grad_joined[:, model_width:][None],
        totals[0],
        totals[1],
        totals[2],
        totals[3],
        totals[4],
        totals[5],
        totals[6],
    )


def dot_plain(left_side, right_side):
    return jnp.dot(left_side, right_side, preferred_element_type=jnp.float32)


def dot_across(left_side, right_side):
    return lax.dot_general(
        left_side, right_side, (((1,), (1,)), ((), ())), preferred_element_type=jnp.float32
    )


def ring_place(rank):
    odd = lax.rem(rank, 2)
    return (1 - odd) * (rank // 2) + odd * ((15 - rank) // 2)


def ring_rank(place):
    upper = place // 4
    return (1 - upper) * (2 * place) + upper * (15 - 2 * place)


TICKS = (2, 0, 0, 0, 0, 2, 0, 0, 0, 0, 2, 0, 0, 2, 0, 2, 4, 0, 0, 6, 3, 2, 2)

TILE = 128
UNROLLED = 4
RING_TILE = 32


class Ring:
    def __init__(self, part, land, whole, sems, whole_sems, rank, group_rank, turn=None):
        self.part, self.land, self.whole = part, land, whole
        self.sems, self.whole_sems = sems, whole_sems
        self.rank, self.group_rank = rank, group_rank
        self.place = ring_place(rank)
        self.half = part.shape[1] // 2
        self.copies = {}
        self.puts, self.turns, self.turn = [], [], turn

    def block_at(self, offset):
        return ring_rank(lax.rem(self.place + offset + 2 * RING, RING))

    def rows(self, way):
        return pl.ds(way * self.half, self.half)

    def send(self, kind, step, way, source, target):
        to = ring_rank(lax.rem(self.place + (1 if way == 0 else RING - 1), RING))
        copy = pltpu.make_async_remote_copy(
            src_ref=source,
            dst_ref=target,
            send_sem=self.sems.at[kind, 0, way, step],
            recv_sem=self.sems.at[kind, 1, way, step],
            device_id=(to, self.group_rank),
            device_id_type=MESH,
        )
        copy.start()
        self.copies[kind, step, way] = copy

    def sum_step(self, step):
        if step == 1:
            for way in range(2):
                self.copies[0, 0, way].wait_send()
        for way in range(2):
            block = self.block_at((-1 if way == 0 else 1) * (step + 1))
            rows = self.rows(way)
            if step > 0:
                self.copies[0, step - 1, way].wait_recv()
                tile = min(self.half, RING_TILE)

                def add(i, carry, way=way, block=block, tile=tile):
                    at = pl.ds(pl.multiple_of(way * self.half + i * tile, tile), tile)
                    total = self.part[block, at].astype(jnp.float32) + self.land[
                        step - 1, at
                    ].astype(jnp.float32)
                    self.land[step - 1, at] = total.astype(jnp.bfloat16)
                    return carry

                lax.fori_loop(0, self.half // tile, add, 0)
            if step < RING - 1:
                source = self.part.at[block, rows] if step == 0 else self.land.at[step - 1, rows]
                self.send(0, step, way, source, self.land.at[step, rows])

    def put(self, block, step, way):
        rows = self.rows(way)
        copy = pltpu.make_async_copy(
            self.part.at[block, rows], self.whole.at[block, rows], self.whole_sems.at[way, step]
        )
        copy.start()
        self.puts.append(copy)

    def spread_step(self, step):
        if step == 0:
            self.close_sum()
        for way in range(2):
            block = self.block_at((-1 if way == 0 else 1) * step)
            rows = self.rows(way)
            if step > 0:
                self.copies[1, step - 1, way].wait_recv()
            if step < RING - 1:
                target = self.part.at[block, rows]
                self.send(1, step, way, target, target)
            self.put(block, step, way)

    def begin(self):
        self.sum_step(0)
        self.left = [functools.partial(self.sum_step, step) for step in range(1, RING)]
        self.left += [functools.partial(self.spread_step, step) for step in range(RING)]
        if self.turn is not None:
            self.left.insert(RING - 1, self.turn_out)

    def turn_out(self):
        place, sems = self.turn
        deep = self.part.shape[1] // ROWS

        def rows(group):
            return pl.ds(pl.multiple_of(group * deep, deep), deep)

        for other in (2, 1, 3):
            to = lax.rem(self.group_rank + other, ROWS)
            copy = pltpu.make_async_remote_copy(
                src_ref=self.land.at[RING - 2, rows(to)],
                dst_ref=place.at[rows(self.group_rank)],
                send_sem=sems.at[0, other - 1],
                recv_sem=sems.at[1, other - 1],
                device_id=(self.rank, to),
                device_id_type=MESH,
            )
            copy.start()
            self.turns.append(copy)
        place[rows(self.group_rank)] = self.land[RING - 2, rows(self.group_rank)]

    def close_sum(self):
        for copy in self.turns:
            copy.wait_recv()
        self.part[self.rank] = self.land[RING - 2] if self.turn is None else self.turn[0][...]

    def finish(self):
        for copy in self.turns:
            copy.wait_send()
        for (kind, step, _), copy in self.copies.items():
            if kind or step:
                copy.wait_send()
        for copy in self.puts:
            copy.wait()


def block_kernel(names, *refs):
    n = types.SimpleNamespace(**dict(zip(names, refs)))
    low, full = jnp.bfloat16, jnp.float32
    rank, group_rank = lax.axis_index("blk"), lax.axis_index("grp")
    core, chip = lax.rem(group_rank, 2), group_rank // 2
    sibling = (rank, group_rank + 1 - 2 * core)
    across = (rank, group_rank + 2 - 4 * chip)
    frames, width = n.cotangent.shape
    half = 2 * frames
    columns = width // ROWS
    mine, theirs = core * half, (1 - core) * half
    own_slot = 2 * core + chip
    pair_row, pair_side = rank // 2, lax.rem(rank, 2)
    sent = []

    def lines(offset, size):
        return pl.ds(pl.multiple_of(offset, min(size, 128)), size)

    def slot_of(row):
        return 2 * lax.rem(row, 2) + row // 2

    def row_of(slot):
        return 2 * lax.rem(slot, 2) + slot // 2

    def group(other):
        return lax.rem(group_rank + other, ROWS)

    def block(other):
        return lax.rem(rank + other, RING)

    def link(source, target, send_sem, recv_sem, device):
        return pltpu.make_async_remote_copy(
            src_ref=source,
            dst_ref=target,
            send_sem=send_sem,
            recv_sem=recv_sem,
            device_id=device,
            device_id_type=MESH,
        )

    def push(source, target, sems, index, device):
        copy = link(source, target, sems.at[(0,) + index], sems.at[(1,) + index], device)
        copy.start()
        sent.append(copy)
        return copy

    def load(source, target, index):
        copy = pltpu.make_async_copy(source, target, n.load_sem.at[index])
        copy.start()
        return copy

    def tiles(count, tile, body):
        if count // tile <= UNROLLED:
            for i in range(count // tile):
                body(i * tile)
            return

        def step(i, carry):
            body(pl.multiple_of(i * tile, tile))
            return carry

        lax.fori_loop(0, count // tile, step, 0)

    joined_loads = [
        load((n.inputs, n.skipped)[t // 2].at[:, pl.ds((t % 2) * 512, 512)], n.joined_own.at[t], t)
        for t in range(ROWS)
    ]
    upstream_load = load(n.cotangent, n.upstream.at[lines(own_slot * frames, frames)], 4)
    skip_load = load(n.w_skip, n.skip_held, 5)
    mod_load = load(n.w_mod, n.mod_held, 6)
    out_place = n.out_held.at[lines(group_rank * columns, columns)]
    out_load = load(n.w_out, out_place, 7)
    down_load = load(n.w_down, n.down_held, 8)
    pieces = [(side, kind) for side in range(2) for kind in range(3)]

    def qkv_piece(target, side, kind, first, count):
        at = pl.multiple_of(kind * width + target * columns + side * 128, 128)
        return n.w_qkv.at[lines(first, count), pl.ds(at, 128)]

    def qkv_place(side, kind, first, count):
        rows = lines(group_rank * columns + first, count)
        return n.qkv_held.at[rows, pl.ds((side * 3 + kind) * 128, 128)]

    qkv_loads = [
        load(qkv_piece(group_rank, *piece, 0, columns), qkv_place(*piece, 0, columns), 9 + i)
        for i, piece in enumerate(pieces)
    ]
    hidden_units = n.up_held.shape[1]

    def up_piece(target):
        return n.w_up.at[:, pl.ds(pl.multiple_of(target * hidden_units, 128), hidden_units)]

    up_place = n.up_held.at[lines(group_rank * columns, columns)]
    up_load = load(up_piece(group_rank), up_place, 15)

    def small_tables():
        down = lax.broadcasted_iota(jnp.int32, (8, 128), 0)
        across_lanes = lax.rem(lax.broadcasted_iota(jnp.int32, (8, 128), 1), 64)
        zero = jnp.zeros((8, 128), full)
        step_tile, start_tile, end_tile = zero, zero, zero
        start_lane, end_lane = zero + 1e9, zero
        start = jnp.int32(0)
        for u in range(8):
            end = start + n.lengths[0, u]
            here = down == u
            lane_here = (across_lanes == u) | (across_lanes == u + 8)
            step_tile = jnp.where(here, n.flow_steps[0, u].astype(full), step_tile)
            start_tile = jnp.where(here, start.astype(full), start_tile)
            end_tile = jnp.where(here, end.astype(full), end_tile)
            start_lane = jnp.where(lane_here, start.astype(full), start_lane)
            end_lane = jnp.where(lane_here, end.astype(full), end_lane)
            start = end
        tables = (step_tile, start_tile, end_tile, start_lane, end_lane)
        for i, tile in enumerate(tables):
            n.small[i] = tile
        n.small[5] = n.own_gain[:, 0:128]
        n.small[6] = n.own_gain[:, 128:256]

    barrier = pltpu.get_barrier_semaphore()
    for other in range(1, ROWS):
        pl.semaphore_signal(barrier, inc=1, device_id=(rank, group(other)), device_id_type=MESH)
    for other in range(1, RING):
        pl.semaphore_signal(barrier, inc=1, device_id=(block(other), group_rank), device_id_type=MESH)
    small_tables()
    for copy in joined_loads:
        copy.wait()
    pl.semaphore_wait(barrier, ROWS + RING - 2)

    joined_place = n.joined.at[lines(own_slot * frames, frames)]
    joined_sends = [
        push(n.joined_own.at[group(o)], joined_place, n.joined_sem, (o - 1,), (rank, group(o)))
        for o in (2, 1, 3)
    ]
    small_sends = [
        push(n.small, n.smalls.at[group_rank], n.small_sem, (o - 1,), (rank, group(o)))
        for o in (2, 1, 3)
    ]
    n.joined[lines(own_slot * frames, frames)] = n.joined_own[group_rank]
    n.smalls[group_rank] = n.small[...]
    for copy in small_sends:
        copy.wait_recv()

    steps = jnp.concatenate([n.smalls[(0, 2, 1, 3)[s], 0] for s in range(ROWS)], axis=0)
    steps = jnp.concatenate([steps, steps], axis=1)
    lane = lax.broadcasted_iota(jnp.int32, steps.shape, 1) + lax.rem(group_rank, 2) * columns
    rate = jnp.exp(-math.log(10000.0) * lane.astype(full) / (width // 2))
    angles = 1000.0 * (steps / STEPS) * rate
    turned = jnp.where(group_rank >= 2, jnp.cos(angles), jnp.sin(angles))
    n.condition[...] = (turned / (1.0 + jnp.exp(-turned))).astype(low)
    mod_load.wait()

    def mod_tile(at):
        where = pl.ds(at, 512)
        n.mod_part[:, where] = dot_plain(n.condition[...], n.mod_held[:, where])

    tiles(2 * width, 512, mod_tile)
    mod_first = push(
        n.mod_part.at[pl.ds(pl.multiple_of(16 * (1 - core), 16), 16)], n.mod_land.at[0], n.mod_sem, (0,), sibling
    )

    gains = [n.smalls[r, 5 + i][0:1] for r in range(ROWS) for i in range(2)]
    n.gain[...] = jnp.broadcast_to(jnp.concatenate(gains, axis=1), n.gain.shape)

    def picked(row, first, count):
        spot = (lax.broadcasted_iota(jnp.int32, (count, 128), 0) + first).astype(full)
        return (spot >= n.smalls[row, 3][0:1]) & (spot < n.smalls[row, 4][0:1]), spot

    lanes = lax.broadcasted_iota(jnp.int32, (frames, 128), 1)
    turn_rate = jnp.exp(-math.log(10000.0) * lax.rem(lanes, 32).astype(full) / 32)
    turn_sign = jnp.where(lax.rem(lanes, 64) < 32, -1.0, 1.0)

    def turn_tables(row, first, cosine, sine, at):
        chosen, spot = picked(row, first, frames)
        start = jnp.where(chosen & (lanes < 8), n.smalls[row, 3][0:1], 0.0)
        position = spot - jnp.sum(start, axis=1, keepdims=True)
        angle = position * turn_rate
        cosine[at] = jnp.cos(angle)
        sine[at] = jnp.sin(angle) * turn_sign

    def swapped(value):
        ahead = pltpu.roll(value, 96, 1)
        behind = pltpu.roll(value, 32, 1)
        return jnp.where(lax.rem(lanes, 64) < 32, ahead, behind)

    def partial_sum(index, left_ref, right_tile):
        def to_send(at):
            n.send_one[:, pl.ds(at, 256)] = right_tile(left_ref[lines(theirs, half)], at).astype(low)

        def to_keep(at):
            n.keep[:, pl.ds(at, 256)] = right_tile(left_ref[lines(mine, half)], at)

        if index > 0:
            for copy in group_copies[index - 1][0]:
                copy.wait_send()
        tiles(width, 256, to_send)
        first = [
            push(
                n.send_one.at[pl.ds(k * frames, frames)],
                n.land_one.at[index, pl.ds(k * frames, frames)],
                n.first_sem,
                (index, k),
                sibling,
            )
            for k in range(2)
        ]
        tiles(width, 256, to_keep)
        return first

    def cross_sum(index, first):
        if index > 0:
            for copy in group_copies[index - 1][1]:
                copy.wait_send()
        second = []
        for k in range(2):
            first[k].wait_recv()

            def add(at, k=k):
                where = pl.ds(k * frames + at, TILE)
                total = n.keep[where] + n.land_one[index, where].astype(full)
                n.keep[where] = total
                n.send_two[where] = total.astype(low)

            tiles(frames, TILE, add)
            second.append(
                push(
                    n.send_two.at[pl.ds(k * frames, frames)],
                    n.land_two.at[index, pl.ds(k * frames, frames)],
                    n.second_sem,
                    (index, k),
                    across,
                )
            )
        group_copies[index] = (first, second)
        return second

    group_copies = {}

    down_ring, up_ring, out_ring, qkv_ring, skip_ring = rings = [
        Ring(part, land, whole, sems, n.whole_sem.at[index], rank, group_rank, turn)
        for index, (part, land, whole, sems, turn) in enumerate(
            (
                (n.down_total, n.down_land, n.down_whole, n.down_sem, None),
                (n.up_total, n.up_land, n.up_whole, n.up_ring_sem, (n.up_turn, n.turn_sem.at[0])),
                (n.out_total, n.out_land, n.out_whole, n.out_ring_sem, None),
                (n.qkv_total, n.qkv_land, n.qkv_whole, n.qkv_ring_sem, (n.qkv_turn, n.turn_sem.at[1])),
                (n.skip_total, n.skip_land, n.skip_whole, n.skip_ring_sem, None),
            )
        )
    ]
    running = []

    def begin(ring):
        ring.begin()
        running.append(ring)

    def ticks(count):
        for _ in range(count):
            if running:
                ring = running.pop(0)
                ring.left.pop(0)()
                if ring.left:
                    running.append(ring)

    def mean(value):
        return jnp.mean(value, axis=-1, keepdims=True)

    def share(buffer, k, sems):
        where = lines(mine + k * frames, frames)
        return push(buffer.at[where], buffer.at[where], sems, (k,), sibling)

    skip_load.wait()
    for copy in joined_sends:
        copy.wait_recv()

    side_y, side_z = lax.rem(rank, 2), lax.rem(rank // 2, 2)
    to_y, to_z = 1 - 2 * side_y, 2 - 4 * side_z
    beside = (rank + to_y, group_rank)
    around = (beside, (rank + to_z, group_rank), (rank + to_y + to_z, group_rank))
    part_rows = columns // 2
    few_rows = columns // 4
    first_row = (2 * side_z + side_y) * few_rows
    over_x = (group_rank + 2 - 4 * chip, 2 * (1 - chip) + 1 - core)
    qkv_sends = [
        [
            push(
                qkv_piece(to, *piece, first_row, few_rows),
                qkv_place(*piece, first_row, few_rows),
                n.qkv_sem,
                (i, j),
                (rank, to),
            )
            for j, piece in enumerate(pieces)
        ]
        for i, to in enumerate(over_x)
    ]
    qkv_sends.append(
        [
            push(
                qkv_piece(sibling[1], *piece, 0, columns),
                qkv_place(*piece, 0, columns),
                n.qkv_sem,
                (2, j),
                sibling,
            )
            for j, piece in enumerate(pieces)
        ]
    )

    def skip_tile(left, at):
        return dot_plain(left, n.skip_held[:, pl.ds(at, 256)])

    first = partial_sum(0, n.joined, skip_tile)
    mod_first.wait_recv()
    mod_mine = n.mod_part[pl.ds(pl.multiple_of(16 * core, 16), 16)] + n.mod_land[0]
    n.mod_send[...] = mod_mine.astype(low)
    mod_second = push(n.mod_send, n.mod_cross, n.mod_sem, (1,), across)
    second = cross_sum(0, first)
    own_lines = lines(own_slot * frames, frames)
    for slot in range(ROWS):
        turn_tables(
            (0, 2, 1, 3)[slot],
            rank * frames,
            n.cosine,
            n.sine,
            pl.ds(slot * frames, frames),
        )
    mod_second.wait_recv()
    mod_total = n.mod_send[...].astype(full) + n.mod_cross[...].astype(full)
    for k in range(2):
        row = 2 * k + core
        values = mod_total[8 * k : 8 * k + 8]
        high = values.astype(low).astype(full)
        stack = jnp.concatenate([high, values - high], axis=0).astype(low)
        chosen = picked(row, rank * frames, frames)[0]
        picker = jnp.where(chosen, 1.0, 0.0).astype(low)[:, :16]
        where = pl.ds(k * frames, frames)
        n.scale_one[where] = 1.0 + dot_plain(picker, stack[:, :width])
        n.shift_one[where] = dot_plain(picker, stack[:, width:])

    qkv_passed = []
    for i, source in enumerate(over_x):
        for copy in qkv_sends[i]:
            copy.wait_recv()
        where = n.qkv_held.at[lines(source * columns + first_row, few_rows)]
        for j, to in enumerate(around):
            qkv_passed.append(push(where, where, n.qkv_pass_sem, (i, j), to))
    attn_sends = []
    for k in range(2):
        second[k].wait_recv()

        def norm_one(at, k=k):
            where = pl.ds(k * frames + at, TILE)
            hidden = n.keep[where] + n.land_two[0, where].astype(full)
            n.hidden[where] = hidden
            centred = hidden - mean(hidden)
            spread = lax.rsqrt(mean(centred * centred) + EPSILON)
            normal = centred * spread
            n.normal_one[where] = normal
            n.spread_one[where] = jnp.broadcast_to(spread, (TILE, 128))
            n.attn_in[lines(mine + k * frames + at, TILE)] = (
                normal * n.scale_one[where] + n.shift_one[where]
            ).astype(low)

        tiles(frames, TILE, norm_one)
        attn_sends.append(share(n.attn_in, k, n.attn_sem))

    def part_of(reference, first):
        return reference.at[lines(first + side_y * part_rows, part_rows)]

    up_sends = [
        push(
            part_of(up_piece(to), 0),
            part_of(n.up_held, group_rank * columns),
            n.up_sem,
            (i,),
            (rank, to),
        )
        for i, to in enumerate(over_x)
    ]
    up_sends.append(push(up_piece(sibling[1]), up_place, n.up_sem, (2,), sibling))
    out_sends = [
        push(n.w_out, out_place, n.out_sem, (i,), device) for i, device in enumerate((across, sibling))
    ]

    def pass_on(buffer, copies, sems):
        passed = []
        for i, source in enumerate(over_x):
            copies[i].wait_recv()
            where = part_of(buffer, source * columns)
            passed.append(push(where, where, sems, (i,), beside))
        return passed

    upstream_load.wait()
    upstream_sends = [
        push(n.upstream.at[own_lines], n.upstream.at[own_lines], n.upstream_sem, (i,), device)
        for i, device in enumerate((across, sibling))
    ]

    for copy in qkv_loads:
        copy.wait()
    for copy in qkv_sends[2] + qkv_passed:
        copy.wait_recv()

    def to_heads(offset, value_of, target, sems, send_buffer, columns_of):
        for k in range(2):
            slot = offset // frames + k
            for side in range(2):
                to = 2 * row_of(slot) + side
                if value_of is not None:
                    send_buffer[to] = value_of(k, side, slot)

                @pl.when(to != rank)
                def _():
                    link(
                        send_buffer.at[to, :, columns_of],
                        target.at[lines(rank * frames, frames), columns_of],
                        sems.at[0, to],
                        sems.at[1, rank],
                        (to, group_rank),
                    ).start()

                @pl.when(to == rank)
                def _():
                    target[lines(rank * frames, frames), columns_of] = send_buffer[to, :, columns_of]

    def heads_arrive(target, sems, columns_of, then=None):
        for other in range(RING):
            source = block(other)
            if other:
                where = target.at[lines(source * frames, frames), columns_of]
                link(
                    where, where, sems.at[0, source], sems.at[1, source], (source, group_rank)
                ).wait_recv()
            if then is not None:
                then(pl.multiple_of(source * frames, frames))

    def project_half(offset):
        def project_tile(at):
            n.project[:, pl.ds(at, 256)] = dot_plain(
                n.attn_in[lines(offset, half)], n.qkv_held[:, pl.ds(at, 256)]
            )

        tiles(3 * columns, 256, project_tile)

        def value_of(k, side, slot):
            where = lines(slot * frames, frames)
            cosine, sine = n.cosine[where], n.sine[where]
            blocks = []
            for kind in range(3):
                value = n.project[pl.ds(k * frames, frames), pl.ds((side * 3 + kind) * 128, 128)]
                if kind < 2:
                    value = value * cosine + swapped(value) * sine
                blocks.append(value.astype(low))
            return jnp.concatenate(blocks, axis=1)

        to_heads(offset, value_of, n.paired, n.pair_sem, n.pair_send, pl.ds(0, 256))

    project_half(mine)
    for copy in attn_sends:
        copy.wait_recv()
    project_half(theirs)
    for offset in (mine, theirs):
        to_heads(offset, None, n.paired, n.value_sem, n.pair_send, pl.ds(256, 128))

    def row_tables(at):
        turn_tables(pair_row, at, n.row_cosine, n.row_sine, pl.ds(at, frames))
        chosen = jnp.where(picked(pair_row, at, frames)[0], 1.0, 0.0)
        n.chosen[pl.ds(at, frames)] = chosen.astype(low)

    tiles(RING * frames, frames, row_tables)
    def masked_parts(at):
        where = pl.ds(at, frames)
        query, key = n.paired[where, 0:128], n.paired[where, 128:256]
        chosen = n.chosen[where]
        first_head = lanes < 64
        blocked = jnp.where(
            lax.rem(lanes, 64) < 8, NEGATIVE * (1.0 - chosen.astype(full)), 0.0
        ).astype(low)
        scaled = (query.astype(full) * HEAD_DIM ** (-0.5)).astype(low)
        n.query_head[0, where] = jnp.where(first_head, scaled, chosen)
        n.query_head[1, where] = jnp.where(first_head, chosen, scaled)
        n.key_head[0, where] = jnp.where(first_head, key, blocked)
        n.key_head[1, where] = jnp.where(first_head, blocked, key)

    heads_arrive(n.paired, n.pair_sem, pl.ds(0, 256), masked_parts)
    up_passed = pass_on(n.up_held, up_sends, n.up_pass_sem)
    out_sends[0].wait_recv()
    where = n.out_held.at[lines(across[1] * columns, columns)]
    out_sends.append(push(where, where, n.out_sem, (2,), sibling))
    all_frames = RING * frames
    pair_place = (lines(slot_of(pair_row) * frames, frames), lines(pair_side * 128, 128))

    def score(at):
        where = pl.ds(at, half)
        for head in range(2):
            scores = dot_across(n.query_head[head, where], n.key_head[head])
            top = jnp.max(scores, axis=1, keepdims=True)
            weights = jnp.exp(scores - top)
            total = jnp.sum(weights, axis=1, keepdims=True)
            n.shares[head, where] = (weights * (1.0 / total)).astype(low)

    tiles(all_frames, half, score)
    heads_arrive(n.paired, n.value_sem, pl.ds(256, 128))

    def attend(at):
        where = pl.ds(at, half)
        sums = [dot_plain(n.shares[head, where], n.paired[:, 256:384]) for head in range(2)]
        first_head = lax.broadcasted_iota(jnp.int32, (half, 128), 1) < 64
        value = jnp.where(first_head, sums[0], sums[1])
        n.attended_pair[where] = value
        n.attended_send[where] = value.astype(low)
        for k in range(2):
            to = at // frames + k
            place = lines(at + k * frames, frames)

            @pl.when(to != rank)
            def _():
                link(
                    n.attended_send.at[place],
                    n.attended.at[pair_place],
                    n.attended_sem.at[0, to],
                    n.attended_sem.at[1, rank],
                    (to, group_rank),
                ).start()

            @pl.when(to == rank)
            def _():
                n.attended[pair_place] = n.attended_send[place]

    tiles(all_frames, half, attend)

    def pairs_arrive(buffer, sems, pitch, first, wide):
        for other in range(1, RING):
            source = block(other)
            where = buffer.at[
                lines(slot_of(source // 2) * frames, frames),
                pl.ds(pl.multiple_of(lax.rem(source, 2) * pitch + first, 128), wide),
            ]
            link(where, where, sems.at[0, source], sems.at[1, source], (source, group_rank)).wait_recv()

    upstream_sends[0].wait_recv()
    other_lines = lines((2 * core + 1 - chip) * frames, frames)
    upstream_sends.append(
        push(n.upstream.at[other_lines], n.upstream.at[other_lines], n.upstream_sem, (2,), sibling)
    )
    pairs_arrive(n.attended, n.attended_sem, 128, 0, 128)

    own_columns = pl.ds(pl.multiple_of(group_rank * columns, columns), columns)
    attended_sends = [
        push(
            n.attended.at[lines(first, half)],
            n.attended_all.at[:, own_columns],
            n.attended_all_sem,
            (i,),
            (rank, to),
        )
        for i, (first, to) in enumerate(
            ((mine, over_x[0]), (theirs, over_x[1]), (theirs, sibling[1]))
        )
    ]
    n.attended_all[:, own_columns] = n.attended[lines(mine, half)]
    out_load.wait()
    for copy in out_sends[1:] + attended_sends:
        copy.wait_recv()

    def out_tile(at):
        n.keep[:, pl.ds(at, 256)] = dot_plain(n.attended_all[...], n.out_held[:, pl.ds(at, 256)])

    tiles(width, 256, out_tile)
    ff_sends = []
    for k in range(2):

        def norm_two(at, k=k):
            where = pl.ds(k * frames + at, TILE)
            hidden = n.hidden[where] + n.keep[where]
            n.hidden[where] = hidden
            centred = hidden - mean(hidden)
            spread = lax.rsqrt(mean(centred * centred) + EPSILON)
            normal = centred * spread
            n.normal_two[where] = normal
            n.spread_two[where] = jnp.broadcast_to(spread, (TILE, 128))
            n.ff_in[lines(mine + k * frames + at, TILE)] = (normal * n.gain[0:1]).astype(low)

        tiles(frames, TILE, norm_two)
        ff_sends.append(share(n.ff_in, k, n.ff_sem))

    up_load.wait()
    down_load.wait()
    for copy in up_sends[2:] + up_passed:
        copy.wait_recv()
    for copy in upstream_sends[1:]:
        copy.wait_recv()

    def feed_half(offset):
        where = lines(offset, half)

        def feed_tile(at):
            widened = dot_plain(n.ff_in[where], n.up_held[:, pl.ds(at, 256)])
            grad = dot_across(n.upstream[where], n.down_held[pl.ds(at, 256)])
            share_of = 0.5 * (1.0 + lax.erf(widened * math.sqrt(0.5)))
            slope = share_of + widened * jnp.exp(-0.5 * widened * widened) * (
                1.0 / math.sqrt(2.0 * math.pi)
            )
            n.activated[where, pl.ds(at, 256)] = (widened * share_of).astype(low)
            n.grad_widened[where, pl.ds(at, 256)] = (grad * slope).astype(low)

        tiles(hidden_units, 256, feed_tile)

    feed_half(mine)
    for copy in ff_sends:
        copy.wait_recv()
    feed_half(theirs)
    first = partial_sum(
        1, n.grad_widened, lambda left, at: dot_across(left, n.up_held[pl.ds(at, 256)])
    )
    second = cross_sum(1, first)

    def down_tile(at):
        value = contract_rows(n.activated[:, pl.ds(at, 256)], n.upstream[...]).astype(low)
        n.down_total[at // 128] = value[:128]
        n.down_total[at // 128 + 1] = value[128:]

    tiles(hidden_units, 256, down_tile)
    begin(down_ring)

    def up_tile(at):
        value = contract_rows(n.ff_in[:, pl.ds(at, columns)], n.grad_widened[...]).astype(low)
        deep = columns // RING
        for j in range(RING):
            n.up_total[j, pl.ds(pl.multiple_of(at // RING, deep), deep)] = value[
                j * deep : (j + 1) * deep
            ]

    tiles(width, columns, up_tile)
    begin(up_ring)
    ticks(TICKS[0])

    gain_sums = jnp.zeros((1, width), full)
    grad_sends = []
    for k in range(2):
        second[k].wait_recv()
        weight = (1 - jnp.abs(chip - k)).astype(full)

        def back_two(i, sums, k=k, weight=weight):
            at = pl.multiple_of(i * TILE, TILE)
            where = pl.ds(k * frames + at, TILE)
            grad = n.keep[where] + n.land_two[1, where].astype(full)
            normal = n.normal_two[where]
            scaled = grad * n.gain[0:1]
            back = n.spread_two[where][:, 0:1] * (
                scaled - mean(scaled) - normal * mean(scaled * normal)
            )
            total = n.upstream[lines(mine + k * frames + at, TILE)].astype(full) + back
            n.grad_two[where] = total
            n.grad_two_low[lines(mine + k * frames + at, TILE)] = total.astype(low)
            return sums + weight * jnp.sum(grad * normal, axis=0, keepdims=True)

        gain_sums = lax.fori_loop(0, frames // TILE, back_two, gain_sums)
        grad_sends.append(share(n.grad_two_low, k, n.grad_two_sem))
        ticks(TICKS[1 + k])
    n.mod_sums[8:16] = jnp.zeros((8, 2 * width), full)
    n.mod_sums[8:9, :width] = gain_sums

    def attended_half(offset):
        value = dot_across(
            n.grad_two_low[lines(offset, half)], n.out_held[lines(group_rank * columns, columns)]
        ).astype(low)

        def value_of(k, side, slot):
            return value[k * frames : (k + 1) * frames, side * 128 : side * 128 + 128]

        to_heads(
            offset, value_of, n.grad_pair, n.grad_pair_sem, n.grad_pair_send, pl.ds(0, 128)
        )

    attended_half(mine)
    ticks(TICKS[3])
    for copy in grad_sends:
        copy.wait_recv()
    attended_half(theirs)
    ticks(TICKS[4])
    value = contract_rows(n.attended[...], n.grad_two_low[...]).astype(low)
    for j in range(RING):
        n.out_total[j] = value[j * 32 : (j + 1) * 32]
    ticks(TICKS[5])

    first = partial_sum(2, n.activated, lambda left, at: dot_plain(left, n.down_held[:, pl.ds(at, 256)]))
    ticks(TICKS[6])
    output_second = cross_sum(2, first)
    ticks(TICKS[7])

    def turn_queries(at):
        where = pl.ds(at, frames)
        n.query_turned[:, where] = jnp.transpose(n.paired[where, 0:128].astype(full)).astype(low)

    tiles(RING * frames, frames, turn_queries)

    def turn_upstream(at):
        where = pl.ds(at, frames)
        n.grad_turned[:, where] = jnp.transpose(n.grad_pair[where].astype(full)).astype(low)

    heads_arrive(n.grad_pair, n.grad_pair_sem, pl.ds(0, 128), turn_upstream)
    n.key_turned[...] = jnp.zeros(n.key_turned.shape, full)
    n.value_turned[...] = jnp.zeros(n.value_turned.shape, full)

    def back_turned(value, where):
        return value * n.row_cosine[where] - swapped(value) * n.row_sine[where]

    project_slot = lines(slot_of(pair_row) * frames, frames)

    def project_back(to, place, first, wide, sems):
        source = n.project_send.at[place, pl.ds(first, wide)]
        at = pl.ds(pl.multiple_of(pair_side * 384 + first, 128), wide)

        @pl.when(to != rank)
        def _():
            target = n.grad_project.at[project_slot, at]
            link(source, target, sems.at[0, to], sems.at[1, rank], (to, group_rank)).start()

        @pl.when(to == rank)
        def _():
            n.grad_project[project_slot, at] = source[...]

    def attend_back(at):
        where = pl.ds(at, half)
        first_head = lax.broadcasted_iota(jnp.int32, (half, 128), 1) < 64
        grad = n.grad_pair[where]
        product = grad.astype(full) * n.attended_pair[where]
        terms = []
        for head in range(2):
            here = first_head if head == 0 else jnp.logical_not(first_head)
            delta = jnp.sum(jnp.where(here, product, 0.0), axis=1, keepdims=True)
            grad_head = jnp.where(here, grad, jnp.zeros_like(grad))
            prob_grad = dot_across(grad_head, n.paired[:, 256:384])
            shares = n.shares[head, where]
            score_grad = (shares.astype(full) * (prob_grad - delta)).astype(low)
            terms.append(dot_plain(score_grad, n.paired[:, 128:256]))
            rows = pl.ds(head * 64, 64)
            n.value_turned[rows] += dot_plain(n.grad_turned[rows, where], shares)
            n.key_turned[rows] += dot_plain(n.query_turned[rows, where], score_grad)
        query_grad = jnp.where(first_head, terms[0], terms[1]) * HEAD_DIM ** (-0.5)
        for k in range(2):
            place = lines(at + k * frames, frames)
            n.project_send[place, 0:128] = back_turned(
                query_grad[k * frames : (k + 1) * frames], place
            ).astype(low)
            project_back(at // frames + k, place, 0, 128, n.query_sem)

    for part in range(4):
        attend_back(part * half)
        ticks(TICKS[8 + part])
    def keys_back(at):
        place = pl.ds(at, frames)
        key_grad = jnp.transpose(n.key_turned[:, place]) * HEAD_DIM ** (-0.5)
        n.project_send[place, 128:256] = back_turned(key_grad, place).astype(low)
        n.project_send[place, 256:384] = jnp.transpose(n.value_turned[:, place]).astype(low)
        project_back(at // frames, place, 128, 256, n.project_sem)

    tiles(all_frames, frames, keys_back)

    ticks(TICKS[12])

    for copy in output_second:
        copy.wait_recv()

    def finish_output(at):
        where = lines(chip * frames + at, TILE)
        n.output[pl.ds(at, TILE)] = (
            n.hidden[where] + n.keep[where] + n.land_two[2, where].astype(full)
        ).astype(low)

    tiles(frames, TILE, finish_output)
    ticks(TICKS[13])
    pairs_arrive(n.grad_project, n.query_sem, 384, 0, 128)
    pairs_arrive(n.grad_project, n.project_sem, 384, 128, 256)

    first = partial_sum(
        3, n.grad_project, lambda left, at: dot_across(left, n.qkv_held[pl.ds(at, 256)])
    )
    ticks(TICKS[14])
    second = cross_sum(3, first)
    ticks(TICKS[15])

    def qkv_tile(at):
        value = contract_rows(n.attn_in[:, pl.ds(at, columns)], n.grad_project[...]).astype(low)
        deep = columns // RING
        for j in range(RING):
            n.qkv_total[j, pl.ds(pl.multiple_of(at // RING, deep), deep)] = value[
                j * deep : (j + 1) * deep
            ]

    tiles(width, columns, qkv_tile)
    begin(qkv_ring)
    ticks(TICKS[16])
    hidden_sends = []
    for k in range(2):
        second[k].wait_recv()

        def back_one(at, k=k):
            where = pl.ds(k * frames + at, TILE)
            grad = n.keep[where] + n.land_two[3, where].astype(full)
            normal = n.normal_one[where]
            scaled = grad * n.scale_one[where]
            back = n.spread_one[where][:, 0:1] * (
                scaled - mean(scaled) - normal * mean(scaled * normal)
            )
            n.grad_hidden[lines(mine + k * frames + at, TILE)] = (n.grad_two[where] + back).astype(low)

            @pl.when(chip == k)
            def _():
                n.shift_one[pl.ds(at, TILE)] = grad * normal
                n.shift_one[pl.ds(frames + at, TILE)] = grad

        tiles(frames, TILE, back_one)
        hidden_sends.append(share(n.grad_hidden, k, n.grad_hidden_sem))
        ticks(TICKS[17 + k])

    for copy in hidden_sends:
        copy.wait_recv()

    def skip_weight_tile(at):
        value = contract_rows(n.joined[:, pl.ds(at, 256)], n.grad_hidden[...]).astype(low)
        for j in range(4):
            n.skip_total[at // 64 + j] = value[j * 64 : (j + 1) * 64]

    tiles(n.joined.shape[1], 256, skip_weight_tile)
    begin(skip_ring)
    begin(out_ring)
    ticks(TICKS[19])
    spot = (lax.broadcasted_iota(jnp.int32, (8, frames), 1) + rank * frames).astype(full)
    chosen = (spot >= n.small[1]) & (spot < n.small[2])
    picker = jnp.where(chosen, 1.0, 0.0)

    def mod_sum(at):
        for part in range(2):
            n.mod_sums[0:8, pl.ds(part * width + at, 512)] = jnp.dot(
                picker, n.shift_one[pl.ds(part * frames, frames), pl.ds(at, 512)], precision=HIGHEST
            )

    tiles(width, 512, mod_sum)
    for other in range(1, RING):
        to = block(other)
        push(
            n.mod_sums.at[:, pl.ds(pl.multiple_of(to * 256, 256), 256)],
            n.sums_land.at[rank],
            n.sums_sem,
            (other - 1,),
            (to, group_rank),
        )
    sums_copies = sent[-(RING - 1) :]
    n.sums_land[rank] = n.mod_sums[:, pl.ds(pl.multiple_of(rank * 256, 256), 256)]
    ticks(TICKS[20])
    back = dot_across(n.grad_hidden[...], n.skip_held[...]).astype(low)
    n.joined_send[...] = back
    grad_joined_copies = []
    for other in (2, 1, 3):
        to = group(other)
        grad_joined_copies.append(
            push(
                n.joined_send.at[lines(slot_of(to) * frames, frames)],
                n.grad_joined.at[group_rank],
                n.grad_joined_sem,
                (other - 1,),
                (rank, to),
            )
        )
    n.grad_joined[group_rank] = n.joined_send[own_lines]
    ticks(TICKS[21])
    for copy in sums_copies:
        copy.wait_recv()
    n.sums_send[...] = jnp.sum(n.sums_land[...], axis=0).astype(low)
    n.mod_grad[rank, group_rank] = n.sums_send[...]
    group_sums = [
        push(
            n.sums_send,
            n.mod_grad.at[rank, group_rank],
            n.sums_group_sem,
            (other - 1,),
            (rank, group(other)),
        )
        for other in (2, 1, 3)
    ]
    ticks(TICKS[22])
    for copy in group_sums:
        copy.wait_recv()
    mod_spread = [
        push(
            n.mod_grad.at[rank],
            n.mod_grad.at[rank],
            n.sums_block_sem,
            (other - 1,),
            (block(other), group_rank),
        )
        for other in range(1, RING)
    ]

    ticks(5 * (2 * RING + 1))
    for ring in rings:
        ring.finish()
    for copy in mod_spread + grad_joined_copies:
        copy.wait_recv()
    gain_grad = n.mod_grad[group_rank, 0].astype(full)
    for row in range(1, ROWS):
        gain_grad = gain_grad + n.mod_grad[group_rank, row].astype(full)
    n.gain_grad[...] = gain_grad[8:16]
    for index, copy in enumerate(sent):
        if not any(copy is other for pair in list(group_copies.values())[:-1] for kind in pair for other in kind):
            copy.wait_send()
    for sems, wide in (
        (n.pair_sem, 256),
        (n.value_sem, 128),
        (n.attended_sem, 128),
        (n.grad_pair_sem, 128),
        (n.query_sem, 128),
        (n.project_sem, 256),
    ):
        for other in range(1, RING):
            to = block(other)
            where = n.project_send.at[lines(to * frames, frames), pl.ds(0, wide)]
            link(where, where, sems.at[0, to], sems.at[1, to], (to, group_rank)).wait_send()


def block_call(
    inputs,
    skipped,
    w_skip,
    w_mod,
    w_qkv,
    w_out,
    w_up,
    w_down,
    cotangent,
    own_gain,
    lengths,
    flow_steps,
):
    low, full = jnp.bfloat16, jnp.float32
    frames, width = inputs.shape
    tokens, half = ROWS * frames, 2 * frames
    columns = width // ROWS
    hidden_units = w_down.shape[0]
    joint = w_skip.shape[0]
    all_frames = RING * frames
    deep = width // RING

    held = dict(
        inputs=inputs,
        skipped=skipped,
        w_skip=w_skip,
        w_mod=w_mod,
        w_qkv=w_qkv,
        w_out=w_out,
        w_up=w_up,
        w_down=w_down,
        cotangent=cotangent,
        own_gain=own_gain,
        lengths=lengths,
        flow_steps=flow_steps,
    )
    given = dict(
        output=((frames, width), low),
        grad_joined=((ROWS, frames, joint), low),
        condition=((ROWS * 8, columns), low),
        mod_grad=((RING, ROWS, 16, 256), low),
        gain_grad=((8, columns), full),
        down_whole=((RING, hidden_units // RING, width), low),
        up_whole=((RING, deep, hidden_units), low),
        qkv_whole=((RING, deep, 3 * columns), low),
        skip_whole=((RING, joint // RING, width), low),
        out_whole=((RING, columns // RING, width), low),
    )
    buffers = dict(
        joined_own=((ROWS, frames, joint), low),
        joined=((tokens, joint), low),
        upstream=((tokens, width), low),
        skip_held=(w_skip.shape, low),
        mod_held=(w_mod.shape, low),
        out_held=((width, width), low),
        attended_all=((half, width), low),
        down_held=(w_down.shape, low),
        qkv_held=((width, 3 * columns), low),
        up_held=((width, hidden_units), low),
        small=((7, 8, 128), full),
        smalls=((ROWS, 7, 8, 128), full),
        mod_part=((ROWS * 8, 2 * width), full),
        mod_land=((1, 16, 2 * width), full),
        mod_send=((16, 2 * width), low),
        mod_cross=((16, 2 * width), low),
        gain=((8, width), full),
        cosine=((tokens, 128), full),
        sine=((tokens, 128), full),
        row_cosine=((all_frames, 128), full),
        row_sine=((all_frames, 128), full),
        chosen=((all_frames, 128), low),
        send_one=((half, width), low),
        send_two=((half, width), low),
        keep=((half, width), full),
        land_one=((4, half, width), low),
        land_two=((4, half, width), low),
        scale_one=((half, width), full),
        shift_one=((half, width), full),
        hidden=((half, width), full),
        normal_one=((half, width), full),
        spread_one=((half, 128), full),
        normal_two=((half, width), full),
        spread_two=((half, 128), full),
        grad_two=((half, width), full),
        attn_in=((tokens, width), low),
        project=((half, 3 * columns), full),
        pair_send=((RING, frames, 384), low),
        paired=((all_frames, 384), low),
        query_head=((2, all_frames, 128), low),
        key_head=((2, all_frames, 128), low),
        query_turned=((128, all_frames), low),
        shares=((2, all_frames, all_frames), low),
        attended_pair=((all_frames, 128), full),
        attended_send=((all_frames, 128), low),
        attended=((tokens, columns), low),
        ff_in=((tokens, width), low),
        activated=((tokens, hidden_units), low),
        grad_widened=((tokens, hidden_units), low),
        grad_two_low=((tokens, width), low),
        grad_pair_send=((RING, frames, 128), low),
        grad_pair=((all_frames, 128), low),
        grad_turned=((128, all_frames), low),
        key_turned=((128, all_frames), full),
        value_turned=((128, all_frames), full),
        project_send=((all_frames, 384), low),
        grad_project=((tokens, 3 * columns), low),
        grad_hidden=((tokens, width), low),
        mod_sums=((16, 2 * width), full),
        sums_land=((RING, 16, 256), full),
        sums_send=((16, 256), low),
        joined_send=((tokens, joint), low),
        down_total=((RING, hidden_units // RING, width), low),
        up_total=((RING, deep, hidden_units), low),
        qkv_total=((RING, deep, 3 * columns), low),
        skip_total=((RING, joint // RING, width), low),
        out_total=((RING, columns // RING, width), low),
        down_land=((RING - 1, hidden_units // RING, width), low),
        up_land=((RING - 1, deep, hidden_units), low),
        qkv_land=((RING - 1, deep, 3 * columns), low),
        skip_land=((RING - 1, joint // RING, width), low),
        out_land=((RING - 1, columns // RING, width), low),
        up_turn=((deep, hidden_units), low),
        qkv_turn=((deep, 3 * columns), low),
    )
    sems = dict(
        load_sem=(16,),
        joined_sem=(2, 3),
        small_sem=(2, 3),
        qkv_sem=(2, 3, 6),
        qkv_pass_sem=(2, 2, 3),
        up_sem=(2, 3),
        up_pass_sem=(2, 2),
        out_sem=(2, 3),
        attended_all_sem=(2, 3),
        mod_sem=(2, 2),
        first_sem=(2, 4, 2),
        second_sem=(2, 4, 2),
        upstream_sem=(2, 3),
        attn_sem=(2, 2),
        ff_sem=(2, 2),
        grad_two_sem=(2, 2),
        grad_hidden_sem=(2, 2),
        pair_sem=(2, RING),
        attended_sem=(2, RING),
        grad_pair_sem=(2, RING),
        query_sem=(2, RING),
        project_sem=(2, RING),
        value_sem=(2, RING),
        grad_joined_sem=(2, 3),
        sums_sem=(2, RING - 1),
        sums_group_sem=(2, 3),
        sums_block_sem=(2, RING - 1),
        down_sem=(2, 2, 2, RING - 1),
        up_ring_sem=(2, 2, 2, RING - 1),
        qkv_ring_sem=(2, 2, 2, RING - 1),
        skip_ring_sem=(2, 2, 2, RING - 1),
        out_ring_sem=(2, 2, 2, RING - 1),
        turn_sem=(2, 2, 3),
        whole_sem=(5, 2, RING),
    )
    names = [*held, *given, *buffers, *sems]
    vmem = pl.BlockSpec(memory_space=pltpu.VMEM)
    anywhere = pl.BlockSpec(memory_space=pl.ANY)
    return pl.pallas_call(
        functools.partial(block_kernel, names),
        out_shape=[jax.ShapeDtypeStruct(*spec) for spec in given.values()],
        in_specs=[anywhere] * 9 + [vmem] + [pl.BlockSpec(memory_space=pltpu.SMEM)] * 2,
        out_specs=[anywhere if name.endswith("_whole") else vmem for name in given],
        scratch_shapes=[pltpu.VMEM(*spec) for spec in buffers.values()]
        + [pltpu.SemaphoreType.DMA(shape) for shape in sems.values()],
        compiler_params=pltpu.CompilerParams(
            collective_id=0,
            has_side_effects=True,
            vmem_limit_bytes=63 * 1024 * 1024,
        ),
    )(*held.values())


def finish_kernel(
    joined_ref,
    condition_ref,
    mod_ref,
    gain_ref,
    down_ref,
    up_ref,
    qkv_ref,
    skip_ref,
    out_ref,
    grad_inputs,
    grad_skipped,
    grad_skip,
    grad_mod,
    grad_qkv,
    grad_out,
    grad_gain,
    grad_up,
    grad_down,
):
    full = jnp.float32
    wide = joined_ref.shape[2]
    for r in range(ROWS):
        target = (grad_inputs, grad_skipped)[r // 2]
        target[:, pl.ds((r % 2) * wide, wide)] = joined_ref[r].astype(full)
    grad_down[...] = down_ref[0].astype(full)
    grad_skip[...] = skip_ref[0].astype(full)
    grad_out[...] = out_ref[0].astype(full)
    grad_gain[...] = gain_ref[0:1]
    deep, wide = up_ref.shape[1] // ROWS, up_ref.shape[2]
    for r in range(ROWS):
        rows = pl.ds(r * deep, deep)
        grad_up[:, pl.ds(r * wide, wide)] = up_ref[0, rows].astype(full)
        for side in range(2):
            for kind in range(3):
                source = qkv_ref[0, rows, pl.ds((side * 3 + kind) * 128, 128)]
                at = kind * (ROWS * 256) + r * 256 + side * 128
                grad_qkv[:, pl.ds(at, 128)] = source.astype(full)
    sums = [mod_ref[0, r].astype(full)[0:8] for r in (0, 2, 1, 3)]
    grad_mod[...] = contract_rows(
        condition_ref[...], jnp.concatenate(sums, axis=0).astype(jnp.bfloat16)
    )


def finish_call(joined, condition, mod, gain, down, up, qkv, skip, out):
    full = jnp.float32
    frames, wide = joined.shape[1:]
    columns = condition.shape[1]

    def first(shape):
        return pl.BlockSpec((1,) + shape[1:], lambda i: (i,) + (0,) * (len(shape) - 1))

    def rows(count, width):
        return jax.ShapeDtypeStruct((count, width), full), pl.BlockSpec(
            (count // RING, width), lambda i: (i, 0)
        )

    deep = up.shape[1] // ROWS
    results = [
        rows(frames, 2 * wide),
        rows(frames, 2 * wide),
        rows(RING * skip.shape[1], skip.shape[2]),
        (
            jax.ShapeDtypeStruct((columns, RING * mod.shape[3]), full),
            pl.BlockSpec((columns, mod.shape[3]), lambda i: (0, i)),
        ),
        rows(RING * deep, ROWS * qkv.shape[2]),
        rows(RING * out.shape[1], out.shape[2]),
        (jax.ShapeDtypeStruct((1, columns), full), pl.BlockSpec((1, columns), lambda i: (0, 0))),
        rows(RING * deep, ROWS * up.shape[2]),
        rows(RING * down.shape[1], down.shape[2]),
    ]
    return pl.pallas_call(
        finish_kernel,
        grid=(RING,),
        out_shape=[shape for shape, _ in results],
        in_specs=[
            pl.BlockSpec((ROWS, frames // RING, wide), lambda i: (0, i, 0)),
            pl.BlockSpec(condition.shape, lambda i: (0, 0)),
            first(mod.shape),
            pl.BlockSpec(gain.shape, lambda i: (0, 0)),
            first(down.shape),
            first(up.shape),
            first(qkv.shape),
            first(skip.shape),
            first(out.shape),
        ],
        out_specs=[spec for _, spec in results],
        compiler_params=pltpu.CompilerParams(vmem_limit_bytes=62 * 1024 * 1024),
    )(joined, condition, mod, gain, down, up, qkv, skip, out)


def per_device_block(
    inputs,
    skipped,
    w_skip,
    w_mod,
    w_qkv,
    w_out,
    ff_gain,
    w_up,
    w_down,
    cotangent,
    lengths,
    flow_steps,
):
    gain = jnp.broadcast_to(ff_gain.astype(jnp.float32)[None], (8, ff_gain.shape[0]))
    output, *rest = block_call(
        inputs[0],
        skipped[0],
        w_skip,
        w_mod,
        w_qkv,
        w_out,
        w_up,
        w_down,
        cotangent[0],
        gain,
        lengths,
        flow_steps,
    )
    grad_inputs, grad_skipped, skip, mod, qkv, out, gain, up, down = finish_call(*rest)
    return (
        output[None],
        grad_inputs[None],
        grad_skipped[None],
        skip,
        mod,
        qkv,
        out,
        gain[0],
        up,
        down,
    )


def solution(mesh):
    placed = (
        P("grp", "blk", None),
        P("grp", "blk", None),
        P("grp", None),
        P("grp", None),
        P("grp", None),
        P("grp", None),
        P("grp"),
        P("grp", None),
        P("grp", None),
        P("grp", "blk", None),
        P("grp", None),
        P("grp", None),
    )
    body = per_device
    if mesh.shape["blk"] == RING and mesh.shape["grp"] == ROWS:
        body = per_device_block
    return jax.shard_map(
        body,
        mesh=mesh,
        in_specs=placed,
        out_specs=(
            P("grp", "blk", None),
            P("grp", "blk", None),
            P("grp", "blk", None),
            P("grp", None),
            P("grp", None),
            P("grp", None),
            P("grp", None),
            P("grp"),
            P("grp", None),
            P("grp", None),
        ),
        check_vma=False,
    )
```

```python
import functools
import math
import types

import jax
import jax.numpy as jnp
from jax import lax
from jax.experimental import pallas as pl
from jax.experimental.pallas import tpu as pltpu
from jax.sharding import PartitionSpec as P

HEADS = 16
HEAD_DIM = 64
STEPS = 32


EPSILON = 1e-06
NEGATIVE = -1e30
HIGHEST = lax.Precision.HIGHEST
MESH = pl.DeviceIdType.MESH
RING = 8
ROWS = 4


def from_behind(block, axis, distance):
    devices = range(lax.axis_size(axis))
    route = [((i - distance) % len(devices), i) for i in devices]
    return lax.ppermute(block, axis, route)


def layout(lengths_row, frames):
    end_frame = jnp.cumsum(lengths_row)
    start_frame = end_frame - lengths_row
    segment = jnp.sum((frames[:, None] >= end_frame[None, :]).astype(jnp.int32), axis=1)
    chosen = segment[:, None] == jnp.arange(lengths_row.shape[0], dtype=jnp.int32)[None, :]
    position = frames - jnp.sum(jnp.where(chosen, start_frame[None, :], 0), axis=1)
    return (segment, position)


def flow_condition(steps_row, model_width):
    half_width = model_width // 2
    rate_table = jnp.exp(
        -math.log(10000.0) * jnp.arange(half_width, dtype=jnp.float32) / half_width
    )
    angles = 1000.0 * (steps_row.astype(jnp.float32) / STEPS)[:, None] * rate_table[None, :]
    return jax.nn.silu(jnp.concatenate([jnp.sin(angles), jnp.cos(angles)], axis=1))


def rotation_tables(position, head_width):
    half_width = head_width // 2
    rate_table = jnp.exp(
        -math.log(10000.0) * jnp.arange(half_width, dtype=jnp.float32) / half_width
    )
    angles = position.astype(jnp.float32)[:, None] * rate_table[None, :]
    return (jnp.cos(angles)[:, None, :], jnp.sin(angles)[:, None, :], half_width)


def rotate(head_block, position):
    cosine_part, sine_part, half_width = rotation_tables(position, head_block.shape[-1])
    first_half = head_block[..., :half_width]
    second_half = head_block[..., half_width:]
    return jnp.concatenate(
        [
            first_half * cosine_part - second_half * sine_part,
            second_half * cosine_part + first_half * sine_part,
        ],
        axis=-1,
    )


def rotate_back(head_block, position):
    cosine_part, sine_part, half_width = rotation_tables(position, head_block.shape[-1])
    first_half = head_block[..., :half_width]
    second_half = head_block[..., half_width:]
    return jnp.concatenate(
        [
            first_half * cosine_part + second_half * sine_part,
            second_half * cosine_part - first_half * sine_part,
        ],
        axis=-1,
    )


def normalize(hidden):
    centred = hidden - jnp.mean(hidden, axis=-1, keepdims=True)
    scaled = lax.rsqrt(jnp.mean(centred * centred, axis=-1, keepdims=True) + EPSILON)
    return (centred * scaled, scaled)


def norm_back(grad_normal, normal, scaled):
    centred_grad = grad_normal - jnp.mean(grad_normal, axis=-1, keepdims=True)
    return scaled * (centred_grad - normal * jnp.mean(grad_normal * normal, axis=-1, keepdims=True))


def exact_gelu(values_in):
    return jax.nn.gelu(values_in, approximate=False)


def contract_rows(left_side, right_side):
    return lax.dot_general(
        left_side, right_side, (((0,), (0,)), ((), ())), preferred_element_type=jnp.float32
    )


def heads_of(flat_block):
    return flat_block.reshape(flat_block.shape[0], HEADS, HEAD_DIM)


def per_device(
    inputs,
    skipped,
    w_skip,
    w_mod,
    w_qkv,
    w_out,
    ff_gain,
    w_up,
    w_down,
    cotangent,
    lengths,
    flow_steps,
):
    w_skip, w_mod, w_qkv, w_out, ff_gain, w_up, w_down = (
        lax.all_gather(w_skip, "grp", axis=0, tiled=True),
        lax.all_gather(w_mod, "grp", axis=0, tiled=True),
        lax.all_gather(w_qkv, "grp", axis=0, tiled=True),
        lax.all_gather(w_out, "grp", axis=0, tiled=True),
        lax.all_gather(ff_gain, "grp", axis=0, tiled=True),
        lax.all_gather(w_up, "grp", axis=0, tiled=True),
        lax.all_gather(w_down, "grp", axis=0, tiled=True),
    )
    frame_count = inputs.shape[1]
    model_width = inputs.shape[2]
    cycle_size = lax.axis_size("blk")
    device_rank = lax.axis_index("blk")
    score_scale = HEAD_DIM ** (-0.5)
    local_frames = jnp.arange(frame_count, dtype=jnp.int32)
    lengths_row = lengths[0]
    own_segment, own_position = layout(lengths_row, device_rank * frame_count + local_frames)

    def segment_of(source):
        return layout(lengths_row, source * frame_count + local_frames)[0]

    def scored(query_block, key_block, query_segment, key_segment):
        raw_scores = (
            jnp.einsum(
                "qhd,khd->hqk",
                heads_of(query_block),
                heads_of(key_block),
                preferred_element_type=jnp.float32,
            )
            * score_scale
        )
        allowed = (query_segment[:, None] == key_segment[None, :])[None]
        return (raw_scores, allowed)

    joined = jnp.concatenate([inputs[0], skipped[0]], axis=1)
    hidden = jnp.dot(joined, w_skip, preferred_element_type=jnp.float32)
    condition = flow_condition(flow_steps[0], model_width).astype(jnp.bfloat16)
    modulation = jnp.dot(condition, w_mod, preferred_element_type=jnp.float32)
    picker = (
        own_segment[:, None] == jnp.arange(lengths_row.shape[0], dtype=jnp.int32)[None, :]
    ).astype(jnp.float32)
    per_frame = jnp.dot(picker, modulation, precision=HIGHEST)
    scale_one = 1.0 + per_frame[:, :model_width]
    normal_one, spread_one = normalize(hidden)
    attn_in = (normal_one * scale_one + per_frame[:, model_width:]).astype(jnp.bfloat16)
    project = jnp.dot(attn_in, w_qkv, preferred_element_type=jnp.float32).reshape(
        frame_count, 3, HEADS, HEAD_DIM
    )
    queries = (
        rotate(project[:, 0], own_position).astype(jnp.bfloat16).reshape(frame_count, model_width)
    )
    keys_own = (
        rotate(project[:, 1], own_position).astype(jnp.bfloat16).reshape(frame_count, model_width)
    )
    values_own = project[:, 2].astype(jnp.bfloat16).reshape(frame_count, model_width)

    def forward_turn(turn_index, carried):
        key_now, value_now, running_top, running_total, running_sum = carried
        source = (device_rank - turn_index) % cycle_size
        raw_scores, allowed = scored(queries, key_now, own_segment, segment_of(source))
        raw_scores = jnp.where(allowed, raw_scores, NEGATIVE)
        new_top = jnp.maximum(running_top, jnp.max(raw_scores, axis=2, keepdims=True))
        weights = jnp.where(allowed, jnp.exp(raw_scores - new_top), 0.0)
        shrink = jnp.exp(running_top - new_top)
        running_total = running_total * shrink + jnp.sum(weights, axis=2, keepdims=True)
        running_sum = running_sum * shrink + jnp.einsum(
            "hqk,khd->hqd",
            weights.astype(jnp.bfloat16),
            heads_of(value_now),
            preferred_element_type=jnp.float32,
        )
        key_now, value_now = from_behind((key_now, value_now), "blk", 1)
        return (key_now, value_now, new_top, running_total, running_sum)

    initial = (
        keys_own,
        values_own,
        jnp.full((HEADS, frame_count, 1), NEGATIVE, jnp.float32),
        jnp.zeros((HEADS, frame_count, 1), jnp.float32),
        jnp.zeros((HEADS, frame_count, HEAD_DIM), jnp.float32),
    )
    finished = lax.fori_loop(0, cycle_size, forward_turn, initial)
    running_top, running_total, running_sum = (finished[2], finished[3], finished[4])
    attended = jnp.transpose(running_sum / running_total, (1, 0, 2)).reshape(
        frame_count, model_width
    )
    log_total = (running_top + jnp.log(running_total))[:, :, 0]
    attended_low = attended.astype(jnp.bfloat16)
    hidden_two = hidden + jnp.dot(attended_low, w_out, preferred_element_type=jnp.float32)
    normal_two, spread_two = normalize(hidden_two)
    gain_vector = ff_gain.astype(jnp.float32)
    ff_in = (normal_two * gain_vector).astype(jnp.bfloat16)
    widened = jnp.dot(ff_in, w_up, preferred_element_type=jnp.float32)
    activated, gelu_back = jax.vjp(exact_gelu, widened)
    activated_low = activated.astype(jnp.bfloat16)
    output = (
        hidden_two + jnp.dot(activated_low, w_down, preferred_element_type=jnp.float32)
    ).astype(jnp.bfloat16)
    upstream = cotangent[0]
    grad_down = contract_rows(activated_low, upstream)
    grad_activated = jnp.dot(upstream, w_down.T, preferred_element_type=jnp.float32)
    grad_widened = gelu_back(grad_activated)[0].astype(jnp.bfloat16)
    grad_up = contract_rows(ff_in, grad_widened)
    grad_ff_in = jnp.dot(grad_widened, w_up.T, preferred_element_type=jnp.float32)
    grad_gain = jnp.sum(grad_ff_in * normal_two, axis=0)
    grad_hidden_two = upstream.astype(jnp.float32) + norm_back(
        grad_ff_in * gain_vector, normal_two, spread_two
    )
    grad_two_low = grad_hidden_two.astype(jnp.bfloat16)
    grad_out = contract_rows(attended_low, grad_two_low)
    grad_attended = jnp.dot(grad_two_low, w_out.T, preferred_element_type=jnp.float32).astype(
        jnp.bfloat16
    )
    delta = jnp.transpose(jnp.sum(heads_of(grad_attended.astype(jnp.float32) * attended), axis=2))
    zero_grad = jnp.zeros((frame_count, model_width), jnp.float32)

    def pair_terms(
        query_block,
        upstream_block,
        key_block,
        value_block,
        total_block,
        delta_block,
        query_segment,
        key_segment,
    ):
        raw_scores, allowed = scored(query_block, key_block, query_segment, key_segment)
        prob_block = jnp.where(allowed, jnp.exp(raw_scores - total_block[:, :, None]), 0.0)
        value_term = jnp.einsum(
            "hqk,qhd->khd",
            prob_block.astype(jnp.bfloat16),
            heads_of(upstream_block),
            preferred_element_type=jnp.float32,
        ).reshape(frame_count, model_width)
        prob_grad = jnp.einsum(
            "qhd,khd->hqk",
            heads_of(upstream_block),
            heads_of(value_block),
            preferred_element_type=jnp.float32,
        )
        score_grad = (prob_block * (prob_grad - delta_block[:, :, None])).astype(jnp.bfloat16)
        query_term = (
            jnp.einsum(
                "hqk,khd->qhd", score_grad, heads_of(key_block), preferred_element_type=jnp.float32
            ).reshape(frame_count, model_width)
            * score_scale
        )
        key_term = (
            jnp.einsum(
                "hqk,qhd->khd",
                score_grad,
                heads_of(query_block),
                preferred_element_type=jnp.float32,
            ).reshape(frame_count, model_width)
            * score_scale
        )
        return (query_term, key_term, value_term)

    def keys_turn(turn_index, carried):
        key_now, value_now, key_grad, value_grad, query_grad = carried
        source = (device_rank - turn_index) % cycle_size
        query_term, key_term, value_term = pair_terms(
            queries,
            grad_attended,
            key_now,
            value_now,
            log_total,
            delta,
            own_segment,
            segment_of(source),
        )
        key_now, value_now = from_behind((key_now, value_now), "blk", 1)
        key_grad, value_grad = (
            from_behind((key_grad + key_term).astype(jnp.bfloat16), "blk", 1).astype(jnp.float32),
            from_behind((value_grad + value_term).astype(jnp.bfloat16), "blk", 1).astype(
                jnp.float32
            ),
        )
        return (key_now, value_now, key_grad, value_grad, query_grad + query_term)

    done = lax.fori_loop(
        0, cycle_size, keys_turn, (keys_own, values_own, zero_grad, zero_grad, zero_grad)
    )
    key_grad, value_grad, query_grad = (done[2], done[3], done[4])
    grad_project = jnp.concatenate(
        [
            rotate_back(heads_of(query_grad), own_position).reshape(frame_count, model_width),
            rotate_back(heads_of(key_grad), own_position).reshape(frame_count, model_width),
            value_grad,
        ],
        axis=1,
    ).astype(jnp.bfloat16)
    grad_qkv = contract_rows(attn_in, grad_project)
    grad_attn_in = jnp.dot(grad_project, w_qkv.T, preferred_element_type=jnp.float32)
    mod_terms = jnp.concatenate([grad_attn_in * normal_one, grad_attn_in], axis=1)
    grad_modulation = jnp.dot(picker.T, mod_terms, precision=HIGHEST)
    grad_mod = jnp.dot(condition.astype(jnp.float32).T, grad_modulation, precision=HIGHEST)
    grad_hidden = grad_hidden_two + norm_back(grad_attn_in * scale_one, normal_one, spread_one)
    grad_hidden_low = grad_hidden.astype(jnp.bfloat16)
    grad_skip_weight = contract_rows(joined, grad_hidden_low)
    grad_joined = jnp.dot(grad_hidden_low, w_skip.T, preferred_element_type=jnp.float32)
    shards = (
        lax.psum_scatter(
            grad_skip_weight.astype(jnp.bfloat16), "grp", scatter_dimension=0, tiled=True
        ).astype(jnp.float32),
        lax.psum_scatter(
            grad_mod.astype(jnp.bfloat16), "grp", scatter_dimension=0, tiled=True
        ).astype(jnp.float32),
        lax.psum_scatter(
            grad_qkv.astype(jnp.bfloat16), "grp", scatter_dimension=0, tiled=True
        ).astype(jnp.float32),
        lax.psum_scatter(
            grad_out.astype(jnp.bfloat16), "grp", scatter_dimension=0, tiled=True
        ).astype(jnp.float32),
        lax.psum_scatter(
            grad_gain.astype(jnp.bfloat16), "grp", scatter_dimension=0, tiled=True
        ).astype(jnp.float32),
        lax.psum_scatter(
            grad_up.astype(jnp.bfloat16), "grp", scatter_dimension=0, tiled=True
        ).astype(jnp.float32),
        lax.psum_scatter(
            grad_down.astype(jnp.bfloat16), "grp", scatter_dimension=0, tiled=True
        ).astype(jnp.float32),
    )
    totals = lax.psum(
        (shards[0], shards[1], shards[2], shards[3], shards[4], shards[5], shards[6]), "blk"
    )
    return (
        output[None],
        grad_joined[:, :model_width][None],
        grad_joined[:, model_width:][None],
        totals[0],
        totals[1],
        totals[2],
        totals[3],
        totals[4],
        totals[5],
        totals[6],
    )


def dot_plain(left_side, right_side):
    return jnp.dot(left_side, right_side, preferred_element_type=jnp.float32)


def dot_across(left_side, right_side):
    return lax.dot_general(
        left_side, right_side, (((1,), (1,)), ((), ())), preferred_element_type=jnp.float32
    )


def ring_place(rank):
    odd = lax.rem(rank, 2)
    return (1 - odd) * (rank // 2) + odd * ((15 - rank) // 2)


def ring_rank(place):
    upper = place // 4
    return (1 - upper) * (2 * place) + upper * (15 - 2 * place)


TICKS = (2, 0, 0, 0, 0, 2, 0, 0, 0, 0, 2, 0, 0, 2, 0, 2, 3, 0, 0, 6, 3, 2, 2)

TILE = 128
UNROLLED = 4
MAIN_MIB = 55
LAST_MIB = 24
RING_TILE = 32


class Ring:
    def __init__(self, part, land, sems, rank, group_rank, turn=None):
        self.part, self.land, self.sems = part, land, sems
        self.rank, self.group_rank = rank, group_rank
        self.place = ring_place(rank)
        self.half = part.shape[1] // 2
        self.copies = {}
        self.turns, self.turn = [], turn

    def block_at(self, offset):
        return ring_rank(lax.rem(self.place + offset + 2 * RING, RING))

    def rows(self, way):
        return pl.ds(way * self.half, self.half)

    def send(self, kind, step, way, source, target):
        to = ring_rank(lax.rem(self.place + (1 if way == 0 else RING - 1), RING))
        copy = pltpu.make_async_remote_copy(
            src_ref=source,
            dst_ref=target,
            send_sem=self.sems.at[kind, 0, way, step],
            recv_sem=self.sems.at[kind, 1, way, step],
            device_id=(to, self.group_rank),
            device_id_type=MESH,
        )
        copy.start()
        self.copies[kind, step, way] = copy

    def sum_step(self, step):
        if step == 1:
            for way in range(2):
                self.copies[0, 0, way].wait_send()
        for way in range(2):
            block = self.block_at((-1 if way == 0 else 1) * (step + 1))
            rows = self.rows(way)
            if step > 0:
                self.copies[0, step - 1, way].wait_recv()
                tile = min(self.half, RING_TILE)

                def add(i, carry, way=way, block=block, tile=tile):
                    at = pl.ds(pl.multiple_of(way * self.half + i * tile, tile), tile)
                    total = self.part[block, at].astype(jnp.float32) + self.land[
                        step - 1, at
                    ].astype(jnp.float32)
                    self.land[step - 1, at] = total.astype(jnp.bfloat16)
                    return carry

                lax.fori_loop(0, self.half // tile, add, 0)
            if step < RING - 1:
                source = self.part.at[block, rows] if step == 0 else self.land.at[step - 1, rows]
                self.send(0, step, way, source, self.land.at[step, rows])

    def spread_step(self, step):
        if step == 0:
            self.close_sum()
        for way in range(2):
            block = self.block_at((-1 if way == 0 else 1) * step)
            rows = self.rows(way)
            if step > 0:
                self.copies[1, step - 1, way].wait_recv()
            if step < RING - 1:
                target = self.part.at[block, rows]
                self.send(1, step, way, target, target)

    def begin(self):
        self.sum_step(0)
        self.left = [functools.partial(self.sum_step, step) for step in range(1, RING)]
        self.left += [functools.partial(self.spread_step, step) for step in range(RING)]
        if self.turn is not None:
            self.left.insert(RING - 1, self.turn_out)

    def turn_out(self):
        place, sems = self.turn
        deep = self.part.shape[1] // ROWS

        def rows(group):
            return pl.ds(pl.multiple_of(group * deep, deep), deep)

        for other in (2, 1, 3):
            to = lax.rem(self.group_rank + other, ROWS)
            copy = pltpu.make_async_remote_copy(
                src_ref=self.land.at[RING - 2, rows(to)],
                dst_ref=place.at[rows(self.group_rank)],
                send_sem=sems.at[0, other - 1],
                recv_sem=sems.at[1, other - 1],
                device_id=(self.rank, to),
                device_id_type=MESH,
            )
            copy.start()
            self.turns.append(copy)
        place[rows(self.group_rank)] = self.land[RING - 2, rows(self.group_rank)]

    def close_sum(self):
        for copy in self.turns:
            copy.wait_recv()
        self.part[self.rank] = self.land[RING - 2] if self.turn is None else self.turn[0][...]

    def finish(self):
        for copy in self.turns:
            copy.wait_send()
        for (kind, step, _), copy in self.copies.items():
            if kind or step:
                copy.wait_send()


def block_kernel(names, *refs):
    n = types.SimpleNamespace(**dict(zip(names, refs)))
    low, full = jnp.bfloat16, jnp.float32
    rank, group_rank = lax.axis_index("blk"), lax.axis_index("grp")
    core, chip = lax.rem(group_rank, 2), group_rank // 2
    sibling = (rank, group_rank + 1 - 2 * core)
    across = (rank, group_rank + 2 - 4 * chip)
    frames, width = n.cotangent.shape
    half = 2 * frames
    columns = width // ROWS
    mine, theirs = core * half, (1 - core) * half
    own_slot = 2 * core + chip
    pair_row, pair_side = rank // 2, lax.rem(rank, 2)
    sent = []

    def lines(offset, size):
        return pl.ds(pl.multiple_of(offset, min(size, 128)), size)

    def slot_of(row):
        return 2 * lax.rem(row, 2) + row // 2

    def row_of(slot):
        return 2 * lax.rem(slot, 2) + slot // 2

    def group(other):
        return lax.rem(group_rank + other, ROWS)

    def block(other):
        return lax.rem(rank + other, RING)

    def link(source, target, send_sem, recv_sem, device):
        return pltpu.make_async_remote_copy(
            src_ref=source,
            dst_ref=target,
            send_sem=send_sem,
            recv_sem=recv_sem,
            device_id=device,
            device_id_type=MESH,
        )

    def push(source, target, sems, index, device):
        copy = link(source, target, sems.at[(0,) + index], sems.at[(1,) + index], device)
        copy.start()
        sent.append(copy)
        return copy

    def load(source, target, index):
        copy = pltpu.make_async_copy(source, target, n.load_sem.at[index])
        copy.start()
        return copy

    def tiles(count, tile, body):
        if count // tile <= UNROLLED:
            for i in range(count // tile):
                body(i * tile)
            return

        def step(i, carry):
            body(pl.multiple_of(i * tile, tile))
            return carry

        lax.fori_loop(0, count // tile, step, 0)

    joined_loads = [
        load((n.inputs, n.skipped)[t // 2].at[:, pl.ds((t % 2) * 512, 512)], n.joined_own.at[t], t)
        for t in range(ROWS)
    ]
    upstream_load = load(n.cotangent, n.upstream.at[lines(own_slot * frames, frames)], 4)
    skip_load = load(n.w_skip, n.skip_held, 5)
    mod_load = load(n.w_mod, n.mod_held, 6)
    out_place = n.out_held.at[lines(group_rank * columns, columns)]
    out_load = load(n.w_out, out_place, 7)
    down_load = load(n.w_down, n.down_held, 8)
    pieces = [(side, kind) for side in range(2) for kind in range(3)]

    def qkv_piece(target, side, kind, first, count):
        at = pl.multiple_of(kind * width + target * columns + side * 128, 128)
        return n.w_qkv.at[lines(first, count), pl.ds(at, 128)]

    def qkv_place(side, kind, first, count):
        rows = lines(group_rank * columns + first, count)
        return n.qkv_held.at[rows, pl.ds((side * 3 + kind) * 128, 128)]

    qkv_loads = [
        load(qkv_piece(group_rank, *piece, 0, columns), qkv_place(*piece, 0, columns), 9 + i)
        for i, piece in enumerate(pieces)
    ]
    hidden_units = n.up_held.shape[1]

    def up_piece(target):
        return n.w_up.at[:, pl.ds(pl.multiple_of(target * hidden_units, 128), hidden_units)]

    up_place = n.up_held.at[lines(group_rank * columns, columns)]
    up_load = load(up_piece(group_rank), up_place, 15)

    def small_tables():
        down = lax.broadcasted_iota(jnp.int32, (8, 128), 0)
        across_lanes = lax.rem(lax.broadcasted_iota(jnp.int32, (8, 128), 1), 64)
        zero = jnp.zeros((8, 128), full)
        step_tile, start_tile, end_tile = zero, zero, zero
        start_lane, end_lane = zero + 1e9, zero
        start = jnp.int32(0)
        for u in range(8):
            end = start + n.lengths[0, u]
            here = down == u
            lane_here = (across_lanes == u) | (across_lanes == u + 8)
            step_tile = jnp.where(here, n.flow_steps[0, u].astype(full), step_tile)
            start_tile = jnp.where(here, start.astype(full), start_tile)
            end_tile = jnp.where(here, end.astype(full), end_tile)
            start_lane = jnp.where(lane_here, start.astype(full), start_lane)
            end_lane = jnp.where(lane_here, end.astype(full), end_lane)
            start = end
        tables = (step_tile, start_tile, end_tile, start_lane, end_lane)
        for i, tile in enumerate(tables):
            n.small[i] = tile
        gain = jnp.broadcast_to(n.own_gain[...].astype(full).reshape(1, columns), (8, columns))
        n.small[5] = gain[:, 0:128]
        n.small[6] = gain[:, 128:256]

    barrier = pltpu.get_barrier_semaphore()
    for other in range(1, ROWS):
        pl.semaphore_signal(barrier, inc=1, device_id=(rank, group(other)), device_id_type=MESH)
    for other in range(1, RING):
        pl.semaphore_signal(barrier, inc=1, device_id=(block(other), group_rank), device_id_type=MESH)
    small_tables()
    for copy in joined_loads:
        copy.wait()
    pl.semaphore_wait(barrier, ROWS + RING - 2)

    joined_place = n.joined.at[lines(own_slot * frames, frames)]
    joined_sends = [
        push(n.joined_own.at[group(o)], joined_place, n.joined_sem, (o - 1,), (rank, group(o)))
        for o in (2, 1, 3)
    ]
    small_sends = [
        push(n.small, n.smalls.at[group_rank], n.small_sem, (o - 1,), (rank, group(o)))
        for o in (2, 1, 3)
    ]
    n.joined[lines(own_slot * frames, frames)] = n.joined_own[group_rank]
    n.smalls[group_rank] = n.small[...]
    for copy in small_sends:
        copy.wait_recv()

    steps = jnp.concatenate([n.smalls[(0, 2, 1, 3)[s], 0] for s in range(ROWS)], axis=0)
    steps = jnp.concatenate([steps, steps], axis=1)
    lane = lax.broadcasted_iota(jnp.int32, steps.shape, 1) + lax.rem(group_rank, 2) * columns
    rate = jnp.exp(-math.log(10000.0) * lane.astype(full) / (width // 2))
    angles = 1000.0 * (steps / STEPS) * rate
    turned = jnp.where(group_rank >= 2, jnp.cos(angles), jnp.sin(angles))
    n.condition[...] = (turned / (1.0 + jnp.exp(-turned))).astype(low)
    mod_load.wait()

    def mod_tile(at):
        where = pl.ds(at, 512)
        n.mod_part[:, where] = dot_plain(n.condition[...], n.mod_held[:, where])

    tiles(2 * width, 512, mod_tile)
    mod_first = push(
        n.mod_part.at[pl.ds(pl.multiple_of(16 * (1 - core), 16), 16)], n.mod_land.at[0], n.mod_sem, (0,), sibling
    )

    gains = [n.smalls[r, 5 + i][0:1] for r in range(ROWS) for i in range(2)]
    n.gain[...] = jnp.broadcast_to(jnp.concatenate(gains, axis=1), n.gain.shape)

    def picked(row, first, count):
        spot = (lax.broadcasted_iota(jnp.int32, (count, 128), 0) + first).astype(full)
        return (spot >= n.smalls[row, 3][0:1]) & (spot < n.smalls[row, 4][0:1]), spot

    lanes = lax.broadcasted_iota(jnp.int32, (frames, 128), 1)
    turn_rate = jnp.exp(-math.log(10000.0) * lax.rem(lanes, 32).astype(full) / 32)
    turn_sign = jnp.where(lax.rem(lanes, 64) < 32, -1.0, 1.0)

    def turn_tables(row, first, cosine, sine, at):
        chosen, spot = picked(row, first, frames)
        start = jnp.where(chosen & (lanes < 8), n.smalls[row, 3][0:1], 0.0)
        position = spot - jnp.sum(start, axis=1, keepdims=True)
        angle = position * turn_rate
        cosine[at] = jnp.cos(angle)
        sine[at] = jnp.sin(angle) * turn_sign

    def swapped(value):
        ahead = pltpu.roll(value, 96, 1)
        behind = pltpu.roll(value, 32, 1)
        return jnp.where(lax.rem(lanes, 64) < 32, ahead, behind)

    def partial_sum(index, left_ref, right_tile):
        def to_send(at):
            n.send_one[:, pl.ds(at, 256)] = right_tile(left_ref[lines(theirs, half)], at).astype(low)

        def to_keep(at):
            n.keep[:, pl.ds(at, 256)] = right_tile(left_ref[lines(mine, half)], at)

        if index > 0:
            for copy in group_copies[index - 1][0]:
                copy.wait_send()
        tiles(width, 256, to_send)
        first = [
            push(
                n.send_one.at[pl.ds(k * frames, frames)],
                n.land_one.at[index, pl.ds(k * frames, frames)],
                n.first_sem,
                (index, k),
                sibling,
            )
            for k in range(2)
        ]
        tiles(width, 256, to_keep)
        return first

    def cross_sum(index, first):
        if index > 0:
            for copy in group_copies[index - 1][1]:
                copy.wait_send()
        second = []
        for k in range(2):
            first[k].wait_recv()

            def add(at, k=k):
                where = pl.ds(k * frames + at, TILE)
                total = n.keep[where] + n.land_one[index, where].astype(full)
                n.keep[where] = total
                n.send_two[where] = total.astype(low)

            tiles(frames, TILE, add)
            second.append(
                push(
                    n.send_two.at[pl.ds(k * frames, frames)],
                    n.land_two.at[index, pl.ds(k * frames, frames)],
                    n.second_sem,
                    (index, k),
                    across,
                )
            )
        group_copies[index] = (first, second)
        return second

    group_copies = {}

    down_ring, up_ring, out_ring, qkv_ring, skip_ring = rings = [
        Ring(part, land, sems, rank, group_rank, turn)
        for part, land, sems, turn in (
            (n.down_total, n.down_land, n.down_sem, None),
            (n.up_total, n.up_land, n.up_ring_sem, (n.up_turn, n.turn_sem.at[0])),
            (n.out_total, n.out_land, n.out_ring_sem, None),
            (n.qkv_total, n.qkv_land, n.qkv_ring_sem, (n.qkv_turn, n.turn_sem.at[1])),
            (n.skip_total, n.skip_land, n.skip_ring_sem, None),
        )
    ]
    running = []

    def begin(ring):
        ring.begin()
        running.append(ring)

    def ticks(count):
        for _ in range(count):
            if running:
                ring = running.pop(0)
                ring.left.pop(0)()
                if ring.left:
                    running.append(ring)

    def mean(value):
        return jnp.mean(value, axis=-1, keepdims=True)

    def share(buffer, k, sems):
        where = lines(mine + k * frames, frames)
        return push(buffer.at[where], buffer.at[where], sems, (k,), sibling)

    skip_load.wait()
    for copy in joined_sends:
        copy.wait_recv()

    side_y, side_z = lax.rem(rank, 2), lax.rem(rank // 2, 2)
    to_y, to_z = 1 - 2 * side_y, 2 - 4 * side_z
    beside = (rank + to_y, group_rank)
    around = (beside, (rank + to_z, group_rank), (rank + to_y + to_z, group_rank))
    part_rows = columns // 2
    few_rows = columns // 4
    first_row = (2 * side_z + side_y) * few_rows
    over_x = (group_rank + 2 - 4 * chip, 2 * (1 - chip) + 1 - core)
    qkv_sends = [
        [
            push(
                qkv_piece(to, *piece, first_row, few_rows),
                qkv_place(*piece, first_row, few_rows),
                n.qkv_sem,
                (i, j),
                (rank, to),
            )
            for j, piece in enumerate(pieces)
        ]
        for i, to in enumerate(over_x)
    ]
    qkv_sends.append(
        [
            push(
                qkv_piece(sibling[1], *piece, 0, columns),
                qkv_place(*piece, 0, columns),
                n.qkv_sem,
                (2, j),
                sibling,
            )
            for j, piece in enumerate(pieces)
        ]
    )

    def skip_tile(left, at):
        return dot_plain(left, n.skip_held[:, pl.ds(at, 256)])

    first = partial_sum(0, n.joined, skip_tile)
    mod_first.wait_recv()
    mod_mine = n.mod_part[pl.ds(pl.multiple_of(16 * core, 16), 16)] + n.mod_land[0]
    n.mod_send[...] = mod_mine.astype(low)
    mod_second = push(n.mod_send, n.mod_cross, n.mod_sem, (1,), across)
    second = cross_sum(0, first)
    own_lines = lines(own_slot * frames, frames)
    for slot in range(ROWS):
        turn_tables(
            (0, 2, 1, 3)[slot],
            rank * frames,
            n.cosine,
            n.sine,
            pl.ds(slot * frames, frames),
        )
    mod_second.wait_recv()
    mod_total = n.mod_send[...].astype(full) + n.mod_cross[...].astype(full)
    for k in range(2):
        row = 2 * k + core
        values = mod_total[8 * k : 8 * k + 8]
        high = values.astype(low).astype(full)
        stack = jnp.concatenate([high, values - high], axis=0).astype(low)
        chosen = picked(row, rank * frames, frames)[0]
        picker = jnp.where(chosen, 1.0, 0.0).astype(low)[:, :16]
        where = pl.ds(k * frames, frames)
        n.scale_one[where] = 1.0 + dot_plain(picker, stack[:, :width])
        n.shift_one[where] = dot_plain(picker, stack[:, width:])

    qkv_passed = []
    for i, source in enumerate(over_x):
        for copy in qkv_sends[i]:
            copy.wait_recv()
        where = n.qkv_held.at[lines(source * columns + first_row, few_rows)]
        for j, to in enumerate(around):
            qkv_passed.append(push(where, where, n.qkv_pass_sem, (i, j), to))
    attn_sends = []
    for k in range(2):
        second[k].wait_recv()

        def norm_one(at, k=k):
            where = pl.ds(k * frames + at, TILE)
            hidden = n.keep[where] + n.land_two[0, where].astype(full)
            n.hidden[where] = hidden
            centred = hidden - mean(hidden)
            spread = lax.rsqrt(mean(centred * centred) + EPSILON)
            normal = centred * spread
            n.normal_one[where] = normal
            n.spread_one[where] = jnp.broadcast_to(spread, (TILE, 128))
            n.attn_in[lines(mine + k * frames + at, TILE)] = (
                normal * n.scale_one[where] + n.shift_one[where]
            ).astype(low)

        tiles(frames, TILE, norm_one)
        attn_sends.append(share(n.attn_in, k, n.attn_sem))

    def part_of(reference, first):
        return reference.at[lines(first + side_y * part_rows, part_rows)]

    up_sends = [
        push(
            part_of(up_piece(to), 0),
            part_of(n.up_held, group_rank * columns),
            n.up_sem,
            (i,),
            (rank, to),
        )
        for i, to in enumerate(over_x)
    ]
    up_sends.append(push(up_piece(sibling[1]), up_place, n.up_sem, (2,), sibling))
    out_sends = [
        push(n.w_out, out_place, n.out_sem, (i,), device) for i, device in enumerate((across, sibling))
    ]

    def pass_on(buffer, copies, sems):
        passed = []
        for i, source in enumerate(over_x):
            copies[i].wait_recv()
            where = part_of(buffer, source * columns)
            passed.append(push(where, where, sems, (i,), beside))
        return passed

    upstream_load.wait()
    upstream_sends = [
        push(n.upstream.at[own_lines], n.upstream.at[own_lines], n.upstream_sem, (i,), device)
        for i, device in enumerate((across, sibling))
    ]

    for copy in qkv_loads:
        copy.wait()
    for copy in qkv_sends[2] + qkv_passed:
        copy.wait_recv()

    def to_heads(offset, value_of, target, sems, send_buffer, columns_of):
        for k in range(2):
            slot = offset // frames + k
            for side in range(2):
                to = 2 * row_of(slot) + side
                if value_of is not None:
                    send_buffer[to] = value_of(k, side, slot)

                @pl.when(to != rank)
                def _():
                    link(
                        send_buffer.at[to, :, columns_of],
                        target.at[lines(rank * frames, frames), columns_of],
                        sems.at[0, to],
                        sems.at[1, rank],
                        (to, group_rank),
                    ).start()

                @pl.when(to == rank)
                def _():
                    target[lines(rank * frames, frames), columns_of] = send_buffer[to, :, columns_of]

    def heads_arrive(target, sems, columns_of, then=None):
        for other in range(RING):
            source = block(other)
            if other:
                where = target.at[lines(source * frames, frames), columns_of]
                link(
                    where, where, sems.at[0, source], sems.at[1, source], (source, group_rank)
                ).wait_recv()
            if then is not None:
                then(pl.multiple_of(source * frames, frames))

    def project_half(offset):
        def project_tile(at):
            n.project[:, pl.ds(at, 256)] = dot_plain(
                n.attn_in[lines(offset, half)], n.qkv_held[:, pl.ds(at, 256)]
            )

        tiles(3 * columns, 256, project_tile)

        def value_of(k, side, slot):
            where = lines(slot * frames, frames)
            cosine, sine = n.cosine[where], n.sine[where]
            blocks = []
            for kind in range(3):
                value = n.project[pl.ds(k * frames, frames), pl.ds((side * 3 + kind) * 128, 128)]
                if kind < 2:
                    value = value * cosine + swapped(value) * sine
                blocks.append(value.astype(low))
            return jnp.concatenate(blocks, axis=1)

        to_heads(offset, value_of, n.paired, n.pair_sem, n.pair_send, pl.ds(0, 256))

    project_half(mine)
    for copy in attn_sends:
        copy.wait_recv()
    project_half(theirs)
    for offset in (mine, theirs):
        to_heads(offset, None, n.paired, n.value_sem, n.pair_send, pl.ds(256, 128))

    def row_tables(at):
        turn_tables(pair_row, at, n.row_cosine, n.row_sine, pl.ds(at, frames))
        chosen = jnp.where(picked(pair_row, at, frames)[0], 1.0, 0.0)
        n.chosen[pl.ds(at, frames)] = chosen.astype(low)

    tiles(RING * frames, frames, row_tables)
    def masked_parts(at):
        where = pl.ds(at, frames)
        query, key = n.paired[where, 0:128], n.paired[where, 128:256]
        chosen = n.chosen[where]
        first_head = lanes < 64
        blocked = jnp.where(
            lax.rem(lanes, 64) < 8, NEGATIVE * (1.0 - chosen.astype(full)), 0.0
        ).astype(low)
        scaled = (query.astype(full) * HEAD_DIM ** (-0.5)).astype(low)
        n.query_head[0, where] = jnp.where(first_head, scaled, chosen)
        n.query_head[1, where] = jnp.where(first_head, chosen, scaled)
        n.key_head[0, where] = jnp.where(first_head, key, blocked)
        n.key_head[1, where] = jnp.where(first_head, blocked, key)

    heads_arrive(n.paired, n.pair_sem, pl.ds(0, 256), masked_parts)
    up_passed = pass_on(n.up_held, up_sends, n.up_pass_sem)
    out_sends[0].wait_recv()
    where = n.out_held.at[lines(across[1] * columns, columns)]
    out_sends.append(push(where, where, n.out_sem, (2,), sibling))
    all_frames = RING * frames
    pair_place = (lines(slot_of(pair_row) * frames, frames), lines(pair_side * 128, 128))

    def score(at):
        where = pl.ds(at, half)
        for head in range(2):
            scores = dot_across(n.query_head[head, where], n.key_head[head])
            top = jnp.max(scores, axis=1, keepdims=True)
            weights = jnp.exp(scores - top)
            total = jnp.sum(weights, axis=1, keepdims=True)
            n.shares[head, where] = (weights * (1.0 / total)).astype(low)

    tiles(all_frames, half, score)
    heads_arrive(n.paired, n.value_sem, pl.ds(256, 128))

    def attend(at):
        where = pl.ds(at, half)
        sums = [dot_plain(n.shares[head, where], n.paired[:, 256:384]) for head in range(2)]
        first_head = lax.broadcasted_iota(jnp.int32, (half, 128), 1) < 64
        value = jnp.where(first_head, sums[0], sums[1])
        n.attended_pair[where] = value
        n.attended_send[where] = value.astype(low)
        for k in range(2):
            to = at // frames + k
            place = lines(at + k * frames, frames)

            @pl.when(to != rank)
            def _():
                link(
                    n.attended_send.at[place],
                    n.attended.at[pair_place],
                    n.attended_sem.at[0, to],
                    n.attended_sem.at[1, rank],
                    (to, group_rank),
                ).start()

            @pl.when(to == rank)
            def _():
                n.attended[pair_place] = n.attended_send[place]

    tiles(all_frames, half, attend)

    def pairs_arrive(buffer, sems, pitch, first, wide):
        for other in range(1, RING):
            source = block(other)
            where = buffer.at[
                lines(slot_of(source // 2) * frames, frames),
                pl.ds(pl.multiple_of(lax.rem(source, 2) * pitch + first, 128), wide),
            ]
            link(where, where, sems.at[0, source], sems.at[1, source], (source, group_rank)).wait_recv()

    upstream_sends[0].wait_recv()
    other_lines = lines((2 * core + 1 - chip) * frames, frames)
    upstream_sends.append(
        push(n.upstream.at[other_lines], n.upstream.at[other_lines], n.upstream_sem, (2,), sibling)
    )
    pairs_arrive(n.attended, n.attended_sem, 128, 0, 128)

    own_columns = pl.ds(pl.multiple_of(group_rank * columns, columns), columns)
    attended_sends = [
        push(
            n.attended.at[lines(first, half)],
            n.attended_all.at[:, own_columns],
            n.attended_all_sem,
            (i,),
            (rank, to),
        )
        for i, (first, to) in enumerate(
            ((mine, over_x[0]), (theirs, over_x[1]), (theirs, sibling[1]))
        )
    ]
    n.attended_all[:, own_columns] = n.attended[lines(mine, half)]
    out_load.wait()
    for copy in out_sends[1:] + attended_sends:
        copy.wait_recv()

    def out_tile(at):
        n.keep[:, pl.ds(at, 256)] = dot_plain(n.attended_all[...], n.out_held[:, pl.ds(at, 256)])

    tiles(width, 256, out_tile)
    ff_sends = []
    for k in range(2):

        def norm_two(at, k=k):
            where = pl.ds(k * frames + at, TILE)
            hidden = n.hidden[where] + n.keep[where]
            n.hidden[where] = hidden
            centred = hidden - mean(hidden)
            spread = lax.rsqrt(mean(centred * centred) + EPSILON)
            normal = centred * spread
            n.normal_two[where] = normal
            n.spread_two[where] = jnp.broadcast_to(spread, (TILE, 128))
            n.ff_in[lines(mine + k * frames + at, TILE)] = (normal * n.gain[0:1]).astype(low)

        tiles(frames, TILE, norm_two)
        ff_sends.append(share(n.ff_in, k, n.ff_sem))

    up_load.wait()
    down_load.wait()
    for copy in up_sends[2:] + up_passed:
        copy.wait_recv()
    for copy in upstream_sends[1:]:
        copy.wait_recv()

    def feed_half(offset):
        where = lines(offset, half)

        def feed_tile(at):
            widened = dot_plain(n.ff_in[where], n.up_held[:, pl.ds(at, 256)])
            grad = dot_across(n.upstream[where], n.down_held[pl.ds(at, 256)])
            share_of = 0.5 * (1.0 + lax.erf(widened * math.sqrt(0.5)))
            slope = share_of + widened * jnp.exp(-0.5 * widened * widened) * (
                1.0 / math.sqrt(2.0 * math.pi)
            )
            n.activated[where, pl.ds(at, 256)] = (widened * share_of).astype(low)
            n.grad_widened[where, pl.ds(at, 256)] = (grad * slope).astype(low)

        tiles(hidden_units, 256, feed_tile)

    feed_half(mine)
    for copy in ff_sends:
        copy.wait_recv()
    feed_half(theirs)
    first = partial_sum(
        1, n.grad_widened, lambda left, at: dot_across(left, n.up_held[pl.ds(at, 256)])
    )
    second = cross_sum(1, first)

    def down_tile(at):
        value = contract_rows(n.activated[:, pl.ds(at, 256)], n.upstream[...]).astype(low)
        n.down_total[at // 128] = value[:128]
        n.down_total[at // 128 + 1] = value[128:]

    tiles(hidden_units, 256, down_tile)
    begin(down_ring)

    def up_tile(at):
        value = contract_rows(n.ff_in[:, pl.ds(at, columns)], n.grad_widened[...]).astype(low)
        deep = columns // RING
        for j in range(RING):
            n.up_total[j, pl.ds(pl.multiple_of(at // RING, deep), deep)] = value[
                j * deep : (j + 1) * deep
            ]

    tiles(width, columns, up_tile)
    begin(up_ring)
    ticks(TICKS[0])

    gain_sums = jnp.zeros((1, width), full)
    grad_sends = []
    for k in range(2):
        second[k].wait_recv()
        weight = (1 - jnp.abs(chip - k)).astype(full)

        def back_two(i, sums, k=k, weight=weight):
            at = pl.multiple_of(i * TILE, TILE)
            where = pl.ds(k * frames + at, TILE)
            grad = n.keep[where] + n.land_two[1, where].astype(full)
            normal = n.normal_two[where]
            scaled = grad * n.gain[0:1]
            back = n.spread_two[where][:, 0:1] * (
                scaled - mean(scaled) - normal * mean(scaled * normal)
            )
            total = n.upstream[lines(mine + k * frames + at, TILE)].astype(full) + back
            n.grad_two[where] = total
            n.grad_two_low[lines(mine + k * frames + at, TILE)] = total.astype(low)
            return sums + weight * jnp.sum(grad * normal, axis=0, keepdims=True)

        gain_sums = lax.fori_loop(0, frames // TILE, back_two, gain_sums)
        grad_sends.append(share(n.grad_two_low, k, n.grad_two_sem))
        ticks(TICKS[1 + k])
    n.mod_sums[8:16] = jnp.zeros((8, 2 * width), full)
    n.mod_sums[8:9, :width] = gain_sums

    def attended_half(offset):
        value = dot_across(
            n.grad_two_low[lines(offset, half)], n.out_held[lines(group_rank * columns, columns)]
        ).astype(low)

        def value_of(k, side, slot):
            return value[k * frames : (k + 1) * frames, side * 128 : side * 128 + 128]

        to_heads(
            offset, value_of, n.grad_pair, n.grad_pair_sem, n.grad_pair_send, pl.ds(0, 128)
        )

    attended_half(mine)
    ticks(TICKS[3])
    for copy in grad_sends:
        copy.wait_recv()
    attended_half(theirs)
    ticks(TICKS[4])
    value = contract_rows(n.attended[...], n.grad_two_low[...]).astype(low)
    for j in range(RING):
        n.out_total[j] = value[j * 32 : (j + 1) * 32]
    ticks(TICKS[5])

    first = partial_sum(2, n.activated, lambda left, at: dot_plain(left, n.down_held[:, pl.ds(at, 256)]))
    ticks(TICKS[6])
    output_second = cross_sum(2, first)
    ticks(TICKS[7])

    def turn_queries(at):
        where = pl.ds(at, frames)
        n.query_turned[:, where] = jnp.transpose(n.paired[where, 0:128].astype(full)).astype(low)

    tiles(RING * frames, frames, turn_queries)

    def turn_upstream(at):
        where = pl.ds(at, frames)
        n.grad_turned[:, where] = jnp.transpose(n.grad_pair[where].astype(full)).astype(low)

    heads_arrive(n.grad_pair, n.grad_pair_sem, pl.ds(0, 128), turn_upstream)
    n.key_turned[...] = jnp.zeros(n.key_turned.shape, full)
    n.value_turned[...] = jnp.zeros(n.value_turned.shape, full)

    def back_turned(value, where):
        return value * n.row_cosine[where] - swapped(value) * n.row_sine[where]

    project_slot = lines(slot_of(pair_row) * frames, frames)

    def project_back(to, place, first, wide, sems):
        source = n.project_send.at[place, pl.ds(first, wide)]
        at = pl.ds(pl.multiple_of(pair_side * 384 + first, 128), wide)

        @pl.when(to != rank)
        def _():
            target = n.grad_project.at[project_slot, at]
            link(source, target, sems.at[0, to], sems.at[1, rank], (to, group_rank)).start()

        @pl.when(to == rank)
        def _():
            n.grad_project[project_slot, at] = source[...]

    def attend_back(at):
        where = pl.ds(at, half)
        first_head = lax.broadcasted_iota(jnp.int32, (half, 128), 1) < 64
        grad = n.grad_pair[where]
        product = grad.astype(full) * n.attended_pair[where]
        terms = []
        for head in range(2):
            here = first_head if head == 0 else jnp.logical_not(first_head)
            delta = jnp.sum(jnp.where(here, product, 0.0), axis=1, keepdims=True)
            grad_head = jnp.where(here, grad, jnp.zeros_like(grad))
            prob_grad = dot_across(grad_head, n.paired[:, 256:384])
            shares = n.shares[head, where]
            score_grad = (shares.astype(full) * (prob_grad - delta)).astype(low)
            terms.append(dot_plain(score_grad, n.paired[:, 128:256]))
            rows = pl.ds(head * 64, 64)
            n.value_turned[rows] += dot_plain(n.grad_turned[rows, where], shares)
            n.key_turned[rows] += dot_plain(n.query_turned[rows, where], score_grad)
        query_grad = jnp.where(first_head, terms[0], terms[1]) * HEAD_DIM ** (-0.5)
        for k in range(2):
            place = lines(at + k * frames, frames)
            n.project_send[place, 0:128] = back_turned(
                query_grad[k * frames : (k + 1) * frames], place
            ).astype(low)
            project_back(at // frames + k, place, 0, 128, n.query_sem)

    for part in range(4):
        attend_back(part * half)
        ticks(TICKS[8 + part])
    def keys_back(at):
        place = pl.ds(at, frames)
        key_grad = jnp.transpose(n.key_turned[:, place]) * HEAD_DIM ** (-0.5)
        n.project_send[place, 128:256] = back_turned(key_grad, place).astype(low)
        n.project_send[place, 256:384] = jnp.transpose(n.value_turned[:, place]).astype(low)
        project_back(at // frames, place, 128, 256, n.project_sem)

    tiles(all_frames, frames, keys_back)

    ticks(TICKS[12])

    for copy in output_second:
        copy.wait_recv()

    def finish_output(at):
        where = lines(chip * frames + at, TILE)
        n.output[pl.ds(at, TILE)] = (
            n.hidden[where] + n.keep[where] + n.land_two[2, where].astype(full)
        ).astype(low)

    tiles(frames, TILE, finish_output)
    ticks(TICKS[13])
    pairs_arrive(n.grad_project, n.query_sem, 384, 0, 128)
    pairs_arrive(n.grad_project, n.project_sem, 384, 128, 256)

    first = partial_sum(
        3, n.grad_project, lambda left, at: dot_across(left, n.qkv_held[pl.ds(at, 256)])
    )
    ticks(TICKS[14])
    second = cross_sum(3, first)
    ticks(TICKS[15])

    def qkv_tile(at):
        value = contract_rows(n.attn_in[:, pl.ds(at, columns)], n.grad_project[...]).astype(low)
        deep = columns // RING
        for j in range(RING):
            n.qkv_total[j, pl.ds(pl.multiple_of(at // RING, deep), deep)] = value[
                j * deep : (j + 1) * deep
            ]

    tiles(width, columns, qkv_tile)
    begin(qkv_ring)
    ticks(TICKS[16])
    hidden_sends = []
    for k in range(2):
        second[k].wait_recv()

        def back_one(at, k=k):
            where = pl.ds(k * frames + at, TILE)
            grad = n.keep[where] + n.land_two[3, where].astype(full)
            normal = n.normal_one[where]
            scaled = grad * n.scale_one[where]
            back = n.spread_one[where][:, 0:1] * (
                scaled - mean(scaled) - normal * mean(scaled * normal)
            )
            n.grad_hidden[lines(mine + k * frames + at, TILE)] = (n.grad_two[where] + back).astype(low)

            @pl.when(chip == k)
            def _():
                n.shift_one[pl.ds(at, TILE)] = grad * normal
                n.shift_one[pl.ds(frames + at, TILE)] = grad

        tiles(frames, TILE, back_one)
        hidden_sends.append(share(n.grad_hidden, k, n.grad_hidden_sem))
        ticks(TICKS[17 + k])

    for copy in hidden_sends:
        copy.wait_recv()

    def skip_weight_tile(at):
        value = contract_rows(n.joined[:, pl.ds(at, 256)], n.grad_hidden[...]).astype(low)
        for j in range(4):
            n.skip_total[at // 64 + j] = value[j * 64 : (j + 1) * 64]

    tiles(n.joined.shape[1], 256, skip_weight_tile)
    begin(skip_ring)
    begin(out_ring)
    ticks(TICKS[19])
    spot = (lax.broadcasted_iota(jnp.int32, (8, frames), 1) + rank * frames).astype(full)
    chosen = (spot >= n.small[1]) & (spot < n.small[2])
    picker = jnp.where(chosen, 1.0, 0.0)

    def mod_sum(at):
        for part in range(2):
            n.mod_sums[0:8, pl.ds(part * width + at, 512)] = jnp.dot(
                picker, n.shift_one[pl.ds(part * frames, frames), pl.ds(at, 512)], precision=HIGHEST
            )

    tiles(width, 512, mod_sum)
    for other in range(1, RING):
        to = block(other)
        push(
            n.mod_sums.at[:, pl.ds(pl.multiple_of(to * 256, 256), 256)],
            n.sums_land.at[rank],
            n.sums_sem,
            (other - 1,),
            (to, group_rank),
        )
    sums_copies = sent[-(RING - 1) :]
    n.sums_land[rank] = n.mod_sums[:, pl.ds(pl.multiple_of(rank * 256, 256), 256)]
    ticks(TICKS[20])
    back = dot_across(n.grad_hidden[...], n.skip_held[...]).astype(low)
    n.joined_send[...] = back
    grad_joined_copies = []
    for other in (2, 1, 3):
        to = group(other)
        grad_joined_copies.append(
            push(
                n.joined_send.at[lines(slot_of(to) * frames, frames)],
                n.grad_joined.at[group_rank],
                n.grad_joined_sem,
                (other - 1,),
                (rank, to),
            )
        )
    n.grad_joined[group_rank] = n.joined_send[own_lines]
    ticks(TICKS[21])
    for copy in sums_copies:
        copy.wait_recv()
    n.sums_send[...] = jnp.sum(n.sums_land[...], axis=0).astype(low)
    n.mod_grad[rank, group_rank] = n.sums_send[...]
    group_sums = [
        push(
            n.sums_send,
            n.mod_grad.at[rank, group_rank],
            n.sums_group_sem,
            (other - 1,),
            (rank, group(other)),
        )
        for other in (2, 1, 3)
    ]
    ticks(TICKS[22])
    for copy in group_sums:
        copy.wait_recv()
    mod_spread = [
        push(
            n.mod_grad.at[rank],
            n.mod_grad.at[rank],
            n.sums_block_sem,
            (other - 1,),
            (block(other), group_rank),
        )
        for other in range(1, RING)
    ]

    ticks(5 * (2 * RING + 1))
    for ring in rings:
        ring.finish()
    for copy in mod_spread + grad_joined_copies:
        copy.wait_recv()
    gain_grad = n.mod_grad[group_rank, 0].astype(full)
    for row in range(1, ROWS):
        gain_grad = gain_grad + n.mod_grad[group_rank, row].astype(full)
    n.gain_grad[...] = gain_grad[8:16]
    for index, copy in enumerate(sent):
        if not any(copy is other for pair in list(group_copies.values())[:-1] for kind in pair for other in kind):
            copy.wait_send()
    for sems, wide in (
        (n.pair_sem, 256),
        (n.value_sem, 128),
        (n.attended_sem, 128),
        (n.grad_pair_sem, 128),
        (n.query_sem, 128),
        (n.project_sem, 256),
    ):
        for other in range(1, RING):
            to = block(other)
            where = n.project_send.at[lines(to * frames, frames), pl.ds(0, wide)]
            link(where, where, sems.at[0, to], sems.at[1, to], (to, group_rank)).wait_send()


def block_call(
    inputs,
    skipped,
    w_skip,
    w_mod,
    w_qkv,
    w_out,
    w_up,
    w_down,
    cotangent,
    own_gain,
    lengths,
    flow_steps,
):
    low, full = jnp.bfloat16, jnp.float32
    frames, width = inputs.shape
    tokens, half = ROWS * frames, 2 * frames
    columns = width // ROWS
    hidden_units = w_down.shape[0]
    joint = w_skip.shape[0]
    all_frames = RING * frames
    deep = width // RING

    held = dict(
        inputs=inputs,
        skipped=skipped,
        w_skip=w_skip,
        w_mod=w_mod,
        w_qkv=w_qkv,
        w_out=w_out,
        w_up=w_up,
        w_down=w_down,
        cotangent=cotangent,
        own_gain=own_gain,
        lengths=lengths,
        flow_steps=flow_steps,
    )
    given = dict(
        output=((frames, width), low),
        grad_joined=((ROWS, frames, joint), low),
        condition=((ROWS * 8, columns), low),
        mod_grad=((RING, ROWS, 16, 256), low),
        gain_grad=((8, columns), full),
        down_total=((RING, hidden_units // RING, width), low),
        up_total=((RING, deep, hidden_units), low),
        qkv_total=((RING, deep, 3 * columns), low),
        skip_total=((RING, joint // RING, width), low),
        out_total=((RING, columns // RING, width), low),
    )
    buffers = dict(
        joined_own=((ROWS, frames, joint), low),
        joined=((tokens, joint), low),
        upstream=((tokens, width), low),
        skip_held=(w_skip.shape, low),
        mod_held=(w_mod.shape, low),
        out_held=((width, width), low),
        attended_all=((half, width), low),
        down_held=(w_down.shape, low),
        qkv_held=((width, 3 * columns), low),
        up_held=((width, hidden_units), low),
        small=((7, 8, 128), full),
        smalls=((ROWS, 7, 8, 128), full),
        mod_part=((ROWS * 8, 2 * width), full),
        mod_land=((1, 16, 2 * width), full),
        mod_send=((16, 2 * width), low),
        mod_cross=((16, 2 * width), low),
        gain=((8, width), full),
        cosine=((tokens, 128), full),
        sine=((tokens, 128), full),
        row_cosine=((all_frames, 128), full),
        row_sine=((all_frames, 128), full),
        chosen=((all_frames, 128), low),
        send_one=((half, width), low),
        send_two=((half, width), low),
        keep=((half, width), full),
        land_one=((4, half, width), low),
        land_two=((4, half, width), low),
        scale_one=((half, width), full),
        shift_one=((half, width), full),
        hidden=((half, width), full),
        normal_one=((half, width), full),
        spread_one=((half, 128), full),
        normal_two=((half, width), full),
        spread_two=((half, 128), full),
        grad_two=((half, width), full),
        attn_in=((tokens, width), low),
        project=((half, 3 * columns), full),
        pair_send=((RING, frames, 384), low),
        paired=((all_frames, 384), low),
        query_head=((2, all_frames, 128), low),
        key_head=((2, all_frames, 128), low),
        query_turned=((128, all_frames), low),
        shares=((2, all_frames, all_frames), low),
        attended_pair=((all_frames, 128), full),
        attended_send=((all_frames, 128), low),
        attended=((tokens, columns), low),
        ff_in=((tokens, width), low),
        activated=((tokens, hidden_units), low),
        grad_widened=((tokens, hidden_units), low),
        grad_two_low=((tokens, width), low),
        grad_pair_send=((RING, frames, 128), low),
        grad_pair=((all_frames, 128), low),
        grad_turned=((128, all_frames), low),
        key_turned=((128, all_frames), full),
        value_turned=((128, all_frames), full),
        project_send=((all_frames, 384), low),
        grad_project=((tokens, 3 * columns), low),
        grad_hidden=((tokens, width), low),
        mod_sums=((16, 2 * width), full),
        sums_land=((RING, 16, 256), full),
        sums_send=((16, 256), low),
        joined_send=((tokens, joint), low),
        down_land=((RING - 1, hidden_units // RING, width), low),
        up_land=((RING - 1, deep, hidden_units), low),
        qkv_land=((RING - 1, deep, 3 * columns), low),
        skip_land=((RING - 1, joint // RING, width), low),
        out_land=((RING - 1, columns // RING, width), low),
        up_turn=((deep, hidden_units), low),
        qkv_turn=((deep, 3 * columns), low),
    )
    sems = dict(
        load_sem=(16,),
        joined_sem=(2, 3),
        small_sem=(2, 3),
        qkv_sem=(2, 3, 6),
        qkv_pass_sem=(2, 2, 3),
        up_sem=(2, 3),
        up_pass_sem=(2, 2),
        out_sem=(2, 3),
        attended_all_sem=(2, 3),
        mod_sem=(2, 2),
        first_sem=(2, 4, 2),
        second_sem=(2, 4, 2),
        upstream_sem=(2, 3),
        attn_sem=(2, 2),
        ff_sem=(2, 2),
        grad_two_sem=(2, 2),
        grad_hidden_sem=(2, 2),
        pair_sem=(2, RING),
        attended_sem=(2, RING),
        grad_pair_sem=(2, RING),
        query_sem=(2, RING),
        project_sem=(2, RING),
        value_sem=(2, RING),
        grad_joined_sem=(2, 3),
        sums_sem=(2, RING - 1),
        sums_group_sem=(2, 3),
        sums_block_sem=(2, RING - 1),
        down_sem=(2, 2, 2, RING - 1),
        up_ring_sem=(2, 2, 2, RING - 1),
        qkv_ring_sem=(2, 2, 2, RING - 1),
        skip_ring_sem=(2, 2, 2, RING - 1),
        out_ring_sem=(2, 2, 2, RING - 1),
        turn_sem=(2, 2, 3),
    )
    names = [*held, *given, *buffers, *sems]
    vmem = pl.BlockSpec(memory_space=pltpu.VMEM)
    anywhere = pl.BlockSpec(memory_space=pl.ANY)
    return pl.pallas_call(
        functools.partial(block_kernel, names),
        out_shape=[pltpu.VMEM(*spec) for spec in given.values()],
        in_specs=[anywhere] * 9 + [vmem] + [pl.BlockSpec(memory_space=pltpu.SMEM)] * 2,
        out_specs=[vmem] * len(given),
        scratch_shapes=[pltpu.VMEM(*spec) for spec in buffers.values()]
        + [pltpu.SemaphoreType.DMA(shape) for shape in sems.values()],
        compiler_params=pltpu.CompilerParams(
            collective_id=0,
            has_side_effects=True,
            vmem_limit_bytes=MAIN_MIB * 1024 * 1024,
        ),
    )(*held.values())


def finish_kernel(names, *refs):
    n = types.SimpleNamespace(**dict(zip(names, refs)))
    full = jnp.float32
    pieces = 4
    chunks = RING // pieces

    def start(source, target, sem):
        copy = pltpu.make_async_copy(source, target, sem)
        copy.start()
        return copy

    def widen_rows(source, target, p):
        deep, wide = source.shape[1:]
        target[pl.ds(p * chunks * deep, chunks * deep)] = (
            source[pl.ds(p * chunks, chunks)].astype(full).reshape(chunks * deep, wide)
        )

    def widen_columns(source, target, p):
        deep, wide = source.shape[1] // ROWS, source.shape[2]
        kinds = wide // 256 if wide % 1024 else 1
        step = 128 if kinds > 1 else wide
        for j in range(chunks):
            to = pl.ds((p * chunks + j) * deep, deep)
            for r in range(ROWS):
                value = source[p * chunks + j, pl.ds(r * deep, deep)].astype(full)
                for i in range(wide // step):
                    side, kind = i // kinds, i % kinds
                    at = kind * (ROWS * wide // kinds) + r * (wide // kinds) + side * step
                    target[to, pl.ds(at, step)] = value[:, i * step : (i + 1) * step]

    work = (
        (n.down, n.down_out, n.grad_down, widen_rows),
        (n.up, n.up_out, n.grad_up, widen_columns),
        (n.qkv, n.qkv_out, n.grad_qkv, widen_columns),
        (n.skip, n.skip_out, n.grad_skip, widen_rows),
        (n.out, n.out_out, n.grad_out, widen_rows),
    )
    sent = [start(n.output, n.output_back, n.small_sem.at[3])]
    for p in range(pieces):
        for i, (held, wide, target, widen) in enumerate(work):
            widen(held, wide, p)
            deep = target.shape[0] // pieces
            rows = pl.ds(p * deep, deep)
            sent.append(start(wide.at[rows], target.at[rows], n.out_sem.at[i, p]))
    for i in range(RING):
        sums = [n.mod[i, r].astype(full)[0:8] for r in (0, 2, 1, 3)]
        n.mod_out[:, pl.ds(i * 256, 256)] = contract_rows(
            n.condition[...], jnp.concatenate(sums, axis=0).astype(jnp.bfloat16)
        )
    sent.append(start(n.mod_out, n.grad_mod, n.small_sem.at[4]))
    wide = n.joined.shape[2]
    for r in range(ROWS):
        n.joined_out[r // 2, :, pl.ds((r % 2) * wide, wide)] = n.joined[r].astype(full)
    sent.append(start(n.joined_out.at[0], n.grad_inputs, n.small_sem.at[5]))
    sent.append(start(n.joined_out.at[1], n.grad_skipped, n.small_sem.at[6]))
    n.grad_gain[...] = n.gain[0:1]
    for copy in sent:
        copy.wait()


def finish_call(output, joined, condition, mod, gain, down, up, qkv, skip, out):
    low, full = jnp.bfloat16, jnp.float32
    frames, wide = joined.shape[1:]
    columns = condition.shape[1]
    deep = up.shape[1] // ROWS
    held = dict(
        output=output,
        joined=joined,
        condition=condition,
        mod=mod,
        gain=gain,
        down=down,
        up=up,
        qkv=qkv,
        skip=skip,
        out=out,
    )
    given = dict(
        output_back=(output.shape, low),
        grad_inputs=((frames, 2 * wide), full),
        grad_skipped=((frames, 2 * wide), full),
        grad_skip=((RING * skip.shape[1], skip.shape[2]), full),
        grad_mod=((columns, RING * mod.shape[3]), full),
        grad_qkv=((RING * deep, ROWS * qkv.shape[2]), full),
        grad_out=((RING * out.shape[1], out.shape[2]), full),
        grad_gain=((1, columns), full),
        grad_up=((RING * deep, ROWS * up.shape[2]), full),
        grad_down=((RING * down.shape[1], down.shape[2]), full),
    )
    buffers = dict(
        joined_out=((2, frames, 2 * wide), full),
        mod_out=given["grad_mod"],
        down_out=given["grad_down"],
        up_out=given["grad_up"],
        qkv_out=given["grad_qkv"],
        skip_out=given["grad_skip"],
        out_out=given["grad_out"],
    )
    sems = dict(out_sem=(5, 4), small_sem=(7,))
    names = [*held, *given, *buffers, *sems]
    vmem = pl.BlockSpec(memory_space=pltpu.VMEM)
    anywhere = pl.BlockSpec(memory_space=pl.ANY)
    return pl.pallas_call(
        functools.partial(finish_kernel, names),
        out_shape=[jax.ShapeDtypeStruct(*spec) for spec in given.values()],
        in_specs=[vmem] * len(held),
        out_specs=[vmem if name == "grad_gain" else anywhere for name in given],
        scratch_shapes=[pltpu.VMEM(*spec) for spec in buffers.values()]
        + [pltpu.SemaphoreType.DMA(shape) for shape in sems.values()],
        compiler_params=pltpu.CompilerParams(vmem_limit_bytes=LAST_MIB * 1024 * 1024),
    )(*held.values())


def per_device_block(
    inputs,
    skipped,
    w_skip,
    w_mod,
    w_qkv,
    w_out,
    ff_gain,
    w_up,
    w_down,
    cotangent,
    lengths,
    flow_steps,
):
    finished = block_call(
        inputs[0],
        skipped[0],
        w_skip,
        w_mod,
        w_qkv,
        w_out,
        w_up,
        w_down,
        cotangent[0],
        ff_gain,
        lengths,
        flow_steps,
    )
    output, grad_inputs, grad_skipped, skip, mod, qkv, out, gain, up, down = finish_call(*finished)
    return (
        output[None],
        grad_inputs[None],
        grad_skipped[None],
        skip,
        mod,
        qkv,
        out,
        gain[0],
        up,
        down,
    )


def solution(mesh):
    placed = (
        P("grp", "blk", None),
        P("grp", "blk", None),
        P("grp", None),
        P("grp", None),
        P("grp", None),
        P("grp", None),
        P("grp"),
        P("grp", None),
        P("grp", None),
        P("grp", "blk", None),
        P("grp", None),
        P("grp", None),
    )
    body = per_device
    if mesh.shape["blk"] == RING and mesh.shape["grp"] == ROWS:
        body = per_device_block
    return jax.shard_map(
        body,
        mesh=mesh,
        in_specs=placed,
        out_specs=(
            P("grp", "blk", None),
            P("grp", "blk", None),
            P("grp", "blk", None),
            P("grp", None),
            P("grp", None),
            P("grp", None),
            P("grp", None),
            P("grp"),
            P("grp", None),
            P("grp", None),
        ),
        check_vma=False,
    )
```

```python
import functools
import math
import types

import jax
import jax.numpy as jnp
from jax import lax
from jax.experimental import pallas as pl
from jax.experimental.pallas import tpu as pltpu
from jax.sharding import PartitionSpec as P

HEADS = 16
HEAD_DIM = 64
STEPS = 32


EPSILON = 1e-06
NEGATIVE = -1e30
HIGHEST = lax.Precision.HIGHEST
MESH = pl.DeviceIdType.MESH
RING = 8
ROWS = 4


def from_behind(block, axis, distance):
    devices = range(lax.axis_size(axis))
    route = [((i - distance) % len(devices), i) for i in devices]
    return lax.ppermute(block, axis, route)


def layout(lengths_row, frames):
    end_frame = jnp.cumsum(lengths_row)
    start_frame = end_frame - lengths_row
    segment = jnp.sum((frames[:, None] >= end_frame[None, :]).astype(jnp.int32), axis=1)
    chosen = segment[:, None] == jnp.arange(lengths_row.shape[0], dtype=jnp.int32)[None, :]
    position = frames - jnp.sum(jnp.where(chosen, start_frame[None, :], 0), axis=1)
    return (segment, position)


def flow_condition(steps_row, model_width):
    half_width = model_width // 2
    rate_table = jnp.exp(
        -math.log(10000.0) * jnp.arange(half_width, dtype=jnp.float32) / half_width
    )
    angles = 1000.0 * (steps_row.astype(jnp.float32) / STEPS)[:, None] * rate_table[None, :]
    return jax.nn.silu(jnp.concatenate([jnp.sin(angles), jnp.cos(angles)], axis=1))


def rotation_tables(position, head_width):
    half_width = head_width // 2
    rate_table = jnp.exp(
        -math.log(10000.0) * jnp.arange(half_width, dtype=jnp.float32) / half_width
    )
    angles = position.astype(jnp.float32)[:, None] * rate_table[None, :]
    return (jnp.cos(angles)[:, None, :], jnp.sin(angles)[:, None, :], half_width)


def rotate(head_block, position):
    cosine_part, sine_part, half_width = rotation_tables(position, head_block.shape[-1])
    first_half = head_block[..., :half_width]
    second_half = head_block[..., half_width:]
    return jnp.concatenate(
        [
            first_half * cosine_part - second_half * sine_part,
            second_half * cosine_part + first_half * sine_part,
        ],
        axis=-1,
    )


def rotate_back(head_block, position):
    cosine_part, sine_part, half_width = rotation_tables(position, head_block.shape[-1])
    first_half = head_block[..., :half_width]
    second_half = head_block[..., half_width:]
    return jnp.concatenate(
        [
            first_half * cosine_part + second_half * sine_part,
            second_half * cosine_part - first_half * sine_part,
        ],
        axis=-1,
    )


def normalize(hidden):
    centred = hidden - jnp.mean(hidden, axis=-1, keepdims=True)
    scaled = lax.rsqrt(jnp.mean(centred * centred, axis=-1, keepdims=True) + EPSILON)
    return (centred * scaled, scaled)


def norm_back(grad_normal, normal, scaled):
    centred_grad = grad_normal - jnp.mean(grad_normal, axis=-1, keepdims=True)
    return scaled * (centred_grad - normal * jnp.mean(grad_normal * normal, axis=-1, keepdims=True))


def exact_gelu(values_in):
    return jax.nn.gelu(values_in, approximate=False)


def contract_rows(left_side, right_side):
    return lax.dot_general(
        left_side, right_side, (((0,), (0,)), ((), ())), preferred_element_type=jnp.float32
    )


def heads_of(flat_block):
    return flat_block.reshape(flat_block.shape[0], HEADS, HEAD_DIM)


def per_device(
    inputs,
    skipped,
    w_skip,
    w_mod,
    w_qkv,
    w_out,
    ff_gain,
    w_up,
    w_down,
    cotangent,
    lengths,
    flow_steps,
):
    w_skip, w_mod, w_qkv, w_out, ff_gain, w_up, w_down = (
        lax.all_gather(w_skip, "grp", axis=0, tiled=True),
        lax.all_gather(w_mod, "grp", axis=0, tiled=True),
        lax.all_gather(w_qkv, "grp", axis=0, tiled=True),
        lax.all_gather(w_out, "grp", axis=0, tiled=True),
        lax.all_gather(ff_gain, "grp", axis=0, tiled=True),
        lax.all_gather(w_up, "grp", axis=0, tiled=True),
        lax.all_gather(w_down, "grp", axis=0, tiled=True),
    )
    frame_count = inputs.shape[1]
    model_width = inputs.shape[2]
    cycle_size = lax.axis_size("blk")
    device_rank = lax.axis_index("blk")
    score_scale = HEAD_DIM ** (-0.5)
    local_frames = jnp.arange(frame_count, dtype=jnp.int32)
    lengths_row = lengths[0]
    own_segment, own_position = layout(lengths_row, device_rank * frame_count + local_frames)

    def segment_of(source):
        return layout(lengths_row, source * frame_count + local_frames)[0]

    def scored(query_block, key_block, query_segment, key_segment):
        raw_scores = (
            jnp.einsum(
                "qhd,khd->hqk",
                heads_of(query_block),
                heads_of(key_block),
                preferred_element_type=jnp.float32,
            )
            * score_scale
        )
        allowed = (query_segment[:, None] == key_segment[None, :])[None]
        return (raw_scores, allowed)

    joined = jnp.concatenate([inputs[0], skipped[0]], axis=1)
    hidden = jnp.dot(joined, w_skip, preferred_element_type=jnp.float32)
    condition = flow_condition(flow_steps[0], model_width).astype(jnp.bfloat16)
    modulation = jnp.dot(condition, w_mod, preferred_element_type=jnp.float32)
    picker = (
        own_segment[:, None] == jnp.arange(lengths_row.shape[0], dtype=jnp.int32)[None, :]
    ).astype(jnp.float32)
    per_frame = jnp.dot(picker, modulation, precision=HIGHEST)
    scale_one = 1.0 + per_frame[:, :model_width]
    normal_one, spread_one = normalize(hidden)
    attn_in = (normal_one * scale_one + per_frame[:, model_width:]).astype(jnp.bfloat16)
    project = jnp.dot(attn_in, w_qkv, preferred_element_type=jnp.float32).reshape(
        frame_count, 3, HEADS, HEAD_DIM
    )
    queries = (
        rotate(project[:, 0], own_position).astype(jnp.bfloat16).reshape(frame_count, model_width)
    )
    keys_own = (
        rotate(project[:, 1], own_position).astype(jnp.bfloat16).reshape(frame_count, model_width)
    )
    values_own = project[:, 2].astype(jnp.bfloat16).reshape(frame_count, model_width)

    def forward_turn(turn_index, carried):
        key_now, value_now, running_top, running_total, running_sum = carried
        source = (device_rank - turn_index) % cycle_size
        raw_scores, allowed = scored(queries, key_now, own_segment, segment_of(source))
        raw_scores = jnp.where(allowed, raw_scores, NEGATIVE)
        new_top = jnp.maximum(running_top, jnp.max(raw_scores, axis=2, keepdims=True))
        weights = jnp.where(allowed, jnp.exp(raw_scores - new_top), 0.0)
        shrink = jnp.exp(running_top - new_top)
        running_total = running_total * shrink + jnp.sum(weights, axis=2, keepdims=True)
        running_sum = running_sum * shrink + jnp.einsum(
            "hqk,khd->hqd",
            weights.astype(jnp.bfloat16),
            heads_of(value_now),
            preferred_element_type=jnp.float32,
        )
        key_now, value_now = from_behind((key_now, value_now), "blk", 1)
        return (key_now, value_now, new_top, running_total, running_sum)

    initial = (
        keys_own,
        values_own,
        jnp.full((HEADS, frame_count, 1), NEGATIVE, jnp.float32),
        jnp.zeros((HEADS, frame_count, 1), jnp.float32),
        jnp.zeros((HEADS, frame_count, HEAD_DIM), jnp.float32),
    )
    finished = lax.fori_loop(0, cycle_size, forward_turn, initial)
    running_top, running_total, running_sum = (finished[2], finished[3], finished[4])
    attended = jnp.transpose(running_sum / running_total, (1, 0, 2)).reshape(
        frame_count, model_width
    )
    log_total = (running_top + jnp.log(running_total))[:, :, 0]
    attended_low = attended.astype(jnp.bfloat16)
    hidden_two = hidden + jnp.dot(attended_low, w_out, preferred_element_type=jnp.float32)
    normal_two, spread_two = normalize(hidden_two)
    gain_vector = ff_gain.astype(jnp.float32)
    ff_in = (normal_two * gain_vector).astype(jnp.bfloat16)
    widened = jnp.dot(ff_in, w_up, preferred_element_type=jnp.float32)
    activated, gelu_back = jax.vjp(exact_gelu, widened)
    activated_low = activated.astype(jnp.bfloat16)
    output = (
        hidden_two + jnp.dot(activated_low, w_down, preferred_element_type=jnp.float32)
    ).astype(jnp.bfloat16)
    upstream = cotangent[0]
    grad_down = contract_rows(activated_low, upstream)
    grad_activated = jnp.dot(upstream, w_down.T, preferred_element_type=jnp.float32)
    grad_widened = gelu_back(grad_activated)[0].astype(jnp.bfloat16)
    grad_up = contract_rows(ff_in, grad_widened)
    grad_ff_in = jnp.dot(grad_widened, w_up.T, preferred_element_type=jnp.float32)
    grad_gain = jnp.sum(grad_ff_in * normal_two, axis=0)
    grad_hidden_two = upstream.astype(jnp.float32) + norm_back(
        grad_ff_in * gain_vector, normal_two, spread_two
    )
    grad_two_low = grad_hidden_two.astype(jnp.bfloat16)
    grad_out = contract_rows(attended_low, grad_two_low)
    grad_attended = jnp.dot(grad_two_low, w_out.T, preferred_element_type=jnp.float32).astype(
        jnp.bfloat16
    )
    delta = jnp.transpose(jnp.sum(heads_of(grad_attended.astype(jnp.float32) * attended), axis=2))
    zero_grad = jnp.zeros((frame_count, model_width), jnp.float32)

    def pair_terms(
        query_block,
        upstream_block,
        key_block,
        value_block,
        total_block,
        delta_block,
        query_segment,
        key_segment,
    ):
        raw_scores, allowed = scored(query_block, key_block, query_segment, key_segment)
        prob_block = jnp.where(allowed, jnp.exp(raw_scores - total_block[:, :, None]), 0.0)
        value_term = jnp.einsum(
            "hqk,qhd->khd",
            prob_block.astype(jnp.bfloat16),
            heads_of(upstream_block),
            preferred_element_type=jnp.float32,
        ).reshape(frame_count, model_width)
        prob_grad = jnp.einsum(
            "qhd,khd->hqk",
            heads_of(upstream_block),
            heads_of(value_block),
            preferred_element_type=jnp.float32,
        )
        score_grad = (prob_block * (prob_grad - delta_block[:, :, None])).astype(jnp.bfloat16)
        query_term = (
            jnp.einsum(
                "hqk,khd->qhd", score_grad, heads_of(key_block), preferred_element_type=jnp.float32
            ).reshape(frame_count, model_width)
            * score_scale
        )
        key_term = (
            jnp.einsum(
                "hqk,qhd->khd",
                score_grad,
                heads_of(query_block),
                preferred_element_type=jnp.float32,
            ).reshape(frame_count, model_width)
            * score_scale
        )
        return (query_term, key_term, value_term)

    def keys_turn(turn_index, carried):
        key_now, value_now, key_grad, value_grad, query_grad = carried
        source = (device_rank - turn_index) % cycle_size
        query_term, key_term, value_term = pair_terms(
            queries,
            grad_attended,
            key_now,
            value_now,
            log_total,
            delta,
            own_segment,
            segment_of(source),
        )
        key_now, value_now = from_behind((key_now, value_now), "blk", 1)
        key_grad, value_grad = (
            from_behind((key_grad + key_term).astype(jnp.bfloat16), "blk", 1).astype(jnp.float32),
            from_behind((value_grad + value_term).astype(jnp.bfloat16), "blk", 1).astype(
                jnp.float32
            ),
        )
        return (key_now, value_now, key_grad, value_grad, query_grad + query_term)

    done = lax.fori_loop(
        0, cycle_size, keys_turn, (keys_own, values_own, zero_grad, zero_grad, zero_grad)
    )
    key_grad, value_grad, query_grad = (done[2], done[3], done[4])
    grad_project = jnp.concatenate(
        [
            rotate_back(heads_of(query_grad), own_position).reshape(frame_count, model_width),
            rotate_back(heads_of(key_grad), own_position).reshape(frame_count, model_width),
            value_grad,
        ],
        axis=1,
    ).astype(jnp.bfloat16)
    grad_qkv = contract_rows(attn_in, grad_project)
    grad_attn_in = jnp.dot(grad_project, w_qkv.T, preferred_element_type=jnp.float32)
    mod_terms = jnp.concatenate([grad_attn_in * normal_one, grad_attn_in], axis=1)
    grad_modulation = jnp.dot(picker.T, mod_terms, precision=HIGHEST)
    grad_mod = jnp.dot(condition.astype(jnp.float32).T, grad_modulation, precision=HIGHEST)
    grad_hidden = grad_hidden_two + norm_back(grad_attn_in * scale_one, normal_one, spread_one)
    grad_hidden_low = grad_hidden.astype(jnp.bfloat16)
    grad_skip_weight = contract_rows(joined, grad_hidden_low)
    grad_joined = jnp.dot(grad_hidden_low, w_skip.T, preferred_element_type=jnp.float32)
    shards = (
        lax.psum_scatter(
            grad_skip_weight.astype(jnp.bfloat16), "grp", scatter_dimension=0, tiled=True
        ).astype(jnp.float32),
        lax.psum_scatter(
            grad_mod.astype(jnp.bfloat16), "grp", scatter_dimension=0, tiled=True
        ).astype(jnp.float32),
        lax.psum_scatter(
            grad_qkv.astype(jnp.bfloat16), "grp", scatter_dimension=0, tiled=True
        ).astype(jnp.float32),
        lax.psum_scatter(
            grad_out.astype(jnp.bfloat16), "grp", scatter_dimension=0, tiled=True
        ).astype(jnp.float32),
        lax.psum_scatter(
            grad_gain.astype(jnp.bfloat16), "grp", scatter_dimension=0, tiled=True
        ).astype(jnp.float32),
        lax.psum_scatter(
            grad_up.astype(jnp.bfloat16), "grp", scatter_dimension=0, tiled=True
        ).astype(jnp.float32),
        lax.psum_scatter(
            grad_down.astype(jnp.bfloat16), "grp", scatter_dimension=0, tiled=True
        ).astype(jnp.float32),
    )
    totals = lax.psum(
        (shards[0], shards[1], shards[2], shards[3], shards[4], shards[5], shards[6]), "blk"
    )
    return (
        output[None],
        grad_joined[:, :model_width][None],
        grad_joined[:, model_width:][None],
        totals[0],
        totals[1],
        totals[2],
        totals[3],
        totals[4],
        totals[5],
        totals[6],
    )


def dot_plain(left_side, right_side):
    return jnp.dot(left_side, right_side, preferred_element_type=jnp.float32)


def dot_across(left_side, right_side):
    return lax.dot_general(
        left_side, right_side, (((1,), (1,)), ((), ())), preferred_element_type=jnp.float32
    )


def ring_place(rank):
    odd = lax.rem(rank, 2)
    return (1 - odd) * (rank // 2) + odd * ((15 - rank) // 2)


def ring_rank(place):
    upper = place // 4
    return (1 - upper) * (2 * place) + upper * (15 - 2 * place)


TICKS = (2, 0, 0, 0, 0, 2, 0, 0, 0, 0, 2, 0, 0, 2, 0, 2, 3, 0, 0, 10, 5, 5, 5)

TILE = 128
UNROLLED = 4
MAIN_MIB = 55
LAST_MIB = 24
RING_TILE = 32


class Ring:
    def __init__(self, part, land, sems, rank, group_rank, turn=None):
        self.part, self.land, self.sems = part, land, sems
        self.rank, self.group_rank = rank, group_rank
        self.place = ring_place(rank)
        self.half = part.shape[1] // 2
        self.copies = {}
        self.turns, self.turn = [], turn

    def block_at(self, offset):
        return ring_rank(lax.rem(self.place + offset + 2 * RING, RING))

    def rows(self, way):
        return pl.ds(way * self.half, self.half)

    def send(self, kind, step, way, source, target):
        to = ring_rank(lax.rem(self.place + (1 if way == 0 else RING - 1), RING))
        copy = pltpu.make_async_remote_copy(
            src_ref=source,
            dst_ref=target,
            send_sem=self.sems.at[kind, 0, way, step],
            recv_sem=self.sems.at[kind, 1, way, step],
            device_id=(to, self.group_rank),
            device_id_type=MESH,
        )
        copy.start()
        self.copies[kind, step, way] = copy

    def sum_step(self, step):
        if step == 1:
            for way in range(2):
                self.copies[0, 0, way].wait_send()
        for way in range(2):
            block = self.block_at((-1 if way == 0 else 1) * (step + 1))
            rows = self.rows(way)
            if step > 0:
                self.copies[0, step - 1, way].wait_recv()
                tile = min(self.half, RING_TILE)

                def add(i, carry, way=way, block=block, tile=tile):
                    at = pl.ds(pl.multiple_of(way * self.half + i * tile, tile), tile)
                    total = self.part[block, at].astype(jnp.float32) + self.land[
                        step - 1, at
                    ].astype(jnp.float32)
                    self.land[step - 1, at] = total.astype(jnp.bfloat16)
                    return carry

                lax.fori_loop(0, self.half // tile, add, 0)
            if step < RING - 1:
                source = self.part.at[block, rows] if step == 0 else self.land.at[step - 1, rows]
                self.send(0, step, way, source, self.land.at[step, rows])

    def spread_step(self, step):
        if step == 0:
            self.close_sum()
        for way in range(2):
            block = self.block_at((-1 if way == 0 else 1) * step)
            rows = self.rows(way)
            if step > 0:
                self.copies[1, step - 1, way].wait_recv()
            if step < RING - 1:
                target = self.part.at[block, rows]
                self.send(1, step, way, target, target)

    def begin(self):
        self.sum_step(0)
        self.left = [functools.partial(self.sum_step, step) for step in range(1, RING)]
        self.left += [functools.partial(self.spread_step, step) for step in range(RING)]
        if self.turn is not None:
            self.left.insert(RING - 1, self.turn_out)

    def turn_out(self):
        place, sems = self.turn
        deep = self.part.shape[1] // ROWS

        def rows(group):
            return pl.ds(pl.multiple_of(group * deep, deep), deep)

        for other in (2, 1, 3):
            to = lax.rem(self.group_rank + other, ROWS)
            copy = pltpu.make_async_remote_copy(
                src_ref=self.land.at[RING - 2, rows(to)],
                dst_ref=place.at[rows(self.group_rank)],
                send_sem=sems.at[0, other - 1],
                recv_sem=sems.at[1, other - 1],
                device_id=(self.rank, to),
                device_id_type=MESH,
            )
            copy.start()
            self.turns.append(copy)
        place[rows(self.group_rank)] = self.land[RING - 2, rows(self.group_rank)]

    def close_sum(self):
        for copy in self.turns:
            copy.wait_recv()
        self.part[self.rank] = self.land[RING - 2] if self.turn is None else self.turn[0][...]

    def finish(self):
        for copy in self.turns:
            copy.wait_send()
        for (kind, step, _), copy in self.copies.items():
            if kind or step:
                copy.wait_send()


def block_kernel(names, *refs):
    n = types.SimpleNamespace(**dict(zip(names, refs)))
    low, full = jnp.bfloat16, jnp.float32
    rank, group_rank = lax.axis_index("blk"), lax.axis_index("grp")
    core, chip = lax.rem(group_rank, 2), group_rank // 2
    sibling = (rank, group_rank + 1 - 2 * core)
    across = (rank, group_rank + 2 - 4 * chip)
    frames, width = n.cotangent.shape
    half = 2 * frames
    columns = width // ROWS
    mine, theirs = core * half, (1 - core) * half
    own_slot = 2 * core + chip
    pair_row, pair_side = rank // 2, lax.rem(rank, 2)
    sent = []

    def lines(offset, size):
        return pl.ds(pl.multiple_of(offset, min(size, 128)), size)

    def slot_of(row):
        return 2 * lax.rem(row, 2) + row // 2

    def row_of(slot):
        return 2 * lax.rem(slot, 2) + slot // 2

    def group(other):
        return lax.rem(group_rank + other, ROWS)

    def block(other):
        return lax.rem(rank + other, RING)

    def link(source, target, send_sem, recv_sem, device):
        return pltpu.make_async_remote_copy(
            src_ref=source,
            dst_ref=target,
            send_sem=send_sem,
            recv_sem=recv_sem,
            device_id=device,
            device_id_type=MESH,
        )

    def push(source, target, sems, index, device):
        copy = link(source, target, sems.at[(0,) + index], sems.at[(1,) + index], device)
        copy.start()
        sent.append(copy)
        return copy

    def load(source, target, index):
        copy = pltpu.make_async_copy(source, target, n.load_sem.at[index])
        copy.start()
        return copy

    def tiles(count, tile, body):
        if count // tile <= UNROLLED:
            for i in range(count // tile):
                body(i * tile)
            return

        def step(i, carry):
            body(pl.multiple_of(i * tile, tile))
            return carry

        lax.fori_loop(0, count // tile, step, 0)

    joined_loads = [
        load((n.inputs, n.skipped)[t // 2].at[:, pl.ds((t % 2) * 512, 512)], n.joined_own.at[t], t)
        for t in range(ROWS)
    ]
    upstream_load = load(n.cotangent, n.upstream.at[lines(own_slot * frames, frames)], 4)
    skip_load = load(n.w_skip, n.skip_held, 5)
    mod_load = load(n.w_mod, n.mod_held, 6)
    out_place = n.out_held.at[lines(group_rank * columns, columns)]
    out_load = load(n.w_out, out_place, 7)
    down_load = load(n.w_down, n.down_held, 8)
    pieces = [(side, kind) for side in range(2) for kind in range(3)]

    def qkv_piece(target, side, kind, first, count):
        at = pl.multiple_of(kind * width + target * columns + side * 128, 128)
        return n.w_qkv.at[lines(first, count), pl.ds(at, 128)]

    def qkv_place(side, kind, first, count):
        rows = lines(group_rank * columns + first, count)
        return n.qkv_held.at[rows, pl.ds((side * 3 + kind) * 128, 128)]

    qkv_loads = [
        load(qkv_piece(group_rank, *piece, 0, columns), qkv_place(*piece, 0, columns), 9 + i)
        for i, piece in enumerate(pieces)
    ]
    hidden_units = n.up_held.shape[1]

    def up_piece(target):
        return n.w_up.at[:, pl.ds(pl.multiple_of(target * hidden_units, 128), hidden_units)]

    up_place = n.up_held.at[lines(group_rank * columns, columns)]
    up_load = load(up_piece(group_rank), up_place, 15)

    def small_tables():
        down = lax.broadcasted_iota(jnp.int32, (8, 128), 0)
        across_lanes = lax.rem(lax.broadcasted_iota(jnp.int32, (8, 128), 1), 64)
        zero = jnp.zeros((8, 128), full)
        step_tile, start_tile, end_tile = zero, zero, zero
        start_lane, end_lane = zero + 1e9, zero
        start = jnp.int32(0)
        for u in range(8):
            end = start + n.lengths[0, u]
            here = down == u
            lane_here = (across_lanes == u) | (across_lanes == u + 8)
            step_tile = jnp.where(here, n.flow_steps[0, u].astype(full), step_tile)
            start_tile = jnp.where(here, start.astype(full), start_tile)
            end_tile = jnp.where(here, end.astype(full), end_tile)
            start_lane = jnp.where(lane_here, start.astype(full), start_lane)
            end_lane = jnp.where(lane_here, end.astype(full), end_lane)
            start = end
        tables = (step_tile, start_tile, end_tile, start_lane, end_lane)
        for i, tile in enumerate(tables):
            n.small[i] = tile
        gain = jnp.broadcast_to(n.own_gain[...].astype(full).reshape(1, columns), (8, columns))
        n.small[5] = gain[:, 0:128]
        n.small[6] = gain[:, 128:256]

    barrier = pltpu.get_barrier_semaphore()
    for other in range(1, ROWS):
        pl.semaphore_signal(barrier, inc=1, device_id=(rank, group(other)), device_id_type=MESH)
    for other in range(1, RING):
        pl.semaphore_signal(barrier, inc=1, device_id=(block(other), group_rank), device_id_type=MESH)
    small_tables()
    for copy in joined_loads:
        copy.wait()
    pl.semaphore_wait(barrier, ROWS + RING - 2)

    joined_place = n.joined.at[lines(own_slot * frames, frames)]
    over_x = (group_rank + 2 - 4 * chip, 2 * (1 - chip) + 1 - core)
    joined_sends = [
        push(n.joined_own.at[to], joined_place, n.joined_sem, (i,), (rank, to))
        for i, to in enumerate((*over_x, sibling[1]))
    ]
    small_sends = [
        push(n.small, n.smalls.at[group_rank], n.small_sem, (o - 1,), (rank, group(o)))
        for o in (2, 1, 3)
    ]
    n.joined[lines(own_slot * frames, frames)] = n.joined_own[group_rank]
    n.smalls[group_rank] = n.small[...]
    def skip_rows(k):
        own_rows, their_rows = lines(mine + k * frames, frames), lines(theirs + k * frames, frames)
        rows = lines(k * frames, frames)
        n.send_one[rows] = dot_plain(n.joined[their_rows], n.skip_held[...]).astype(low)
        copy = push(n.send_one.at[rows], n.land_one.at[0, rows], n.first_sem, (0, k), sibling)
        kept = dot_plain(n.joined[own_rows], n.skip_held[...])
        copy.wait_recv()
        kept = kept + n.land_one[0, rows].astype(full)
        n.keep[rows] = kept
        n.send_two[rows] = kept.astype(low)
        return copy, push(n.send_two.at[rows], n.land_two.at[0, rows], n.second_sem, (0, k), across)

    skip_load.wait()
    joined_sends[2].wait_recv()
    skip_sums = [skip_rows(chip)]

    for copy in small_sends:
        copy.wait_recv()

    steps = jnp.concatenate([n.smalls[(0, 2, 1, 3)[s], 0] for s in range(ROWS)], axis=0)
    steps = jnp.concatenate([steps, steps], axis=1)
    lane = lax.broadcasted_iota(jnp.int32, steps.shape, 1) + lax.rem(group_rank, 2) * columns
    rate = jnp.exp(-math.log(10000.0) * lane.astype(full) / (width // 2))
    angles = 1000.0 * (steps / STEPS) * rate
    turned = jnp.where(group_rank >= 2, jnp.cos(angles), jnp.sin(angles))
    n.condition[...] = (turned / (1.0 + jnp.exp(-turned))).astype(low)
    mod_load.wait()

    def mod_tile(at):
        where = pl.ds(at, 512)
        n.mod_part[:, where] = dot_plain(n.condition[...], n.mod_held[:, where])

    tiles(2 * width, 512, mod_tile)
    mod_first = push(
        n.mod_part.at[pl.ds(pl.multiple_of(16 * (1 - core), 16), 16)], n.mod_land.at[0], n.mod_sem, (0,), sibling
    )

    gains = [n.smalls[r, 5 + i][0:1] for r in range(ROWS) for i in range(2)]
    n.gain[...] = jnp.broadcast_to(jnp.concatenate(gains, axis=1), n.gain.shape)

    def picked(row, first, count):
        spot = (lax.broadcasted_iota(jnp.int32, (count, 128), 0) + first).astype(full)
        return (spot >= n.smalls[row, 3][0:1]) & (spot < n.smalls[row, 4][0:1]), spot

    lanes = lax.broadcasted_iota(jnp.int32, (frames, 128), 1)
    turn_rate = jnp.exp(-math.log(10000.0) * lax.rem(lanes, 32).astype(full) / 32)
    turn_sign = jnp.where(lax.rem(lanes, 64) < 32, -1.0, 1.0)

    def turn_tables(row, first, cosine, sine, at):
        chosen, spot = picked(row, first, frames)
        start = jnp.where(chosen & (lanes < 8), n.smalls[row, 3][0:1], 0.0)
        position = spot - jnp.sum(start, axis=1, keepdims=True)
        angle = position * turn_rate
        cosine[at] = jnp.cos(angle)
        sine[at] = jnp.sin(angle) * turn_sign

    def swapped(value):
        ahead = pltpu.roll(value, 96, 1)
        behind = pltpu.roll(value, 32, 1)
        return jnp.where(lax.rem(lanes, 64) < 32, ahead, behind)

    def partial_sum(index, left_ref, right_tile):
        def to_send(at):
            n.send_one[:, pl.ds(at, 256)] = right_tile(left_ref[lines(theirs, half)], at).astype(low)

        def to_keep(at):
            n.keep[:, pl.ds(at, 256)] = right_tile(left_ref[lines(mine, half)], at)

        if index > 0:
            for copy in group_copies[index - 1][0]:
                copy.wait_send()
        tiles(width, 256, to_send)
        first = [
            push(
                n.send_one.at[pl.ds(k * frames, frames)],
                n.land_one.at[index, pl.ds(k * frames, frames)],
                n.first_sem,
                (index, k),
                sibling,
            )
            for k in range(2)
        ]
        tiles(width, 256, to_keep)
        return first

    def cross_sum(index, first):
        if index > 0:
            for copy in group_copies[index - 1][1]:
                copy.wait_send()
        second = []
        for k in range(2):
            first[k].wait_recv()

            def add(at, k=k):
                where = pl.ds(k * frames + at, TILE)
                total = n.keep[where] + n.land_one[index, where].astype(full)
                n.keep[where] = total
                n.send_two[where] = total.astype(low)

            tiles(frames, TILE, add)
            second.append(
                push(
                    n.send_two.at[pl.ds(k * frames, frames)],
                    n.land_two.at[index, pl.ds(k * frames, frames)],
                    n.second_sem,
                    (index, k),
                    across,
                )
            )
        group_copies[index] = (first, second)
        return second

    group_copies = {}

    down_ring, up_ring, out_ring, qkv_ring, skip_ring = rings = [
        Ring(part, land, sems, rank, group_rank, turn)
        for part, land, sems, turn in (
            (n.down_total, n.down_land, n.down_sem, None),
            (n.up_total, n.up_land, n.up_ring_sem, (n.up_turn, n.turn_sem.at[0])),
            (n.out_total, n.out_land, n.out_ring_sem, None),
            (n.qkv_total, n.qkv_land, n.qkv_ring_sem, (n.qkv_turn, n.turn_sem.at[1])),
            (n.skip_total, n.skip_land, n.skip_ring_sem, None),
        )
    ]
    running = []

    def begin(ring):
        ring.begin()
        running.append(ring)

    def ticks(count):
        for _ in range(count):
            if running:
                ring = running.pop(0)
                ring.left.pop(0)()
                if ring.left:
                    running.append(ring)

    def mean(value):
        return jnp.mean(value, axis=-1, keepdims=True)

    def share(buffer, k, sems, step=None):
        where = lines(mine + k * frames, frames)
        return push(buffer.at[where], buffer.at[where], sems, (k if step is None else step,), sibling)

    side_y, side_z = lax.rem(rank, 2), lax.rem(rank // 2, 2)
    to_y, to_z = 1 - 2 * side_y, 2 - 4 * side_z
    beside = (rank + to_y, group_rank)
    around = (beside, (rank + to_z, group_rank), (rank + to_y + to_z, group_rank))
    part_rows = columns // 2
    few_rows = columns // 4
    first_row = (2 * side_z + side_y) * few_rows
    qkv_sends = [
        [
            push(
                qkv_piece(to, *piece, first_row, few_rows),
                qkv_place(*piece, first_row, few_rows),
                n.qkv_sem,
                (i, j),
                (rank, to),
            )
            for j, piece in enumerate(pieces)
        ]
        for i, to in enumerate(over_x)
    ]
    qkv_sends.append(
        [
            push(
                qkv_piece(sibling[1], *piece, 0, columns),
                qkv_place(*piece, 0, columns),
                n.qkv_sem,
                (2, j),
                sibling,
            )
            for j, piece in enumerate(pieces)
        ]
    )

    mod_first.wait_recv()
    mod_mine = n.mod_part[pl.ds(pl.multiple_of(16 * core, 16), 16)] + n.mod_land[0]
    n.mod_send[...] = mod_mine.astype(low)
    mod_second = push(n.mod_send, n.mod_cross, n.mod_sem, (1,), across)
    for copy in joined_sends[:2]:
        copy.wait_recv()
    skip_sums.append(skip_rows(1 - chip))
    group_copies[0] = tuple(zip(*skip_sums))
    own_lines = lines(own_slot * frames, frames)
    for slot in range(ROWS):
        turn_tables(
            (0, 2, 1, 3)[slot],
            rank * frames,
            n.cosine,
            n.sine,
            pl.ds(slot * frames, frames),
        )
    mod_second.wait_recv()
    mod_total = n.mod_send[...].astype(full) + n.mod_cross[...].astype(full)
    for k in range(2):
        row = 2 * k + core
        values = mod_total[8 * k : 8 * k + 8]
        high = values.astype(low).astype(full)
        stack = jnp.concatenate([high, values - high], axis=0).astype(low)
        chosen = picked(row, rank * frames, frames)[0]
        picker = jnp.where(chosen, 1.0, 0.0).astype(low)[:, :16]
        where = pl.ds(k * frames, frames)
        n.scale_one[where] = 1.0 + dot_plain(picker, stack[:, :width])
        n.shift_one[where] = dot_plain(picker, stack[:, width:])

    qkv_passed = []
    for i, source in enumerate(over_x):
        for copy in qkv_sends[i]:
            copy.wait_recv()
        where = n.qkv_held.at[lines(source * columns + first_row, few_rows)]
        for j, to in enumerate(around):
            qkv_passed.append(push(where, where, n.qkv_pass_sem, (i, j), to))
    attn_sends = []
    for step in range(2):
        k = chip if step else 1 - chip
        skip_rows_here = lines(k * frames, frames)
        link(
            n.send_two.at[skip_rows_here],
            n.land_two.at[0, skip_rows_here],
            n.second_sem.at[0, 0, k],
            n.second_sem.at[1, 0, k],
            across,
        ).wait_recv()

        def norm_one(at, k=k):
            where = lines(k * frames + at, TILE)
            hidden = n.keep[where] + n.land_two[0, where].astype(full)
            n.hidden[where] = hidden
            centred = hidden - mean(hidden)
            spread = lax.rsqrt(mean(centred * centred) + EPSILON)
            normal = centred * spread
            n.normal_one[where] = normal
            n.spread_one[where] = jnp.broadcast_to(spread, (TILE, 128))
            n.attn_in[lines(mine + k * frames + at, TILE)] = (
                normal * n.scale_one[where] + n.shift_one[where]
            ).astype(low)

        tiles(frames, TILE, norm_one)
        attn_sends.append(share(n.attn_in, k, n.attn_sem, step))

    def part_of(reference, first):
        return reference.at[lines(first + side_y * part_rows, part_rows)]

    up_sends = [
        push(
            part_of(up_piece(to), 0),
            part_of(n.up_held, group_rank * columns),
            n.up_sem,
            (i,),
            (rank, to),
        )
        for i, to in enumerate(over_x)
    ]
    up_sends.append(push(up_piece(sibling[1]), up_place, n.up_sem, (2,), sibling))
    out_sends = [
        push(n.w_out, out_place, n.out_sem, (i,), device) for i, device in enumerate((across, sibling))
    ]

    def pass_on(buffer, copies, sems):
        passed = []
        for i, source in enumerate(over_x):
            copies[i].wait_recv()
            where = part_of(buffer, source * columns)
            passed.append(push(where, where, sems, (i,), beside))
        return passed

    upstream_load.wait()
    upstream_sends = [
        push(n.upstream.at[own_lines], n.upstream.at[own_lines], n.upstream_sem, (i,), device)
        for i, device in enumerate((across, sibling))
    ]

    for copy in qkv_loads:
        copy.wait()
    for copy in qkv_sends[2] + qkv_passed:
        copy.wait_recv()

    def to_heads(offset, value_of, target, sems, send_buffer, columns_of):
        for k in range(2):
            slot = offset // frames + k
            for side in range(2):
                to = 2 * row_of(slot) + side
                if value_of is not None:
                    send_buffer[to] = value_of(k, side, slot)

                @pl.when(to != rank)
                def _():
                    link(
                        send_buffer.at[to, :, columns_of],
                        target.at[lines(rank * frames, frames), columns_of],
                        sems.at[0, to],
                        sems.at[1, rank],
                        (to, group_rank),
                    ).start()

                @pl.when(to == rank)
                def _():
                    target[lines(rank * frames, frames), columns_of] = send_buffer[to, :, columns_of]

    def heads_arrive(target, sems, columns_of, then=None):
        for other in range(RING):
            source = block(other)
            if other:
                where = target.at[lines(source * frames, frames), columns_of]
                link(
                    where, where, sems.at[0, source], sems.at[1, source], (source, group_rank)
                ).wait_recv()
            if then is not None:
                then(pl.multiple_of(source * frames, frames))

    def project_half(offset):
        def project_tile(at):
            n.project[:, pl.ds(at, 256)] = dot_plain(
                n.attn_in[lines(offset, half)], n.qkv_held[:, pl.ds(at, 256)]
            )

        tiles(3 * columns, 256, project_tile)

        def value_of(k, side, slot):
            where = lines(slot * frames, frames)
            cosine, sine = n.cosine[where], n.sine[where]
            blocks = []
            for kind in range(3):
                value = n.project[pl.ds(k * frames, frames), pl.ds((side * 3 + kind) * 128, 128)]
                if kind < 2:
                    value = value * cosine + swapped(value) * sine
                blocks.append(value.astype(low))
            return jnp.concatenate(blocks, axis=1)

        to_heads(offset, value_of, n.paired, n.pair_sem, n.pair_send, pl.ds(0, 256))

    project_half(mine)
    for copy in attn_sends:
        copy.wait_recv()
    project_half(theirs)
    for offset in (mine, theirs):
        to_heads(offset, None, n.paired, n.value_sem, n.pair_send, pl.ds(256, 128))

    def row_tables(at):
        turn_tables(pair_row, at, n.row_cosine, n.row_sine, pl.ds(at, frames))
        chosen = jnp.where(picked(pair_row, at, frames)[0], 1.0, 0.0)
        n.chosen[pl.ds(at, frames)] = chosen.astype(low)

    tiles(RING * frames, frames, row_tables)
    def masked_parts(at):
        where = pl.ds(at, frames)
        query, key = n.paired[where, 0:128], n.paired[where, 128:256]
        chosen = n.chosen[where]
        first_head = lanes < 64
        blocked = jnp.where(
            lax.rem(lanes, 64) < 8, NEGATIVE * (1.0 - chosen.astype(full)), 0.0
        ).astype(low)
        scaled = (query.astype(full) * HEAD_DIM ** (-0.5)).astype(low)
        n.query_head[0, where] = jnp.where(first_head, scaled, chosen)
        n.query_head[1, where] = jnp.where(first_head, chosen, scaled)
        n.key_head[0, where] = jnp.where(first_head, key, blocked)
        n.key_head[1, where] = jnp.where(first_head, blocked, key)

    heads_arrive(n.paired, n.pair_sem, pl.ds(0, 256), masked_parts)
    up_passed = pass_on(n.up_held, up_sends, n.up_pass_sem)
    out_sends[0].wait_recv()
    where = n.out_held.at[lines(across[1] * columns, columns)]
    out_sends.append(push(where, where, n.out_sem, (2,), sibling))
    all_frames = RING * frames
    pair_place = (lines(slot_of(pair_row) * frames, frames), lines(pair_side * 128, 128))

    def score(at):
        where = pl.ds(at, half)
        for head in range(2):
            scores = dot_across(n.query_head[head, where], n.key_head[head])
            top = jnp.max(scores, axis=1, keepdims=True)
            weights = jnp.exp(scores - top)
            total = jnp.sum(weights, axis=1, keepdims=True)
            n.shares[head, where] = (weights * (1.0 / total)).astype(low)

    tiles(all_frames, half, score)
    heads_arrive(n.paired, n.value_sem, pl.ds(256, 128))

    def attend(at):
        where = pl.ds(at, half)
        sums = [dot_plain(n.shares[head, where], n.paired[:, 256:384]) for head in range(2)]
        first_head = lax.broadcasted_iota(jnp.int32, (half, 128), 1) < 64
        value = jnp.where(first_head, sums[0], sums[1])
        n.attended_pair[where] = value
        n.attended_send[where] = value.astype(low)
        for k in range(2):
            to = at // frames + k
            place = lines(at + k * frames, frames)

            @pl.when(to != rank)
            def _():
                link(
                    n.attended_send.at[place],
                    n.attended.at[pair_place],
                    n.attended_sem.at[0, to],
                    n.attended_sem.at[1, rank],
                    (to, group_rank),
                ).start()

            @pl.when(to == rank)
            def _():
                n.attended[pair_place] = n.attended_send[place]

    tiles(all_frames, half, attend)

    def pairs_arrive(buffer, sems, pitch, first, wide):
        for other in range(1, RING):
            source = block(other)
            where = buffer.at[
                lines(slot_of(source // 2) * frames, frames),
                pl.ds(pl.multiple_of(lax.rem(source, 2) * pitch + first, 128), wide),
            ]
            link(where, where, sems.at[0, source], sems.at[1, source], (source, group_rank)).wait_recv()

    upstream_sends[0].wait_recv()
    other_lines = lines((2 * core + 1 - chip) * frames, frames)
    upstream_sends.append(
        push(n.upstream.at[other_lines], n.upstream.at[other_lines], n.upstream_sem, (2,), sibling)
    )
    pairs_arrive(n.attended, n.attended_sem, 128, 0, 128)

    own_columns = pl.ds(pl.multiple_of(group_rank * columns, columns), columns)
    attended_sends = [
        push(
            n.attended.at[lines(first, half)],
            n.attended_all.at[:, own_columns],
            n.attended_all_sem,
            (i,),
            (rank, to),
        )
        for i, (first, to) in enumerate(
            ((mine, over_x[0]), (theirs, over_x[1]), (theirs, sibling[1]))
        )
    ]
    n.attended_all[:, own_columns] = n.attended[lines(mine, half)]
    out_load.wait()
    for copy in out_sends[1:] + attended_sends:
        copy.wait_recv()

    def out_tile(at):
        n.keep[:, pl.ds(at, 256)] = dot_plain(n.attended_all[...], n.out_held[:, pl.ds(at, 256)])

    tiles(width, 256, out_tile)
    ff_sends = []
    for k in range(2):

        def norm_two(at, k=k):
            where = pl.ds(k * frames + at, TILE)
            hidden = n.hidden[where] + n.keep[where]
            n.hidden[where] = hidden
            centred = hidden - mean(hidden)
            spread = lax.rsqrt(mean(centred * centred) + EPSILON)
            normal = centred * spread
            n.normal_two[where] = normal
            n.spread_two[where] = jnp.broadcast_to(spread, (TILE, 128))
            n.ff_in[lines(mine + k * frames + at, TILE)] = (normal * n.gain[0:1]).astype(low)

        tiles(frames, TILE, norm_two)
        ff_sends.append(share(n.ff_in, k, n.ff_sem))

    up_load.wait()
    down_load.wait()
    for copy in up_sends[2:] + up_passed:
        copy.wait_recv()
    for copy in upstream_sends[1:]:
        copy.wait_recv()

    def feed_half(offset):
        where = lines(offset, half)

        def feed_tile(at):
            widened = dot_plain(n.ff_in[where], n.up_held[:, pl.ds(at, 256)])
            grad = dot_across(n.upstream[where], n.down_held[pl.ds(at, 256)])
            share_of = 0.5 * (1.0 + lax.erf(widened * math.sqrt(0.5)))
            slope = share_of + widened * jnp.exp(-0.5 * widened * widened) * (
                1.0 / math.sqrt(2.0 * math.pi)
            )
            n.activated[where, pl.ds(at, 256)] = (widened * share_of).astype(low)
            n.grad_widened[where, pl.ds(at, 256)] = (grad * slope).astype(low)

        tiles(hidden_units, 256, feed_tile)

    feed_half(mine)
    for copy in ff_sends:
        copy.wait_recv()
    feed_half(theirs)
    first = partial_sum(
        1, n.grad_widened, lambda left, at: dot_across(left, n.up_held[pl.ds(at, 256)])
    )
    second = cross_sum(1, first)

    def down_tile(at):
        value = contract_rows(n.activated[:, pl.ds(at, 256)], n.upstream[...]).astype(low)
        n.down_total[at // 128] = value[:128]
        n.down_total[at // 128 + 1] = value[128:]

    tiles(hidden_units, 256, down_tile)
    begin(down_ring)

    def up_tile(at):
        value = contract_rows(n.ff_in[:, pl.ds(at, columns)], n.grad_widened[...]).astype(low)
        deep = columns // RING
        for j in range(RING):
            n.up_total[j, pl.ds(pl.multiple_of(at // RING, deep), deep)] = value[
                j * deep : (j + 1) * deep
            ]

    tiles(width, columns, up_tile)
    begin(up_ring)
    ticks(TICKS[0])

    gain_sums = jnp.zeros((1, width), full)
    grad_sends = []
    for k in range(2):
        second[k].wait_recv()
        weight = (1 - jnp.abs(chip - k)).astype(full)

        def back_two(i, sums, k=k, weight=weight):
            at = pl.multiple_of(i * TILE, TILE)
            where = pl.ds(k * frames + at, TILE)
            grad = n.keep[where] + n.land_two[1, where].astype(full)
            normal = n.normal_two[where]
            scaled = grad * n.gain[0:1]
            back = n.spread_two[where][:, 0:1] * (
                scaled - mean(scaled) - normal * mean(scaled * normal)
            )
            total = n.upstream[lines(mine + k * frames + at, TILE)].astype(full) + back
            n.grad_two[where] = total
            n.grad_two_low[lines(mine + k * frames + at, TILE)] = total.astype(low)
            return sums + weight * jnp.sum(grad * normal, axis=0, keepdims=True)

        gain_sums = lax.fori_loop(0, frames // TILE, back_two, gain_sums)
        grad_sends.append(share(n.grad_two_low, k, n.grad_two_sem))
        ticks(TICKS[1 + k])
    n.mod_sums[8:16] = jnp.zeros((8, 2 * width), full)
    n.mod_sums[8:9, :width] = gain_sums

    def attended_half(offset):
        value = dot_across(
            n.grad_two_low[lines(offset, half)], n.out_held[lines(group_rank * columns, columns)]
        ).astype(low)

        def value_of(k, side, slot):
            return value[k * frames : (k + 1) * frames, side * 128 : side * 128 + 128]

        to_heads(
            offset, value_of, n.grad_pair, n.grad_pair_sem, n.grad_pair_send, pl.ds(0, 128)
        )

    attended_half(mine)
    ticks(TICKS[3])
    for copy in grad_sends:
        copy.wait_recv()
    attended_half(theirs)
    ticks(TICKS[4])
    value = contract_rows(n.attended[...], n.grad_two_low[...]).astype(low)
    for j in range(RING):
        n.out_total[j] = value[j * 32 : (j + 1) * 32]
    ticks(TICKS[5])

    first = partial_sum(2, n.activated, lambda left, at: dot_plain(left, n.down_held[:, pl.ds(at, 256)]))
    ticks(TICKS[6])
    output_second = cross_sum(2, first)
    ticks(TICKS[7])

    def turn_queries(at):
        where = pl.ds(at, frames)
        n.query_turned[:, where] = jnp.transpose(n.paired[where, 0:128].astype(full)).astype(low)

    tiles(RING * frames, frames, turn_queries)

    def turn_upstream(at):
        where = pl.ds(at, frames)
        n.grad_turned[:, where] = jnp.transpose(n.grad_pair[where].astype(full)).astype(low)

    heads_arrive(n.grad_pair, n.grad_pair_sem, pl.ds(0, 128), turn_upstream)
    n.key_turned[...] = jnp.zeros(n.key_turned.shape, full)
    n.value_turned[...] = jnp.zeros(n.value_turned.shape, full)

    def back_turned(value, where):
        return value * n.row_cosine[where] - swapped(value) * n.row_sine[where]

    project_slot = lines(slot_of(pair_row) * frames, frames)

    def project_back(to, place, first, wide, sems):
        source = n.project_send.at[place, pl.ds(first, wide)]
        at = pl.ds(pl.multiple_of(pair_side * 384 + first, 128), wide)

        @pl.when(to != rank)
        def _():
            target = n.grad_project.at[project_slot, at]
            link(source, target, sems.at[0, to], sems.at[1, rank], (to, group_rank)).start()

        @pl.when(to == rank)
        def _():
            n.grad_project[project_slot, at] = source[...]

    def attend_back(at):
        where = pl.ds(at, half)
        first_head = lax.broadcasted_iota(jnp.int32, (half, 128), 1) < 64
        grad = n.grad_pair[where]
        product = grad.astype(full) * n.attended_pair[where]
        terms = []
        for head in range(2):
            here = first_head if head == 0 else jnp.logical_not(first_head)
            delta = jnp.sum(jnp.where(here, product, 0.0), axis=1, keepdims=True)
            grad_head = jnp.where(here, grad, jnp.zeros_like(grad))
            prob_grad = dot_across(grad_head, n.paired[:, 256:384])
            shares = n.shares[head, where]
            score_grad = (shares.astype(full) * (prob_grad - delta)).astype(low)
            terms.append(dot_plain(score_grad, n.paired[:, 128:256]))
            rows = pl.ds(head * 64, 64)
            n.value_turned[rows] += dot_plain(n.grad_turned[rows, where], shares)
            n.key_turned[rows] += dot_plain(n.query_turned[rows, where], score_grad)
        query_grad = jnp.where(first_head, terms[0], terms[1]) * HEAD_DIM ** (-0.5)
        for k in range(2):
            place = lines(at + k * frames, frames)
            n.project_send[place, 0:128] = back_turned(
                query_grad[k * frames : (k + 1) * frames], place
            ).astype(low)
            project_back(at // frames + k, place, 0, 128, n.query_sem)

    for part in range(4):
        attend_back(part * half)
        ticks(TICKS[8 + part])
    def keys_back(at):
        place = pl.ds(at, frames)
        key_grad = jnp.transpose(n.key_turned[:, place]) * HEAD_DIM ** (-0.5)
        n.project_send[place, 128:256] = back_turned(key_grad, place).astype(low)
        n.project_send[place, 256:384] = jnp.transpose(n.value_turned[:, place]).astype(low)
        project_back(at // frames, place, 128, 256, n.project_sem)

    tiles(all_frames, frames, keys_back)

    ticks(TICKS[12])

    for copy in output_second:
        copy.wait_recv()

    def finish_output(at):
        where = lines(chip * frames + at, TILE)
        n.output[pl.ds(at, TILE)] = (
            n.hidden[where] + n.keep[where] + n.land_two[2, where].astype(full)
        ).astype(low)

    tiles(frames, TILE, finish_output)
    ticks(TICKS[13])
    pairs_arrive(n.grad_project, n.query_sem, 384, 0, 128)
    pairs_arrive(n.grad_project, n.project_sem, 384, 128, 256)

    first = partial_sum(
        3, n.grad_project, lambda left, at: dot_across(left, n.qkv_held[pl.ds(at, 256)])
    )
    ticks(TICKS[14])
    second = cross_sum(3, first)
    ticks(TICKS[15])

    def qkv_tile(at):
        value = contract_rows(n.attn_in[:, pl.ds(at, columns)], n.grad_project[...]).astype(low)
        deep = columns // RING
        for j in range(RING):
            n.qkv_total[j, pl.ds(pl.multiple_of(at // RING, deep), deep)] = value[
                j * deep : (j + 1) * deep
            ]

    tiles(width, columns, qkv_tile)
    begin(qkv_ring)
    ticks(TICKS[16])
    hidden_sends = []
    for k in range(2):
        second[k].wait_recv()

        def back_one(at, k=k):
            where = pl.ds(k * frames + at, TILE)
            grad = n.keep[where] + n.land_two[3, where].astype(full)
            normal = n.normal_one[where]
            scaled = grad * n.scale_one[where]
            back = n.spread_one[where][:, 0:1] * (
                scaled - mean(scaled) - normal * mean(scaled * normal)
            )
            n.grad_hidden[lines(mine + k * frames + at, TILE)] = (n.grad_two[where] + back).astype(low)

            @pl.when(chip == k)
            def _():
                n.shift_one[pl.ds(at, TILE)] = grad * normal
                n.shift_one[pl.ds(frames + at, TILE)] = grad

        tiles(frames, TILE, back_one)
        hidden_sends.append(share(n.grad_hidden, k, n.grad_hidden_sem))
        ticks(TICKS[17 + k])

    for copy in hidden_sends:
        copy.wait_recv()

    def skip_weight_tile(at):
        value = contract_rows(n.joined[:, pl.ds(at, 256)], n.grad_hidden[...]).astype(low)
        for j in range(4):
            n.skip_total[at // 64 + j] = value[j * 64 : (j + 1) * 64]

    tiles(n.joined.shape[1], 256, skip_weight_tile)
    begin(skip_ring)
    begin(out_ring)
    ticks(TICKS[19])
    spot = (lax.broadcasted_iota(jnp.int32, (8, frames), 1) + rank * frames).astype(full)
    chosen = (spot >= n.small[1]) & (spot < n.small[2])
    picker = jnp.where(chosen, 1.0, 0.0)

    def mod_sum(at):
        for part in range(2):
            n.mod_sums[0:8, pl.ds(part * width + at, 512)] = jnp.dot(
                picker, n.shift_one[pl.ds(part * frames, frames), pl.ds(at, 512)], precision=HIGHEST
            )

    tiles(width, 512, mod_sum)
    for other in range(1, RING):
        to = block(other)
        push(
            n.mod_sums.at[:, pl.ds(pl.multiple_of(to * 256, 256), 256)],
            n.sums_land.at[rank],
            n.sums_sem,
            (other - 1,),
            (to, group_rank),
        )
    sums_copies = sent[-(RING - 1) :]
    n.sums_land[rank] = n.mod_sums[:, pl.ds(pl.multiple_of(rank * 256, 256), 256)]
    ticks(TICKS[20])
    back = dot_across(n.grad_hidden[...], n.skip_held[...]).astype(low)
    n.joined_send[...] = back
    grad_joined_copies = []
    for other in (2, 1, 3):
        to = group(other)
        grad_joined_copies.append(
            push(
                n.joined_send.at[lines(slot_of(to) * frames, frames)],
                n.grad_joined.at[group_rank],
                n.grad_joined_sem,
                (other - 1,),
                (rank, to),
            )
        )
    n.grad_joined[group_rank] = n.joined_send[own_lines]
    ticks(TICKS[21])
    for copy in sums_copies:
        copy.wait_recv()
    n.sums_send[...] = jnp.sum(n.sums_land[...], axis=0).astype(low)
    n.mod_grad[rank, group_rank] = n.sums_send[...]
    group_sums = [
        push(
            n.sums_send,
            n.mod_grad.at[rank, group_rank],
            n.sums_group_sem,
            (other - 1,),
            (rank, group(other)),
        )
        for other in (2, 1, 3)
    ]
    ticks(TICKS[22])
    for copy in group_sums:
        copy.wait_recv()
    mod_spread = [
        push(
            n.mod_grad.at[rank],
            n.mod_grad.at[rank],
            n.sums_block_sem,
            (other - 1,),
            (block(other), group_rank),
        )
        for other in range(1, RING)
    ]

    ticks(5 * (2 * RING + 1))
    for ring in rings:
        ring.finish()
    for copy in mod_spread + grad_joined_copies:
        copy.wait_recv()
    gain_grad = n.mod_grad[group_rank, 0].astype(full)
    for row in range(1, ROWS):
        gain_grad = gain_grad + n.mod_grad[group_rank, row].astype(full)
    n.gain_grad[...] = gain_grad[8:16]
    for index, copy in enumerate(sent):
        if not any(copy is other for pair in list(group_copies.values())[:-1] for kind in pair for other in kind):
            copy.wait_send()
    for sems, wide in (
        (n.pair_sem, 256),
        (n.value_sem, 128),
        (n.attended_sem, 128),
        (n.grad_pair_sem, 128),
        (n.query_sem, 128),
        (n.project_sem, 256),
    ):
        for other in range(1, RING):
            to = block(other)
            where = n.project_send.at[lines(to * frames, frames), pl.ds(0, wide)]
            link(where, where, sems.at[0, to], sems.at[1, to], (to, group_rank)).wait_send()


def block_call(
    inputs,
    skipped,
    w_skip,
    w_mod,
    w_qkv,
    w_out,
    w_up,
    w_down,
    cotangent,
    own_gain,
    lengths,
    flow_steps,
):
    low, full = jnp.bfloat16, jnp.float32
    frames, width = inputs.shape
    tokens, half = ROWS * frames, 2 * frames
    columns = width // ROWS
    hidden_units = w_down.shape[0]
    joint = w_skip.shape[0]
    all_frames = RING * frames
    deep = width // RING

    held = dict(
        inputs=inputs,
        skipped=skipped,
        w_skip=w_skip,
        w_mod=w_mod,
        w_qkv=w_qkv,
        w_out=w_out,
        w_up=w_up,
        w_down=w_down,
        cotangent=cotangent,
        own_gain=own_gain,
        lengths=lengths,
        flow_steps=flow_steps,
    )
    given = dict(
        output=((frames, width), low),
        grad_joined=((ROWS, frames, joint), low),
        condition=((ROWS * 8, columns), low),
        mod_grad=((RING, ROWS, 16, 256), low),
        gain_grad=((8, columns), full),
        down_total=((RING, hidden_units // RING, width), low),
        up_total=((RING, deep, hidden_units), low),
        qkv_total=((RING, deep, 3 * columns), low),
        skip_total=((RING, joint // RING, width), low),
        out_total=((RING, columns // RING, width), low),
    )
    buffers = dict(
        joined_own=((ROWS, frames, joint), low),
        joined=((tokens, joint), low),
        upstream=((tokens, width), low),
        skip_held=(w_skip.shape, low),
        mod_held=(w_mod.shape, low),
        out_held=((width, width), low),
        attended_all=((half, width), low),
        down_held=(w_down.shape, low),
        qkv_held=((width, 3 * columns), low),
        up_held=((width, hidden_units), low),
        small=((7, 8, 128), full),
        smalls=((ROWS, 7, 8, 128), full),
        mod_part=((ROWS * 8, 2 * width), full),
        mod_land=((1, 16, 2 * width), full),
        mod_send=((16, 2 * width), low),
        mod_cross=((16, 2 * width), low),
        gain=((8, width), full),
        cosine=((tokens, 128), full),
        sine=((tokens, 128), full),
        row_cosine=((all_frames, 128), full),
        row_sine=((all_frames, 128), full),
        chosen=((all_frames, 128), low),
        send_one=((half, width), low),
        send_two=((half, width), low),
        keep=((half, width), full),
        land_one=((4, half, width), low),
        land_two=((4, half, width), low),
        scale_one=((half, width), full),
        shift_one=((half, width), full),
        hidden=((half, width), full),
        normal_one=((half, width), full),
        spread_one=((half, 128), full),
        normal_two=((half, width), full),
        spread_two=((half, 128), full),
        grad_two=((half, width), full),
        attn_in=((tokens, width), low),
        project=((half, 3 * columns), full),
        pair_send=((RING, frames, 384), low),
        paired=((all_frames, 384), low),
        query_head=((2, all_frames, 128), low),
        key_head=((2, all_frames, 128), low),
        query_turned=((128, all_frames), low),
        shares=((2, all_frames, all_frames), low),
        attended_pair=((all_frames, 128), full),
        attended_send=((all_frames, 128), low),
        attended=((tokens, columns), low),
        ff_in=((tokens, width), low),
        activated=((tokens, hidden_units), low),
        grad_widened=((tokens, hidden_units), low),
        grad_two_low=((tokens, width), low),
        grad_pair_send=((RING, frames, 128), low),
        grad_pair=((all_frames, 128), low),
        grad_turned=((128, all_frames), low),
        key_turned=((128, all_frames), full),
        value_turned=((128, all_frames), full),
        project_send=((all_frames, 384), low),
        grad_project=((tokens, 3 * columns), low),
        grad_hidden=((tokens, width), low),
        mod_sums=((16, 2 * width), full),
        sums_land=((RING, 16, 256), full),
        sums_send=((16, 256), low),
        joined_send=((tokens, joint), low),
        down_land=((RING - 1, hidden_units // RING, width), low),
        up_land=((RING - 1, deep, hidden_units), low),
        qkv_land=((RING - 1, deep, 3 * columns), low),
        skip_land=((RING - 1, joint // RING, width), low),
        out_land=((RING - 1, columns // RING, width), low),
        up_turn=((deep, hidden_units), low),
        qkv_turn=((deep, 3 * columns), low),
    )
    sems = dict(
        load_sem=(16,),
        joined_sem=(2, 3),
        small_sem=(2, 3),
        qkv_sem=(2, 3, 6),
        qkv_pass_sem=(2, 2, 3),
        up_sem=(2, 3),
        up_pass_sem=(2, 2),
        out_sem=(2, 3),
        attended_all_sem=(2, 3),
        mod_sem=(2, 2),
        first_sem=(2, 4, 2),
        second_sem=(2, 4, 2),
        upstream_sem=(2, 3),
        attn_sem=(2, 2),
        ff_sem=(2, 2),
        grad_two_sem=(2, 2),
        grad_hidden_sem=(2, 2),
        pair_sem=(2, RING),
        attended_sem=(2, RING),
        grad_pair_sem=(2, RING),
        query_sem=(2, RING),
        project_sem=(2, RING),
        value_sem=(2, RING),
        grad_joined_sem=(2, 3),
        sums_sem=(2, RING - 1),
        sums_group_sem=(2, 3),
        sums_block_sem=(2, RING - 1),
        down_sem=(2, 2, 2, RING - 1),
        up_ring_sem=(2, 2, 2, RING - 1),
        qkv_ring_sem=(2, 2, 2, RING - 1),
        skip_ring_sem=(2, 2, 2, RING - 1),
        out_ring_sem=(2, 2, 2, RING - 1),
        turn_sem=(2, 2, 3),
    )
    names = [*held, *given, *buffers, *sems]
    vmem = pl.BlockSpec(memory_space=pltpu.VMEM)
    anywhere = pl.BlockSpec(memory_space=pl.ANY)
    return pl.pallas_call(
        functools.partial(block_kernel, names),
        out_shape=[pltpu.VMEM(*spec) for spec in given.values()],
        in_specs=[anywhere] * 9 + [vmem] + [pl.BlockSpec(memory_space=pltpu.SMEM)] * 2,
        out_specs=[vmem] * len(given),
        scratch_shapes=[pltpu.VMEM(*spec) for spec in buffers.values()]
        + [pltpu.SemaphoreType.DMA(shape) for shape in sems.values()],
        compiler_params=pltpu.CompilerParams(
            collective_id=0,
            has_side_effects=True,
            vmem_limit_bytes=MAIN_MIB * 1024 * 1024,
        ),
    )(*held.values())


def finish_kernel(names, *refs):
    n = types.SimpleNamespace(**dict(zip(names, refs)))
    full = jnp.float32
    pieces = 4
    chunks = RING // pieces

    def start(source, target, sem):
        copy = pltpu.make_async_copy(source, target, sem)
        copy.start()
        return copy

    def widen_rows(source, target, p):
        deep, wide = source.shape[1:]
        target[pl.ds(p * chunks * deep, chunks * deep)] = (
            source[pl.ds(p * chunks, chunks)].astype(full).reshape(chunks * deep, wide)
        )

    def widen_columns(source, target, p):
        deep, wide = source.shape[1] // ROWS, source.shape[2]
        kinds = wide // 256 if wide % 1024 else 1
        step = 128 if kinds > 1 else wide
        for j in range(chunks):
            to = pl.ds((p * chunks + j) * deep, deep)
            for r in range(ROWS):
                value = source[p * chunks + j, pl.ds(r * deep, deep)].astype(full)
                for i in range(wide // step):
                    side, kind = i // kinds, i % kinds
                    at = kind * (ROWS * wide // kinds) + r * (wide // kinds) + side * step
                    target[to, pl.ds(at, step)] = value[:, i * step : (i + 1) * step]

    work = (
        (n.down, n.down_out, n.grad_down, widen_rows),
        (n.up, n.up_out, n.grad_up, widen_columns),
        (n.qkv, n.qkv_out, n.grad_qkv, widen_columns),
        (n.skip, n.skip_out, n.grad_skip, widen_rows),
        (n.out, n.out_out, n.grad_out, widen_rows),
    )
    sent = [start(n.output, n.output_back, n.small_sem.at[3])]
    for p in range(pieces):
        for i, (held, wide, target, widen) in enumerate(work):
            widen(held, wide, p)
            deep = target.shape[0] // pieces
            rows = pl.ds(p * deep, deep)
            sent.append(start(wide.at[rows], target.at[rows], n.out_sem.at[i, p]))
    for i in range(RING):
        sums = [n.mod[i, r].astype(full)[0:8] for r in (0, 2, 1, 3)]
        n.mod_out[:, pl.ds(i * 256, 256)] = contract_rows(
            n.condition[...], jnp.concatenate(sums, axis=0).astype(jnp.bfloat16)
        )
    sent.append(start(n.mod_out, n.grad_mod, n.small_sem.at[4]))
    wide = n.joined.shape[2]
    for r in range(ROWS):
        n.joined_out[r // 2, :, pl.ds((r % 2) * wide, wide)] = n.joined[r].astype(full)
    sent.append(start(n.joined_out.at[0], n.grad_inputs, n.small_sem.at[5]))
    sent.append(start(n.joined_out.at[1], n.grad_skipped, n.small_sem.at[6]))
    n.grad_gain[...] = n.gain[0:1]
    for copy in sent:
        copy.wait()


def finish_call(output, joined, condition, mod, gain, down, up, qkv, skip, out):
    low, full = jnp.bfloat16, jnp.float32
    frames, wide = joined.shape[1:]
    columns = condition.shape[1]
    deep = up.shape[1] // ROWS
    held = dict(
        output=output,
        joined=joined,
        condition=condition,
        mod=mod,
        gain=gain,
        down=down,
        up=up,
        qkv=qkv,
        skip=skip,
        out=out,
    )
    given = dict(
        output_back=(output.shape, low),
        grad_inputs=((frames, 2 * wide), full),
        grad_skipped=((frames, 2 * wide), full),
        grad_skip=((RING * skip.shape[1], skip.shape[2]), full),
        grad_mod=((columns, RING * mod.shape[3]), full),
        grad_qkv=((RING * deep, ROWS * qkv.shape[2]), full),
        grad_out=((RING * out.shape[1], out.shape[2]), full),
        grad_gain=((1, columns), full),
        grad_up=((RING * deep, ROWS * up.shape[2]), full),
        grad_down=((RING * down.shape[1], down.shape[2]), full),
    )
    buffers = dict(
        joined_out=((2, frames, 2 * wide), full),
        mod_out=given["grad_mod"],
        down_out=given["grad_down"],
        up_out=given["grad_up"],
        qkv_out=given["grad_qkv"],
        skip_out=given["grad_skip"],
        out_out=given["grad_out"],
    )
    sems = dict(out_sem=(5, 4), small_sem=(7,))
    names = [*held, *given, *buffers, *sems]
    vmem = pl.BlockSpec(memory_space=pltpu.VMEM)
    anywhere = pl.BlockSpec(memory_space=pl.ANY)
    return pl.pallas_call(
        functools.partial(finish_kernel, names),
        out_shape=[jax.ShapeDtypeStruct(*spec) for spec in given.values()],
        in_specs=[vmem] * len(held),
        out_specs=[vmem if name == "grad_gain" else anywhere for name in given],
        scratch_shapes=[pltpu.VMEM(*spec) for spec in buffers.values()]
        + [pltpu.SemaphoreType.DMA(shape) for shape in sems.values()],
        compiler_params=pltpu.CompilerParams(vmem_limit_bytes=LAST_MIB * 1024 * 1024),
    )(*held.values())


def per_device_block(
    inputs,
    skipped,
    w_skip,
    w_mod,
    w_qkv,
    w_out,
    ff_gain,
    w_up,
    w_down,
    cotangent,
    lengths,
    flow_steps,
):
    finished = block_call(
        inputs[0],
        skipped[0],
        w_skip,
        w_mod,
        w_qkv,
        w_out,
        w_up,
        w_down,
        cotangent[0],
        ff_gain,
        lengths,
        flow_steps,
    )
    output, grad_inputs, grad_skipped, skip, mod, qkv, out, gain, up, down = finish_call(*finished)
    return (
        output[None],
        grad_inputs[None],
        grad_skipped[None],
        skip,
        mod,
        qkv,
        out,
        gain[0],
        up,
        down,
    )


def solution(mesh):
    placed = (
        P("grp", "blk", None),
        P("grp", "blk", None),
        P("grp", None),
        P("grp", None),
        P("grp", None),
        P("grp", None),
        P("grp"),
        P("grp", None),
        P("grp", None),
        P("grp", "blk", None),
        P("grp", None),
        P("grp", None),
    )
    body = per_device
    if mesh.shape["blk"] == RING and mesh.shape["grp"] == ROWS:
        body = per_device_block
    return jax.shard_map(
        body,
        mesh=mesh,
        in_specs=placed,
        out_specs=(
            P("grp", "blk", None),
            P("grp", "blk", None),
            P("grp", "blk", None),
            P("grp", None),
            P("grp", None),
            P("grp", None),
            P("grp", None),
            P("grp"),
            P("grp", None),
            P("grp", None),
        ),
        check_vma=False,
    )
```

```python
import functools
import math
import types

import jax
import jax.numpy as jnp
from jax import lax
from jax.experimental import pallas as pl
from jax.experimental.pallas import tpu as pltpu
from jax.sharding import PartitionSpec as P

HEADS = 16
HEAD_DIM = 64
STEPS = 32


EPSILON = 1e-06
NEGATIVE = -1e30
HIGHEST = lax.Precision.HIGHEST
MESH = pl.DeviceIdType.MESH
RING = 8
ROWS = 4


def from_behind(block, axis, distance):
    devices = range(lax.axis_size(axis))
    route = [((i - distance) % len(devices), i) for i in devices]
    return lax.ppermute(block, axis, route)


def layout(lengths_row, frames):
    end_frame = jnp.cumsum(lengths_row)
    start_frame = end_frame - lengths_row
    segment = jnp.sum((frames[:, None] >= end_frame[None, :]).astype(jnp.int32), axis=1)
    chosen = segment[:, None] == jnp.arange(lengths_row.shape[0], dtype=jnp.int32)[None, :]
    position = frames - jnp.sum(jnp.where(chosen, start_frame[None, :], 0), axis=1)
    return (segment, position)


def flow_condition(steps_row, model_width):
    half_width = model_width // 2
    rate_table = jnp.exp(
        -math.log(10000.0) * jnp.arange(half_width, dtype=jnp.float32) / half_width
    )
    angles = 1000.0 * (steps_row.astype(jnp.float32) / STEPS)[:, None] * rate_table[None, :]
    return jax.nn.silu(jnp.concatenate([jnp.sin(angles), jnp.cos(angles)], axis=1))


def rotation_tables(position, head_width):
    half_width = head_width // 2
    rate_table = jnp.exp(
        -math.log(10000.0) * jnp.arange(half_width, dtype=jnp.float32) / half_width
    )
    angles = position.astype(jnp.float32)[:, None] * rate_table[None, :]
    return (jnp.cos(angles)[:, None, :], jnp.sin(angles)[:, None, :], half_width)


def rotate(head_block, position):
    cosine_part, sine_part, half_width = rotation_tables(position, head_block.shape[-1])
    first_half = head_block[..., :half_width]
    second_half = head_block[..., half_width:]
    return jnp.concatenate(
        [
            first_half * cosine_part - second_half * sine_part,
            second_half * cosine_part + first_half * sine_part,
        ],
        axis=-1,
    )


def rotate_back(head_block, position):
    cosine_part, sine_part, half_width = rotation_tables(position, head_block.shape[-1])
    first_half = head_block[..., :half_width]
    second_half = head_block[..., half_width:]
    return jnp.concatenate(
        [
            first_half * cosine_part + second_half * sine_part,
            second_half * cosine_part - first_half * sine_part,
        ],
        axis=-1,
    )


def normalize(hidden):
    centred = hidden - jnp.mean(hidden, axis=-1, keepdims=True)
    scaled = lax.rsqrt(jnp.mean(centred * centred, axis=-1, keepdims=True) + EPSILON)
    return (centred * scaled, scaled)


def norm_back(grad_normal, normal, scaled):
    centred_grad = grad_normal - jnp.mean(grad_normal, axis=-1, keepdims=True)
    return scaled * (centred_grad - normal * jnp.mean(grad_normal * normal, axis=-1, keepdims=True))


def exact_gelu(values_in):
    return jax.nn.gelu(values_in, approximate=False)


def contract_rows(left_side, right_side):
    return lax.dot_general(
        left_side, right_side, (((0,), (0,)), ((), ())), preferred_element_type=jnp.float32
    )


def heads_of(flat_block):
    return flat_block.reshape(flat_block.shape[0], HEADS, HEAD_DIM)


def per_device(
    inputs,
    skipped,
    w_skip,
    w_mod,
    w_qkv,
    w_out,
    ff_gain,
    w_up,
    w_down,
    cotangent,
    lengths,
    flow_steps,
):
    w_skip, w_mod, w_qkv, w_out, ff_gain, w_up, w_down = (
        lax.all_gather(w_skip, "grp", axis=0, tiled=True),
        lax.all_gather(w_mod, "grp", axis=0, tiled=True),
        lax.all_gather(w_qkv, "grp", axis=0, tiled=True),
        lax.all_gather(w_out, "grp", axis=0, tiled=True),
        lax.all_gather(ff_gain, "grp", axis=0, tiled=True),
        lax.all_gather(w_up, "grp", axis=0, tiled=True),
        lax.all_gather(w_down, "grp", axis=0, tiled=True),
    )
    frame_count = inputs.shape[1]
    model_width = inputs.shape[2]
    cycle_size = lax.axis_size("blk")
    device_rank = lax.axis_index("blk")
    score_scale = HEAD_DIM ** (-0.5)
    local_frames = jnp.arange(frame_count, dtype=jnp.int32)
    lengths_row = lengths[0]
    own_segment, own_position = layout(lengths_row, device_rank * frame_count + local_frames)

    def segment_of(source):
        return layout(lengths_row, source * frame_count + local_frames)[0]

    def scored(query_block, key_block, query_segment, key_segment):
        raw_scores = (
            jnp.einsum(
                "qhd,khd->hqk",
                heads_of(query_block),
                heads_of(key_block),
                preferred_element_type=jnp.float32,
            )
            * score_scale
        )
        allowed = (query_segment[:, None] == key_segment[None, :])[None]
        return (raw_scores, allowed)

    joined = jnp.concatenate([inputs[0], skipped[0]], axis=1)
    hidden = jnp.dot(joined, w_skip, preferred_element_type=jnp.float32)
    condition = flow_condition(flow_steps[0], model_width).astype(jnp.bfloat16)
    modulation = jnp.dot(condition, w_mod, preferred_element_type=jnp.float32)
    picker = (
        own_segment[:, None] == jnp.arange(lengths_row.shape[0], dtype=jnp.int32)[None, :]
    ).astype(jnp.float32)
    per_frame = jnp.dot(picker, modulation, precision=HIGHEST)
    scale_one = 1.0 + per_frame[:, :model_width]
    normal_one, spread_one = normalize(hidden)
    attn_in = (normal_one * scale_one + per_frame[:, model_width:]).astype(jnp.bfloat16)
    project = jnp.dot(attn_in, w_qkv, preferred_element_type=jnp.float32).reshape(
        frame_count, 3, HEADS, HEAD_DIM
    )
    queries = (
        rotate(project[:, 0], own_position).astype(jnp.bfloat16).reshape(frame_count, model_width)
    )
    keys_own = (
        rotate(project[:, 1], own_position).astype(jnp.bfloat16).reshape(frame_count, model_width)
    )
    values_own = project[:, 2].astype(jnp.bfloat16).reshape(frame_count, model_width)

    def forward_turn(turn_index, carried):
        key_now, value_now, running_top, running_total, running_sum = carried
        source = (device_rank - turn_index) % cycle_size
        raw_scores, allowed = scored(queries, key_now, own_segment, segment_of(source))
        raw_scores = jnp.where(allowed, raw_scores, NEGATIVE)
        new_top = jnp.maximum(running_top, jnp.max(raw_scores, axis=2, keepdims=True))
        weights = jnp.where(allowed, jnp.exp(raw_scores - new_top), 0.0)
        shrink = jnp.exp(running_top - new_top)
        running_total = running_total * shrink + jnp.sum(weights, axis=2, keepdims=True)
        running_sum = running_sum * shrink + jnp.einsum(
            "hqk,khd->hqd",
            weights.astype(jnp.bfloat16),
            heads_of(value_now),
            preferred_element_type=jnp.float32,
        )
        key_now, value_now = from_behind((key_now, value_now), "blk", 1)
        return (key_now, value_now, new_top, running_total, running_sum)

    initial = (
        keys_own,
        values_own,
        jnp.full((HEADS, frame_count, 1), NEGATIVE, jnp.float32),
        jnp.zeros((HEADS, frame_count, 1), jnp.float32),
        jnp.zeros((HEADS, frame_count, HEAD_DIM), jnp.float32),
    )
    finished = lax.fori_loop(0, cycle_size, forward_turn, initial)
    running_top, running_total, running_sum = (finished[2], finished[3], finished[4])
    attended = jnp.transpose(running_sum / running_total, (1, 0, 2)).reshape(
        frame_count, model_width
    )
    log_total = (running_top + jnp.log(running_total))[:, :, 0]
    attended_low = attended.astype(jnp.bfloat16)
    hidden_two = hidden + jnp.dot(attended_low, w_out, preferred_element_type=jnp.float32)
    normal_two, spread_two = normalize(hidden_two)
    gain_vector = ff_gain.astype(jnp.float32)
    ff_in = (normal_two * gain_vector).astype(jnp.bfloat16)
    widened = jnp.dot(ff_in, w_up, preferred_element_type=jnp.float32)
    activated, gelu_back = jax.vjp(exact_gelu, widened)
    activated_low = activated.astype(jnp.bfloat16)
    output = (
        hidden_two + jnp.dot(activated_low, w_down, preferred_element_type=jnp.float32)
    ).astype(jnp.bfloat16)
    upstream = cotangent[0]
    grad_down = contract_rows(activated_low, upstream)
    grad_activated = jnp.dot(upstream, w_down.T, preferred_element_type=jnp.float32)
    grad_widened = gelu_back(grad_activated)[0].astype(jnp.bfloat16)
    grad_up = contract_rows(ff_in, grad_widened)
    grad_ff_in = jnp.dot(grad_widened, w_up.T, preferred_element_type=jnp.float32)
    grad_gain = jnp.sum(grad_ff_in * normal_two, axis=0)
    grad_hidden_two = upstream.astype(jnp.float32) + norm_back(
        grad_ff_in * gain_vector, normal_two, spread_two
    )
    grad_two_low = grad_hidden_two.astype(jnp.bfloat16)
    grad_out = contract_rows(attended_low, grad_two_low)
    grad_attended = jnp.dot(grad_two_low, w_out.T, preferred_element_type=jnp.float32).astype(
        jnp.bfloat16
    )
    delta = jnp.transpose(jnp.sum(heads_of(grad_attended.astype(jnp.float32) * attended), axis=2))
    zero_grad = jnp.zeros((frame_count, model_width), jnp.float32)

    def pair_terms(
        query_block,
        upstream_block,
        key_block,
        value_block,
        total_block,
        delta_block,
        query_segment,
        key_segment,
    ):
        raw_scores, allowed = scored(query_block, key_block, query_segment, key_segment)
        prob_block = jnp.where(allowed, jnp.exp(raw_scores - total_block[:, :, None]), 0.0)
        value_term = jnp.einsum(
            "hqk,qhd->khd",
            prob_block.astype(jnp.bfloat16),
            heads_of(upstream_block),
            preferred_element_type=jnp.float32,
        ).reshape(frame_count, model_width)
        prob_grad = jnp.einsum(
            "qhd,khd->hqk",
            heads_of(upstream_block),
            heads_of(value_block),
            preferred_element_type=jnp.float32,
        )
        score_grad = (prob_block * (prob_grad - delta_block[:, :, None])).astype(jnp.bfloat16)
        query_term = (
            jnp.einsum(
                "hqk,khd->qhd", score_grad, heads_of(key_block), preferred_element_type=jnp.float32
            ).reshape(frame_count, model_width)
            * score_scale
        )
        key_term = (
            jnp.einsum(
                "hqk,qhd->khd",
                score_grad,
                heads_of(query_block),
                preferred_element_type=jnp.float32,
            ).reshape(frame_count, model_width)
            * score_scale
        )
        return (query_term, key_term, value_term)

    def keys_turn(turn_index, carried):
        key_now, value_now, key_grad, value_grad, query_grad = carried
        source = (device_rank - turn_index) % cycle_size
        query_term, key_term, value_term = pair_terms(
            queries,
            grad_attended,
            key_now,
            value_now,
            log_total,
            delta,
            own_segment,
            segment_of(source),
        )
        key_now, value_now = from_behind((key_now, value_now), "blk", 1)
        key_grad, value_grad = (
            from_behind((key_grad + key_term).astype(jnp.bfloat16), "blk", 1).astype(jnp.float32),
            from_behind((value_grad + value_term).astype(jnp.bfloat16), "blk", 1).astype(
                jnp.float32
            ),
        )
        return (key_now, value_now, key_grad, value_grad, query_grad + query_term)

    done = lax.fori_loop(
        0, cycle_size, keys_turn, (keys_own, values_own, zero_grad, zero_grad, zero_grad)
    )
    key_grad, value_grad, query_grad = (done[2], done[3], done[4])
    grad_project = jnp.concatenate(
        [
            rotate_back(heads_of(query_grad), own_position).reshape(frame_count, model_width),
            rotate_back(heads_of(key_grad), own_position).reshape(frame_count, model_width),
            value_grad,
        ],
        axis=1,
    ).astype(jnp.bfloat16)
    grad_qkv = contract_rows(attn_in, grad_project)
    grad_attn_in = jnp.dot(grad_project, w_qkv.T, preferred_element_type=jnp.float32)
    mod_terms = jnp.concatenate([grad_attn_in * normal_one, grad_attn_in], axis=1)
    grad_modulation = jnp.dot(picker.T, mod_terms, precision=HIGHEST)
    grad_mod = jnp.dot(condition.astype(jnp.float32).T, grad_modulation, precision=HIGHEST)
    grad_hidden = grad_hidden_two + norm_back(grad_attn_in * scale_one, normal_one, spread_one)
    grad_hidden_low = grad_hidden.astype(jnp.bfloat16)
    grad_skip_weight = contract_rows(joined, grad_hidden_low)
    grad_joined = jnp.dot(grad_hidden_low, w_skip.T, preferred_element_type=jnp.float32)
    shards = (
        lax.psum_scatter(
            grad_skip_weight.astype(jnp.bfloat16), "grp", scatter_dimension=0, tiled=True
        ).astype(jnp.float32),
        lax.psum_scatter(
            grad_mod.astype(jnp.bfloat16), "grp", scatter_dimension=0, tiled=True
        ).astype(jnp.float32),
        lax.psum_scatter(
            grad_qkv.astype(jnp.bfloat16), "grp", scatter_dimension=0, tiled=True
        ).astype(jnp.float32),
        lax.psum_scatter(
            grad_out.astype(jnp.bfloat16), "grp", scatter_dimension=0, tiled=True
        ).astype(jnp.float32),
        lax.psum_scatter(
            grad_gain.astype(jnp.bfloat16), "grp", scatter_dimension=0, tiled=True
        ).astype(jnp.float32),
        lax.psum_scatter(
            grad_up.astype(jnp.bfloat16), "grp", scatter_dimension=0, tiled=True
        ).astype(jnp.float32),
        lax.psum_scatter(
            grad_down.astype(jnp.bfloat16), "grp", scatter_dimension=0, tiled=True
        ).astype(jnp.float32),
    )
    totals = lax.psum(
        (shards[0], shards[1], shards[2], shards[3], shards[4], shards[5], shards[6]), "blk"
    )
    return (
        output[None],
        grad_joined[:, :model_width][None],
        grad_joined[:, model_width:][None],
        totals[0],
        totals[1],
        totals[2],
        totals[3],
        totals[4],
        totals[5],
        totals[6],
    )


def dot_plain(left_side, right_side):
    return jnp.dot(left_side, right_side, preferred_element_type=jnp.float32)


def dot_across(left_side, right_side):
    return lax.dot_general(
        left_side, right_side, (((1,), (1,)), ((), ())), preferred_element_type=jnp.float32
    )


def ring_place(rank):
    odd = lax.rem(rank, 2)
    return (1 - odd) * (rank // 2) + odd * ((15 - rank) // 2)


def ring_rank(place):
    upper = place // 4
    return (1 - upper) * (2 * place) + upper * (15 - 2 * place)


TICKS = (2, 0, 0, 0, 0, 2, 3, 0, 0, 0, 2, 0, 0, 2, 3, 2, 3, 0, 0, 8, 5, 5, 5)

TILE = 128
UNROLLED = 4
MAIN_MIB = 55
LAST_MIB = 24
RING_TILE = 32


class Ring:
    def __init__(self, part, land, sems, rank, group_rank, turn=None):
        self.part, self.land, self.sems = part, land, sems
        self.rank, self.group_rank = rank, group_rank
        self.place = ring_place(rank)
        self.half = part.shape[1] // 2
        self.copies = {}
        self.turns, self.turn = [], turn

    def block_at(self, offset):
        return ring_rank(lax.rem(self.place + offset + 2 * RING, RING))

    def rows(self, way):
        return pl.ds(way * self.half, self.half)

    def send(self, kind, step, way, source, target):
        to = ring_rank(lax.rem(self.place + (1 if way == 0 else RING - 1), RING))
        copy = pltpu.make_async_remote_copy(
            src_ref=source,
            dst_ref=target,
            send_sem=self.sems.at[kind, 0, way, step],
            recv_sem=self.sems.at[kind, 1, way, step],
            device_id=(to, self.group_rank),
            device_id_type=MESH,
        )
        copy.start()
        self.copies[kind, step, way] = copy

    def sum_step(self, step):
        if step == 1:
            for way in range(2):
                self.copies[0, 0, way].wait_send()
        for way in range(2):
            block = self.block_at((-1 if way == 0 else 1) * (step + 1))
            rows = self.rows(way)
            if step > 0:
                self.copies[0, step - 1, way].wait_recv()
                tile = min(self.half, RING_TILE)

                def add(i, carry, way=way, block=block, tile=tile):
                    at = pl.ds(pl.multiple_of(way * self.half + i * tile, tile), tile)
                    total = self.part[block, at].astype(jnp.float32) + self.land[
                        step - 1, at
                    ].astype(jnp.float32)
                    self.land[step - 1, at] = total.astype(jnp.bfloat16)
                    return carry

                lax.fori_loop(0, self.half // tile, add, 0)
            if step < RING - 1:
                source = self.part.at[block, rows] if step == 0 else self.land.at[step - 1, rows]
                self.send(0, step, way, source, self.land.at[step, rows])

    def spread_step(self, step):
        if step == 0:
            self.close_sum()
        for way in range(2):
            block = self.block_at((-1 if way == 0 else 1) * step)
            rows = self.rows(way)
            if step > 0:
                self.copies[1, step - 1, way].wait_recv()
            if step < RING - 1:
                target = self.part.at[block, rows]
                self.send(1, step, way, target, target)

    def begin(self):
        self.sum_step(0)
        self.left = [functools.partial(self.sum_step, step) for step in range(1, RING)]
        self.left += [functools.partial(self.spread_step, step) for step in range(RING)]
        if self.turn is not None:
            self.left.insert(RING - 1, self.turn_out)

    def turn_out(self):
        place, sems = self.turn
        deep = self.part.shape[1] // ROWS

        def rows(group):
            return pl.ds(pl.multiple_of(group * deep, deep), deep)

        for other in (2, 1, 3):
            to = lax.rem(self.group_rank + other, ROWS)
            copy = pltpu.make_async_remote_copy(
                src_ref=self.land.at[RING - 2, rows(to)],
                dst_ref=place.at[rows(self.group_rank)],
                send_sem=sems.at[0, other - 1],
                recv_sem=sems.at[1, other - 1],
                device_id=(self.rank, to),
                device_id_type=MESH,
            )
            copy.start()
            self.turns.append(copy)
        place[rows(self.group_rank)] = self.land[RING - 2, rows(self.group_rank)]

    def close_sum(self):
        for copy in self.turns:
            copy.wait_recv()
        self.part[self.rank] = self.land[RING - 2] if self.turn is None else self.turn[0][...]

    def finish(self):
        for copy in self.turns:
            copy.wait_send()
        for (kind, step, _), copy in self.copies.items():
            if kind or step:
                copy.wait_send()


def block_kernel(names, *refs):
    n = types.SimpleNamespace(**dict(zip(names, refs)))
    low, full = jnp.bfloat16, jnp.float32
    rank, group_rank = lax.axis_index("blk"), lax.axis_index("grp")
    core, chip = lax.rem(group_rank, 2), group_rank // 2
    sibling = (rank, group_rank + 1 - 2 * core)
    across = (rank, group_rank + 2 - 4 * chip)
    frames, width = n.cotangent.shape
    half = 2 * frames
    columns = width // ROWS
    mine, theirs = core * half, (1 - core) * half
    own_slot = 2 * core + chip
    pair_row, pair_side = rank // 2, lax.rem(rank, 2)
    sent = []

    def lines(offset, size):
        return pl.ds(pl.multiple_of(offset, min(size, 128)), size)

    def slot_of(row):
        return 2 * lax.rem(row, 2) + row // 2

    def row_of(slot):
        return 2 * lax.rem(slot, 2) + slot // 2

    def group(other):
        return lax.rem(group_rank + other, ROWS)

    def block(other):
        return lax.rem(rank + other, RING)

    def link(source, target, send_sem, recv_sem, device):
        return pltpu.make_async_remote_copy(
            src_ref=source,
            dst_ref=target,
            send_sem=send_sem,
            recv_sem=recv_sem,
            device_id=device,
            device_id_type=MESH,
        )

    def push(source, target, sems, index, device):
        copy = link(source, target, sems.at[(0,) + index], sems.at[(1,) + index], device)
        copy.start()
        sent.append(copy)
        return copy

    def load(source, target, index):
        copy = pltpu.make_async_copy(source, target, n.load_sem.at[index])
        copy.start()
        return copy

    def tiles(count, tile, body):
        if count // tile <= UNROLLED:
            for i in range(count // tile):
                body(i * tile)
            return

        def step(i, carry):
            body(pl.multiple_of(i * tile, tile))
            return carry

        lax.fori_loop(0, count // tile, step, 0)

    joined_loads = [
        load((n.inputs, n.skipped)[t // 2].at[:, pl.ds((t % 2) * 512, 512)], n.joined_own.at[t], t)
        for t in range(ROWS)
    ]
    upstream_load = load(n.cotangent, n.upstream.at[lines(own_slot * frames, frames)], 4)
    skip_load = load(n.w_skip, n.skip_held, 5)
    mod_load = load(n.w_mod, n.mod_held, 6)
    out_place = n.out_held.at[lines(group_rank * columns, columns)]
    out_load = load(n.w_out, out_place, 7)
    down_load = load(n.w_down, n.down_held, 8)
    pieces = [(side, kind) for side in range(2) for kind in range(3)]

    def qkv_piece(target, side, kind, first, count):
        at = pl.multiple_of(kind * width + target * columns + side * 128, 128)
        return n.w_qkv.at[lines(first, count), pl.ds(at, 128)]

    def qkv_place(side, kind, first, count):
        rows = lines(group_rank * columns + first, count)
        return n.qkv_held.at[rows, pl.ds((side * 3 + kind) * 128, 128)]

    qkv_loads = [
        load(qkv_piece(group_rank, *piece, 0, columns), qkv_place(*piece, 0, columns), 9 + i)
        for i, piece in enumerate(pieces)
    ]
    hidden_units = n.up_held.shape[1]

    def up_piece(target):
        return n.w_up.at[:, pl.ds(pl.multiple_of(target * hidden_units, 128), hidden_units)]

    up_place = n.up_held.at[lines(group_rank * columns, columns)]
    up_load = load(up_piece(group_rank), up_place, 15)

    def small_tables():
        down = lax.broadcasted_iota(jnp.int32, (8, 128), 0)
        across_lanes = lax.rem(lax.broadcasted_iota(jnp.int32, (8, 128), 1), 64)
        zero = jnp.zeros((8, 128), full)
        step_tile, start_tile, end_tile = zero, zero, zero
        start_lane, end_lane = zero + 1e9, zero
        start = jnp.int32(0)
        for u in range(8):
            end = start + n.lengths[0, u]
            here = down == u
            lane_here = (across_lanes == u) | (across_lanes == u + 8)
            step_tile = jnp.where(here, n.flow_steps[0, u].astype(full), step_tile)
            start_tile = jnp.where(here, start.astype(full), start_tile)
            end_tile = jnp.where(here, end.astype(full), end_tile)
            start_lane = jnp.where(lane_here, start.astype(full), start_lane)
            end_lane = jnp.where(lane_here, end.astype(full), end_lane)
            start = end
        tables = (step_tile, start_tile, end_tile, start_lane, end_lane)
        for i, tile in enumerate(tables):
            n.small[i] = tile
        gain = jnp.broadcast_to(n.own_gain[...].astype(full).reshape(1, columns), (8, columns))
        n.small[5] = gain[:, 0:128]
        n.small[6] = gain[:, 128:256]

    barrier = pltpu.get_barrier_semaphore()
    for other in range(1, ROWS):
        pl.semaphore_signal(barrier, inc=1, device_id=(rank, group(other)), device_id_type=MESH)
    for other in range(1, RING):
        pl.semaphore_signal(barrier, inc=1, device_id=(block(other), group_rank), device_id_type=MESH)
    small_tables()
    for copy in joined_loads:
        copy.wait()
    pl.semaphore_wait(barrier, ROWS + RING - 2)

    joined_place = n.joined.at[lines(own_slot * frames, frames)]
    over_x = (group_rank + 2 - 4 * chip, 2 * (1 - chip) + 1 - core)
    joined_sends = [
        push(n.joined_own.at[to], joined_place, n.joined_sem, (i,), (rank, to))
        for i, to in enumerate((*over_x, sibling[1]))
    ]
    small_sends = [
        push(n.small, n.smalls.at[group_rank], n.small_sem, (o - 1,), (rank, group(o)))
        for o in (2, 1, 3)
    ]
    n.joined[lines(own_slot * frames, frames)] = n.joined_own[group_rank]
    n.smalls[group_rank] = n.small[...]
    def skip_rows(k):
        own_rows, their_rows = lines(mine + k * frames, frames), lines(theirs + k * frames, frames)
        rows = lines(k * frames, frames)
        n.send_one[rows] = dot_plain(n.joined[their_rows], n.skip_held[...]).astype(low)
        copy = push(n.send_one.at[rows], n.land_one.at[0, rows], n.first_sem, (0, k), sibling)
        kept = dot_plain(n.joined[own_rows], n.skip_held[...])
        copy.wait_recv()
        kept = kept + n.land_one[0, rows].astype(full)
        n.keep[rows] = kept
        n.send_two[rows] = kept.astype(low)
        return copy, push(n.send_two.at[rows], n.land_two.at[0, rows], n.second_sem, (0, k), across)

    skip_load.wait()
    joined_sends[2].wait_recv()
    skip_sums = [skip_rows(chip)]

    for copy in small_sends:
        copy.wait_recv()

    steps = jnp.concatenate([n.smalls[(0, 2, 1, 3)[s], 0] for s in range(ROWS)], axis=0)
    steps = jnp.concatenate([steps, steps], axis=1)
    lane = lax.broadcasted_iota(jnp.int32, steps.shape, 1) + lax.rem(group_rank, 2) * columns
    rate = jnp.exp(-math.log(10000.0) * lane.astype(full) / (width // 2))
    angles = 1000.0 * (steps / STEPS) * rate
    turned = jnp.where(group_rank >= 2, jnp.cos(angles), jnp.sin(angles))
    n.condition[...] = (turned / (1.0 + jnp.exp(-turned))).astype(low)
    mod_load.wait()

    def mod_tile(at):
        where = pl.ds(at, 512)
        n.mod_part[:, where] = dot_plain(n.condition[...], n.mod_held[:, where])

    tiles(2 * width, 512, mod_tile)
    mod_first = push(
        n.mod_part.at[pl.ds(pl.multiple_of(16 * (1 - core), 16), 16)], n.mod_land.at[0], n.mod_sem, (0,), sibling
    )

    gains = [n.smalls[r, 5 + i][0:1] for r in range(ROWS) for i in range(2)]
    n.gain[...] = jnp.broadcast_to(jnp.concatenate(gains, axis=1), n.gain.shape)

    def picked(row, first, count):
        spot = (lax.broadcasted_iota(jnp.int32, (count, 128), 0) + first).astype(full)
        return (spot >= n.smalls[row, 3][0:1]) & (spot < n.smalls[row, 4][0:1]), spot

    lanes = lax.broadcasted_iota(jnp.int32, (frames, 128), 1)
    turn_rate = jnp.exp(-math.log(10000.0) * lax.rem(lanes, 32).astype(full) / 32)
    turn_sign = jnp.where(lax.rem(lanes, 64) < 32, -1.0, 1.0)

    def turn_tables(row, first, cosine, sine, at):
        chosen, spot = picked(row, first, frames)
        start = jnp.where(chosen & (lanes < 8), n.smalls[row, 3][0:1], 0.0)
        position = spot - jnp.sum(start, axis=1, keepdims=True)
        angle = position * turn_rate
        cosine[at] = jnp.cos(angle)
        sine[at] = jnp.sin(angle) * turn_sign

    def swapped(value):
        ahead = pltpu.roll(value, 96, 1)
        behind = pltpu.roll(value, 32, 1)
        return jnp.where(lax.rem(lanes, 64) < 32, ahead, behind)

    def partial_sum(index, left_ref, right_tile):
        def to_send(at):
            n.send_one[:, pl.ds(at, 256)] = right_tile(left_ref[lines(theirs, half)], at).astype(low)

        def to_keep(at):
            n.keep[:, pl.ds(at, 256)] = right_tile(left_ref[lines(mine, half)], at)

        if index > 0:
            for copy in group_copies[index - 1][0]:
                copy.wait_send()
        tiles(width, 256, to_send)
        first = [
            push(
                n.send_one.at[pl.ds(k * frames, frames)],
                n.land_one.at[index, pl.ds(k * frames, frames)],
                n.first_sem,
                (index, k),
                sibling,
            )
            for k in range(2)
        ]
        tiles(width, 256, to_keep)
        return first

    def cross_sum(index, first):
        if index > 0:
            for copy in group_copies[index - 1][1]:
                copy.wait_send()
        second = []
        for k in range(2):
            first[k].wait_recv()

            def add(at, k=k):
                where = pl.ds(k * frames + at, TILE)
                total = n.keep[where] + n.land_one[index, where].astype(full)
                n.keep[where] = total
                n.send_two[where] = total.astype(low)

            tiles(frames, TILE, add)
            second.append(
                push(
                    n.send_two.at[pl.ds(k * frames, frames)],
                    n.land_two.at[index, pl.ds(k * frames, frames)],
                    n.second_sem,
                    (index, k),
                    across,
                )
            )
        group_copies[index] = (first, second)
        return second

    group_copies = {}

    down_ring, up_ring, out_ring, qkv_ring, skip_ring = rings = [
        Ring(part, land, sems, rank, group_rank, turn)
        for part, land, sems, turn in (
            (n.down_total, n.down_land, n.down_sem, None),
            (n.up_total, n.up_land, n.up_ring_sem, (n.up_turn, n.turn_sem.at[0])),
            (n.out_total, n.out_land, n.out_ring_sem, None),
            (n.qkv_total, n.qkv_land, n.qkv_ring_sem, (n.qkv_turn, n.turn_sem.at[1])),
            (n.skip_total, n.skip_land, n.skip_ring_sem, None),
        )
    ]
    running = []

    def begin(ring):
        ring.begin()
        running.append(ring)

    def ticks(count):
        for _ in range(count):
            if running:
                ring = running.pop(0)
                ring.left.pop(0)()
                if ring.left:
                    running.append(ring)

    def mean(value):
        return jnp.mean(value, axis=-1, keepdims=True)

    def share(buffer, k, sems, step=None):
        where = lines(mine + k * frames, frames)
        return push(buffer.at[where], buffer.at[where], sems, (k if step is None else step,), sibling)

    side_y, side_z = lax.rem(rank, 2), lax.rem(rank // 2, 2)
    to_y, to_z = 1 - 2 * side_y, 2 - 4 * side_z
    beside = (rank + to_y, group_rank)
    around = (beside, (rank + to_z, group_rank), (rank + to_y + to_z, group_rank))
    part_rows = columns // 2
    few_rows = columns // 4
    first_row = (2 * side_z + side_y) * few_rows
    qkv_sends = [
        [
            push(
                qkv_piece(to, *piece, first_row, few_rows),
                qkv_place(*piece, first_row, few_rows),
                n.qkv_sem,
                (i, j),
                (rank, to),
            )
            for j, piece in enumerate(pieces)
        ]
        for i, to in enumerate(over_x)
    ]
    qkv_sends.append(
        [
            push(
                qkv_piece(sibling[1], *piece, 0, columns),
                qkv_place(*piece, 0, columns),
                n.qkv_sem,
                (2, j),
                sibling,
            )
            for j, piece in enumerate(pieces)
        ]
    )

    mod_first.wait_recv()
    mod_mine = n.mod_part[pl.ds(pl.multiple_of(16 * core, 16), 16)] + n.mod_land[0]
    n.mod_send[...] = mod_mine.astype(low)
    mod_second = push(n.mod_send, n.mod_cross, n.mod_sem, (1,), across)
    for copy in joined_sends[:2]:
        copy.wait_recv()
    skip_sums.append(skip_rows(1 - chip))
    group_copies[0] = tuple(zip(*skip_sums))
    own_lines = lines(own_slot * frames, frames)
    for slot in range(ROWS):
        turn_tables(
            (0, 2, 1, 3)[slot],
            rank * frames,
            n.cosine,
            n.sine,
            pl.ds(slot * frames, frames),
        )
    mod_second.wait_recv()
    mod_total = n.mod_send[...].astype(full) + n.mod_cross[...].astype(full)
    for k in range(2):
        row = 2 * k + core
        values = mod_total[8 * k : 8 * k + 8]
        high = values.astype(low).astype(full)
        stack = jnp.concatenate([high, values - high], axis=0).astype(low)
        chosen = picked(row, rank * frames, frames)[0]
        picker = jnp.where(chosen, 1.0, 0.0).astype(low)[:, :16]
        where = pl.ds(k * frames, frames)
        n.scale_one[where] = 1.0 + dot_plain(picker, stack[:, :width])
        n.shift_one[where] = dot_plain(picker, stack[:, width:])

    qkv_passed = []
    for i, source in enumerate(over_x):
        for copy in qkv_sends[i]:
            copy.wait_recv()
        where = n.qkv_held.at[lines(source * columns + first_row, few_rows)]
        for j, to in enumerate(around):
            qkv_passed.append(push(where, where, n.qkv_pass_sem, (i, j), to))
    attn_sends = []
    for step in range(2):
        k = chip if step else 1 - chip
        skip_rows_here = lines(k * frames, frames)
        link(
            n.send_two.at[skip_rows_here],
            n.land_two.at[0, skip_rows_here],
            n.second_sem.at[0, 0, k],
            n.second_sem.at[1, 0, k],
            across,
        ).wait_recv()

        def norm_one(at, k=k):
            where = lines(k * frames + at, TILE)
            hidden = n.keep[where] + n.land_two[0, where].astype(full)
            n.hidden[where] = hidden
            centred = hidden - mean(hidden)
            spread = lax.rsqrt(mean(centred * centred) + EPSILON)
            normal = centred * spread
            n.normal_one[where] = normal
            n.spread_one[where] = jnp.broadcast_to(spread, (TILE, 128))
            n.attn_in[lines(mine + k * frames + at, TILE)] = (
                normal * n.scale_one[where] + n.shift_one[where]
            ).astype(low)

        tiles(frames, TILE, norm_one)
        attn_sends.append(share(n.attn_in, k, n.attn_sem, step))

    def part_of(reference, first):
        return reference.at[lines(first + side_y * part_rows, part_rows)]

    up_sends = [
        push(
            part_of(up_piece(to), 0),
            part_of(n.up_held, group_rank * columns),
            n.up_sem,
            (i,),
            (rank, to),
        )
        for i, to in enumerate(over_x)
    ]
    up_sends.append(push(up_piece(sibling[1]), up_place, n.up_sem, (2,), sibling))
    out_sends = [
        push(n.w_out, out_place, n.out_sem, (i,), device) for i, device in enumerate((across, sibling))
    ]

    def pass_on(buffer, copies, sems):
        passed = []
        for i, source in enumerate(over_x):
            copies[i].wait_recv()
            where = part_of(buffer, source * columns)
            passed.append(push(where, where, sems, (i,), beside))
        return passed

    upstream_load.wait()
    upstream_sends = [
        push(n.upstream.at[own_lines], n.upstream.at[own_lines], n.upstream_sem, (i,), device)
        for i, device in enumerate((across, sibling))
    ]

    for copy in qkv_loads:
        copy.wait()
    for copy in qkv_sends[2] + qkv_passed:
        copy.wait_recv()

    def to_heads(offset, value_of, target, sems, send_buffer, columns_of):
        for k in range(2):
            slot = offset // frames + k
            for side in range(2):
                to = 2 * row_of(slot) + side
                if value_of is not None:
                    send_buffer[to] = value_of(k, side, slot)

                @pl.when(to != rank)
                def _():
                    link(
                        send_buffer.at[to, :, columns_of],
                        target.at[lines(rank * frames, frames), columns_of],
                        sems.at[0, to],
                        sems.at[1, rank],
                        (to, group_rank),
                    ).start()

                @pl.when(to == rank)
                def _():
                    target[lines(rank * frames, frames), columns_of] = send_buffer[to, :, columns_of]

    def heads_arrive(target, sems, columns_of, then=None):
        for other in range(RING):
            source = block(other)
            if other:
                where = target.at[lines(source * frames, frames), columns_of]
                link(
                    where, where, sems.at[0, source], sems.at[1, source], (source, group_rank)
                ).wait_recv()
            if then is not None:
                then(pl.multiple_of(source * frames, frames))

    def project_half(offset):
        def project_tile(at):
            n.project[:, pl.ds(at, 256)] = dot_plain(
                n.attn_in[lines(offset, half)], n.qkv_held[:, pl.ds(at, 256)]
            )

        tiles(3 * columns, 256, project_tile)

        def value_of(k, side, slot):
            where = lines(slot * frames, frames)
            cosine, sine = n.cosine[where], n.sine[where]
            blocks = []
            for kind in range(3):
                value = n.project[pl.ds(k * frames, frames), pl.ds((side * 3 + kind) * 128, 128)]
                if kind < 2:
                    value = value * cosine + swapped(value) * sine
                blocks.append(value.astype(low))
            return jnp.concatenate(blocks, axis=1)

        to_heads(offset, value_of, n.paired, n.pair_sem, n.pair_send, pl.ds(0, 256))

    project_half(mine)
    for copy in attn_sends:
        copy.wait_recv()
    project_half(theirs)
    for offset in (mine, theirs):
        to_heads(offset, None, n.paired, n.value_sem, n.pair_send, pl.ds(256, 128))

    def row_tables(at):
        turn_tables(pair_row, at, n.row_cosine, n.row_sine, pl.ds(at, frames))
        chosen = jnp.where(picked(pair_row, at, frames)[0], 1.0, 0.0)
        n.chosen[pl.ds(at, frames)] = chosen.astype(low)

    tiles(RING * frames, frames, row_tables)
    def masked_parts(at):
        where = pl.ds(at, frames)
        query, key = n.paired[where, 0:128], n.paired[where, 128:256]
        chosen = n.chosen[where]
        first_head = lanes < 64
        blocked = jnp.where(
            lax.rem(lanes, 64) < 8, NEGATIVE * (1.0 - chosen.astype(full)), 0.0
        ).astype(low)
        scaled = (query.astype(full) * HEAD_DIM ** (-0.5)).astype(low)
        n.query_head[0, where] = jnp.where(first_head, scaled, chosen)
        n.query_head[1, where] = jnp.where(first_head, chosen, scaled)
        n.key_head[0, where] = jnp.where(first_head, key, blocked)
        n.key_head[1, where] = jnp.where(first_head, blocked, key)

    heads_arrive(n.paired, n.pair_sem, pl.ds(0, 256), masked_parts)
    up_passed = pass_on(n.up_held, up_sends, n.up_pass_sem)
    out_sends[0].wait_recv()
    where = n.out_held.at[lines(across[1] * columns, columns)]
    out_sends.append(push(where, where, n.out_sem, (2,), sibling))
    all_frames = RING * frames
    pair_place = (lines(slot_of(pair_row) * frames, frames), lines(pair_side * 128, 128))

    def score(at):
        where = pl.ds(at, half)
        for head in range(2):
            scores = dot_across(n.query_head[head, where], n.key_head[head])
            top = jnp.max(scores, axis=1, keepdims=True)
            weights = jnp.exp(scores - top)
            total = jnp.sum(weights, axis=1, keepdims=True)
            n.shares[head, where] = (weights * (1.0 / total)).astype(low)

    tiles(all_frames, half, score)
    heads_arrive(n.paired, n.value_sem, pl.ds(256, 128))

    def attend(at):
        where = pl.ds(at, half)
        sums = [dot_plain(n.shares[head, where], n.paired[:, 256:384]) for head in range(2)]
        first_head = lax.broadcasted_iota(jnp.int32, (half, 128), 1) < 64
        value = jnp.where(first_head, sums[0], sums[1])
        n.attended_pair[where] = value
        n.attended_send[where] = value.astype(low)
        for k in range(2):
            to = at // frames + k
            place = lines(at + k * frames, frames)

            @pl.when(to != rank)
            def _():
                link(
                    n.attended_send.at[place],
                    n.attended.at[pair_place],
                    n.attended_sem.at[0, to],
                    n.attended_sem.at[1, rank],
                    (to, group_rank),
                ).start()

            @pl.when(to == rank)
            def _():
                n.attended[pair_place] = n.attended_send[place]

    tiles(all_frames, half, attend)

    def pairs_arrive(buffer, sems, pitch, first, wide):
        for other in range(1, RING):
            source = block(other)
            where = buffer.at[
                lines(slot_of(source // 2) * frames, frames),
                pl.ds(pl.multiple_of(lax.rem(source, 2) * pitch + first, 128), wide),
            ]
            link(where, where, sems.at[0, source], sems.at[1, source], (source, group_rank)).wait_recv()

    upstream_sends[0].wait_recv()
    other_lines = lines((2 * core + 1 - chip) * frames, frames)
    upstream_sends.append(
        push(n.upstream.at[other_lines], n.upstream.at[other_lines], n.upstream_sem, (2,), sibling)
    )
    pairs_arrive(n.attended, n.attended_sem, 128, 0, 128)

    own_columns = pl.ds(pl.multiple_of(group_rank * columns, columns), columns)
    attended_sends = [
        push(
            n.attended.at[lines(first, half)],
            n.attended_all.at[:, own_columns],
            n.attended_all_sem,
            (i,),
            (rank, to),
        )
        for i, (first, to) in enumerate(
            ((mine, over_x[0]), (theirs, over_x[1]), (theirs, sibling[1]))
        )
    ]
    n.attended_all[:, own_columns] = n.attended[lines(mine, half)]
    out_load.wait()
    for copy in out_sends[1:] + attended_sends:
        copy.wait_recv()

    def out_tile(at):
        n.keep[:, pl.ds(at, 256)] = dot_plain(n.attended_all[...], n.out_held[:, pl.ds(at, 256)])

    tiles(width, 256, out_tile)
    ff_sends = []
    for k in range(2):

        def norm_two(at, k=k):
            where = pl.ds(k * frames + at, TILE)
            hidden = n.hidden[where] + n.keep[where]
            n.hidden[where] = hidden
            centred = hidden - mean(hidden)
            spread = lax.rsqrt(mean(centred * centred) + EPSILON)
            normal = centred * spread
            n.normal_two[where] = normal
            n.spread_two[where] = jnp.broadcast_to(spread, (TILE, 128))
            n.ff_in[lines(mine + k * frames + at, TILE)] = (normal * n.gain[0:1]).astype(low)

        tiles(frames, TILE, norm_two)
        ff_sends.append(share(n.ff_in, k, n.ff_sem))

    up_load.wait()
    down_load.wait()
    for copy in up_sends[2:] + up_passed:
        copy.wait_recv()
    for copy in upstream_sends[1:]:
        copy.wait_recv()

    def feed_half(offset):
        where = lines(offset, half)

        def feed_tile(at):
            widened = dot_plain(n.ff_in[where], n.up_held[:, pl.ds(at, 256)])
            grad = dot_across(n.upstream[where], n.down_held[pl.ds(at, 256)])
            share_of = 0.5 * (1.0 + lax.erf(widened * math.sqrt(0.5)))
            slope = share_of + widened * jnp.exp(-0.5 * widened * widened) * (
                1.0 / math.sqrt(2.0 * math.pi)
            )
            n.activated[where, pl.ds(at, 256)] = (widened * share_of).astype(low)
            n.grad_widened[where, pl.ds(at, 256)] = (grad * slope).astype(low)

        tiles(hidden_units, 256, feed_tile)

    feed_half(mine)
    for copy in ff_sends:
        copy.wait_recv()
    feed_half(theirs)
    first = partial_sum(
        1, n.grad_widened, lambda left, at: dot_across(left, n.up_held[pl.ds(at, 256)])
    )
    second = cross_sum(1, first)

    def down_tile(at):
        value = contract_rows(n.activated[:, pl.ds(at, 256)], n.upstream[...]).astype(low)
        n.down_total[at // 128] = value[:128]
        n.down_total[at // 128 + 1] = value[128:]

    tiles(hidden_units, 256, down_tile)
    begin(down_ring)

    def up_tile(at):
        value = contract_rows(n.ff_in[:, pl.ds(at, columns)], n.grad_widened[...]).astype(low)
        deep = columns // RING
        for j in range(RING):
            n.up_total[j, pl.ds(pl.multiple_of(at // RING, deep), deep)] = value[
                j * deep : (j + 1) * deep
            ]

    tiles(width, columns, up_tile)
    begin(up_ring)
    ticks(TICKS[0])

    gain_sums = jnp.zeros((1, width), full)
    grad_sends = []
    for k in range(2):
        second[k].wait_recv()
        weight = (1 - jnp.abs(chip - k)).astype(full)

        def back_two(i, sums, k=k, weight=weight):
            at = pl.multiple_of(i * TILE, TILE)
            where = pl.ds(k * frames + at, TILE)
            grad = n.keep[where] + n.land_two[1, where].astype(full)
            normal = n.normal_two[where]
            scaled = grad * n.gain[0:1]
            back = n.spread_two[where][:, 0:1] * (
                scaled - mean(scaled) - normal * mean(scaled * normal)
            )
            total = n.upstream[lines(mine + k * frames + at, TILE)].astype(full) + back
            n.grad_two[where] = total
            n.grad_two_low[lines(mine + k * frames + at, TILE)] = total.astype(low)
            return sums + weight * jnp.sum(grad * normal, axis=0, keepdims=True)

        gain_sums = lax.fori_loop(0, frames // TILE, back_two, gain_sums)
        grad_sends.append(share(n.grad_two_low, k, n.grad_two_sem))
        ticks(TICKS[1 + k])
    n.mod_sums[8:16] = jnp.zeros((8, 2 * width), full)
    n.mod_sums[8:9, :width] = gain_sums

    def attended_half(offset):
        value = dot_across(
            n.grad_two_low[lines(offset, half)], n.out_held[lines(group_rank * columns, columns)]
        ).astype(low)

        def value_of(k, side, slot):
            return value[k * frames : (k + 1) * frames, side * 128 : side * 128 + 128]

        to_heads(
            offset, value_of, n.grad_pair, n.grad_pair_sem, n.grad_pair_send, pl.ds(0, 128)
        )

    attended_half(mine)
    ticks(TICKS[3])
    for copy in grad_sends:
        copy.wait_recv()
    attended_half(theirs)
    ticks(TICKS[4])
    value = contract_rows(n.attended[...], n.grad_two_low[...]).astype(low)
    for j in range(RING):
        n.out_total[j] = value[j * 32 : (j + 1) * 32]
    ticks(TICKS[5])

    ticks(TICKS[7])

    def turn_queries(at):
        where = pl.ds(at, frames)
        n.query_turned[:, where] = jnp.transpose(n.paired[where, 0:128].astype(full)).astype(low)

    tiles(RING * frames, frames, turn_queries)

    def turn_upstream(at):
        where = pl.ds(at, frames)
        n.grad_turned[:, where] = jnp.transpose(n.grad_pair[where].astype(full)).astype(low)

    heads_arrive(n.grad_pair, n.grad_pair_sem, pl.ds(0, 128), turn_upstream)
    n.key_turned[...] = jnp.zeros(n.key_turned.shape, full)
    n.value_turned[...] = jnp.zeros(n.value_turned.shape, full)

    def back_turned(value, where):
        return value * n.row_cosine[where] - swapped(value) * n.row_sine[where]

    project_slot = lines(slot_of(pair_row) * frames, frames)

    def project_back(to, place, first, wide, sems):
        source = n.project_send.at[place, pl.ds(first, wide)]
        at = pl.ds(pl.multiple_of(pair_side * 384 + first, 128), wide)

        @pl.when(to != rank)
        def _():
            target = n.grad_project.at[project_slot, at]
            link(source, target, sems.at[0, to], sems.at[1, rank], (to, group_rank)).start()

        @pl.when(to == rank)
        def _():
            n.grad_project[project_slot, at] = source[...]

    def attend_back(at):
        where = pl.ds(at, half)
        first_head = lax.broadcasted_iota(jnp.int32, (half, 128), 1) < 64
        grad = n.grad_pair[where]
        product = grad.astype(full) * n.attended_pair[where]
        terms = []
        for head in range(2):
            here = first_head if head == 0 else jnp.logical_not(first_head)
            delta = jnp.sum(jnp.where(here, product, 0.0), axis=1, keepdims=True)
            grad_head = jnp.where(here, grad, jnp.zeros_like(grad))
            prob_grad = dot_across(grad_head, n.paired[:, 256:384])
            shares = n.shares[head, where]
            score_grad = (shares.astype(full) * (prob_grad - delta)).astype(low)
            terms.append(dot_plain(score_grad, n.paired[:, 128:256]))
            rows = pl.ds(head * 64, 64)
            n.value_turned[rows] += dot_plain(n.grad_turned[rows, where], shares)
            n.key_turned[rows] += dot_plain(n.query_turned[rows, where], score_grad)
        query_grad = jnp.where(first_head, terms[0], terms[1]) * HEAD_DIM ** (-0.5)
        for k in range(2):
            place = lines(at + k * frames, frames)
            n.project_send[place, 0:128] = back_turned(
                query_grad[k * frames : (k + 1) * frames], place
            ).astype(low)
            project_back(at // frames + k, place, 0, 128, n.query_sem)

    for part in range(4):
        attend_back(part * half)
        ticks(TICKS[8 + part])
    def keys_back(at):
        place = pl.ds(at, frames)
        key_grad = jnp.transpose(n.key_turned[:, place]) * HEAD_DIM ** (-0.5)
        n.project_send[place, 128:256] = back_turned(key_grad, place).astype(low)
        n.project_send[place, 256:384] = jnp.transpose(n.value_turned[:, place]).astype(low)
        project_back(at // frames, place, 128, 256, n.project_sem)

    tiles(all_frames, frames, keys_back)

    ticks(TICKS[12])

    ticks(TICKS[13])
    pairs_arrive(n.grad_project, n.query_sem, 384, 0, 128)
    pairs_arrive(n.grad_project, n.project_sem, 384, 128, 256)

    first = partial_sum(
        2, n.grad_project, lambda left, at: dot_across(left, n.qkv_held[pl.ds(at, 256)])
    )
    second = cross_sum(2, first)
    ticks(TICKS[15])

    def qkv_tile(at):
        value = contract_rows(n.attn_in[:, pl.ds(at, columns)], n.grad_project[...]).astype(low)
        deep = columns // RING
        for j in range(RING):
            n.qkv_total[j, pl.ds(pl.multiple_of(at // RING, deep), deep)] = value[
                j * deep : (j + 1) * deep
            ]

    tiles(width, columns, qkv_tile)
    begin(qkv_ring)
    ticks(TICKS[16])
    hidden_sends = []
    for k in range(2):
        second[k].wait_recv()

        def back_one(at, k=k):
            where = pl.ds(k * frames + at, TILE)
            grad = n.keep[where] + n.land_two[2, where].astype(full)
            normal = n.normal_one[where]
            scaled = grad * n.scale_one[where]
            back = n.spread_one[where][:, 0:1] * (
                scaled - mean(scaled) - normal * mean(scaled * normal)
            )
            n.grad_hidden[lines(mine + k * frames + at, TILE)] = (n.grad_two[where] + back).astype(low)

            @pl.when(chip == k)
            def _():
                n.shift_one[pl.ds(at, TILE)] = grad * normal
                n.shift_one[pl.ds(frames + at, TILE)] = grad

        tiles(frames, TILE, back_one)
        hidden_sends.append(share(n.grad_hidden, k, n.grad_hidden_sem))
        ticks(TICKS[17 + k])

    for copy in hidden_sends:
        copy.wait_recv()

    def skip_weight_tile(at):
        value = contract_rows(n.joined[:, pl.ds(at, 256)], n.grad_hidden[...]).astype(low)
        for j in range(4):
            n.skip_total[at // 64 + j] = value[j * 64 : (j + 1) * 64]

    tiles(n.joined.shape[1], 256, skip_weight_tile)
    begin(skip_ring)
    begin(out_ring)
    ticks(TICKS[19])

    first = partial_sum(
        3, n.activated, lambda left, at: dot_plain(left, n.down_held[:, pl.ds(at, 256)])
    )
    ticks(TICKS[6])
    output_second = cross_sum(3, first)
    ticks(TICKS[14])
    spot = (lax.broadcasted_iota(jnp.int32, (8, frames), 1) + rank * frames).astype(full)
    chosen = (spot >= n.small[1]) & (spot < n.small[2])
    picker = jnp.where(chosen, 1.0, 0.0)

    def mod_sum(at):
        for part in range(2):
            n.mod_sums[0:8, pl.ds(part * width + at, 512)] = jnp.dot(
                picker, n.shift_one[pl.ds(part * frames, frames), pl.ds(at, 512)], precision=HIGHEST
            )

    tiles(width, 512, mod_sum)
    for other in range(1, RING):
        to = block(other)
        push(
            n.mod_sums.at[:, pl.ds(pl.multiple_of(to * 256, 256), 256)],
            n.sums_land.at[rank],
            n.sums_sem,
            (other - 1,),
            (to, group_rank),
        )
    sums_copies = sent[-(RING - 1) :]
    n.sums_land[rank] = n.mod_sums[:, pl.ds(pl.multiple_of(rank * 256, 256), 256)]
    ticks(TICKS[20])
    back = dot_across(n.grad_hidden[...], n.skip_held[...]).astype(low)
    n.joined_send[...] = back
    grad_joined_copies = []
    for other in (2, 1, 3):
        to = group(other)
        grad_joined_copies.append(
            push(
                n.joined_send.at[lines(slot_of(to) * frames, frames)],
                n.grad_joined.at[group_rank],
                n.grad_joined_sem,
                (other - 1,),
                (rank, to),
            )
        )
    n.grad_joined[group_rank] = n.joined_send[own_lines]
    ticks(TICKS[21])
    for copy in sums_copies:
        copy.wait_recv()
    n.sums_send[...] = jnp.sum(n.sums_land[...], axis=0).astype(low)
    n.mod_grad[rank, group_rank] = n.sums_send[...]
    group_sums = [
        push(
            n.sums_send,
            n.mod_grad.at[rank, group_rank],
            n.sums_group_sem,
            (other - 1,),
            (rank, group(other)),
        )
        for other in (2, 1, 3)
    ]
    ticks(TICKS[22])
    for copy in group_sums:
        copy.wait_recv()
    mod_spread = [
        push(
            n.mod_grad.at[rank],
            n.mod_grad.at[rank],
            n.sums_block_sem,
            (other - 1,),
            (block(other), group_rank),
        )
        for other in range(1, RING)
    ]

    for copy in output_second:
        copy.wait_recv()

    def finish_output(at):
        where = lines(chip * frames + at, TILE)
        n.output[pl.ds(at, TILE)] = (
            n.hidden[where] + n.keep[where] + n.land_two[3, where].astype(full)
        ).astype(low)

    tiles(frames, TILE, finish_output)
    ticks(5 * (2 * RING + 1))
    for ring in rings:
        ring.finish()
    for copy in mod_spread + grad_joined_copies:
        copy.wait_recv()
    gain_grad = n.mod_grad[group_rank, 0].astype(full)
    for row in range(1, ROWS):
        gain_grad = gain_grad + n.mod_grad[group_rank, row].astype(full)
    n.gain_grad[...] = gain_grad[8:16]
    for index, copy in enumerate(sent):
        if not any(copy is other for pair in list(group_copies.values())[:-1] for kind in pair for other in kind):
            copy.wait_send()
    for sems, wide in (
        (n.pair_sem, 256),
        (n.value_sem, 128),
        (n.attended_sem, 128),
        (n.grad_pair_sem, 128),
        (n.query_sem, 128),
        (n.project_sem, 256),
    ):
        for other in range(1, RING):
            to = block(other)
            where = n.project_send.at[lines(to * frames, frames), pl.ds(0, wide)]
            link(where, where, sems.at[0, to], sems.at[1, to], (to, group_rank)).wait_send()


def block_call(
    inputs,
    skipped,
    w_skip,
    w_mod,
    w_qkv,
    w_out,
    w_up,
    w_down,
    cotangent,
    own_gain,
    lengths,
    flow_steps,
):
    low, full = jnp.bfloat16, jnp.float32
    frames, width = inputs.shape
    tokens, half = ROWS * frames, 2 * frames
    columns = width // ROWS
    hidden_units = w_down.shape[0]
    joint = w_skip.shape[0]
    all_frames = RING * frames
    deep = width // RING

    held = dict(
        inputs=inputs,
        skipped=skipped,
        w_skip=w_skip,
        w_mod=w_mod,
        w_qkv=w_qkv,
        w_out=w_out,
        w_up=w_up,
        w_down=w_down,
        cotangent=cotangent,
        own_gain=own_gain,
        lengths=lengths,
        flow_steps=flow_steps,
    )
    given = dict(
        output=((frames, width), low),
        grad_joined=((ROWS, frames, joint), low),
        condition=((ROWS * 8, columns), low),
        mod_grad=((RING, ROWS, 16, 256), low),
        gain_grad=((8, columns), full),
        down_total=((RING, hidden_units // RING, width), low),
        up_total=((RING, deep, hidden_units), low),
        qkv_total=((RING, deep, 3 * columns), low),
        skip_total=((RING, joint // RING, width), low),
        out_total=((RING, columns // RING, width), low),
    )
    buffers = dict(
        joined_own=((ROWS, frames, joint), low),
        joined=((tokens, joint), low),
        upstream=((tokens, width), low),
        skip_held=(w_skip.shape, low),
        mod_held=(w_mod.shape, low),
        out_held=((width, width), low),
        attended_all=((half, width), low),
        down_held=(w_down.shape, low),
        qkv_held=((width, 3 * columns), low),
        up_held=((width, hidden_units), low),
        small=((7, 8, 128), full),
        smalls=((ROWS, 7, 8, 128), full),
        mod_part=((ROWS * 8, 2 * width), full),
        mod_land=((1, 16, 2 * width), full),
        mod_send=((16, 2 * width), low),
        mod_cross=((16, 2 * width), low),
        gain=((8, width), full),
        cosine=((tokens, 128), full),
        sine=((tokens, 128), full),
        row_cosine=((all_frames, 128), full),
        row_sine=((all_frames, 128), full),
        chosen=((all_frames, 128), low),
        send_one=((half, width), low),
        send_two=((half, width), low),
        keep=((half, width), full),
        land_one=((4, half, width), low),
        land_two=((4, half, width), low),
        scale_one=((half, width), full),
        shift_one=((half, width), full),
        hidden=((half, width), full),
        normal_one=((half, width), full),
        spread_one=((half, 128), full),
        normal_two=((half, width), full),
        spread_two=((half, 128), full),
        grad_two=((half, width), full),
        attn_in=((tokens, width), low),
        project=((half, 3 * columns), full),
        pair_send=((RING, frames, 384), low),
        paired=((all_frames, 384), low),
        query_head=((2, all_frames, 128), low),
        key_head=((2, all_frames, 128), low),
        query_turned=((128, all_frames), low),
        shares=((2, all_frames, all_frames), low),
        attended_pair=((all_frames, 128), full),
        attended_send=((all_frames, 128), low),
        attended=((tokens, columns), low),
        ff_in=((tokens, width), low),
        activated=((tokens, hidden_units), low),
        grad_widened=((tokens, hidden_units), low),
        grad_two_low=((tokens, width), low),
        grad_pair_send=((RING, frames, 128), low),
        grad_pair=((all_frames, 128), low),
        grad_turned=((128, all_frames), low),
        key_turned=((128, all_frames), full),
        value_turned=((128, all_frames), full),
        project_send=((all_frames, 384), low),
        grad_project=((tokens, 3 * columns), low),
        grad_hidden=((tokens, width), low),
        mod_sums=((16, 2 * width), full),
        sums_land=((RING, 16, 256), full),
        sums_send=((16, 256), low),
        joined_send=((tokens, joint), low),
        down_land=((RING - 1, hidden_units // RING, width), low),
        up_land=((RING - 1, deep, hidden_units), low),
        qkv_land=((RING - 1, deep, 3 * columns), low),
        skip_land=((RING - 1, joint // RING, width), low),
        out_land=((RING - 1, columns // RING, width), low),
        up_turn=((deep, hidden_units), low),
        qkv_turn=((deep, 3 * columns), low),
    )
    sems = dict(
        load_sem=(16,),
        joined_sem=(2, 3),
        small_sem=(2, 3),
        qkv_sem=(2, 3, 6),
        qkv_pass_sem=(2, 2, 3),
        up_sem=(2, 3),
        up_pass_sem=(2, 2),
        out_sem=(2, 3),
        attended_all_sem=(2, 3),
        mod_sem=(2, 2),
        first_sem=(2, 4, 2),
        second_sem=(2, 4, 2),
        upstream_sem=(2, 3),
        attn_sem=(2, 2),
        ff_sem=(2, 2),
        grad_two_sem=(2, 2),
        grad_hidden_sem=(2, 2),
        pair_sem=(2, RING),
        attended_sem=(2, RING),
        grad_pair_sem=(2, RING),
        query_sem=(2, RING),
        project_sem=(2, RING),
        value_sem=(2, RING),
        grad_joined_sem=(2, 3),
        sums_sem=(2, RING - 1),
        sums_group_sem=(2, 3),
        sums_block_sem=(2, RING - 1),
        down_sem=(2, 2, 2, RING - 1),
        up_ring_sem=(2, 2, 2, RING - 1),
        qkv_ring_sem=(2, 2, 2, RING - 1),
        skip_ring_sem=(2, 2, 2, RING - 1),
        out_ring_sem=(2, 2, 2, RING - 1),
        turn_sem=(2, 2, 3),
    )
    names = [*held, *given, *buffers, *sems]
    vmem = pl.BlockSpec(memory_space=pltpu.VMEM)
    anywhere = pl.BlockSpec(memory_space=pl.ANY)
    return pl.pallas_call(
        functools.partial(block_kernel, names),
        out_shape=[pltpu.VMEM(*spec) for spec in given.values()],
        in_specs=[anywhere] * 9 + [vmem] + [pl.BlockSpec(memory_space=pltpu.SMEM)] * 2,
        out_specs=[vmem] * len(given),
        scratch_shapes=[pltpu.VMEM(*spec) for spec in buffers.values()]
        + [pltpu.SemaphoreType.DMA(shape) for shape in sems.values()],
        compiler_params=pltpu.CompilerParams(
            collective_id=0,
            has_side_effects=True,
            vmem_limit_bytes=MAIN_MIB * 1024 * 1024,
        ),
    )(*held.values())


def finish_kernel(names, *refs):
    n = types.SimpleNamespace(**dict(zip(names, refs)))
    full = jnp.float32
    pieces = 4
    chunks = RING // pieces

    def start(source, target, sem):
        copy = pltpu.make_async_copy(source, target, sem)
        copy.start()
        return copy

    def widen_rows(source, target, p):
        deep, wide = source.shape[1:]
        target[pl.ds(p * chunks * deep, chunks * deep)] = (
            source[pl.ds(p * chunks, chunks)].astype(full).reshape(chunks * deep, wide)
        )

    def widen_columns(source, target, p):
        deep, wide = source.shape[1] // ROWS, source.shape[2]
        kinds = wide // 256 if wide % 1024 else 1
        step = 128 if kinds > 1 else wide
        for j in range(chunks):
            to = pl.ds((p * chunks + j) * deep, deep)
            for r in range(ROWS):
                value = source[p * chunks + j, pl.ds(r * deep, deep)].astype(full)
                for i in range(wide // step):
                    side, kind = i // kinds, i % kinds
                    at = kind * (ROWS * wide // kinds) + r * (wide // kinds) + side * step
                    target[to, pl.ds(at, step)] = value[:, i * step : (i + 1) * step]

    work = (
        (n.down, n.down_out, n.grad_down, widen_rows),
        (n.up, n.up_out, n.grad_up, widen_columns),
        (n.qkv, n.qkv_out, n.grad_qkv, widen_columns),
        (n.skip, n.skip_out, n.grad_skip, widen_rows),
        (n.out, n.out_out, n.grad_out, widen_rows),
    )
    sent = [start(n.output, n.output_back, n.small_sem.at[3])]
    for p in range(pieces):
        for i, (held, wide, target, widen) in enumerate(work):
            widen(held, wide, p)
            deep = target.shape[0] // pieces
            rows = pl.ds(p * deep, deep)
            sent.append(start(wide.at[rows], target.at[rows], n.out_sem.at[i, p]))
    for i in range(RING):
        sums = [n.mod[i, r].astype(full)[0:8] for r in (0, 2, 1, 3)]
        n.mod_out[:, pl.ds(i * 256, 256)] = contract_rows(
            n.condition[...], jnp.concatenate(sums, axis=0).astype(jnp.bfloat16)
        )
    sent.append(start(n.mod_out, n.grad_mod, n.small_sem.at[4]))
    wide = n.joined.shape[2]
    for r in range(ROWS):
        n.joined_out[r // 2, :, pl.ds((r % 2) * wide, wide)] = n.joined[r].astype(full)
    sent.append(start(n.joined_out.at[0], n.grad_inputs, n.small_sem.at[5]))
    sent.append(start(n.joined_out.at[1], n.grad_skipped, n.small_sem.at[6]))
    n.grad_gain[...] = n.gain[0:1]
    for copy in sent:
        copy.wait()


def finish_call(output, joined, condition, mod, gain, down, up, qkv, skip, out):
    low, full = jnp.bfloat16, jnp.float32
    frames, wide = joined.shape[1:]
    columns = condition.shape[1]
    deep = up.shape[1] // ROWS
    held = dict(
        output=output,
        joined=joined,
        condition=condition,
        mod=mod,
        gain=gain,
        down=down,
        up=up,
        qkv=qkv,
        skip=skip,
        out=out,
    )
    given = dict(
        output_back=(output.shape, low),
        grad_inputs=((frames, 2 * wide), full),
        grad_skipped=((frames, 2 * wide), full),
        grad_skip=((RING * skip.shape[1], skip.shape[2]), full),
        grad_mod=((columns, RING * mod.shape[3]), full),
        grad_qkv=((RING * deep, ROWS * qkv.shape[2]), full),
        grad_out=((RING * out.shape[1], out.shape[2]), full),
        grad_gain=((1, columns), full),
        grad_up=((RING * deep, ROWS * up.shape[2]), full),
        grad_down=((RING * down.shape[1], down.shape[2]), full),
    )
    buffers = dict(
        joined_out=((2, frames, 2 * wide), full),
        mod_out=given["grad_mod"],
        down_out=given["grad_down"],
        up_out=given["grad_up"],
        qkv_out=given["grad_qkv"],
        skip_out=given["grad_skip"],
        out_out=given["grad_out"],
    )
    sems = dict(out_sem=(5, 4), small_sem=(7,))
    names = [*held, *given, *buffers, *sems]
    vmem = pl.BlockSpec(memory_space=pltpu.VMEM)
    anywhere = pl.BlockSpec(memory_space=pl.ANY)
    return pl.pallas_call(
        functools.partial(finish_kernel, names),
        out_shape=[jax.ShapeDtypeStruct(*spec) for spec in given.values()],
        in_specs=[vmem] * len(held),
        out_specs=[vmem if name == "grad_gain" else anywhere for name in given],
        scratch_shapes=[pltpu.VMEM(*spec) for spec in buffers.values()]
        + [pltpu.SemaphoreType.DMA(shape) for shape in sems.values()],
        compiler_params=pltpu.CompilerParams(vmem_limit_bytes=LAST_MIB * 1024 * 1024),
    )(*held.values())


def per_device_block(
    inputs,
    skipped,
    w_skip,
    w_mod,
    w_qkv,
    w_out,
    ff_gain,
    w_up,
    w_down,
    cotangent,
    lengths,
    flow_steps,
):
    finished = block_call(
        inputs[0],
        skipped[0],
        w_skip,
        w_mod,
        w_qkv,
        w_out,
        w_up,
        w_down,
        cotangent[0],
        ff_gain,
        lengths,
        flow_steps,
    )
    output, grad_inputs, grad_skipped, skip, mod, qkv, out, gain, up, down = finish_call(*finished)
    return (
        output[None],
        grad_inputs[None],
        grad_skipped[None],
        skip,
        mod,
        qkv,
        out,
        gain[0],
        up,
        down,
    )


def solution(mesh):
    placed = (
        P("grp", "blk", None),
        P("grp", "blk", None),
        P("grp", None),
        P("grp", None),
        P("grp", None),
        P("grp", None),
        P("grp"),
        P("grp", None),
        P("grp", None),
        P("grp", "blk", None),
        P("grp", None),
        P("grp", None),
    )
    body = per_device
    if mesh.shape["blk"] == RING and mesh.shape["grp"] == ROWS:
        body = per_device_block
    return jax.shard_map(
        body,
        mesh=mesh,
        in_specs=placed,
        out_specs=(
            P("grp", "blk", None),
            P("grp", "blk", None),
            P("grp", "blk", None),
            P("grp", None),
            P("grp", None),
            P("grp", None),
            P("grp", None),
            P("grp"),
            P("grp", None),
            P("grp", None),
        ),
        check_vma=False,
    )
```
